32 devices in a mesh: shard: 8 (over z, y), rep: 4 (over x, core).
Axes of the slice: x: 2, y: 2, z: 4, core: 2. Of those that a mesh axis runs over, the one named last changes fastest.
Arguments:
- tokens: bfloat16 [64, 512, 768], P(('shard', 'rep')), may hold values from -6 to 6
- lengths: int32 [64], P(('shard', 'rep')), may hold values from 1 to 512, 20480 in all
- w_qkv: bfloat16 [768, 2304], P('shard'), may hold values from -0.21875 to 0.21875
- b_query: bfloat16 [768], P('shard'), may hold values from -3 to 3
- b_value: bfloat16 [768], P('shard'), may hold values from -3 to 3
- w_out: bfloat16 [768, 768], P('shard'), may hold values from -0.625 to 0.625
- b_out: bfloat16 [768], P('shard'), may hold values from -3 to 3
- ln1_gain: bfloat16 [768], P('shard'), may hold values from 0.5 to 1.5
- ln1_bias: bfloat16 [768], P('shard'), may hold values from -3 to 3
- w_up: bfloat16 [768, 3072], P('shard'), may hold values from -0.21875 to 0.21875
- b_up: bfloat16 [3072], P('shard'), may hold values from -3 to 3
- w_down: bfloat16 [3072, 768], P('shard'), may hold values from -0.109375 to 0.109375
- b_down: bfloat16 [768], P('shard'), may hold values from -3 to 3
- ln2_gain: bfloat16 [768], P('shard'), may hold values from 0.5 to 1.5
- ln2_bias: bfloat16 [768], P('shard'), may hold values from -3 to 3
- cotangent: bfloat16 [64, 512, 768], P(('shard', 'rep')), may hold values from -6 to 6
Outputs:
- layer_out: bfloat16 [64, 512, 768], P(('shard', 'rep'))
- input_grad: float32 [64, 512, 768], P(('shard', 'rep'))
- grad_w_qkv: float32 [768, 2304], P('shard')
- grad_b_query: float32 [768], P('shard')
- grad_b_value: float32 [768], P('shard')
- grad_w_out: float32 [768, 768], P('shard')
- grad_b_out: float32 [768], P('shard')
- grad_ln1_gain: float32 [768], P('shard')
- grad_ln1_bias: float32 [768], P('shard')
- grad_w_up: float32 [768, 3072], P('shard')
- grad_b_up: float32 [3072], P('shard')
- grad_w_down: float32 [3072, 768], P('shard')
- grad_b_down: float32 [768], P('shard')
- grad_ln2_gain: float32 [768], P('shard')
- grad_ln2_bias: float32 [768], P('shard')
The draws below stay inside these ranges and needn't reach their ends.
Inputs may be any that keep to these rules, and one draw needn't show every extreme that they name: `lengths`: each sequence has at least one token; they add up to 64 * 512 * 5 // 8 tokens, and the longest has exactly 512.
All inputs are finite; a program needn't handle non-finite values. No bound on the sum of `lengths` on one device may be relied on, other than what follows from the above.
Results may differ from the reference program's by a relative error of at most 0.017.
Values may be sent and summed in bfloat16 or wider, within the bound.
No kernel may reach another device: no remote copies, remote signals or barrier semaphores. Data moves between devices by JAX's collectives and lax.ppermute only.
A program may use at most 192 MiB of HBM per device.

```python
import math
import jax
import jax.numpy as jnp
import numpy as np
from jax import lax

D = 768
HEADS = 12
FF = 3072
HEAD_DIM = 64
SEQLEN = 512
SEQS = 64


def block_scale(stream_key, dims, pieces, least, largest):
    def one(dim, parts):
        draws = jax.random.uniform(jax.random.fold_in(jax.random.fold_in(stream_key, 6), dim), (parts,), jnp.float32, least / len(pieces), largest / len(pieces))
        return jnp.repeat(jnp.exp(draws), dims[dim] // parts).reshape((-1,) + (1,) * (len(dims) - dim - 1))

    factor_of = one(*pieces[0])
    for cut in pieces[1:]:
        factor_of = factor_of * one(*cut)
    return factor_of


def length_profile(amount, total, limit, skew):
    portions = [(1 << 20) // math.isqrt(rank ** skew) + 1 for rank in range(2, amount + 1)]
    spare, holding = total - limit - (amount - 1), [1] * (amount - 1)
    while spare > 0:
        candidates = [i for i in range(amount - 1) if holding[i] < limit]
        whole, remaining = sum([portions[i] for i in candidates]), spare
        for i in candidates:
            more = min(limit - holding[i], max(1, remaining * portions[i] // whole), spare)
            holding[i] = holding[i] + more
            spare = spare - more
    return np.array([limit] + holding)


def uneven_parts(key, count, total, most, skew):
    if count == 2:
        one = jax.random.randint(key, (), max(1, total - most), min(most, total - 1) + 1)
        return jnp.stack([one, total - one])
    sizes = jnp.asarray(length_profile(count, total, most, skew), jnp.int32)
    couples = (count - 1) // 2
    donor, taker = sizes[1:1 + 2 * couples:2], sizes[2:2 + 2 * couples:2]
    margin = jnp.minimum(donor - 1, most - taker)
    shifted = jax.random.randint(jax.random.fold_in(key, 1), (couples,), 0, 1 << 20) % (margin + 1)
    sizes = sizes.at[1:1 + 2 * couples:2].set(donor - shifted).at[2:2 + 2 * couples:2].set(taker + shifted)
    return sizes[jax.random.permutation(jax.random.fold_in(key, 2), count)]


def centred(rng, shape, scale, most, shards=(), held_as=jnp.bfloat16):
    array = scale * jax.random.normal(rng, shape, jnp.float32)
    if shards:
        array = array * block_scale(rng, shape, shards, -0.22, 0.18)
    return jnp.clip(array, -most, most).astype(held_as)


def setup_inputs(seed: int = 0) -> dict:
    streams_of = jax.random.split(jax.random.key(seed), 17)
    return {
        "tokens": centred(streams_of[0], (SEQS, SEQLEN, D), 1.0, 6.0, ((0, 32),)),
        "lengths": uneven_parts(streams_of[1], SEQS, SEQS * SEQLEN * 5 // 8, SEQLEN, 2).astype(jnp.int32),
        "w_qkv": centred(streams_of[2], (D, 3 * D), D ** -0.5, 0.21875, ((0, 8),)),
        "b_query": centred(streams_of[3], (D,), 0.5, 3.0, ((0, 8),)),
        "b_value": centred(streams_of[4], (D,), 0.5, 3.0, ((0, 8),)),
        "w_out": centred(streams_of[5], (D, D), (D // 8) ** -0.5, 0.625, ((0, 8),)),
        "b_out": centred(streams_of[6], (D,), 0.5, 3.0, ((0, 8),)),
        "ln1_gain": jnp.clip(1.0 + 0.1 * jax.random.normal(streams_of[7], (D,), jnp.float32), 0.5, 1.5).astype(jnp.bfloat16),
        "ln1_bias": centred(streams_of[8], (D,), 0.5, 3.0, ((0, 8),)),
        "w_up": centred(streams_of[9], (D, FF), D ** -0.5, 0.21875, ((0, 8),)),
        "b_up": centred(streams_of[10], (FF,), 0.5, 3.0, ((0, 8),)),
        "w_down": centred(streams_of[11], (FF, D), FF ** -0.5, 0.109375, ((0, 8),)),
        "b_down": centred(streams_of[12], (D,), 0.5, 3.0, ((0, 8),)),
        "ln2_gain": jnp.clip(1.0 + 0.1 * jax.random.normal(streams_of[13], (D,), jnp.float32), 0.5, 1.5).astype(jnp.bfloat16),
        "ln2_bias": centred(streams_of[14], (D,), 0.5, 3.0, ((0, 8),)),
        "cotangent": centred(streams_of[15], (SEQS, SEQLEN, D), 1.0, 6.0, ((0, 32),)),
    }


EPS = 1e-05
HIGH = lax.Precision.HIGHEST

@jax.custom_vjp
def low(v):
    return lax.optimization_barrier(v.astype(jnp.bfloat16)).astype(jnp.float32)

@jax.custom_vjp
def low_back(v):
    return v

def low_keep(v):
    return (low(v), None)

def low_pass(kept, grad):
    return (grad,)

def back_keep(v):
    return (v, None)

def back_low(kept, grad):
    return (low(grad),)
low.defvjp(low_keep, low_pass)
low_back.defvjp(back_keep, back_low)

def layer_norm(hidden, gain, shift):
    center = hidden - lax.optimization_barrier(jnp.mean(hidden, axis=-1, keepdims=True))
    spread = lax.optimization_barrier(jnp.mean(center * center, axis=-1, keepdims=True))
    return center * lax.rsqrt(spread + EPS) * gain + shift

def attend_one(packed):
    qkv_rows, valid = packed
    length = qkv_rows.shape[0]
    split = qkv_rows.reshape(length, 3, HEADS, HEAD_DIM)
    query_rows = split[:, 0]
    key_rows = split[:, 1]
    value_rows = split[:, 2]
    scores = low_back(jnp.einsum('qhd,khd->hqk', query_rows, key_rows, precision=HIGH) * HEAD_DIM ** (-0.5))
    scores = jnp.where(valid[None, None, :], scores, -1e+30)
    top = lax.optimization_barrier(jnp.max(scores, axis=-1, keepdims=True))
    exp_scores = jnp.exp(scores - top)
    attn_prob = exp_scores / lax.optimization_barrier(jnp.sum(exp_scores, axis=-1, keepdims=True))
    mixed = jnp.einsum('hqk,khd->qhd', low(attn_prob), value_rows, precision=HIGH)
    return mixed.reshape(length, HEADS * HEAD_DIM)

def forward(rows, valid, w_qkv, b_query, b_value, w_out, b_out, ln1_gain, ln1_bias, w_up, b_up, w_down, b_down, ln2_gain, ln2_bias):
    bias = jnp.concatenate([b_query, jnp.zeros_like(b_query), b_value])
    qkv_rows = low_back(low(jnp.dot(rows, w_qkv, precision=HIGH) + bias))
    mixed = lax.map(jax.checkpoint(attend_one), (qkv_rows, valid))
    mixed = low_back(low(mixed))
    branch = low_back(jnp.dot(mixed, w_out, precision=HIGH) + b_out)
    normed = layer_norm(rows + branch, ln1_gain, ln1_bias)
    hidden = low_back(jnp.dot(low(normed), w_up, precision=HIGH) + b_up)
    active = low(jax.nn.gelu(hidden, approximate=False))
    second = low_back(jnp.dot(active, w_down, precision=HIGH) + b_down)
    result = layer_norm(normed + second, ln2_gain, ln2_bias)
    return jnp.where(valid[..., None], result, 0.0)

def reference(tokens, lengths, w_qkv, b_query, b_value, w_out, b_out, ln1_gain, ln1_bias, w_up, b_up, w_down, b_down, ln2_gain, ln2_bias, cotangent):
    params = tuple((weight.astype(jnp.float32) for weight in (w_qkv, b_query, b_value, w_out, b_out, ln1_gain, ln1_bias, w_up, b_up, w_down, b_down, ln2_gain, ln2_bias)))
    places = jnp.arange(SEQLEN, dtype=jnp.int32)
    valid = places[None, :] < lengths[:, None]
    groups = SEQS // 8
    x_blocks = tokens.astype(jnp.float32).reshape(groups, 8, SEQLEN, D)
    mask_blocks = valid.reshape(groups, 8, SEQLEN)
    cot_blocks = cotangent.astype(jnp.float32).reshape(groups, 8, SEQLEN, D)

    def one_block(totals, item):
        x_block, mask_block, cot_block = item

        def local_fn(x_in, *weights):
            return forward(x_in, mask_block, *weights)
        result, pull = jax.vjp(local_fn, x_block, *params)
        grads = pull(cot_block)
        totals = tuple((total + grad for total, grad in zip(totals, grads[1:])))
        return (totals, (result.astype(jnp.bfloat16), grads[0]))
    init = tuple((jnp.zeros_like(weight) for weight in params))
    totals, (out_blocks, grad_blocks) = lax.scan(one_block, init, (x_blocks, mask_blocks, cot_blocks))
    layer_out = out_blocks.reshape(SEQS, SEQLEN, D)
    input_grad = grad_blocks.reshape(SEQS, SEQLEN, D)
    return (layer_out, input_grad, totals[0], totals[1], totals[2], totals[3], totals[4], totals[5], totals[6], totals[7], totals[8], totals[9], totals[10], totals[11], totals[12])
```

```python
import functools

import jax
import jax.numpy as jnp
from jax import lax
from jax.experimental import pallas as pl
from jax.experimental.pallas import tpu as pltpu
from jax.sharding import PartitionSpec as P

HEADS = 12
EPS = 1e-05
F32 = jnp.float32
BF16 = jnp.bfloat16
BLOCKS = 8
VMEM_LIMIT = 58 * 1024 * 1024


def dot_nn(a, b):
    return lax.dot_general(a, b, (((1,), (0,)), ((), ())), preferred_element_type=F32)


def dot_nt(a, b):
    return lax.dot_general(a, b, (((1,), (1,)), ((), ())), preferred_element_type=F32)


def dot_tn(a, b):
    return lax.dot_general(a, b, (((0,), (0,)), ((), ())), preferred_element_type=F32)


def params(grid_dims):
    return pltpu.CompilerParams(
        dimension_semantics=("arbitrary",) * grid_dims, vmem_limit_bytes=VMEM_LIMIT
    )


def cost(flops, nbytes, trans=0):
    return pl.CostEstimate(flops=int(flops), bytes_accessed=int(nbytes), transcendentals=int(trans))


def turned(place):
    return ((place & 1) << 2) | (place & 2) | ((place >> 2) & 1)


def place_rows(meta, source, target, columns, cut):
    rows = source.shape[2]
    for half in range(2):
        for block in range(BLOCKS):
            start = (meta[0] ^ turned(block)) * (2 * rows) + (meta[1] ^ half) * rows
            target[pl.ds(pl.multiple_of(start, 16), rows), cut] = source[half, block, :, columns]


def attend_kernel(meta, x_ref, mine_ref, other_ref, bias_ref, qkv_ref, mixed_ref, lse_ref, w_scr):
    half, seq = pl.program_id(0), pl.program_id(1)
    wide = w_scr.shape[1]
    part = wide // 3

    @pl.when((seq == 0) & (half == 0))
    def _():
        place_rows(meta, mine_ref, w_scr, slice(None), slice(None))

    @pl.when((seq == 0) & (half == 1))
    def _():
        place_rows(meta, other_ref, w_scr, slice(None), slice(None))

    length = meta[3 + seq]
    qkv = (dot_nn(x_ref[0], w_scr[...]) + bias_ref[0]).astype(BF16)
    qkv_ref[0, 0] = qkv
    rows = qkv.shape[0]
    lane = lax.broadcasted_iota(jnp.int32, (rows, 128), 1)
    key_ok = lax.broadcasted_iota(jnp.int32, (rows, rows), 0) < length
    for pair in range(part // 128):
        cut = pair * 128
        query = qkv[:, cut : cut + 128] * jnp.asarray(0.125, BF16)
        key = qkv[:, part + cut : part + cut + 128]
        value_t = qkv[:, 2 * part + cut : 2 * part + cut + 128].T
        outs = []
        for head in range(2):
            query_one = jnp.where((lane >= 64) == (head == 1), query, jnp.zeros_like(query))
            scores = jnp.where(key_ok, dot_nt(key, query_one), -1e30)
            top = jnp.max(scores, axis=0, keepdims=True)
            exp_scores = jnp.exp(scores - top)
            total = jnp.sum(exp_scores, axis=0, keepdims=True)
            lse_ref[0, 0, 2 * pair + head] = top + jnp.log(total)
            out = dot_nn(value_t[64 * head : 64 * head + 64], exp_scores.astype(BF16))
            outs.append(out * (1.0 / total))
        mixed_ref[0, :, cut : cut + 128] = jnp.concatenate(outs, axis=0).T.astype(BF16)


def attend(meta, x, mine, other, bias):
    seqs, length, width = x.shape
    wide = mine.shape[3]
    half_heads = HEADS // 2
    whole = lambda h, s, m: (0, 0, 0, 0)
    return pl.pallas_call(
        attend_kernel,
        grid_spec=pltpu.PrefetchScalarGridSpec(
            num_scalar_prefetch=1,
            grid=(2, seqs),
            in_specs=[
                pl.BlockSpec((1, length, width), lambda h, s, m: (s, 0, 0)),
                pl.BlockSpec(mine.shape, whole, pipeline_mode=pl.Buffered(1)),
                pl.BlockSpec(other.shape, whole, pipeline_mode=pl.Buffered(1)),
                pl.BlockSpec((1, 1, wide), lambda h, s, m: (m[2] ^ h, 0, 0)),
            ],
            out_specs=[
                pl.BlockSpec((1, 1, length, wide), lambda h, s, m: (m[2] ^ h, s, 0, 0)),
                pl.BlockSpec((1, length, wide // 3), lambda h, s, m: (s, 0, m[2] ^ h)),
                pl.BlockSpec(
                    (1, 1, half_heads, 1, length), lambda h, s, m: (m[2] ^ h, s, 0, 0, 0)
                ),
            ],
            scratch_shapes=[pltpu.VMEM((width, wide), BF16)],
        ),
        out_shape=[
            jax.ShapeDtypeStruct((2, seqs, length, wide), BF16),
            jax.ShapeDtypeStruct((seqs, length, width), BF16),
            jax.ShapeDtypeStruct((2, seqs, half_heads, 1, length), F32),
        ],
        compiler_params=params(2),
        cost_estimate=cost(
            4 * seqs * length * width * wide + 4 * seqs * length * length * width * 4,
            20e6,
            seqs * length * length * HEADS,
        ),
        name="attend_forward",
    )(meta, x, mine, other, bias)


def gelu_and_slope(hidden):
    size = jnp.abs(hidden)
    bell = jnp.exp(-0.5 * hidden * hidden)
    t = 1.0 / (1.0 + (0.3275911 * 0.7071067811865476) * size)
    poly = t * (
        0.5 * 0.254829592
        + t
        * (
            0.5 * -0.284496736
            + t * (0.5 * 1.421413741 + t * (0.5 * -1.453152027 + t * (0.5 * 1.061405429)))
        )
    )
    tail = poly * bell
    phi = jnp.where(hidden < 0.0, tail, 1.0 - tail)
    return hidden * phi, phi + hidden * bell * 0.3989422804014327


def norm_forward(hidden):
    center = hidden - jnp.mean(hidden, axis=-1, keepdims=True)
    scale = lax.rsqrt(jnp.mean(center * center, axis=-1, keepdims=True) + EPS)
    return center * scale, scale


def norm_back(grad, hat, scale, gain):
    grad_hat = grad * gain
    shift = jnp.mean(grad_hat, axis=-1, keepdims=True)
    along = jnp.mean(grad_hat * hat, axis=-1, keepdims=True)
    return scale * (grad_hat - shift - hat * along)


def column_sum(rows):
    return jnp.sum(rows.astype(F32), axis=0, keepdims=True)


def feed_kernel(
    seq_len,
    meta,
    x_ref,
    mixed_ref,
    cot_ref,
    up_mine,
    up_other,
    down_mine,
    down_other,
    vec_ref,
    b_up_ref,
    out_ref,
    norm_ref,
    active_ref,
    grad_hidden_ref,
    grad_second_ref,
    grad_branch_ref,
    grad_mixed_ref,
    grad_vec_ref,
    grad_b_up_ref,
    w_up,
    w_out,
    w_down,
    slope_scr,
):
    step = pl.program_id(0)
    tile, width = x_ref.shape
    hidden_width = w_up.shape[1]
    groups = 3
    up_cut, out_cut = hidden_width // (2 * groups), width // (2 * groups)

    @pl.when(step == 0)
    def _():
        grad_vec_ref[...] = jnp.zeros_like(grad_vec_ref)
        grad_b_up_ref[...] = jnp.zeros_like(grad_b_up_ref)
        for rel, source in enumerate((up_mine, up_other)):
            core = meta[2] ^ rel
            for group in range(groups):
                base = group * (up_cut + out_cut)
                up_to = pl.multiple_of(core * (hidden_width // 2) + group * up_cut, 128)
                out_to = pl.multiple_of(core * (width // 2) + group * out_cut, 128)
                place_rows(meta, source, w_up, slice(base, base + up_cut), pl.ds(up_to, up_cut))
                place_rows(
                    meta,
                    source,
                    w_out,
                    slice(base + up_cut, base + up_cut + out_cut),
                    pl.ds(out_to, out_cut),
                )
        rows = down_mine.shape[2]
        for rel, source in enumerate((down_mine, down_other)):
            for half in range(2):
                for block in range(BLOCKS):
                    start = (
                        (meta[0] ^ turned(block)) * (4 * rows)
                        + (meta[2] ^ rel) * (2 * rows)
                        + (meta[1] ^ half) * rows
                    )
                    w_down[pl.ds(pl.multiple_of(start, 16), rows), :] = source[half, block]

    vec = vec_ref[...]
    b_out, gain_one, shift_one, b_down, gain_two, shift_two = [vec[i : i + 1] for i in range(6)]
    seq = lax.div(step * tile, seq_len)
    place = lax.broadcasted_iota(jnp.int32, (tile, 1), 0) + lax.rem(step * tile, seq_len)
    valid = place < meta[3 + seq]

    hat_one, scale_one = norm_forward(
        x_ref[...].astype(F32) + (dot_nn(mixed_ref[...], w_out[...]) + b_out)
    )
    normed = hat_one * gain_one + shift_one
    normed_low = normed.astype(BF16)
    norm_ref[...] = normed_low
    chunk = 512
    second = jnp.zeros((tile, width), F32)
    for start in range(0, hidden_width, chunk):
        cut = slice(start, start + chunk)
        hidden = dot_nn(normed_low, w_up[:, cut]) + b_up_ref[:, cut]
        active, slope = gelu_and_slope(hidden)
        slope_scr[:, cut] = slope
        active_low = active.astype(BF16)
        active_ref[:, cut] = active_low
        second = second + dot_nn(active_low, w_down[cut, :])
    hat_two, scale_two = norm_forward(normed + (second + b_down))
    out_ref[...] = jnp.where(valid, hat_two * gain_two + shift_two, 0.0).astype(BF16)

    grad_result = jnp.where(valid, cot_ref[...].astype(F32), 0.0)
    grad_two = norm_back(grad_result, hat_two, scale_two, gain_two)
    grad_second = grad_two.astype(BF16)
    grad_second_ref[...] = grad_second
    grad_normed = grad_two
    for start in range(0, hidden_width, chunk):
        cut = slice(start, start + chunk)
        grad_active = dot_nt(grad_second, w_down[cut, :])
        grad_hidden = (slope_scr[:, cut] * grad_active).astype(BF16)
        grad_hidden_ref[:, cut] = grad_hidden
        grad_b_up_ref[:, cut] += column_sum(grad_hidden)
        grad_normed = grad_normed + dot_nt(grad_hidden, w_up[:, cut])
    grad_one = norm_back(grad_normed, hat_one, scale_one, gain_one)
    grad_branch = grad_one.astype(BF16)
    grad_branch_ref[...] = grad_branch
    grad_mixed_ref[...] = dot_nt(grad_branch, w_out[...]).astype(BF16)
    sums = (
        column_sum(grad_branch),
        column_sum(grad_normed * hat_one),
        column_sum(grad_normed),
        column_sum(grad_second),
        column_sum(grad_result * hat_two),
        column_sum(grad_result),
    )
    for i, total in enumerate(sums):
        grad_vec_ref[i : i + 1, :] += total


def feed(meta, x, mixed, cot, up, down, vec, b_up, seq_len):
    rows, width = x.shape
    hidden_width = b_up.shape[1]
    tile = min(256, rows)
    by_row = lambda cols: pl.BlockSpec((tile, cols), lambda i, m: (i, 0))
    whole = lambda a: pl.BlockSpec(
        a.shape, lambda i, m: (0,) * a.ndim, pipeline_mode=pl.Buffered(1)
    )
    rows_of = lambda cols: jax.ShapeDtypeStruct((rows, cols), BF16)
    return pl.pallas_call(
        functools.partial(feed_kernel, seq_len),
        grid_spec=pltpu.PrefetchScalarGridSpec(
            num_scalar_prefetch=1,
            grid=(rows // tile,),
            in_specs=[by_row(width)] * 3 + [whole(a) for a in (*up, *down, vec, b_up)],
            out_specs=[
                by_row(width),
                by_row(width),
                by_row(hidden_width),
                by_row(hidden_width),
                by_row(width),
                by_row(width),
                by_row(width),
                pl.BlockSpec((8, width), lambda i, m: (0, 0)),
                pl.BlockSpec((1, hidden_width), lambda i, m: (0, 0)),
            ],
            scratch_shapes=[
                pltpu.VMEM((width, hidden_width), BF16),
                pltpu.VMEM((width, width), BF16),
                pltpu.VMEM((hidden_width, width), BF16),
                pltpu.VMEM((tile, hidden_width), F32),
            ],
        ),
        out_shape=[
            rows_of(width),
            rows_of(width),
            rows_of(hidden_width),
            rows_of(hidden_width),
            rows_of(width),
            rows_of(width),
            rows_of(width),
            jax.ShapeDtypeStruct((8, width), F32),
            jax.ShapeDtypeStruct((1, hidden_width), F32),
        ],
        compiler_params=params(1),
        cost_estimate=cost(
            8 * rows * width * hidden_width + 4 * rows * width * width,
            40e6,
            2 * rows * hidden_width,
        ),
        name="feed_forward_and_back",
    )(meta, x, mixed, cot, *up, *down, vec, b_up)


def store_blocks(meta, out_ref, value, cut):
    rows = out_ref.shape[2]
    for block in range(BLOCKS):
        for half in range(2):
            start = (2 * block + half) * rows
            out_ref[meta[1] ^ half, turned(meta[0] ^ block), :, cut] = value[
                start : start + rows
            ].astype(BF16)


def grad_up_kernel(meta, norm_ref, mixed_ref, grad_hidden_ref, grad_branch_ref, out_ref):
    up_cut = grad_hidden_ref.shape[1]
    store_blocks(meta, out_ref, dot_tn(norm_ref[...], grad_hidden_ref[...]), slice(0, up_cut))
    store_blocks(
        meta,
        out_ref,
        dot_tn(mixed_ref[...], grad_branch_ref[...]),
        slice(up_cut, out_ref.shape[3]),
    )


def grad_up(rel, meta, normed, mixed, grad_hidden, grad_branch):
    rows, width = normed.shape
    hidden_width = grad_hidden.shape[1]
    groups = 3
    up_cut, out_cut = hidden_width // (2 * groups), width // (2 * groups)
    block_rows = width // (2 * BLOCKS)
    whole = pl.BlockSpec((rows, width), lambda n, m: (0, 0), pipeline_mode=pl.Buffered(1))
    turn = lambda n, m: (0, (m[2] ^ rel) * groups + n)
    return pl.pallas_call(
        grad_up_kernel,
        grid_spec=pltpu.PrefetchScalarGridSpec(
            num_scalar_prefetch=1,
            grid=(groups,),
            in_specs=[
                whole,
                whole,
                pl.BlockSpec((rows, up_cut), turn),
                pl.BlockSpec((rows, out_cut), turn),
            ],
            out_specs=pl.BlockSpec(
                (2, BLOCKS, block_rows, up_cut + out_cut), lambda n, m: (0, 0, 0, n)
            ),
        ),
        out_shape=jax.ShapeDtypeStruct(
            (2, BLOCKS, block_rows, groups * (up_cut + out_cut)), BF16
        ),
        compiler_params=params(1),
        cost_estimate=cost(rows * width * (hidden_width + width), 12e6),
        name="grad_up",
    )(meta, normed, mixed, grad_hidden, grad_branch)


def grad_down_kernel(meta, active_ref, grad_second_ref, keep_ref, send_ref):
    value = dot_tn(active_ref[...], grad_second_ref[...])
    rows = keep_ref.shape[2]
    mine = meta[2] == 0
    low, high = value[: 2 * rows], value[2 * rows :]
    keep = jnp.where(mine, low, high).astype(BF16)
    send = jnp.where(mine, high, low).astype(BF16)
    for half in range(2):
        keep_ref[meta[1] ^ half, 0] = keep[half * rows : (half + 1) * rows]
        send_ref[meta[1] ^ half, 0] = send[half * rows : (half + 1) * rows]


def grad_down(meta, active, grad_second):
    rows, hidden_width = active.shape
    width = grad_second.shape[1]
    block = hidden_width // BLOCKS
    out = jax.ShapeDtypeStruct((2, BLOCKS, block // 4, width), BF16)
    spec = pl.BlockSpec((2, 1, block // 4, width), lambda j, m: (0, j, 0, 0))
    return pl.pallas_call(
        grad_down_kernel,
        grid_spec=pltpu.PrefetchScalarGridSpec(
            num_scalar_prefetch=1,
            grid=(BLOCKS,),
            in_specs=[
                pl.BlockSpec((rows, block), lambda j, m: (0, m[0] ^ turned(j))),
                pl.BlockSpec((rows, width), lambda j, m: (0, 0), pipeline_mode=pl.Buffered(1)),
            ],
            out_specs=[spec, spec],
        ),
        out_shape=[out, out],
        compiler_params=params(1),
        cost_estimate=cost(2 * rows * hidden_width * width, 16e6),
        name="grad_down",
    )(meta, active, grad_second)


def attend_back_kernel(
    meta,
    x_ref,
    qkv_ref,
    mixed_ref,
    grad_mixed_ref,
    lse_ref,
    grad_qkv_ref,
    grad_w_ref,
    grad_bias_ref,
    grad_scr,
):
    seq = pl.program_id(0)
    length = meta[3 + seq]
    rows, wide = qkv_ref.shape[2:]
    part = wide // 3
    lane = lax.broadcasted_iota(jnp.int32, (rows, 128), 1)
    key_ok = lax.broadcasted_iota(jnp.int32, (rows, rows), 0) < length

    @pl.when(seq == 0)
    def _():
        grad_bias_ref[...] = jnp.zeros_like(grad_bias_ref)

    grads = [[], [], []]
    for pair in range(part // 128):
        cut = pair * 128
        query = qkv_ref[0, 0, :, cut : cut + 128] * jnp.asarray(0.125, BF16)
        key = qkv_ref[0, 0, :, part + cut : part + cut + 128]
        value = qkv_ref[0, 0, :, 2 * part + cut : 2 * part + cut + 128]
        grad_out = grad_mixed_ref[0, :, cut : cut + 128]
        product = (grad_out.astype(F32) * mixed_ref[0, :, cut : cut + 128].astype(F32)).T
        key_t = key.T
        grad_query, grad_key, grad_value = [], 0.0, 0.0
        for head in range(2):
            keep = (lane >= 64) == (head == 1)
            query_one = jnp.where(keep, query, jnp.zeros_like(query))
            grad_one = jnp.where(keep, grad_out, jnp.zeros_like(grad_out))
            inner = slice(64 * head, 64 * head + 64)
            delta = jnp.sum(product[inner], axis=0, keepdims=True)
            log_total = lse_ref[0, 0, 2 * pair + head]
            scores = jnp.where(key_ok, dot_nt(key, query_one), -1e30)
            prob = jnp.exp(scores - log_total)
            grad_prob = dot_nt(value, grad_one)
            grad_scores = (prob * (grad_prob - delta)).astype(BF16)
            grad_value = grad_value + dot_nn(prob.astype(BF16), grad_one)
            grad_key = grad_key + dot_nn(grad_scores, query_one)
            grad_query.append(dot_nn(key_t[inner], grad_scores) * 0.125)
        grads[0].append(jnp.concatenate(grad_query, axis=0).T.astype(BF16))
        grads[1].append(grad_key.astype(BF16))
        grads[2].append(grad_value.astype(BF16))
    start = pl.multiple_of(seq * rows, 128)
    for kind in range(3):
        for pair, grad in enumerate(grads[kind]):
            cut = slice(kind * part + pair * 128, kind * part + (pair + 1) * 128)
            grad_scr[pl.ds(start, rows), cut] = grad
            grad_qkv_ref[0, :, cut] = grad
            grad_bias_ref[:, cut] += column_sum(grad)

    @pl.when(seq == pl.num_programs(0) - 1)
    def _():
        store_blocks(meta, grad_w_ref, dot_tn(x_ref[...], grad_scr[...]), slice(None))


def attend_back(rel, meta, x, qkv, mixed, grad_mixed, lse):
    _, seqs, length, wide = qkv.shape
    width = mixed.shape[2]
    rows = seqs * length
    half_heads = HEADS // 2
    block_rows = width // (2 * BLOCKS)
    by_half = pl.BlockSpec((1, length, wide // 3), lambda s, m: (s, 0, m[2] ^ rel))
    return pl.pallas_call(
        attend_back_kernel,
        grid_spec=pltpu.PrefetchScalarGridSpec(
            num_scalar_prefetch=1,
            grid=(seqs,),
            in_specs=[
                pl.BlockSpec((rows, width), lambda s, m: (0, 0), pipeline_mode=pl.Buffered(1)),
                pl.BlockSpec((1, 1, length, wide), lambda s, m: (m[2] ^ rel, s, 0, 0)),
                by_half,
                by_half,
                pl.BlockSpec(
                    (1, 1, half_heads, 1, length), lambda s, m: (m[2] ^ rel, s, 0, 0, 0)
                ),
            ],
            out_specs=[
                pl.BlockSpec((1, length, wide), lambda s, m: (s, 0, 0)),
                pl.BlockSpec((2, BLOCKS, block_rows, wide), lambda s, m: (0, 0, 0, 0)),
                pl.BlockSpec((1, wide), lambda s, m: (0, 0)),
            ],
            scratch_shapes=[pltpu.VMEM((rows, wide), BF16)],
        ),
        out_shape=[
            jax.ShapeDtypeStruct((seqs, length, wide), BF16),
            jax.ShapeDtypeStruct((2, BLOCKS, block_rows, wide), BF16),
            jax.ShapeDtypeStruct((1, wide), F32),
        ],
        compiler_params=params(1),
        cost_estimate=cost(
            2 * rows * width * wide + 5 * rows * length * width * 4,
            16e6,
            rows * length * half_heads,
        ),
        name="attend_back",
    )(meta, x.reshape(rows, width), qkv, mixed, grad_mixed, lse)


def input_kernel(meta, branch_ref, mine_ref, other_ref, w_mine, w_other, out_ref, scr_mine, scr_other):
    @pl.when(pl.program_id(0) == 0)
    def _():
        place_rows(meta, w_mine, scr_mine, slice(None), slice(None))
        place_rows(meta, w_other, scr_other, slice(None), slice(None))

    out_ref[...] = (
        branch_ref[...].astype(F32)
        + dot_nt(mine_ref[...], scr_mine[...])
        + dot_nt(other_ref[...], scr_other[...])
    )


def input_grad_of(meta, grad_branch, grad_mine, grad_other, w_mine, w_other):
    rows, width = grad_branch.shape
    wide = grad_mine.shape[1]
    tile = min(256, rows)
    whole = pl.BlockSpec(w_mine.shape, lambda i, m: (0, 0, 0, 0), pipeline_mode=pl.Buffered(1))
    by_row = lambda cols: pl.BlockSpec((tile, cols), lambda i, m: (i, 0))
    return pl.pallas_call(
        input_kernel,
        grid_spec=pltpu.PrefetchScalarGridSpec(
            num_scalar_prefetch=1,
            grid=(rows // tile,),
            in_specs=[by_row(width), by_row(wide), by_row(wide), whole, whole],
            out_specs=by_row(width),
            scratch_shapes=[pltpu.VMEM((width, wide), BF16)] * 2,
        ),
        out_shape=jax.ShapeDtypeStruct((rows, width), F32),
        compiler_params=params(1),
        cost_estimate=cost(4 * rows * width * wide, 14e6),
        name="input_grad",
    )(meta, grad_branch, grad_mine, grad_other, w_mine, w_other)


def swap(array, axis, size, bit):
    return lax.ppermute(array, axis, [(i, i ^ bit) for i in range(size)])


def gather_quarters(piece):
    held = piece[None]
    for bit in (4, 2, 1):
        came = swap(held, "shard", BLOCKS, bit)
        held = jnp.concatenate([held, came], axis=0)
    came = swap(held, "rep", 4, 2)
    mine = jnp.stack([held, came])
    return mine, swap(mine, "rep", 4, 1)


def add(left, right):
    return (left.astype(F32) + right.astype(F32)).astype(BF16)


def reduce_quarters(keep, send):
    came = swap(send, "rep", 4, 1)
    low, high = add(keep[0], came[0]), add(keep[1], came[1])
    came = swap(high, "rep", 4, 2)
    count = BLOCKS
    for bit in (1, 2, 4):
        count //= 2
        low, high, came_low, came_high = low[:count], low[count:], came[:count], came[count:]
        low, high = add(low, came_low), add(high, came_high)
        came = swap(high, "shard", BLOCKS, bit)
    return add(low, came)[0]


def share_quarters(piece, rep):
    parts = [piece] + [swap(piece, "rep", 4, bit) for bit in (1, 2, 3)]
    out = []
    for place in range(4):
        pick = parts[3]
        for rel in range(3):
            pick = jnp.where(rep == place ^ rel, parts[rel], pick)
        out.append(pick.astype(F32))
    return out


def local(
    fast,
    tokens,
    lengths,
    w_qkv,
    b_query,
    b_value,
    w_out,
    b_out,
    ln1_gain,
    ln1_bias,
    w_up,
    b_up,
    w_down,
    b_down,
    ln2_gain,
    ln2_bias,
    cotangent,
):
    seqs, seq_len, width = tokens.shape
    rows = seqs * seq_len
    hidden_width = w_up.shape[1]
    half = width // 2
    groups = 3
    up_cut, out_cut = hidden_width // (2 * groups), half // groups
    vectors = (b_query, b_value, b_out, ln1_gain, ln1_bias, b_down, ln2_gain, ln2_bias, b_up)
    names = len(vectors)

    if fast:
        shard, rep = lax.axis_index("shard"), lax.axis_index("rep")
        x_at, core = rep // 2, rep % 2
    else:
        shard = rep = x_at = core = jnp.int32(0)
    block = width // BLOCKS
    quarter = block // 2
    meta = jnp.concatenate(
        [jnp.stack([shard, x_at, core]).astype(jnp.int32), lengths.astype(jnp.int32)]
    )

    def qkv_parts(w):
        return w.reshape(-1, 2, quarter, 3, 2, half)

    def up_parts(up, out):
        up = up.reshape(-1, 2, quarter, 2, groups, up_cut)
        out = out.reshape(-1, 2, quarter, 2, groups, out_cut)
        return jnp.concatenate([up, out], axis=-1)

    if fast:
        table = jnp.concatenate(vectors).reshape(1, -1)
        for bit in (4, 2, 1):
            table = jnp.concatenate([table, swap(table, "shard", BLOCKS, bit)], axis=0)
        table = jnp.take(table, turned(jnp.arange(BLOCKS) ^ shard), axis=0)

        def pick(array, axis_x, axis_core):
            array = lax.dynamic_index_in_dim(array, core, axis_core, keepdims=False)
            return lax.dynamic_index_in_dim(array, x_at, axis_x, keepdims=False)

        qkv_piece = pick(qkv_parts(w_qkv)[0], 0, 3).reshape(quarter, 3 * half)
        up_piece = pick(up_parts(w_up, w_out)[0], 0, 2).reshape(quarter, -1)
        down_piece = pick(w_down.reshape(2, 2, -1, width), 0, 0)
        qkv_w = gather_quarters(qkv_piece)
        up_w = gather_quarters(up_piece)
        down_w = gather_quarters(down_piece)
    else:
        everything = lambda a: lax.all_gather(a, "shard", axis=0, tiled=True)
        table = None
        full = [everything(v) for v in vectors]
        order = [turned(p) for p in range(BLOCKS)]
        both = lambda a: (a[0][:, order], a[1][:, order])
        qkv_w = both(
            qkv_parts(everything(w_qkv))
            .transpose(4, 1, 0, 2, 3, 5)
            .reshape(2, 2, BLOCKS, quarter, 3 * half)
        )
        up_w = both(
            up_parts(everything(w_up), everything(w_out))
            .transpose(3, 1, 0, 2, 4, 5)
            .reshape(2, 2, BLOCKS, quarter, -1)
        )
        down_w = both(
            everything(w_down).reshape(BLOCKS, 2, 2, -1, width).transpose(1, 2, 0, 3, 4)
        )
    if fast:
        full, start = [], 0
        for v in vectors:
            full.append(table[:, start : start + v.shape[0]].reshape(-1))
            start += v.shape[0]
    full = [v.astype(F32) for v in full]
    bias = jnp.stack(
        [full[0].reshape(2, half), jnp.zeros((2, half), F32), full[1].reshape(2, half)], axis=1
    ).reshape(2, 1, 3 * half)
    vec = jnp.stack(full[2:8] + [jnp.zeros_like(full[0])] * 2)

    qkv, mixed, lse = attend(meta, tokens, *qkv_w, bias)
    x_rows = tokens.reshape(rows, width)
    mixed_rows = mixed.reshape(rows, width)
    (
        layer_out,
        normed,
        active,
        grad_hidden,
        grad_second,
        grad_branch,
        grad_mixed,
        grad_vec,
        grad_b_up,
    ) = feed(
        meta,
        x_rows,
        mixed_rows,
        cotangent.reshape(rows, width),
        up_w,
        down_w,
        vec,
        full[8].reshape(1, -1),
        seq_len,
    )
    down_keep, down_send = grad_down(meta, active, grad_second)
    up_send = grad_up(1, meta, normed, mixed_rows, grad_hidden, grad_branch)
    up_keep = grad_up(0, meta, normed, mixed_rows, grad_hidden, grad_branch)
    grad_mixed = grad_mixed.reshape(seqs, seq_len, width)
    other_qkv, qkv_send, other_bias = attend_back(1, meta, tokens, qkv, mixed, grad_mixed, lse)
    mine_qkv, qkv_keep, mine_bias = attend_back(0, meta, tokens, qkv, mixed, grad_mixed, lse)
    input_grad = input_grad_of(
        meta,
        grad_branch,
        mine_qkv.reshape(rows, -1),
        other_qkv.reshape(rows, -1),
        *qkv_w,
    )

    bias_halves = jnp.stack([mine_bias, other_bias]).reshape(2, 3, half)
    bias_halves = jnp.where(core == 0, bias_halves, bias_halves[::-1])
    grad_vectors = [
        bias_halves[:, 0].reshape(-1),
        bias_halves[:, 2].reshape(-1),
        *[grad_vec[i] for i in range(6)],
        grad_b_up[0],
    ]
    if fast:
        total = jnp.concatenate([g.reshape(BLOCKS, -1) for g in grad_vectors], axis=1)
        for axis, size, bit in (
            ("rep", 4, 1),
            ("rep", 4, 2),
            ("shard", BLOCKS, 1),
            ("shard", BLOCKS, 2),
            ("shard", BLOCKS, 4),
        ):
            total = total + swap(total, axis, size, bit)
        total = lax.dynamic_index_in_dim(total, shard, 0, keepdims=False)
        sums, start = [], 0
        for v in vectors:
            sums.append(total[start : start + v.shape[0]])
            start += v.shape[0]
        down = share_quarters(reduce_quarters(down_keep, down_send), rep)
        up = share_quarters(reduce_quarters(up_keep, up_send), rep)
        qkv_sum = share_quarters(reduce_quarters(qkv_keep, qkv_send), rep)
        grad_w_down = jnp.stack(down).reshape(2, 2, -1, width).transpose(1, 0, 2, 3)
        grad_w_down = grad_w_down.reshape(-1, width)
        up = jnp.stack(up).reshape(2, 2, quarter, groups, up_cut + out_cut)
        up = up.transpose(0, 2, 1, 3, 4)
        grad_w_up = up[..., :up_cut].reshape(block, hidden_width)
        grad_w_out = up[..., up_cut:].reshape(block, width)
        qkv_sum = jnp.stack(qkv_sum).reshape(2, 2, quarter, 3, half)
        grad_w_qkv = qkv_sum.transpose(0, 2, 3, 1, 4).reshape(block, 3 * width)
    else:
        total_of = lambda a: lax.psum(
            lax.psum_scatter(a, "shard", scatter_dimension=0, tiled=True), "rep"
        )
        sums = [total_of(g) for g in grad_vectors]
        order = [turned(p) for p in range(BLOCKS)]
        down_keep, down_send, up_keep, up_send, qkv_keep, qkv_send = (
            a[:, order] for a in (down_keep, down_send, up_keep, up_send, qkv_keep, qkv_send)
        )
        down = jnp.stack([down_keep, down_send]).transpose(2, 0, 1, 3, 4)
        grad_w_down = total_of(down.reshape(hidden_width, width).astype(F32))
        up = jnp.stack([up_keep, up_send]).reshape(
            2, 2, BLOCKS, quarter, groups, up_cut + out_cut
        )
        up = up.transpose(2, 1, 3, 0, 4, 5)
        grad_w_up = total_of(up[..., :up_cut].reshape(width, hidden_width).astype(F32))
        grad_w_out = total_of(up[..., up_cut:].reshape(width, width).astype(F32))
        qkv_sum = jnp.stack([qkv_keep, qkv_send]).reshape(2, 2, BLOCKS, quarter, 3, half)
        qkv_sum = qkv_sum.transpose(2, 1, 3, 4, 0, 5).reshape(width, 3 * width)
        grad_w_qkv = total_of(qkv_sum.astype(F32))
    return (
        layer_out.reshape(seqs, seq_len, width),
        input_grad.reshape(seqs, seq_len, width),
        grad_w_qkv,
        sums[0],
        sums[1],
        grad_w_out,
        sums[2],
        sums[3],
        sums[4],
        grad_w_up,
        sums[8],
        grad_w_down,
        sums[5],
        sums[6],
        sums[7],
    )


def solution(mesh):
    fast = mesh.shape["shard"] == BLOCKS and mesh.shape["rep"] == 4
    by_seq = P(("shard", "rep"), None, None)
    one, two = P("shard"), P("shard", None)
    in_specs = (by_seq, P(("shard", "rep")), two, one, one, two, one, one, one)
    in_specs = in_specs + (two, one, two, one, one, one, by_seq)
    out_specs = (by_seq, by_seq, two, one, one, two, one, one, one, two, one, two, one, one, one)
    return jax.shard_map(
        functools.partial(local, fast),
        mesh=mesh,
        in_specs=in_specs,
        out_specs=out_specs,
        check_vma=False,
    )
```

```python
import functools

import jax
import jax.numpy as jnp
from jax import lax
from jax.experimental import pallas as pl
from jax.experimental.pallas import tpu as pltpu
from jax.sharding import PartitionSpec as P

HEADS = 12
EPS = 1e-05
F32 = jnp.float32
BF16 = jnp.bfloat16
BLOCKS = 8
VMEM_LIMIT = 58 * 1024 * 1024


def dot_nn(a, b):
    return lax.dot_general(a, b, (((1,), (0,)), ((), ())), preferred_element_type=F32)


def dot_nt(a, b):
    return lax.dot_general(a, b, (((1,), (1,)), ((), ())), preferred_element_type=F32)


def dot_tn(a, b):
    return lax.dot_general(a, b, (((0,), (0,)), ((), ())), preferred_element_type=F32)


def params(grid_dims):
    return pltpu.CompilerParams(
        dimension_semantics=("arbitrary",) * grid_dims, vmem_limit_bytes=VMEM_LIMIT
    )


def cost(flops, nbytes, trans=0):
    return pl.CostEstimate(
        flops=int(flops) // 16, bytes_accessed=int(nbytes) // 16, transcendentals=int(trans) // 16
    )


def gated(kernel, inputs, gates):
    def body(*refs):
        kernel(*refs[: inputs + 1], *refs[inputs + 1 + gates :])

    return body


def gate_specs(gates):
    return [pl.BlockSpec(memory_space=pl.ANY)] * len(gates)


def turned(place):
    return ((place & 1) << 2) | (place & 2) | ((place >> 2) & 1)


def place_rows(meta, source, target, columns, cut):
    rows = source.shape[2]
    for half in range(2):
        for block in range(BLOCKS):
            start = (meta[0] ^ turned(block)) * (2 * rows) + (meta[1] ^ half) * rows
            target[pl.ds(pl.multiple_of(start, 16), rows), cut] = source[half, block, :, columns]


def attend_kernel(meta, x_ref, w_ref, bias_ref, qkv_ref, mixed_ref, mixed_t_ref, lse_ref, w_scr):
    seq = pl.program_id(0)
    wide = w_scr.shape[1]
    part = wide // 3

    @pl.when(seq == 0)
    def _():
        place_rows(meta, w_ref, w_scr, slice(None), slice(None))

    length = meta[3 + seq]
    qkv = (dot_nn(x_ref[0], w_scr[...]) + bias_ref[...]).astype(BF16)
    qkv_ref[0] = qkv
    rows = qkv.shape[0]
    lane = lax.broadcasted_iota(jnp.int32, (rows, 128), 1)
    key_ok = lax.broadcasted_iota(jnp.int32, (rows, rows), 0) < length
    for pair in range(part // 128):
        cut = pair * 128
        query = qkv[:, cut : cut + 128] * jnp.asarray(0.125, BF16)
        key = qkv[:, part + cut : part + cut + 128]
        value_t = qkv[:, 2 * part + cut : 2 * part + cut + 128].T
        outs = []
        for head in range(2):
            query_one = jnp.where((lane >= 64) == (head == 1), query, jnp.zeros_like(query))
            scores = jnp.where(key_ok, dot_nt(key, query_one), -1e30)
            top = jnp.max(scores, axis=0, keepdims=True)
            exp_scores = jnp.exp(scores - top)
            total = jnp.sum(exp_scores, axis=0, keepdims=True)
            lse_ref[0, 2 * pair + head] = top + jnp.log(total)
            out = dot_nn(value_t[64 * head : 64 * head + 64], exp_scores.astype(BF16))
            outs.append(out * (1.0 / total))
        mixed_t = jnp.concatenate(outs, axis=0)
        mixed_t_ref[cut : cut + 128, :] = mixed_t.astype(BF16)
        mixed_ref[0, :, cut : cut + 128] = mixed_t.T.astype(BF16)


def attend(meta, x, weight, bias):
    seqs, length, width = x.shape
    wide = weight.shape[3]
    part = wide // 3
    half_heads = HEADS // 2
    whole = lambda s, m: (0, 0, 0, 0)
    return pl.pallas_call(
        attend_kernel,
        grid_spec=pltpu.PrefetchScalarGridSpec(
            num_scalar_prefetch=1,
            grid=(seqs,),
            in_specs=[
                pl.BlockSpec((1, length, width), lambda s, m: (s, 0, 0)),
                pl.BlockSpec(weight.shape, whole, pipeline_mode=pl.Buffered(1)),
                pl.BlockSpec((1, wide), lambda s, m: (0, 0)),
            ],
            out_specs=[
                pl.BlockSpec((1, length, wide), lambda s, m: (s, 0, 0)),
                pl.BlockSpec((1, length, part), lambda s, m: (s, 0, 0)),
                pl.BlockSpec((part, length), lambda s, m: (0, s)),
                pl.BlockSpec((1, half_heads, 1, length), lambda s, m: (s, 0, 0, 0)),
            ],
            scratch_shapes=[pltpu.VMEM((width, wide), BF16)],
        ),
        out_shape=[
            jax.ShapeDtypeStruct((seqs, length, wide), BF16),
            jax.ShapeDtypeStruct((seqs, length, part), BF16),
            jax.ShapeDtypeStruct((part, seqs * length), BF16),
            jax.ShapeDtypeStruct((seqs, half_heads, 1, length), F32),
        ],
        compiler_params=params(1),
        cost_estimate=cost(
            2 * seqs * length * width * wide + 8 * seqs * length * length * width,
            10e6,
            seqs * length * length * half_heads,
        ),
        name="attend_forward",
    )(meta, x, weight, bias)


def gelu_and_slope(hidden):
    size = jnp.abs(hidden)
    bell = jnp.exp(-0.5 * hidden * hidden)
    t = 1.0 / (1.0 + (0.3275911 * 0.7071067811865476) * size)
    poly = t * (
        0.5 * 0.254829592
        + t
        * (
            0.5 * -0.284496736
            + t * (0.5 * 1.421413741 + t * (0.5 * -1.453152027 + t * (0.5 * 1.061405429)))
        )
    )
    tail = poly * bell
    phi = jnp.where(hidden < 0.0, tail, 1.0 - tail)
    return hidden * phi, phi + hidden * bell * 0.3989422804014327


def norm_forward(hidden):
    center = hidden - jnp.mean(hidden, axis=-1, keepdims=True)
    scale = lax.rsqrt(jnp.mean(center * center, axis=-1, keepdims=True) + EPS)
    return center * scale, scale


def norm_back(grad, hat, scale, gain):
    grad_hat = grad * gain
    shift = jnp.mean(grad_hat, axis=-1, keepdims=True)
    along = jnp.mean(grad_hat * hat, axis=-1, keepdims=True)
    return scale * (grad_hat - shift - hat * along)


def column_sum(rows):
    return jnp.sum(rows.astype(F32), axis=0, keepdims=True)


def feed_kernel(
    seq_len,
    meta,
    x_ref,
    mixed_mine,
    mixed_other,
    cot_ref,
    up_mine,
    up_other,
    down_mine,
    down_other,
    vec_ref,
    b_up_ref,
    out_ref,
    norm_t_ref,
    active_t_ref,
    grad_hidden_ref,
    grad_second_ref,
    grad_branch_ref,
    grad_mixed_mine,
    grad_mixed_other,
    grad_vec_ref,
    grad_b_up_ref,
    w_up,
    w_out,
    w_down,
    slope_scr,
):
    step = pl.program_id(0)
    tile, width = x_ref.shape
    hidden_width = w_up.shape[1]
    groups = 3
    up_cut, out_cut = hidden_width // (2 * groups), width // (2 * groups)

    @pl.when(step == 0)
    def _():
        grad_vec_ref[...] = jnp.zeros_like(grad_vec_ref)
        grad_b_up_ref[...] = jnp.zeros_like(grad_b_up_ref)
        for rel, source in enumerate((up_mine, up_other)):
            core = meta[2] ^ rel
            for group in range(groups):
                base = group * (up_cut + out_cut)
                up_to = pl.multiple_of(core * (hidden_width // 2) + group * up_cut, 128)
                out_to = pl.multiple_of(core * (width // 2) + group * out_cut, 128)
                place_rows(meta, source, w_up, slice(base, base + up_cut), pl.ds(up_to, up_cut))
                place_rows(
                    meta,
                    source,
                    w_out,
                    slice(base + up_cut, base + up_cut + out_cut),
                    pl.ds(out_to, out_cut),
                )
        rows = down_mine.shape[2]
        for rel, source in enumerate((down_mine, down_other)):
            for half in range(2):
                for block in range(BLOCKS):
                    start = (
                        (meta[0] ^ turned(block)) * (4 * rows)
                        + (meta[2] ^ rel) * (2 * rows)
                        + (meta[1] ^ half) * rows
                    )
                    w_down[pl.ds(pl.multiple_of(start, 16), rows), :] = source[half, block]

    vec = vec_ref[...]
    b_out, gain_one, shift_one, b_down, gain_two, shift_two = [vec[i : i + 1] for i in range(6)]
    seq = lax.div(step * tile, seq_len)
    place = lax.broadcasted_iota(jnp.int32, (tile, 1), 0) + lax.rem(step * tile, seq_len)
    valid = place < meta[3 + seq]

    half = width // 2
    rows_mine = pl.ds(pl.multiple_of(meta[2] * half, 128), half)
    rows_other = pl.ds(pl.multiple_of((1 - meta[2]) * half, 128), half)
    branch = dot_nn(mixed_mine[...], w_out[rows_mine, :])
    branch = branch + dot_nn(mixed_other[...], w_out[rows_other, :])
    hat_one, scale_one = norm_forward(x_ref[...].astype(F32) + (branch + b_out))
    normed = hat_one * gain_one + shift_one
    normed_low = normed.astype(BF16)
    norm_t_ref[...] = normed_low.T
    chunk = 512
    second = jnp.zeros((tile, width), F32)
    for start in range(0, hidden_width, chunk):
        cut = slice(start, start + chunk)
        hidden = dot_nn(normed_low, w_up[:, cut]) + b_up_ref[:, cut]
        active, slope = gelu_and_slope(hidden)
        slope_scr[:, cut] = slope
        active_low = active.astype(BF16)
        active_t_ref[cut, :] = active_low.T
        second = second + dot_nn(active_low, w_down[cut, :])
    hat_two, scale_two = norm_forward(normed + (second + b_down))
    out_ref[...] = jnp.where(valid, hat_two * gain_two + shift_two, 0.0).astype(BF16)

    grad_result = jnp.where(valid, cot_ref[...].astype(F32), 0.0)
    grad_two = norm_back(grad_result, hat_two, scale_two, gain_two)
    grad_second = grad_two.astype(BF16)
    grad_second_ref[...] = grad_second
    grad_normed = grad_two
    for start in range(0, hidden_width, chunk):
        cut = slice(start, start + chunk)
        grad_active = dot_nt(grad_second, w_down[cut, :])
        grad_hidden = (slope_scr[:, cut] * grad_active).astype(BF16)
        grad_hidden_ref[:, cut] = grad_hidden
        grad_b_up_ref[:, cut] += column_sum(grad_hidden)
        grad_normed = grad_normed + dot_nt(grad_hidden, w_up[:, cut])
    grad_one = norm_back(grad_normed, hat_one, scale_one, gain_one)
    grad_branch = grad_one.astype(BF16)
    grad_branch_ref[...] = grad_branch
    grad_mixed_mine[...] = dot_nt(grad_branch, w_out[rows_mine, :]).astype(BF16)
    grad_mixed_other[...] = dot_nt(grad_branch, w_out[rows_other, :]).astype(BF16)
    sums = (
        column_sum(grad_branch),
        column_sum(grad_normed * hat_one),
        column_sum(grad_normed),
        column_sum(grad_second),
        column_sum(grad_result * hat_two),
        column_sum(grad_result),
    )
    for i, total in enumerate(sums):
        grad_vec_ref[i : i + 1, :] += total


def feed(meta, x, mixed, cot, up, down, vec, b_up, seq_len):
    rows, width = x.shape
    hidden_width = b_up.shape[1]
    tile = min(256, rows)
    by_row = lambda cols: pl.BlockSpec((tile, cols), lambda i, m: (i, 0))
    by_col = lambda tall: pl.BlockSpec((tall, tile), lambda i, m: (0, i))
    whole = lambda a: pl.BlockSpec(
        a.shape, lambda i, m: (0,) * a.ndim, pipeline_mode=pl.Buffered(1)
    )
    rows_of = lambda cols: jax.ShapeDtypeStruct((rows, cols), BF16)
    cols_of = lambda tall: jax.ShapeDtypeStruct((tall, rows), BF16)
    half = width // 2
    return pl.pallas_call(
        functools.partial(feed_kernel, seq_len),
        grid_spec=pltpu.PrefetchScalarGridSpec(
            num_scalar_prefetch=1,
            grid=(rows // tile,),
            in_specs=[by_row(width), by_row(half), by_row(half), by_row(width)]
            + [whole(a) for a in (*up, *down, vec, b_up)],
            out_specs=[
                by_row(width),
                by_col(width),
                by_col(hidden_width),
                by_row(hidden_width),
                by_row(width),
                by_row(width),
                by_row(half),
                by_row(half),
                pl.BlockSpec((8, width), lambda i, m: (0, 0)),
                pl.BlockSpec((1, hidden_width), lambda i, m: (0, 0)),
            ],
            scratch_shapes=[
                pltpu.VMEM((width, hidden_width), BF16),
                pltpu.VMEM((width, width), BF16),
                pltpu.VMEM((hidden_width, width), BF16),
                pltpu.VMEM((tile, hidden_width), F32),
            ],
        ),
        out_shape=[
            rows_of(width),
            cols_of(width),
            cols_of(hidden_width),
            rows_of(hidden_width),
            rows_of(width),
            rows_of(width),
            rows_of(half),
            rows_of(half),
            jax.ShapeDtypeStruct((8, width), F32),
            jax.ShapeDtypeStruct((1, hidden_width), F32),
        ],
        compiler_params=params(1),
        cost_estimate=cost(
            8 * rows * width * hidden_width + 4 * rows * width * width,
            40e6,
            2 * rows * hidden_width,
        ),
        name="feed_forward_and_back",
    )(meta, x, *mixed, cot, *up, *down, vec, b_up)


def store_blocks(meta, out_ref, value, cut, first=0):
    rows = out_ref.shape[2]
    for block in range(value.shape[0] // (2 * rows)):
        for half in range(2):
            start = (2 * block + half) * rows
            out_ref[meta[1] ^ half, turned(meta[0] ^ (first + block)), :, cut] = value[
                start : start + rows
            ].astype(BF16)


def grad_up_kernel(
    meta, norm_t_ref, mixed_mine, mixed_other, grad_hidden_ref, grad_branch_ref, out_ref
):
    up_cut = grad_hidden_ref.shape[1]
    store_blocks(meta, out_ref, dot_nn(norm_t_ref[...], grad_hidden_ref[...]), slice(0, up_cut))
    cut = slice(up_cut, out_ref.shape[3])
    few = BLOCKS // 2
    grad_branch = grad_branch_ref[...]
    store_blocks(meta, out_ref, dot_nn(mixed_mine[...], grad_branch), cut, meta[2] * few)
    store_blocks(meta, out_ref, dot_nn(mixed_other[...], grad_branch), cut, (1 - meta[2]) * few)


def grad_up(rel, meta, norm_t, mixed_t, grad_hidden, grad_branch, *gates):
    width, rows = norm_t.shape
    hidden_width = grad_hidden.shape[1]
    groups = 3
    up_cut, out_cut = hidden_width // (2 * groups), width // (2 * groups)
    block_rows = width // (2 * BLOCKS)
    whole = lambda tall: pl.BlockSpec(
        (tall, rows), lambda n, m: (0, 0), pipeline_mode=pl.Buffered(1)
    )
    turn = lambda n, m: (0, (m[2] ^ rel) * groups + n)
    return pl.pallas_call(
        gated(grad_up_kernel, 5, len(gates)),
        grid_spec=pltpu.PrefetchScalarGridSpec(
            num_scalar_prefetch=1,
            grid=(groups,),
            in_specs=[
                whole(width),
                whole(width // 2),
                whole(width // 2),
                pl.BlockSpec((rows, up_cut), turn),
                pl.BlockSpec((rows, out_cut), turn),
                *gate_specs(gates),
            ],
            out_specs=pl.BlockSpec(
                (2, BLOCKS, block_rows, up_cut + out_cut), lambda n, m: (0, 0, 0, n)
            ),
        ),
        out_shape=jax.ShapeDtypeStruct(
            (2, BLOCKS, block_rows, groups * (up_cut + out_cut)), BF16
        ),
        compiler_params=params(1),
        cost_estimate=cost(rows * width * (hidden_width + width), 12e6),
        name="grad_up",
    )(meta, norm_t, *mixed_t, grad_hidden, grad_branch, *gates)


def grad_down_kernel(meta, active_t_ref, grad_second_ref, keep_ref, send_ref):
    value = dot_nn(active_t_ref[...], grad_second_ref[...])
    rows = keep_ref.shape[2]
    mine = meta[2] == 0
    low, high = value[: 2 * rows], value[2 * rows :]
    keep = jnp.where(mine, low, high).astype(BF16)
    send = jnp.where(mine, high, low).astype(BF16)
    for half in range(2):
        keep_ref[meta[1] ^ half, 0] = keep[half * rows : (half + 1) * rows]
        send_ref[meta[1] ^ half, 0] = send[half * rows : (half + 1) * rows]


def grad_down(meta, active_t, grad_second):
    hidden_width, rows = active_t.shape
    width = grad_second.shape[1]
    block = hidden_width // BLOCKS
    out = jax.ShapeDtypeStruct((2, BLOCKS, block // 4, width), BF16)
    spec = pl.BlockSpec((2, 1, block // 4, width), lambda j, m: (0, j, 0, 0))
    return pl.pallas_call(
        grad_down_kernel,
        grid_spec=pltpu.PrefetchScalarGridSpec(
            num_scalar_prefetch=1,
            grid=(BLOCKS,),
            in_specs=[
                pl.BlockSpec((block, rows), lambda j, m: (m[0] ^ turned(j), 0)),
                pl.BlockSpec((rows, width), lambda j, m: (0, 0), pipeline_mode=pl.Buffered(1)),
            ],
            out_specs=[spec, spec],
        ),
        out_shape=[out, out],
        compiler_params=params(1),
        cost_estimate=cost(2 * rows * hidden_width * width, 16e6),
        name="grad_down",
    )(meta, active_t, grad_second)


def attend_back_kernel(
    meta,
    x_t_ref,
    query_ref,
    key_ref,
    value_ref,
    mixed_t_ref,
    grad_mixed_ref,
    lse_ref,
    grad_qkv_ref,
    grad_w_ref,
    grad_bias_ref,
    grad_scr,
):
    seq = pl.program_id(0)
    length = meta[3 + seq]
    rows, wide = query_ref.shape[1:]
    lane = lax.broadcasted_iota(jnp.int32, (rows, wide), 1)
    key_ok = lax.broadcasted_iota(jnp.int32, (rows, rows), 0) < length

    @pl.when(seq == 0)
    def _():
        grad_bias_ref[...] = jnp.zeros_like(grad_bias_ref)

    query = query_ref[0] * jnp.asarray(0.125, BF16)
    key, value, grad_out = key_ref[0], value_ref[0], grad_mixed_ref[0]
    product = grad_out.astype(F32).T * mixed_t_ref[...].astype(F32)
    key_t = key.T
    grad_query, grad_key, grad_value = [], 0.0, 0.0
    for head in range(2):
        keep = (lane >= 64) == (head == 1)
        query_one = jnp.where(keep, query, jnp.zeros_like(query))
        grad_one = jnp.where(keep, grad_out, jnp.zeros_like(grad_out))
        inner = slice(64 * head, 64 * head + 64)
        delta = jnp.sum(product[inner], axis=0, keepdims=True)
        scores = jnp.where(key_ok, dot_nt(key, query_one), -1e30)
        prob = jnp.exp(scores - lse_ref[0, head])
        grad_prob = dot_nt(value, grad_one)
        grad_scores = (prob * (grad_prob - delta)).astype(BF16)
        grad_value = grad_value + dot_nn(prob.astype(BF16), grad_one)
        grad_key = grad_key + dot_nn(grad_scores, query_one)
        grad_query.append(dot_nn(key_t[inner], grad_scores) * 0.125)
    grads = (jnp.concatenate(grad_query, axis=0).T, grad_key, grad_value)
    start = pl.multiple_of(seq * rows, 128)
    for kind, grad in enumerate(grads):
        grad = grad.astype(BF16)
        cut = slice(kind * wide, (kind + 1) * wide)
        grad_scr[pl.ds(start, rows), cut] = grad
        grad_qkv_ref[0, :, cut] = grad
        grad_bias_ref[:, cut] += column_sum(grad)

    @pl.when(seq == pl.num_programs(0) - 1)
    def _():
        store_blocks(meta, grad_w_ref, dot_nn(x_t_ref[...], grad_scr[...]), slice(None))


def attend_back(pair, meta, x_t, qkv, mixed_t, grad_mixed, lse, *gates):
    seqs, length, wide = qkv.shape
    width, rows = x_t.shape
    pairs = HEADS // 4
    part = wide // (3 * pairs)
    block_rows = width // (2 * BLOCKS)
    of_pair = lambda kind: pl.BlockSpec(
        (1, length, part), lambda s, m: (s, 0, kind * pairs + pair)
    )
    return pl.pallas_call(
        gated(attend_back_kernel, 7, len(gates)),
        grid_spec=pltpu.PrefetchScalarGridSpec(
            num_scalar_prefetch=1,
            grid=(seqs,),
            in_specs=[
                pl.BlockSpec((width, rows), lambda s, m: (0, 0), pipeline_mode=pl.Buffered(1)),
                of_pair(0),
                of_pair(1),
                of_pair(2),
                pl.BlockSpec((part, length), lambda s, m: (pair, s)),
                of_pair(0),
                pl.BlockSpec((1, 2, 1, length), lambda s, m: (s, pair, 0, 0)),
                *gate_specs(gates),
            ],
            out_specs=[
                pl.BlockSpec((1, length, 3 * part), lambda s, m: (s, 0, 0)),
                pl.BlockSpec((2, BLOCKS, block_rows, 3 * part), lambda s, m: (0, 0, 0, 0)),
                pl.BlockSpec((1, 3 * part), lambda s, m: (0, 0)),
            ],
            scratch_shapes=[pltpu.VMEM((rows, 3 * part), BF16)],
        ),
        out_shape=[
            jax.ShapeDtypeStruct((seqs, length, 3 * part), BF16),
            jax.ShapeDtypeStruct((2, BLOCKS, block_rows, 3 * part), BF16),
            jax.ShapeDtypeStruct((1, 3 * part), F32),
        ],
        compiler_params=params(1),
        cost_estimate=cost(
            6 * rows * width * part + 10 * rows * length * 4 * part,
            8e6,
            rows * length * 2,
        ),
        name="attend_back",
    )(meta, x_t, qkv, qkv, qkv, mixed_t, grad_mixed, lse, *gates)


def input_kernel(meta, branch_ref, *refs):
    pairs = HEADS // 4
    grads, weights = refs[: 2 * pairs], refs[2 * pairs : 2 * pairs + 2]
    out_ref, scratch = refs[2 * pairs + 2], refs[2 * pairs + 3 :]

    @pl.when(pl.program_id(0) == 0)
    def _():
        for half in range(2):
            place_rows(meta, weights[half], scratch[half], slice(None), slice(None))

    total = branch_ref[...].astype(F32)
    for half in range(2):
        mine = [grads[half * pairs + pair][...] for pair in range(pairs)]
        one = mine[0].shape[1] // 3
        cols = [g[:, kind * one : (kind + 1) * one] for kind in range(3) for g in mine]
        total = total + dot_nt(jnp.concatenate(cols, axis=1), scratch[half][...])
    out_ref[...] = total


def input_grad_of(meta, grad_branch, grads, weights, *gates):
    rows, width = grad_branch.shape
    part = weights[0].shape[3] // 3
    tile = min(256, rows)
    whole = lambda a: pl.BlockSpec(
        a.shape, lambda i, m: (0, 0, 0, 0), pipeline_mode=pl.Buffered(1)
    )
    by_row = lambda cols: pl.BlockSpec((tile, cols), lambda i, m: (i, 0))
    return pl.pallas_call(
        gated(input_kernel, 1 + len(grads) + len(weights), len(gates)),
        grid_spec=pltpu.PrefetchScalarGridSpec(
            num_scalar_prefetch=1,
            grid=(rows // tile,),
            in_specs=[by_row(width)]
            + [by_row(g.shape[1]) for g in grads]
            + [whole(w) for w in weights]
            + gate_specs(gates),
            out_specs=by_row(width),
            scratch_shapes=[pltpu.VMEM((width, 3 * part), BF16)] * 2,
        ),
        out_shape=jax.ShapeDtypeStruct((rows, width), F32),
        compiler_params=params(1),
        cost_estimate=cost(12 * rows * width * part, 14e6),
        name="input_grad",
    )(meta, grad_branch, *grads, *weights, *gates)


def together(*arrays):
    return lax.optimization_barrier(arrays)


CORE, X, Y, NEAR, FAR = 1, 2, 4, 8, 16
DEVICES = 32


def swap(array, mask):
    pairs = [(i, i ^ mask) for i in range(DEVICES)]
    return lax.ppermute(array, ("shard", "rep"), pairs)


def gather_z(piece):
    came = [swap(piece, mask) for mask in (FAR, NEAR, NEAR | FAR)]
    return jnp.stack([piece] + came)


def gather_plane(held):
    by_y, by_x, across = (swap(held, mask) for mask in (Y, X, X | Y))
    low = jnp.concatenate([held, by_y], axis=0)
    return jnp.stack([low, jnp.concatenate([by_x, across], axis=0)])


def grow(held, mask):
    came = swap(held, mask)
    if mask == X:
        return jnp.stack([held, came])
    return jnp.concatenate([held, came], axis=held.ndim - 3)


def add(*terms):
    total = terms[0].astype(F32)
    for term in terms[1:]:
        total = total + term.astype(F32)
    return total.astype(BF16)


def shrink(kept, came, mask):
    if mask == X:
        low, high = (0,), (1,)
    else:
        cut = BLOCKS // 2
        if kept.ndim == 4:
            low, high = (slice(None), slice(0, cut)), (slice(None), slice(cut, None))
        else:
            low, high = (slice(0, cut),), (slice(cut, None),)
    return add(kept[low], came[low]), add(kept[high], came[high])


def reduce_z(held, came):
    parts = [add(held[i], came[i]) for i in range(4)]
    return sum_z(parts)


def sum_z(parts):
    return add(
        parts[0],
        *[swap(parts[i], mask) for i, mask in ((1, FAR), (2, NEAR), (3, NEAR | FAR))],
    )


def plane_sends(kept, came):
    cut = BLOCKS // 2
    pick = lambda a, x, y: a[x, cut:] if y else a[x, :cut]
    parts = [[add(pick(kept, x, y), pick(came, x, y)) for y in range(2)] for x in range(2)]
    return [
        parts[0][0],
        swap(parts[0][1], Y),
        swap(parts[1][0], X),
        swap(parts[1][1], X | Y),
    ]


def plane_sum(terms):
    return [add(*[t[i] for t in terms]) for i in range(4)]


def share_quarters(piece, rep):
    parts = [piece] + [swap(piece, mask) for mask in (CORE, X, X | CORE)]
    out = []
    for place in range(4):
        pick = parts[3]
        for rel in range(3):
            pick = jnp.where(rep == place ^ rel, parts[rel], pick)
        out.append(pick.astype(F32))
    return out


def local(
    fast,
    tokens,
    lengths,
    w_qkv,
    b_query,
    b_value,
    w_out,
    b_out,
    ln1_gain,
    ln1_bias,
    w_up,
    b_up,
    w_down,
    b_down,
    ln2_gain,
    ln2_bias,
    cotangent,
):
    seqs, seq_len, width = tokens.shape
    rows = seqs * seq_len
    hidden_width = w_up.shape[1]
    half = width // 2
    groups = 3
    up_cut, out_cut = hidden_width // (2 * groups), half // groups
    vectors = (b_query, b_value, b_out, ln1_gain, ln1_bias, b_down, ln2_gain, ln2_bias, b_up)
    names = len(vectors)

    if fast:
        shard, rep = lax.axis_index("shard"), lax.axis_index("rep")
        x_at, core = rep // 2, rep % 2
    else:
        shard = rep = x_at = core = jnp.int32(0)
    block = width // BLOCKS
    quarter = block // 2
    meta = jnp.concatenate(
        [jnp.stack([shard, x_at, core]).astype(jnp.int32), lengths.astype(jnp.int32)]
    )

    def qkv_parts(w):
        return w.reshape(-1, 2, quarter, 3, 2, half)

    def up_parts(up, out):
        up = up.reshape(-1, 2, quarter, 2, groups, up_cut)
        out = out.reshape(-1, 2, quarter, 2, groups, out_cut)
        return jnp.concatenate([up, out], axis=-1)

    if fast:
        table = grow(gather_z(jnp.concatenate(vectors).reshape(1, -1)), Y)
        table = table.reshape(BLOCKS, -1)
        table = jnp.take(table, turned(jnp.arange(BLOCKS) ^ shard), axis=0)

        def piece(weight, columns, start):
            place = (x_at * quarter, start + core * columns)
            return lax.dynamic_slice(weight, place, (quarter, columns))

        qkv_piece = jnp.concatenate([piece(w_qkv, half, k * width) for k in range(3)], axis=1)
        up_piece, out_piece = piece(w_up, hidden_width // 2, 0), piece(w_out, half, 0)
        up_piece = jnp.concatenate(
            [
                part[:, g * cut : (g + 1) * cut]
                for g in range(groups)
                for part, cut in ((up_piece, up_cut), (out_piece, out_cut))
            ],
            axis=1,
        )
        down_rows = w_down.shape[0] // 4
        down_piece = lax.dynamic_slice(
            w_down, ((2 * core + x_at) * down_rows, 0), (down_rows, width)
        )
        qkv_z = gather_z(qkv_piece)
        qkv_z, up_piece, down_piece = together(qkv_z, up_piece, down_piece)
        qkv_mine, up_z, down_z = gather_plane(qkv_z), gather_z(up_piece), gather_z(down_piece)
        qkv_mine, up_z, down_z = together(qkv_mine, up_z, down_z)
        qkv_w = qkv_mine, swap(qkv_mine, CORE)
        up_mine, down_mine = grow(up_z, Y), grow(down_z, X)
        *qkv_w, up_mine, down_mine = together(*qkv_w, up_mine, down_mine)
        up_mine, down_mine = grow(up_mine, X), grow(down_mine, Y)
    else:
        everything = lambda a: lax.all_gather(a, "shard", axis=0, tiled=True)
        table = None
        full = [everything(v) for v in vectors]
        order = [turned(p) for p in range(BLOCKS)]
        both = lambda a: (a[0][:, order], a[1][:, order])
        qkv_w = both(
            qkv_parts(everything(w_qkv))
            .transpose(4, 1, 0, 2, 3, 5)
            .reshape(2, 2, BLOCKS, quarter, 3 * half)
        )
        up_w = both(
            up_parts(everything(w_up), everything(w_out))
            .transpose(3, 1, 0, 2, 4, 5)
            .reshape(2, 2, BLOCKS, quarter, -1)
        )
        down_w = both(
            everything(w_down).reshape(BLOCKS, 2, 2, -1, width).transpose(1, 2, 0, 3, 4)
        )
    if fast:
        full, start = [], 0
        for v in vectors:
            full.append(table[:, start : start + v.shape[0]].reshape(-1))
            start += v.shape[0]
    full = [v.astype(F32) for v in full]
    bias = jnp.stack(
        [full[0].reshape(2, half), jnp.zeros((2, half), F32), full[1].reshape(2, half)], axis=1
    ).reshape(2, 1, 3 * half)
    vec = jnp.stack(full[2:8] + [jnp.zeros_like(full[0])] * 2)

    if fast:
        bias = jnp.where(core == 0, bias, bias[::-1])
    x_rows = tokens.reshape(rows, width)
    x_t = x_rows.T
    heads = [attend(meta, tokens, qkv_w[i], bias[i]) for i in range(2)]
    if fast:
        up_mine, down_mine, *heads[1] = together(up_mine, down_mine, *heads[1])
        up_w = up_mine, swap(up_mine, CORE)
        down_w = down_mine, swap(down_mine, CORE)
    qkv, mixed, mixed_t, lse = zip(*heads)
    mixed_rows = [m.reshape(rows, half) for m in mixed]
    (
        layer_out,
        norm_t,
        active_t,
        grad_hidden,
        grad_second,
        grad_branch,
        *grad_mixed,
        grad_vec,
        grad_b_up,
    ) = feed(
        meta,
        x_rows,
        mixed_rows,
        cotangent.reshape(rows, width),
        up_w,
        down_w,
        vec,
        full[8].reshape(1, -1),
        seq_len,
    )
    grad_mixed = [g.reshape(seqs, seq_len, half) for g in grad_mixed]
    pairs = HEADS // 4
    hop = swap if fast else (lambda a, mask: a)

    def back(pair, i, *gates):
        return attend_back(
            pair, meta, x_t, qkv[i], mixed_t[i], grad_mixed[i], lse[i], *gates
        )

    down_keep, down_send = grad_down(meta, active_t, grad_second)
    down_came = hop(down_send, CORE)
    up_send = grad_up(1, meta, norm_t, mixed_t, grad_hidden, grad_branch, down_send)
    up_came = hop(up_send, CORE)
    down_low, down_high = shrink(down_keep, down_came, X)
    down_came = hop(down_high, X)
    up_keep = grad_up(
        0, meta, norm_t, mixed_t, grad_hidden, grad_branch, up_send, down_low, down_high
    )
    up_low, up_high = shrink(up_keep, up_came, Y)
    up_came = hop(up_high, Y)
    backs, sends, gates = [[None] * pairs, [None] * pairs], [None] * pairs, [up_low, up_high]
    for pair in range(pairs):
        backs[1][pair] = back(pair, 1, *gates)
        q_came = hop(backs[1][pair][1], CORE)
        gates = [backs[1][pair][0]]
        if pair == 1:
            down_low, down_high = shrink(down_low, down_came, Y)
            down_came = hop(down_high, Y)
            gates += [down_low, down_high]
        if pair == 2:
            up_low, up_high = shrink(up_low, up_came, X)
            up_came = hop(up_high, X)
            gates += [up_low, up_high]
        backs[0][pair] = back(pair, 0, *gates)
        gates = [backs[0][pair][0]]
        if fast:
            sends[pair] = plane_sends(backs[0][pair][1], q_came)
            gates.append(sends[pair][0])
            if pair == 1:
                sends[0] = plane_sum(sends[0])
                gates.append(sends[0][0])
            if pair == 2:
                sends[1] = plane_sum(sends[1])
                gates.append(sends[1][0])
    input_grad = input_grad_of(
        meta,
        grad_branch,
        [b[0].reshape(rows, -1) for i in range(2) for b in backs[i]],
        qkv_w,
        *gates,
    )

    bias_halves = jnp.stack([jnp.stack([b[2] for b in backs[i]]) for i in range(2)])
    bias_halves = bias_halves.reshape(2, pairs, 3, -1).transpose(0, 2, 1, 3).reshape(2, 3, half)
    bias_halves = jnp.where(core == 0, bias_halves, bias_halves[::-1])
    grad_vectors = [
        bias_halves[:, 0].reshape(-1),
        bias_halves[:, 2].reshape(-1),
        *[grad_vec[i] for i in range(6)],
        grad_b_up[0],
    ]
    if fast:
        total = jnp.concatenate([g.reshape(BLOCKS, -1) for g in grad_vectors], axis=1)
        for mask in (CORE, X, Y, NEAR, FAR):
            total = total + swap(total, mask)
        total = lax.dynamic_index_in_dim(total, shard, 0, keepdims=False)
        sums, start = [], 0
        for v in vectors:
            sums.append(total[start : start + v.shape[0]])
            start += v.shape[0]
        down = share_quarters(reduce_z(down_low, down_came), rep)
        sends[2] = plane_sum(sends[2])
        parts = [share_quarters(sum_z(send), rep) for send in sends]
        up = share_quarters(reduce_z(up_low, up_came), rep)

        def whole(columns_of):
            rows_of = [
                jnp.concatenate([c for core in range(2) for c in columns_of(2 * x + core)], axis=1)
                for x in range(2)
            ]
            return jnp.concatenate(rows_of, axis=0)

        grad_w_down = jnp.concatenate([down[i] for i in (0, 2, 1, 3)], axis=0)
        step = up_cut + out_cut
        grad_w_up = whole(lambda q: [up[q][:, g * step :][:, :up_cut] for g in range(groups)])
        grad_w_out = whole(
            lambda q: [up[q][:, g * step + up_cut : (g + 1) * step] for g in range(groups)]
        )
        one = half // pairs
        grad_w_qkv = jnp.concatenate(
            [
                whole(lambda q: [p[q][:, kind * one : (kind + 1) * one] for p in parts])
                for kind in range(3)
            ],
            axis=1,
        )
    else:
        total_of = lambda a: lax.psum(
            lax.psum_scatter(a, "shard", scatter_dimension=0, tiled=True), "rep"
        )
        sums = [total_of(g) for g in grad_vectors]
        order = [turned(p) for p in range(BLOCKS)]
        down_keep, down_send, up_keep, up_send = (
            a[:, order] for a in (down_keep, down_send, up_keep, up_send)
        )
        down = jnp.stack([down_keep, down_send]).transpose(2, 0, 1, 3, 4)
        grad_w_down = total_of(down.reshape(hidden_width, width).astype(F32))
        up = jnp.stack([up_keep, up_send]).reshape(
            2, 2, BLOCKS, quarter, groups, up_cut + out_cut
        )
        up = up.transpose(2, 1, 3, 0, 4, 5)
        grad_w_up = total_of(up[..., :up_cut].reshape(width, hidden_width).astype(F32))
        grad_w_out = total_of(up[..., up_cut:].reshape(width, width).astype(F32))
        qkv_sum = jnp.stack([jnp.stack([b[1][:, order] for b in backs[i]]) for i in range(2)])
        qkv_sum = qkv_sum.reshape(2, pairs, 2, BLOCKS, quarter, 3, -1)
        qkv_sum = qkv_sum.transpose(3, 2, 4, 5, 0, 1, 6).reshape(width, 3 * width)
        grad_w_qkv = total_of(qkv_sum.astype(F32))
    return (
        layer_out.reshape(seqs, seq_len, width),
        input_grad.reshape(seqs, seq_len, width),
        grad_w_qkv,
        sums[0],
        sums[1],
        grad_w_out,
        sums[2],
        sums[3],
        sums[4],
        grad_w_up,
        sums[8],
        grad_w_down,
        sums[5],
        sums[6],
        sums[7],
    )


def solution(mesh):
    fast = mesh.shape["shard"] == BLOCKS and mesh.shape["rep"] == 4
    by_seq = P(("shard", "rep"), None, None)
    one, two = P("shard"), P("shard", None)
    in_specs = (by_seq, P(("shard", "rep")), two, one, one, two, one, one, one)
    in_specs = in_specs + (two, one, two, one, one, one, by_seq)
    out_specs = (by_seq, by_seq, two, one, one, two, one, one, one, two, one, two, one, one, one)
    return jax.shard_map(
        functools.partial(local, fast),
        mesh=mesh,
        in_specs=in_specs,
        out_specs=out_specs,
        check_vma=False,
    )
```

```python
import functools

import jax
import jax.numpy as jnp
from jax import lax
from jax.experimental import pallas as pl
from jax.experimental.pallas import tpu as pltpu
from jax.sharding import PartitionSpec as P

HEADS = 12
EPS = 1e-05
F32 = jnp.float32
BF16 = jnp.bfloat16
BLOCKS = 8
GROUPS = 3
VMEM_LIMIT = 58 * 1024 * 1024


def dot_nn(a, b):
    return lax.dot_general(a, b, (((1,), (0,)), ((), ())), preferred_element_type=F32)


def dot_nt(a, b):
    return lax.dot_general(a, b, (((1,), (1,)), ((), ())), preferred_element_type=F32)


def dot_tn(a, b):
    return lax.dot_general(a, b, (((0,), (0,)), ((), ())), preferred_element_type=F32)


def params(grid_dims):
    return pltpu.CompilerParams(
        dimension_semantics=("arbitrary",) * grid_dims, vmem_limit_bytes=VMEM_LIMIT
    )


def cost(flops, nbytes, trans=0):
    return pl.CostEstimate(
        flops=int(flops) // 16, bytes_accessed=int(nbytes) // 16, transcendentals=int(trans) // 16
    )


def gated(kernel, inputs, gates):
    def body(*refs):
        kernel(*refs[: inputs + 1], *refs[inputs + 1 + gates :])

    return body


def gate_specs(gates):
    return [pl.BlockSpec(memory_space=pl.ANY)] * len(gates)


def turned(place):
    return ((place & 1) << 2) | (place & 2) | ((place >> 2) & 1)


def place_rows(meta, source, target, columns, cut):
    rows = source.shape[2]
    for half in range(2):
        for block in range(BLOCKS):
            start = (meta[0] ^ turned(block)) * (2 * rows) + (meta[1] ^ half) * rows
            target[pl.ds(pl.multiple_of(start, 16), rows), cut] = source[half, block, :, columns]


def attend_kernel(meta, x_ref, w_ref, bias_ref, qkv_ref, mixed_ref, mixed_t_ref, lse_ref, w_scr):
    seq = pl.program_id(0)
    wide = w_scr.shape[1]
    part = wide // 3

    @pl.when(seq == 0)
    def _():
        place_rows(meta, w_ref, w_scr, slice(None), slice(None))

    length = meta[3 + seq]
    qkv = (dot_nn(x_ref[0], w_scr[...]) + bias_ref[...]).astype(BF16)
    qkv_ref[0] = qkv
    rows = qkv.shape[0]
    lane = lax.broadcasted_iota(jnp.int32, (rows, 128), 1)
    key_ok = lax.broadcasted_iota(jnp.int32, (rows, rows), 0) < length
    for pair in range(part // 128):
        cut = pair * 128
        query = qkv[:, cut : cut + 128] * jnp.asarray(0.125, BF16)
        key = qkv[:, part + cut : part + cut + 128]
        value_t = qkv[:, 2 * part + cut : 2 * part + cut + 128].T
        outs = []
        for head in range(2):
            query_one = jnp.where((lane >= 64) == (head == 1), query, jnp.zeros_like(query))
            scores = jnp.where(key_ok, dot_nt(key, query_one), -1e30)
            top = jnp.max(scores, axis=0, keepdims=True)
            exp_scores = jnp.exp(scores - top)
            total = jnp.sum(exp_scores, axis=0, keepdims=True)
            lse_ref[0, 2 * pair + head] = top + jnp.log(total)
            out = dot_nn(value_t[64 * head : 64 * head + 64], exp_scores.astype(BF16))
            outs.append(out * (1.0 / total))
        mixed_t = jnp.concatenate(outs, axis=0)
        mixed_t_ref[cut : cut + 128, :] = mixed_t.astype(BF16)
        mixed_ref[0, :, cut : cut + 128] = mixed_t.T.astype(BF16)


def attend(meta, x, weight, bias):
    seqs, length, width = x.shape
    wide = weight.shape[3]
    part = wide // 3
    half_heads = HEADS // 2
    whole = lambda s, m: (0, 0, 0, 0)
    return pl.pallas_call(
        attend_kernel,
        grid_spec=pltpu.PrefetchScalarGridSpec(
            num_scalar_prefetch=1,
            grid=(seqs,),
            in_specs=[
                pl.BlockSpec((1, length, width), lambda s, m: (s, 0, 0)),
                pl.BlockSpec(weight.shape, whole, pipeline_mode=pl.Buffered(1)),
                pl.BlockSpec((1, wide), lambda s, m: (0, 0)),
            ],
            out_specs=[
                pl.BlockSpec((1, length, wide), lambda s, m: (s, 0, 0)),
                pl.BlockSpec((1, length, part), lambda s, m: (s, 0, 0)),
                pl.BlockSpec((part, length), lambda s, m: (0, s)),
                pl.BlockSpec((1, half_heads, 1, length), lambda s, m: (s, 0, 0, 0)),
            ],
            scratch_shapes=[pltpu.VMEM((width, wide), BF16)],
        ),
        out_shape=[
            jax.ShapeDtypeStruct((seqs, length, wide), BF16),
            jax.ShapeDtypeStruct((seqs, length, part), BF16),
            jax.ShapeDtypeStruct((part, seqs * length), BF16),
            jax.ShapeDtypeStruct((seqs, half_heads, 1, length), F32),
        ],
        compiler_params=params(1),
        cost_estimate=cost(
            2 * seqs * length * width * wide + 8 * seqs * length * length * width,
            10e6,
            seqs * length * length * half_heads,
        ),
        name="attend_forward",
    )(meta, x, weight, bias)


def gelu_and_slope(hidden):
    size = jnp.abs(hidden)
    bell = jnp.exp(-0.5 * hidden * hidden)
    t = 1.0 / (1.0 + (0.3275911 * 0.7071067811865476) * size)
    poly = t * (
        0.5 * 0.254829592
        + t
        * (
            0.5 * -0.284496736
            + t * (0.5 * 1.421413741 + t * (0.5 * -1.453152027 + t * (0.5 * 1.061405429)))
        )
    )
    tail = poly * bell
    phi = jnp.where(hidden < 0.0, tail, 1.0 - tail)
    return hidden * phi, phi + hidden * bell * 0.3989422804014327


def norm_forward(hidden):
    center = hidden - jnp.mean(hidden, axis=-1, keepdims=True)
    scale = lax.rsqrt(jnp.mean(center * center, axis=-1, keepdims=True) + EPS)
    return center * scale, scale


def norm_back(grad, hat, scale, gain):
    grad_hat = grad * gain
    shift = jnp.mean(grad_hat, axis=-1, keepdims=True)
    along = jnp.mean(grad_hat * hat, axis=-1, keepdims=True)
    return scale * (grad_hat - shift - hat * along)


def column_sum(rows):
    return jnp.sum(rows.astype(F32), axis=0, keepdims=True)


def place_up(meta, mine, other, w_up, w_out):
    hidden_width, width = w_up.shape[1], w_out.shape[1]
    up_cut, out_cut = hidden_width // (2 * GROUPS), width // (2 * GROUPS)
    for rel, source in enumerate((mine, other)):
        core = meta[2] ^ rel
        for group in range(GROUPS):
            base = group * (up_cut + out_cut)
            up_to = pl.multiple_of(core * (hidden_width // 2) + group * up_cut, 128)
            out_to = pl.multiple_of(core * (width // 2) + group * out_cut, 128)
            place_rows(meta, source, w_up, slice(base, base + up_cut), pl.ds(up_to, up_cut))
            place_rows(
                meta,
                source,
                w_out,
                slice(base + up_cut, base + up_cut + out_cut),
                pl.ds(out_to, out_cut),
            )


def place_down(meta, mine, other, w_down):
    rows = mine.shape[2]
    for rel, source in enumerate((mine, other)):
        for half in range(2):
            for block in range(BLOCKS):
                start = (
                    (meta[0] ^ turned(block)) * (4 * rows)
                    + (meta[2] ^ rel) * (2 * rows)
                    + (meta[1] ^ half) * rows
                )
                w_down[pl.ds(pl.multiple_of(start, 16), rows), :] = source[half, block]


def halves_of(meta, width):
    half = width // 2
    return (
        pl.ds(pl.multiple_of(meta[2] * half, 128), half),
        pl.ds(pl.multiple_of((1 - meta[2]) * half, 128), half),
    )


CHUNK = 512


def up_kernel(
    meta,
    x_ref,
    mixed_mine,
    mixed_other,
    up_mine,
    up_other,
    vec_ref,
    b_up_ref,
    hat_ref,
    scale_ref,
    norm_t_ref,
    active_ref,
    active_t_ref,
    slope_ref,
    w_up,
    w_out,
):
    width, hidden_width = w_up.shape

    @pl.when(pl.program_id(0) == 0)
    def _():
        place_up(meta, up_mine, up_other, w_up, w_out)

    b_out, gain, shift = [vec_ref[i : i + 1, :] for i in range(3)]
    rows_mine, rows_other = halves_of(meta, width)
    branch = dot_nn(mixed_mine[...], w_out[rows_mine, :])
    branch = branch + dot_nn(mixed_other[...], w_out[rows_other, :])
    hat, scale = norm_forward(x_ref[...].astype(F32) + (branch + b_out))
    hat_ref[...] = hat
    scale_ref[...] = jnp.broadcast_to(scale, scale_ref.shape)
    normed_low = (hat * gain + shift).astype(BF16)
    norm_t_ref[...] = normed_low.T
    for start in range(0, hidden_width, CHUNK):
        cut = slice(start, start + CHUNK)
        hidden = dot_nn(normed_low, w_up[:, cut]) + b_up_ref[:, cut]
        active, slope = gelu_and_slope(hidden)
        slope_ref[:, cut] = slope.astype(BF16)
        active_low = active.astype(BF16)
        active_ref[:, cut] = active_low
        active_t_ref[cut, :] = active_low.T


def down_kernel(
    seq_len,
    meta,
    hat_ref,
    active_ref,
    cot_ref,
    down_mine,
    down_other,
    vec_ref,
    out_ref,
    grad_second_ref,
    grad_vec_ref,
    w_down,
):
    step = pl.program_id(0)
    tile = hat_ref.shape[0]

    @pl.when(step == 0)
    def _():
        grad_vec_ref[...] = jnp.zeros_like(grad_vec_ref)
        place_down(meta, down_mine, down_other, w_down)

    gain_one, shift_one, b_down, gain, shift = [vec_ref[i : i + 1, :] for i in range(1, 6)]
    seq = lax.div(step * tile, seq_len)
    place = lax.broadcasted_iota(jnp.int32, (tile, 1), 0) + lax.rem(step * tile, seq_len)
    valid = place < meta[3 + seq]
    second = dot_nn(active_ref[...], w_down[...])
    normed = hat_ref[...] * gain_one + shift_one
    hat, scale = norm_forward(normed + (second + b_down))
    out_ref[...] = jnp.where(valid, hat * gain + shift, 0.0).astype(BF16)
    grad_result = jnp.where(valid, cot_ref[...].astype(F32), 0.0)
    grad_second = norm_back(grad_result, hat, scale, gain).astype(BF16)
    grad_second_ref[...] = grad_second
    sums = column_sum(grad_second), column_sum(grad_result * hat), column_sum(grad_result)
    for i, total in enumerate(sums):
        grad_vec_ref[i : i + 1, :] += total


def rest_kernel(
    meta,
    grad_second_ref,
    slope_ref,
    hat_ref,
    scale_ref,
    up_mine,
    up_other,
    down_mine,
    down_other,
    vec_ref,
    grad_hidden_ref,
    grad_branch_ref,
    grad_mixed_mine,
    grad_mixed_other,
    grad_vec_ref,
    grad_b_up_ref,
    w_up,
    w_out,
    w_down,
):
    width, hidden_width = w_up.shape

    @pl.when(pl.program_id(0) == 0)
    def _():
        grad_vec_ref[...] = jnp.zeros_like(grad_vec_ref)
        grad_b_up_ref[...] = jnp.zeros_like(grad_b_up_ref)
        place_up(meta, up_mine, up_other, w_up, w_out)
        place_down(meta, down_mine, down_other, w_down)

    grad_second = grad_second_ref[...]
    grad_normed = grad_second.astype(F32)
    for start in range(0, hidden_width, CHUNK):
        cut = slice(start, start + CHUNK)
        grad_active = dot_nt(grad_second, w_down[cut, :])
        grad_hidden = (slope_ref[:, cut].astype(F32) * grad_active).astype(BF16)
        grad_hidden_ref[:, cut] = grad_hidden
        grad_b_up_ref[:, cut] += column_sum(grad_hidden)
        grad_normed = grad_normed + dot_nt(grad_hidden, w_up[:, cut])
    hat = hat_ref[...]
    gain = vec_ref[1:2, :]
    grad_branch = norm_back(grad_normed, hat, scale_ref[:, 0:1], gain).astype(BF16)
    grad_branch_ref[...] = grad_branch
    rows_mine, rows_other = halves_of(meta, width)
    grad_mixed_mine[...] = dot_nt(grad_branch, w_out[rows_mine, :]).astype(BF16)
    grad_mixed_other[...] = dot_nt(grad_branch, w_out[rows_other, :]).astype(BF16)
    sums = column_sum(grad_branch), column_sum(grad_normed * hat), column_sum(grad_normed)
    for i, total in enumerate(sums):
        grad_vec_ref[i : i + 1, :] += total


def by_tile(kernel, name, flops, meta, tiled, wholes, gates, outs, scratch):
    rows = tiled[0].shape[0]
    tile = min(256, rows)
    by_row = lambda cols: pl.BlockSpec((tile, cols), lambda i, m: (i, 0))
    whole = lambda a: pl.BlockSpec(
        a.shape, lambda i, m: (0,) * a.ndim, pipeline_mode=pl.Buffered(1)
    )
    specs, shapes = [], []
    for kind, size, dtype in outs:
        if kind == "row":
            specs.append(by_row(size))
            shapes.append(jax.ShapeDtypeStruct((rows, size), dtype))
        elif kind == "col":
            specs.append(pl.BlockSpec((size, tile), lambda i, m: (0, i)))
            shapes.append(jax.ShapeDtypeStruct((size, rows), dtype))
        else:
            specs.append(pl.BlockSpec(size, lambda i, m: (0, 0)))
            shapes.append(jax.ShapeDtypeStruct(size, dtype))
    return pl.pallas_call(
        gated(kernel, len(tiled) + len(wholes), len(gates)),
        grid_spec=pltpu.PrefetchScalarGridSpec(
            num_scalar_prefetch=1,
            grid=(rows // tile,),
            in_specs=[by_row(a.shape[1]) for a in tiled]
            + [whole(a) for a in wholes]
            + gate_specs(gates),
            out_specs=specs,
            scratch_shapes=[pltpu.VMEM(shape, BF16) for shape in scratch],
        ),
        out_shape=shapes,
        compiler_params=params(1),
        cost_estimate=cost(flops, 20e6),
        name=name,
    )(meta, *tiled, *wholes, *gates)


def store_blocks(meta, out_ref, value, cut, first=0):
    rows = out_ref.shape[2]
    for block in range(value.shape[0] // (2 * rows)):
        for half in range(2):
            start = (2 * block + half) * rows
            out_ref[meta[1] ^ half, turned(meta[0] ^ (first + block)), :, cut] = value[
                start : start + rows
            ].astype(BF16)


def grad_up_kernel(
    meta, norm_t_ref, mixed_mine, mixed_other, grad_hidden_ref, grad_branch_ref, out_ref
):
    up_cut = grad_hidden_ref.shape[1]
    store_blocks(meta, out_ref, dot_nn(norm_t_ref[...], grad_hidden_ref[...]), slice(0, up_cut))
    cut = slice(up_cut, out_ref.shape[3])
    few = BLOCKS // 2
    grad_branch = grad_branch_ref[...]
    store_blocks(meta, out_ref, dot_nn(mixed_mine[...], grad_branch), cut, meta[2] * few)
    store_blocks(meta, out_ref, dot_nn(mixed_other[...], grad_branch), cut, (1 - meta[2]) * few)


def grad_up(rel, meta, norm_t, mixed_t, grad_hidden, grad_branch, *gates):
    width, rows = norm_t.shape
    hidden_width = grad_hidden.shape[1]
    groups = 3
    up_cut, out_cut = hidden_width // (2 * groups), width // (2 * groups)
    block_rows = width // (2 * BLOCKS)
    whole = lambda tall: pl.BlockSpec(
        (tall, rows), lambda n, m: (0, 0), pipeline_mode=pl.Buffered(1)
    )
    turn = lambda n, m: (0, (m[2] ^ rel) * groups + n)
    return pl.pallas_call(
        gated(grad_up_kernel, 5, len(gates)),
        grid_spec=pltpu.PrefetchScalarGridSpec(
            num_scalar_prefetch=1,
            grid=(groups,),
            in_specs=[
                whole(width),
                whole(width // 2),
                whole(width // 2),
                pl.BlockSpec((rows, up_cut), turn),
                pl.BlockSpec((rows, out_cut), turn),
                *gate_specs(gates),
            ],
            out_specs=pl.BlockSpec(
                (2, BLOCKS, block_rows, up_cut + out_cut), lambda n, m: (0, 0, 0, n)
            ),
        ),
        out_shape=jax.ShapeDtypeStruct(
            (2, BLOCKS, block_rows, groups * (up_cut + out_cut)), BF16
        ),
        compiler_params=params(1),
        cost_estimate=cost(rows * width * (hidden_width + width), 12e6),
        name="grad_up",
    )(meta, norm_t, *mixed_t, grad_hidden, grad_branch, *gates)


def grad_down_kernel(meta, active_t_ref, grad_second_ref, out_ref):
    value = dot_nn(active_t_ref[...], grad_second_ref[...]).astype(BF16)
    rows = out_ref.shape[2]
    for half in range(2):
        out_ref[meta[1] ^ half, 0] = value[half * rows : (half + 1) * rows]


def grad_down(rel, meta, active_t, grad_second, *gates):
    hidden_width, rows = active_t.shape
    width = grad_second.shape[1]
    block = hidden_width // (2 * BLOCKS)
    return pl.pallas_call(
        gated(grad_down_kernel, 2, len(gates)),
        grid_spec=pltpu.PrefetchScalarGridSpec(
            num_scalar_prefetch=1,
            grid=(BLOCKS,),
            in_specs=[
                pl.BlockSpec(
                    (block, rows), lambda j, m: (2 * (m[0] ^ turned(j)) + (m[2] ^ rel), 0)
                ),
                pl.BlockSpec((rows, width), lambda j, m: (0, 0), pipeline_mode=pl.Buffered(1)),
                *gate_specs(gates),
            ],
            out_specs=pl.BlockSpec((2, 1, block // 2, width), lambda j, m: (0, j, 0, 0)),
        ),
        out_shape=jax.ShapeDtypeStruct((2, BLOCKS, block // 2, width), BF16),
        compiler_params=params(1),
        cost_estimate=cost(rows * hidden_width * width, 8e6),
        name="grad_down",
    )(meta, active_t, grad_second, *gates)


def attend_back_kernel(
    meta,
    x_t_ref,
    qkv_ref,
    mixed_t_ref,
    grad_mixed_ref,
    lse_ref,
    grad_qkv_ref,
    grad_w_ref,
    grad_bias_ref,
    grad_scr,
):
    seq = pl.program_id(0)
    length = meta[3 + seq]
    rows, wide = qkv_ref.shape[1:]
    part = wide // 3
    lane = lax.broadcasted_iota(jnp.int32, (rows, 128), 1)
    key_ok = lax.broadcasted_iota(jnp.int32, (rows, rows), 0) < length
    start = pl.multiple_of(seq * rows, 128)

    @pl.when(seq == 0)
    def _():
        grad_bias_ref[...] = jnp.zeros_like(grad_bias_ref)

    for pair in range(part // 128):
        cut = pair * 128
        query = qkv_ref[0, :, cut : cut + 128] * jnp.asarray(0.125, BF16)
        key = qkv_ref[0, :, part + cut : part + cut + 128]
        value = qkv_ref[0, :, 2 * part + cut : 2 * part + cut + 128]
        grad_out = grad_mixed_ref[0, :, cut : cut + 128]
        product = grad_out.astype(F32).T * mixed_t_ref[cut : cut + 128, :].astype(F32)
        key_t = key.T
        grad_query, grad_key, grad_value = [], 0.0, 0.0
        for head in range(2):
            keep = (lane >= 64) == (head == 1)
            query_one = jnp.where(keep, query, jnp.zeros_like(query))
            grad_one = jnp.where(keep, grad_out, jnp.zeros_like(grad_out))
            inner = slice(64 * head, 64 * head + 64)
            delta = jnp.sum(product[inner], axis=0, keepdims=True)
            scores = jnp.where(key_ok, dot_nt(key, query_one), -1e30)
            prob = jnp.exp(scores - lse_ref[0, 2 * pair + head])
            grad_prob = dot_nt(value, grad_one)
            grad_scores = (prob * (grad_prob - delta)).astype(BF16)
            grad_value = grad_value + dot_nn(prob.astype(BF16), grad_one)
            grad_key = grad_key + dot_nn(grad_scores, query_one)
            grad_query.append(dot_nn(key_t[inner], grad_scores) * 0.125)
        grads = (jnp.concatenate(grad_query, axis=0).T, grad_key, grad_value)
        for kind, grad in enumerate(grads):
            grad = grad.astype(BF16)
            to = slice(kind * part + cut, kind * part + cut + 128)
            grad_scr[pl.ds(start, rows), to] = grad
            grad_qkv_ref[0, :, to] = grad
            grad_bias_ref[:, to] += column_sum(grad)

    @pl.when(seq == pl.num_programs(0) - 1)
    def _():
        store_blocks(meta, grad_w_ref, dot_nn(x_t_ref[...], grad_scr[...]), slice(None))


def attend_back(meta, x_t, qkv, mixed_t, grad_mixed, lse, *gates):
    seqs, length, wide = qkv.shape
    width, rows = x_t.shape
    part = wide // 3
    block_rows = width // (2 * BLOCKS)
    by_seq = lambda cols: pl.BlockSpec((1, length, cols), lambda s, m: (s, 0, 0))
    return pl.pallas_call(
        gated(attend_back_kernel, 5, len(gates)),
        grid_spec=pltpu.PrefetchScalarGridSpec(
            num_scalar_prefetch=1,
            grid=(seqs,),
            in_specs=[
                pl.BlockSpec((width, rows), lambda s, m: (0, 0), pipeline_mode=pl.Buffered(1)),
                by_seq(wide),
                pl.BlockSpec((part, length), lambda s, m: (0, s)),
                by_seq(part),
                pl.BlockSpec((1, HEADS // 2, 1, length), lambda s, m: (s, 0, 0, 0)),
                *gate_specs(gates),
            ],
            out_specs=[
                by_seq(wide),
                pl.BlockSpec((2, BLOCKS, block_rows, wide), lambda s, m: (0, 0, 0, 0)),
                pl.BlockSpec((1, wide), lambda s, m: (0, 0)),
            ],
            scratch_shapes=[pltpu.VMEM((rows, wide), BF16)],
        ),
        out_shape=[
            jax.ShapeDtypeStruct((seqs, length, wide), BF16),
            jax.ShapeDtypeStruct((2, BLOCKS, block_rows, wide), BF16),
            jax.ShapeDtypeStruct((1, wide), F32),
        ],
        compiler_params=params(1),
        cost_estimate=cost(
            2 * rows * width * wide + 10 * rows * length * 4 * part, 8e6, rows * length * 6
        ),
        name="attend_back",
    )(meta, x_t, qkv, mixed_t, grad_mixed, lse, *gates)


def input_kernel(
    meta, branch_ref, grad_mine, grad_other, w_mine, w_other, out_ref, scr_mine, scr_other
):
    @pl.when(pl.program_id(0) == 0)
    def _():
        place_rows(meta, w_mine, scr_mine, slice(None), slice(None))
        place_rows(meta, w_other, scr_other, slice(None), slice(None))

    total = branch_ref[...].astype(F32) + dot_nt(grad_mine[...], scr_mine[...])
    out_ref[...] = total + dot_nt(grad_other[...], scr_other[...])


def finish_kernel(moves, row_step, meta, *refs):
    parts, outs = refs[:2], refs[2:]
    for rel in range(4):
        part = parts[rel & 1].at[rel >> 1]
        x_at, core = meta[1] ^ (rel >> 1), meta[2] ^ (rel & 1)
        rows = part.shape[0]
        at = pl.ds(pl.multiple_of(x_at * rows + core * row_step, 16), rows)
        for columns, out, first, step in moves:
            size = columns.stop - columns.start
            to = pl.ds(pl.multiple_of(first + core * step, 128), size)
            outs[out][at, to] = part[:, columns].astype(F32)


def finish(meta, parts, moves, row_step, shapes):
    whole = lambda shape: pl.BlockSpec(shape, lambda i, m: (0,) * len(shape))
    return pl.pallas_call(
        functools.partial(finish_kernel, moves, row_step),
        grid_spec=pltpu.PrefetchScalarGridSpec(
            num_scalar_prefetch=1,
            grid=(1,),
            in_specs=[whole(p.shape) for p in parts],
            out_specs=[whole(shape) for shape in shapes],
        ),
        out_shape=[jax.ShapeDtypeStruct(shape, F32) for shape in shapes],
        compiler_params=params(1),
        cost_estimate=cost(0, 4e6),
        name="finish",
    )(meta, *parts)


def together(*arrays):
    return lax.optimization_barrier(arrays)


CORE, X, Y, NEAR, FAR = 1, 2, 4, 8, 16
DEVICES = 32


def swap(array, mask):
    pairs = [(i, i ^ mask) for i in range(DEVICES)]
    return lax.ppermute(array, ("shard", "rep"), pairs)


def gather_z(piece):
    came = [swap(piece, mask) for mask in (FAR, NEAR, NEAR | FAR)]
    return jnp.stack([piece] + came)


def double(held, mask):
    return jnp.concatenate([held, swap(held, mask)], axis=0)


def gather_plane(held):
    by_y, by_x, across = (swap(held, mask) for mask in (Y, X, X | Y))
    low = jnp.concatenate([held, by_y], axis=0)
    return jnp.stack([low, jnp.concatenate([by_x, across], axis=0)])


def add(*terms):
    total = terms[0].astype(F32)
    for term in terms[1:]:
        total = total + term.astype(F32)
    return total.astype(BF16)


def sum_z(parts):
    return add(
        parts[0],
        *[swap(parts[i], mask) for i, mask in ((1, FAR), (2, NEAR), (3, NEAR | FAR))],
    )


def halve_z(parts):
    near = swap(jnp.stack(parts[2:]), NEAR)
    low = [add(parts[i], near[i]) for i in range(2)]
    return add(low[0], swap(low[1], FAR))


def plane_sends(kept, came):
    cut = BLOCKS // 2
    pick = lambda a, x, y: a[x, cut:] if y else a[x, :cut]
    parts = [[add(pick(kept, x, y), pick(came, x, y)) for y in range(2)] for x in range(2)]
    return [
        parts[0][0],
        swap(parts[0][1], Y),
        swap(parts[1][0], X),
        swap(parts[1][1], X | Y),
    ]


def plane_sum(terms):
    return [add(*[t[i] for t in terms]) for i in range(4)]


def share(piece):
    both = jnp.stack([piece, swap(piece, X)])
    return both, swap(both, CORE)


def local(
    fast,
    tokens,
    lengths,
    w_qkv,
    b_query,
    b_value,
    w_out,
    b_out,
    ln1_gain,
    ln1_bias,
    w_up,
    b_up,
    w_down,
    b_down,
    ln2_gain,
    ln2_bias,
    cotangent,
):
    seqs, seq_len, width = tokens.shape
    rows = seqs * seq_len
    hidden_width = w_up.shape[1]
    half = width // 2
    groups = GROUPS
    up_cut, out_cut = hidden_width // (2 * groups), half // groups
    vectors = (b_query, b_value, b_out, ln1_gain, ln1_bias, b_down, ln2_gain, ln2_bias, b_up)
    names = len(vectors)

    if fast:
        shard, rep = lax.axis_index("shard"), lax.axis_index("rep")
        x_at, core = rep // 2, rep % 2
    else:
        shard = rep = x_at = core = jnp.int32(0)
    block = width // BLOCKS
    quarter = block // 2
    meta = jnp.concatenate(
        [jnp.stack([shard, x_at, core]).astype(jnp.int32), lengths.astype(jnp.int32)]
    )

    def qkv_parts(w):
        return w.reshape(-1, 2, quarter, 3, 2, half)

    def up_parts(up, out):
        up = up.reshape(-1, 2, quarter, 2, groups, up_cut)
        out = out.reshape(-1, 2, quarter, 2, groups, out_cut)
        return jnp.concatenate([up, out], axis=-1)

    if fast:
        def piece(weight, columns, start):
            place = (x_at * quarter, start + core * columns)
            return lax.dynamic_slice(weight, place, (quarter, columns))

        qkv_piece = jnp.concatenate([piece(w_qkv, half, k * width) for k in range(3)], axis=1)
        up_piece, out_piece = piece(w_up, hidden_width // 2, 0), piece(w_out, half, 0)
        up_piece = jnp.concatenate(
            [
                part[:, g * cut : (g + 1) * cut]
                for g in range(groups)
                for part, cut in ((up_piece, up_cut), (out_piece, out_cut))
            ],
            axis=1,
        )
        down_rows = w_down.shape[0] // 4
        down_piece = lax.dynamic_slice(
            w_down, ((2 * core + x_at) * down_rows, 0), (down_rows, width)
        )
        extra = jnp.pad(jnp.concatenate(vectors).reshape(1, -1), ((0, 15), (0, 0)))
        qkv_piece = jnp.concatenate([qkv_piece, extra], axis=0)
        qkv_z, up_z, down_piece = together(
            gather_z(qkv_piece), double(up_piece[None], FAR), down_piece
        )
        table = qkv_z[:, quarter]
        qkv_mine, up_z, down_z, table = together(
            gather_plane(qkv_z[:, :quarter]),
            double(up_z, NEAR),
            double(down_piece[None], FAR),
            table,
        )
        table = jnp.concatenate([table, swap(table, Y)], axis=0)
        qkv_w = qkv_mine, swap(qkv_mine, CORE)
        up_mine, down_z = gather_plane(up_z), double(down_z, NEAR)
        table = jnp.take(table, turned(jnp.arange(BLOCKS) ^ shard), axis=0)

    else:
        everything = lambda a: lax.all_gather(a, "shard", axis=0, tiled=True)
        table = None
        full = [everything(v) for v in vectors]
        order = [turned(p) for p in range(BLOCKS)]
        both = lambda a: (a[0][:, order], a[1][:, order])
        qkv_w = both(
            qkv_parts(everything(w_qkv))
            .transpose(4, 1, 0, 2, 3, 5)
            .reshape(2, 2, BLOCKS, quarter, 3 * half)
        )
        up_w = both(
            up_parts(everything(w_up), everything(w_out))
            .transpose(3, 1, 0, 2, 4, 5)
            .reshape(2, 2, BLOCKS, quarter, -1)
        )
        down_w = both(
            everything(w_down).reshape(BLOCKS, 2, 2, -1, width).transpose(1, 2, 0, 3, 4)
        )
    if fast:
        full, start = [], 0
        for v in vectors:
            full.append(table[:, start : start + v.shape[0]].reshape(-1))
            start += v.shape[0]
    full = [v.astype(F32) for v in full]
    bias = jnp.stack(
        [full[0].reshape(2, half), jnp.zeros((2, half), F32), full[1].reshape(2, half)], axis=1
    ).reshape(2, 1, 3 * half)
    vec = jnp.stack(full[2:8] + [jnp.zeros_like(full[0])] * 2)

    if fast:
        bias = jnp.where(core == 0, bias, bias[::-1])
    x_rows = tokens.reshape(rows, width)
    x_t = x_rows.T
    heads = [attend(meta, tokens, qkv_w[i], bias[i]) for i in range(2)]
    if fast:
        up_mine, down_z, x_t, *outs = together(up_mine, down_z, x_t, *heads[0], *heads[1])
        heads = outs[:4], outs[4:]
        up_w = up_mine, swap(up_mine, CORE)
        down_mine = gather_plane(down_z)
    qkv, mixed, mixed_t, lse = zip(*heads)
    mixed_rows = [m.reshape(rows, half) for m in mixed]
    row, col, fixed = "row", "col", "sum"
    hat, scale, norm_t, active, active_t, slope = by_tile(
        up_kernel,
        "feed_up",
        2 * rows * width * hidden_width,
        meta,
        (x_rows, *mixed_rows),
        (*up_w, vec, full[8].reshape(1, -1)),
        (),
        (
            (row, width, F32),
            (row, 128, F32),
            (col, width, BF16),
            (row, hidden_width, BF16),
            (col, hidden_width, BF16),
            (row, hidden_width, BF16),
        ),
        ((width, hidden_width), (width, width)),
    )
    if fast:
        down_mine, active = together(down_mine, active)
        down_w = down_mine, swap(down_mine, CORE)
    layer_out, grad_second, vec_two = by_tile(
        functools.partial(down_kernel, seq_len),
        "feed_down",
        2 * rows * width * hidden_width,
        meta,
        (hat, active, cotangent.reshape(rows, width)),
        (*down_w, vec),
        (),
        ((row, width, BF16), (row, width, BF16), (fixed, (8, width), F32)),
        ((hidden_width, width),),
    )
    down_send = grad_down(1, meta, active_t, grad_second)
    down_keep = grad_down(0, meta, active_t, grad_second, down_send)
    gates = (down_keep,)
    if fast:
        down_plane = plane_sends(down_keep, swap(down_send, CORE))
        gates = (down_plane[0],)
    grad_hidden, grad_branch, *grad_mixed, vec_one, grad_b_up = by_tile(
        rest_kernel,
        "feed_back",
        4 * rows * width * hidden_width,
        meta,
        (grad_second, slope, hat, scale),
        (*up_w, *down_w, vec),
        gates,
        (
            (row, hidden_width, BF16),
            (row, width, BF16),
            (row, half, BF16),
            (row, half, BF16),
            (fixed, (8, width), F32),
            (fixed, (1, hidden_width), F32),
        ),
        ((width, hidden_width), (width, width), (hidden_width, width)),
    )
    gates = ()
    if fast:
        down_parts = plane_sum(down_plane)
        gates = tuple(down_parts)
    up_send = grad_up(1, meta, norm_t, mixed_t, grad_hidden, grad_branch, *gates)
    if fast:
        up_send, *down_parts = together(up_send, *down_parts)
    up_keep = grad_up(0, meta, norm_t, mixed_t, grad_hidden, grad_branch, up_send)
    gates = (up_keep,)
    if fast:
        up_plane = plane_sends(up_keep, swap(up_send, CORE))
        down_piece = sum_z(down_parts)
        gates = (up_plane[0],)
    grad_mixed = [g.reshape(seqs, seq_len, half) for g in grad_mixed]

    def back(i, *gates):
        return attend_back(meta, x_t, qkv[i], mixed_t[i], grad_mixed[i], lse[i], *gates)

    other_qkv, qkv_send, other_bias = back(1, *gates)
    gates = (qkv_send,)
    if fast:
        down_piece, qkv_send = together(down_piece, qkv_send)
        down_both = jnp.stack([down_piece, swap(down_piece, X)])
        gates = (qkv_send,)
    mine_qkv, qkv_keep, mine_bias = back(0, *gates)
    gates = (qkv_keep,)
    if fast:
        down_both, qkv_keep, *up_plane = together(down_both, qkv_keep, *up_plane)
        qkv_plane = plane_sends(qkv_keep, swap(qkv_send, CORE))
        up_parts_sum = plane_sum(up_plane)
        down_quarters = down_both, swap(down_both, CORE)
        gates = (qkv_plane[0], *up_parts_sum)
    (input_grad,) = by_tile(
        input_kernel,
        "input_grad",
        6 * rows * width * width,
        meta,
        (grad_branch, mine_qkv.reshape(rows, -1), other_qkv.reshape(rows, -1)),
        qkv_w,
        gates,
        ((row, width, F32),),
        ((width, 3 * half), (width, 3 * half)),
    )

    bias_halves = jnp.stack([mine_bias, other_bias]).reshape(2, 3, half)
    bias_halves = jnp.where(core == 0, bias_halves, bias_halves[::-1])
    grad_vectors = [
        bias_halves[:, 0].reshape(-1),
        bias_halves[:, 2].reshape(-1),
        *[vec_one[i] for i in range(3)],
        *[vec_two[i] for i in range(3)],
        grad_b_up[0],
    ]
    if fast:
        total = jnp.concatenate([g.reshape(BLOCKS, -1) for g in grad_vectors], axis=1)
        total, input_grad, *qkv_plane = together(total, input_grad, *qkv_plane)
        for mask in (CORE, X, Y, NEAR, FAR):
            total = total + swap(total, mask)
        total = lax.dynamic_index_in_dim(total, shard, 0, keepdims=False)
        sums, start = [], 0
        for v in vectors:
            sums.append(total[start : start + v.shape[0]])
            start += v.shape[0]
        step = up_cut + out_cut
        up_moves = [
            move
            for g in range(groups)
            for move in (
                (slice(g * step, g * step + up_cut), 0, g * up_cut, hidden_width // 2),
                (slice(g * step + up_cut, (g + 1) * step), 1, g * out_cut, half),
            )
        ]
        qkv_moves = [(slice(k * half, (k + 1) * half), 0, k * width, half) for k in range(3)]
        up_quarters = share(halve_z(up_parts_sum))
        qkv_quarters = share(sum_z(plane_sum(qkv_plane)))
        (grad_w_down,) = finish(
            meta,
            down_quarters,
            [(slice(0, width), 0, 0, 0)],
            2 * down_rows,
            [w_down.shape],
        )
        grad_w_up, grad_w_out = finish(meta, up_quarters, up_moves, 0, [w_up.shape, w_out.shape])
        (grad_w_qkv,) = finish(meta, qkv_quarters, qkv_moves, 0, [w_qkv.shape])
    else:
        total_of = lambda a: lax.psum(
            lax.psum_scatter(a, "shard", scatter_dimension=0, tiled=True), "rep"
        )
        sums = [total_of(g) for g in grad_vectors]
        order = [turned(p) for p in range(BLOCKS)]
        down_keep, down_send, up_keep, up_send = (
            a[:, order] for a in (down_keep, down_send, up_keep, up_send)
        )
        down = jnp.stack([down_keep, down_send]).transpose(2, 0, 1, 3, 4)
        grad_w_down = total_of(down.reshape(hidden_width, width).astype(F32))
        up = jnp.stack([up_keep, up_send]).reshape(
            2, 2, BLOCKS, quarter, groups, up_cut + out_cut
        )
        up = up.transpose(2, 1, 3, 0, 4, 5)
        grad_w_up = total_of(up[..., :up_cut].reshape(width, hidden_width).astype(F32))
        grad_w_out = total_of(up[..., up_cut:].reshape(width, width).astype(F32))
        qkv_sum = jnp.stack([qkv_keep[:, order], qkv_send[:, order]])
        qkv_sum = qkv_sum.reshape(2, 2, BLOCKS, quarter, 3, half)
        qkv_sum = qkv_sum.transpose(2, 1, 3, 4, 0, 5).reshape(width, 3 * width)
        grad_w_qkv = total_of(qkv_sum.astype(F32))
    return (
        layer_out.reshape(seqs, seq_len, width),
        input_grad.reshape(seqs, seq_len, width),
        grad_w_qkv,
        sums[0],
        sums[1],
        grad_w_out,
        sums[2],
        sums[3],
        sums[4],
        grad_w_up,
        sums[8],
        grad_w_down,
        sums[5],
        sums[6],
        sums[7],
    )


def solution(mesh):
    fast = mesh.shape["shard"] == BLOCKS and mesh.shape["rep"] == 4
    by_seq = P(("shard", "rep"), None, None)
    one, two = P("shard"), P("shard", None)
    in_specs = (by_seq, P(("shard", "rep")), two, one, one, two, one, one, one)
    in_specs = in_specs + (two, one, two, one, one, one, by_seq)
    out_specs = (by_seq, by_seq, two, one, one, two, one, one, one, two, one, two, one, one, one)
    return jax.shard_map(
        functools.partial(local, fast),
        mesh=mesh,
        in_specs=in_specs,
        out_specs=out_specs,
        check_vma=False,
    )
```

```python
import functools

import jax
import jax.numpy as jnp
from jax import lax
from jax.experimental import pallas as pl
from jax.experimental.pallas import tpu as pltpu
from jax.sharding import PartitionSpec as P

HEADS = 12
EPS = 1e-05
F32 = jnp.float32
BF16 = jnp.bfloat16
BLOCKS = 8
GROUPS = 3
VMEM_LIMIT = 58 * 1024 * 1024


def dot_nn(a, b):
    return lax.dot_general(a, b, (((1,), (0,)), ((), ())), preferred_element_type=F32)


def dot_nt(a, b):
    return lax.dot_general(a, b, (((1,), (1,)), ((), ())), preferred_element_type=F32)


def dot_tn(a, b):
    return lax.dot_general(a, b, (((0,), (0,)), ((), ())), preferred_element_type=F32)


def params(grid_dims):
    return pltpu.CompilerParams(
        dimension_semantics=("arbitrary",) * grid_dims, vmem_limit_bytes=VMEM_LIMIT
    )


def cost(flops, nbytes, trans=0):
    return pl.CostEstimate(
        flops=int(flops), bytes_accessed=int(nbytes), transcendentals=int(trans)
    )


def gated(kernel, inputs, gates):
    def body(*refs):
        kernel(*refs[: inputs + 1], *refs[inputs + 1 + gates :])

    return body


def gate_specs(gates):
    return [pl.BlockSpec(memory_space=pl.ANY)] * len(gates)


def turned(place):
    return ((place & 1) << 2) | (place & 2) | ((place >> 2) & 1)


def place_rows(meta, source, target, columns, cut):
    rows = source.shape[2]
    for half in range(2):
        for block in range(BLOCKS):
            start = (meta[0] ^ turned(block)) * (2 * rows) + (meta[1] ^ half) * rows
            target[pl.ds(pl.multiple_of(start, 16), rows), cut] = source[half, block, :, columns]


def attend_kernel(meta, x_ref, w_ref, bias_ref, qkv_ref, mixed_ref, mixed_t_ref, lse_ref, w_scr):
    seq = pl.program_id(0)
    wide = w_scr.shape[1]
    part = wide // 3

    @pl.when(seq == 0)
    def _():
        place_rows(meta, w_ref, w_scr, slice(None), slice(None))

    length = meta[3 + seq]
    qkv = (dot_nn(x_ref[0], w_scr[...]) + bias_ref[...]).astype(BF16)
    qkv_ref[0] = qkv
    rows = qkv.shape[0]
    lane = lax.broadcasted_iota(jnp.int32, (rows, 128), 1)
    key_ok = lax.broadcasted_iota(jnp.int32, (rows, rows), 0) < length
    for pair in range(part // 128):
        cut = pair * 128
        query = qkv[:, cut : cut + 128] * jnp.asarray(0.125, BF16)
        key = qkv[:, part + cut : part + cut + 128]
        value_t = qkv[:, 2 * part + cut : 2 * part + cut + 128].T
        outs = []
        for head in range(2):
            query_one = jnp.where((lane >= 64) == (head == 1), query, jnp.zeros_like(query))
            scores = jnp.where(key_ok, dot_nt(key, query_one), -1e30)
            top = jnp.max(scores, axis=0, keepdims=True)
            exp_scores = jnp.exp(scores - top)
            total = jnp.sum(exp_scores, axis=0, keepdims=True)
            lse_ref[0, 2 * pair + head] = top + jnp.log(total)
            out = dot_nn(value_t[64 * head : 64 * head + 64], exp_scores.astype(BF16))
            outs.append(out * (1.0 / total))
        mixed_t = jnp.concatenate(outs, axis=0)
        mixed_t_ref[cut : cut + 128, :] = mixed_t.astype(BF16)
        mixed_ref[0, :, cut : cut + 128] = mixed_t.T.astype(BF16)


def attend(meta, x, weight, bias):
    seqs, length, width = x.shape
    wide = weight.shape[3]
    part = wide // 3
    half_heads = HEADS // 2
    whole = lambda s, m: (0, 0, 0, 0)
    return pl.pallas_call(
        attend_kernel,
        grid_spec=pltpu.PrefetchScalarGridSpec(
            num_scalar_prefetch=1,
            grid=(seqs,),
            in_specs=[
                pl.BlockSpec((1, length, width), lambda s, m: (s, 0, 0)),
                pl.BlockSpec(weight.shape, whole, pipeline_mode=pl.Buffered(1)),
                pl.BlockSpec((1, wide), lambda s, m: (0, 0)),
            ],
            out_specs=[
                pl.BlockSpec((1, length, wide), lambda s, m: (s, 0, 0)),
                pl.BlockSpec((1, length, part), lambda s, m: (s, 0, 0)),
                pl.BlockSpec((part, length), lambda s, m: (0, s)),
                pl.BlockSpec((1, half_heads, 1, length), lambda s, m: (s, 0, 0, 0)),
            ],
            scratch_shapes=[pltpu.VMEM((width, wide), BF16)],
        ),
        out_shape=[
            jax.ShapeDtypeStruct((seqs, length, wide), BF16),
            jax.ShapeDtypeStruct((seqs, length, part), BF16),
            jax.ShapeDtypeStruct((part, seqs * length), BF16),
            jax.ShapeDtypeStruct((seqs, half_heads, 1, length), F32),
        ],
        compiler_params=params(1),
        cost_estimate=cost(
            2 * seqs * length * width * wide + 8 * seqs * length * length * width,
            10e6,
            seqs * length * length * half_heads,
        ),
        name="attend_forward",
    )(meta, x, weight, bias)


def gelu_and_slope(hidden):
    size = jnp.abs(hidden)
    bell = jnp.exp(-0.5 * hidden * hidden)
    t = 1.0 / (1.0 + (0.3275911 * 0.7071067811865476) * size)
    poly = t * (
        0.5 * 0.254829592
        + t
        * (
            0.5 * -0.284496736
            + t * (0.5 * 1.421413741 + t * (0.5 * -1.453152027 + t * (0.5 * 1.061405429)))
        )
    )
    tail = poly * bell
    phi = jnp.where(hidden < 0.0, tail, 1.0 - tail)
    return hidden * phi, phi + hidden * bell * 0.3989422804014327


def norm_forward(hidden):
    center = hidden - jnp.mean(hidden, axis=-1, keepdims=True)
    scale = lax.rsqrt(jnp.mean(center * center, axis=-1, keepdims=True) + EPS)
    return center * scale, scale


def norm_back(grad, hat, scale, gain):
    grad_hat = grad * gain
    shift = jnp.mean(grad_hat, axis=-1, keepdims=True)
    along = jnp.mean(grad_hat * hat, axis=-1, keepdims=True)
    return scale * (grad_hat - shift - hat * along)


def column_sum(rows):
    return jnp.sum(rows.astype(F32), axis=0, keepdims=True)


def place_up(meta, mine, other, w_up, w_out):
    hidden_width, width = w_up.shape[1], w_out.shape[1]
    up_cut, out_cut = hidden_width // (2 * GROUPS), width // (2 * GROUPS)
    for rel, source in enumerate((mine, other)):
        core = meta[2] ^ rel
        for group in range(GROUPS):
            base = group * (up_cut + out_cut)
            up_to = pl.multiple_of(core * (hidden_width // 2) + group * up_cut, 128)
            out_to = pl.multiple_of(core * (width // 2) + group * out_cut, 128)
            place_rows(meta, source, w_up, slice(base, base + up_cut), pl.ds(up_to, up_cut))
            place_rows(
                meta,
                source,
                w_out,
                slice(base + up_cut, base + up_cut + out_cut),
                pl.ds(out_to, out_cut),
            )


def place_down(meta, mine, other, w_down):
    rows = mine.shape[2]
    for rel, source in enumerate((mine, other)):
        for half in range(2):
            for block in range(BLOCKS):
                start = (
                    (meta[0] ^ turned(block)) * (4 * rows)
                    + (meta[2] ^ rel) * (2 * rows)
                    + (meta[1] ^ half) * rows
                )
                w_down[pl.ds(pl.multiple_of(start, 16), rows), :] = source[half, block]


def halves_of(meta, width):
    half = width // 2
    return (
        pl.ds(pl.multiple_of(meta[2] * half, 128), half),
        pl.ds(pl.multiple_of((1 - meta[2]) * half, 128), half),
    )


CHUNK = 512


def up_kernel(
    meta,
    x_ref,
    mixed_mine,
    mixed_other,
    up_mine,
    up_other,
    vec_ref,
    b_up_ref,
    hat_ref,
    scale_ref,
    norm_t_ref,
    active_ref,
    active_t_ref,
    slope_ref,
    w_up,
    w_out,
    normed_low,
):
    step = pl.program_id(0)
    width = w_out.shape[1]

    @pl.when(step == 0)
    def _():
        place_up(meta, up_mine, up_other, w_up, w_out)
        b_out, gain, shift = [vec_ref[i : i + 1, :] for i in range(3)]
        rows_mine, rows_other = halves_of(meta, width)
        branch = dot_nn(mixed_mine[...], w_out[rows_mine, :])
        branch = branch + dot_nn(mixed_other[...], w_out[rows_other, :])
        hat, scale = norm_forward(x_ref[...].astype(F32) + (branch + b_out))
        hat_ref[...] = hat
        scale_ref[...] = jnp.broadcast_to(scale, scale_ref.shape)
        normed_low[...] = (hat * gain + shift).astype(BF16)
        norm_t_ref[...] = normed_low[...].T

    cut = pl.ds(pl.multiple_of(step * CHUNK, CHUNK), CHUNK)
    hidden = dot_nn(normed_low[...], w_up[:, cut]) + b_up_ref[...]
    active, slope = gelu_and_slope(hidden)
    slope_ref[...] = slope.astype(BF16)
    active_low = active.astype(BF16)
    active_ref[...] = active_low
    active_t_ref[...] = active_low.T


def down_kernel(
    seq_len,
    meta,
    hat_ref,
    active_ref,
    cot_ref,
    down_mine,
    down_other,
    vec_ref,
    out_ref,
    grad_second_ref,
    grad_vec_ref,
    w_down,
):
    step = pl.program_id(0)
    tile = hat_ref.shape[0]

    @pl.when(step == 0)
    def _():
        grad_vec_ref[...] = jnp.zeros_like(grad_vec_ref)
        place_down(meta, down_mine, down_other, w_down)

    gain_one, shift_one, b_down, gain, shift = [vec_ref[i : i + 1, :] for i in range(1, 6)]
    seq = lax.div(step * tile, seq_len)
    place = lax.broadcasted_iota(jnp.int32, (tile, 1), 0) + lax.rem(step * tile, seq_len)
    valid = place < meta[3 + seq]
    second = dot_nn(active_ref[...], w_down[...])
    normed = hat_ref[...] * gain_one + shift_one
    hat, scale = norm_forward(normed + (second + b_down))
    out_ref[...] = jnp.where(valid, hat * gain + shift, 0.0).astype(BF16)
    grad_result = jnp.where(valid, cot_ref[...].astype(F32), 0.0)
    grad_second = norm_back(grad_result, hat, scale, gain).astype(BF16)
    grad_second_ref[...] = grad_second
    sums = column_sum(grad_second), column_sum(grad_result * hat), column_sum(grad_result)
    for i, total in enumerate(sums):
        grad_vec_ref[i : i + 1, :] += total


def rest_kernel(
    meta,
    grad_second_ref,
    hat_ref,
    scale_ref,
    up_mine,
    up_other,
    down_mine,
    down_other,
    vec_ref,
    slope_ref,
    grad_hidden_ref,
    grad_branch_ref,
    grad_mixed_mine,
    grad_mixed_other,
    grad_vec_ref,
    grad_b_up_ref,
    w_up,
    w_out,
    w_down,
    total,
):
    step = pl.program_id(0)
    width = w_out.shape[1]

    @pl.when(step == 0)
    def _():
        place_up(meta, up_mine, up_other, w_up, w_out)
        place_down(meta, down_mine, down_other, w_down)
        total[...] = grad_second_ref[...].astype(F32)

    cut = pl.ds(pl.multiple_of(step * CHUNK, CHUNK), CHUNK)
    grad_active = dot_nt(grad_second_ref[...], w_down[cut, :])
    grad_hidden = (slope_ref[...].astype(F32) * grad_active).astype(BF16)
    grad_hidden_ref[...] = grad_hidden
    grad_b_up_ref[...] = column_sum(grad_hidden)
    total[...] += dot_nt(grad_hidden, w_up[:, cut])

    @pl.when(step == pl.num_programs(0) - 1)
    def _():
        grad_normed, hat, gain = total[...], hat_ref[...], vec_ref[1:2, :]
        grad_branch = norm_back(grad_normed, hat, scale_ref[:, 0:1], gain).astype(BF16)
        grad_branch_ref[...] = grad_branch
        rows_mine, rows_other = halves_of(meta, width)
        grad_mixed_mine[...] = dot_nt(grad_branch, w_out[rows_mine, :]).astype(BF16)
        grad_mixed_other[...] = dot_nt(grad_branch, w_out[rows_other, :]).astype(BF16)
        grad_vec_ref[...] = jnp.zeros_like(grad_vec_ref)
        sums = column_sum(grad_branch), column_sum(grad_normed * hat), column_sum(grad_normed)
        for i, one in enumerate(sums):
            grad_vec_ref[i : i + 1, :] = one


def by_chunk(kernel, name, flops, meta, cut, wholes, gates, outs, scratch):
    hidden_width = cut[-1].shape[1]
    chunked = lambda shape: pl.BlockSpec((shape[0], CHUNK), lambda n, m: (0, n))
    whole = lambda shape: pl.BlockSpec(
        shape, lambda n, m: (0,) * len(shape), pipeline_mode=pl.Buffered(1)
    )
    spec_of = {
        "cols": chunked,
        "rows": lambda shape: pl.BlockSpec((CHUNK, shape[1]), lambda n, m: (n, 0)),
        "whole": lambda shape: pl.BlockSpec(shape, lambda n, m: (0,) * len(shape)),
    }
    return pl.pallas_call(
        gated(kernel, len(cut) + len(wholes), len(gates)),
        grid_spec=pltpu.PrefetchScalarGridSpec(
            num_scalar_prefetch=1,
            grid=(hidden_width // CHUNK,),
            in_specs=[whole(a.shape) for a in wholes]
            + [chunked(a.shape) for a in cut]
            + gate_specs(gates),
            out_specs=[spec_of[kind](shape) for kind, shape, _ in outs],
            scratch_shapes=[pltpu.VMEM(shape, dtype) for shape, dtype in scratch],
        ),
        out_shape=[jax.ShapeDtypeStruct(shape, dtype) for _, shape, dtype in outs],
        compiler_params=params(1),
        cost_estimate=cost(flops, 20e6),
        name=name,
    )(meta, *wholes, *cut, *gates)


def by_tile(kernel, name, flops, meta, tiled, wholes, gates, outs, scratch, most=512):
    rows = tiled[0].shape[0]
    tile = min(most, rows)
    by_row = lambda cols: pl.BlockSpec((tile, cols), lambda i, m: (i, 0))
    whole = lambda a: pl.BlockSpec(
        a.shape, lambda i, m: (0,) * a.ndim, pipeline_mode=pl.Buffered(1)
    )
    specs, shapes = [], []
    for kind, size, dtype in outs:
        if kind == "row":
            specs.append(by_row(size))
            shapes.append(jax.ShapeDtypeStruct((rows, size), dtype))
        elif kind == "col":
            specs.append(pl.BlockSpec((size, tile), lambda i, m: (0, i)))
            shapes.append(jax.ShapeDtypeStruct((size, rows), dtype))
        else:
            specs.append(pl.BlockSpec(size, lambda i, m: (0, 0)))
            shapes.append(jax.ShapeDtypeStruct(size, dtype))
    return pl.pallas_call(
        gated(kernel, len(tiled) + len(wholes), len(gates)),
        grid_spec=pltpu.PrefetchScalarGridSpec(
            num_scalar_prefetch=1,
            grid=(rows // tile,),
            in_specs=[by_row(a.shape[1]) for a in tiled]
            + [whole(a) for a in wholes]
            + gate_specs(gates),
            out_specs=specs,
            scratch_shapes=[pltpu.VMEM(shape, BF16) for shape in scratch],
        ),
        out_shape=shapes,
        compiler_params=params(1),
        cost_estimate=cost(flops, 20e6),
        name=name,
    )(meta, *tiled, *wholes, *gates)


def store_blocks(meta, out_ref, value, cut, first=0):
    rows = out_ref.shape[2]
    for block in range(value.shape[0] // (2 * rows)):
        for half in range(2):
            start = (2 * block + half) * rows
            out_ref[meta[1] ^ half, turned(meta[0] ^ (first + block)), :, cut] = value[
                start : start + rows
            ].astype(BF16)


def grad_up_kernel(
    meta, norm_t_ref, mixed_mine, mixed_other, grad_hidden_ref, grad_branch_ref, out_ref
):
    up_cut = grad_hidden_ref.shape[1]
    store_blocks(meta, out_ref, dot_nn(norm_t_ref[...], grad_hidden_ref[...]), slice(0, up_cut))
    cut = slice(up_cut, out_ref.shape[3])
    few = BLOCKS // 2
    grad_branch = grad_branch_ref[...]
    store_blocks(meta, out_ref, dot_nn(mixed_mine[...], grad_branch), cut, meta[2] * few)
    store_blocks(meta, out_ref, dot_nn(mixed_other[...], grad_branch), cut, (1 - meta[2]) * few)


def grad_up(rel, meta, norm_t, mixed_t, grad_hidden, grad_branch, *gates):
    width, rows = norm_t.shape
    hidden_width = grad_hidden.shape[1]
    groups = 3
    up_cut, out_cut = hidden_width // (2 * groups), width // (2 * groups)
    block_rows = width // (2 * BLOCKS)
    whole = lambda tall: pl.BlockSpec(
        (tall, rows), lambda n, m: (0, 0), pipeline_mode=pl.Buffered(1)
    )
    turn = lambda n, m: (0, (m[2] ^ rel) * groups + n)
    return pl.pallas_call(
        gated(grad_up_kernel, 5, len(gates)),
        grid_spec=pltpu.PrefetchScalarGridSpec(
            num_scalar_prefetch=1,
            grid=(groups,),
            in_specs=[
                whole(width),
                whole(width // 2),
                whole(width // 2),
                pl.BlockSpec((rows, up_cut), turn),
                pl.BlockSpec((rows, out_cut), turn),
                *gate_specs(gates),
            ],
            out_specs=pl.BlockSpec(
                (2, BLOCKS, block_rows, up_cut + out_cut), lambda n, m: (0, 0, 0, n)
            ),
        ),
        out_shape=jax.ShapeDtypeStruct(
            (2, BLOCKS, block_rows, groups * (up_cut + out_cut)), BF16
        ),
        compiler_params=params(1),
        cost_estimate=cost(rows * width * (hidden_width + width), 12e6),
        name="grad_up",
    )(meta, norm_t, *mixed_t, grad_hidden, grad_branch, *gates)


def grad_down_kernel(meta, *refs):
    blocks, (grad_second_ref, out_ref) = refs[:-2], refs[-2:]
    rows = out_ref.shape[2]
    left = jnp.concatenate([b[...] for b in blocks], axis=0)
    value = dot_nn(left, grad_second_ref[...]).astype(BF16)
    for i in range(len(blocks)):
        for half in range(2):
            start = (2 * i + half) * rows
            out_ref[meta[1] ^ half, i] = value[start : start + rows]


def grad_down(rel, meta, active_t, grad_second, *gates):
    hidden_width, rows = active_t.shape
    width = grad_second.shape[1]
    block = hidden_width // (2 * BLOCKS)
    some = 4

    def spec(i):
        return pl.BlockSpec(
            (block, rows), lambda j, m: (2 * (m[0] ^ turned(some * j + i)) + (m[2] ^ rel), 0)
        )

    return pl.pallas_call(
        gated(grad_down_kernel, some + 1, len(gates)),
        grid_spec=pltpu.PrefetchScalarGridSpec(
            num_scalar_prefetch=1,
            grid=(BLOCKS // some,),
            in_specs=[spec(i) for i in range(some)]
            + [pl.BlockSpec((rows, width), lambda j, m: (0, 0), pipeline_mode=pl.Buffered(1))]
            + gate_specs(gates),
            out_specs=pl.BlockSpec((2, some, block // 2, width), lambda j, m: (0, j, 0, 0)),
        ),
        out_shape=jax.ShapeDtypeStruct((2, BLOCKS, block // 2, width), BF16),
        compiler_params=params(1),
        cost_estimate=cost(rows * hidden_width * width, 8e6),
        name="grad_down",
    )(meta, *[active_t] * some, grad_second, *gates)


def attend_back_kernel(
    meta,
    x_t_ref,
    qkv_ref,
    mixed_t_ref,
    grad_mixed_ref,
    lse_ref,
    grad_qkv_ref,
    grad_w_ref,
    grad_bias_ref,
    grad_scr,
):
    seq = pl.program_id(0)
    length = meta[3 + seq]
    rows, wide = qkv_ref.shape[1:]
    part = wide // 3
    lane = lax.broadcasted_iota(jnp.int32, (rows, 128), 1)
    key_ok = lax.broadcasted_iota(jnp.int32, (rows, rows), 0) < length
    start = pl.multiple_of(seq * rows, 128)

    @pl.when(seq == 0)
    def _():
        grad_bias_ref[...] = jnp.zeros_like(grad_bias_ref)

    for pair in range(part // 128):
        cut = pair * 128
        query = qkv_ref[0, :, cut : cut + 128] * jnp.asarray(0.125, BF16)
        key = qkv_ref[0, :, part + cut : part + cut + 128]
        value = qkv_ref[0, :, 2 * part + cut : 2 * part + cut + 128]
        grad_out = grad_mixed_ref[0, :, cut : cut + 128]
        product = grad_out.astype(F32).T * mixed_t_ref[cut : cut + 128, :].astype(F32)
        key_t = key.T
        grad_query, grad_key, grad_value = [], 0.0, 0.0
        for head in range(2):
            keep = (lane >= 64) == (head == 1)
            query_one = jnp.where(keep, query, jnp.zeros_like(query))
            grad_one = jnp.where(keep, grad_out, jnp.zeros_like(grad_out))
            inner = slice(64 * head, 64 * head + 64)
            delta = jnp.sum(product[inner], axis=0, keepdims=True)
            scores = jnp.where(key_ok, dot_nt(key, query_one), -1e30)
            prob = jnp.exp(scores - lse_ref[0, 2 * pair + head])
            grad_prob = dot_nt(value, grad_one)
            grad_scores = (prob * (grad_prob - delta)).astype(BF16)
            grad_value = grad_value + dot_nn(prob.astype(BF16), grad_one)
            grad_key = grad_key + dot_nn(grad_scores, query_one)
            grad_query.append(dot_nn(key_t[inner], grad_scores) * 0.125)
        grads = (jnp.concatenate(grad_query, axis=0).T, grad_key, grad_value)
        for kind, grad in enumerate(grads):
            grad = grad.astype(BF16)
            to = slice(kind * part + cut, kind * part + cut + 128)
            grad_scr[pl.ds(start, rows), to] = grad
            grad_qkv_ref[0, :, to] = grad
            grad_bias_ref[:, to] += column_sum(grad)

    @pl.when(seq == pl.num_programs(0) - 1)
    def _():
        store_blocks(meta, grad_w_ref, dot_nn(x_t_ref[...], grad_scr[...]), slice(None))


def attend_back(meta, x_t, qkv, mixed_t, grad_mixed, lse, *gates):
    seqs, length, wide = qkv.shape
    width, rows = x_t.shape
    part = wide // 3
    block_rows = width // (2 * BLOCKS)
    by_seq = lambda cols: pl.BlockSpec((1, length, cols), lambda s, m: (s, 0, 0))
    return pl.pallas_call(
        gated(attend_back_kernel, 5, len(gates)),
        grid_spec=pltpu.PrefetchScalarGridSpec(
            num_scalar_prefetch=1,
            grid=(seqs,),
            in_specs=[
                pl.BlockSpec((width, rows), lambda s, m: (0, 0), pipeline_mode=pl.Buffered(1)),
                by_seq(wide),
                pl.BlockSpec((part, length), lambda s, m: (0, s)),
                by_seq(part),
                pl.BlockSpec((1, HEADS // 2, 1, length), lambda s, m: (s, 0, 0, 0)),
                *gate_specs(gates),
            ],
            out_specs=[
                by_seq(wide),
                pl.BlockSpec((2, BLOCKS, block_rows, wide), lambda s, m: (0, 0, 0, 0)),
                pl.BlockSpec((1, wide), lambda s, m: (0, 0)),
            ],
            scratch_shapes=[pltpu.VMEM((rows, wide), BF16)],
        ),
        out_shape=[
            jax.ShapeDtypeStruct((seqs, length, wide), BF16),
            jax.ShapeDtypeStruct((2, BLOCKS, block_rows, wide), BF16),
            jax.ShapeDtypeStruct((1, wide), F32),
        ],
        compiler_params=params(1),
        cost_estimate=cost(
            2 * rows * width * wide + 10 * rows * length * 4 * part, 8e6, rows * length * 6
        ),
        name="attend_back",
    )(meta, x_t, qkv, mixed_t, grad_mixed, lse, *gates)


def input_kernel(
    meta, branch_ref, grad_mine, grad_other, w_mine, w_other, out_ref, scr_mine, scr_other
):
    @pl.when(pl.program_id(0) == 0)
    def _():
        place_rows(meta, w_mine, scr_mine, slice(None), slice(None))
        place_rows(meta, w_other, scr_other, slice(None), slice(None))

    total = branch_ref[...].astype(F32) + dot_nt(grad_mine[...], scr_mine[...])
    out_ref[...] = total + dot_nt(grad_other[...], scr_other[...])


def finish_kernel(moves, row_step, meta, *refs):
    parts, outs = refs[:2], refs[2:]
    for rel in range(4):
        part = parts[rel & 1].at[rel >> 1]
        x_at, core = meta[1] ^ (rel >> 1), meta[2] ^ (rel & 1)
        rows = part.shape[0]
        at = pl.ds(pl.multiple_of(x_at * rows + core * row_step, 16), rows)
        for columns, out, first, step in moves:
            size = columns.stop - columns.start
            to = pl.ds(pl.multiple_of(first + core * step, 128), size)
            outs[out][at, to] = part[:, columns].astype(F32)


def finish(meta, parts, moves, row_step, shapes):
    whole = lambda shape: pl.BlockSpec(shape, lambda i, m: (0,) * len(shape))
    return pl.pallas_call(
        functools.partial(finish_kernel, moves, row_step),
        grid_spec=pltpu.PrefetchScalarGridSpec(
            num_scalar_prefetch=1,
            grid=(1,),
            in_specs=[whole(p.shape) for p in parts],
            out_specs=[whole(shape) for shape in shapes],
        ),
        out_shape=[jax.ShapeDtypeStruct(shape, F32) for shape in shapes],
        compiler_params=params(1),
        cost_estimate=cost(0, 4e6),
        name="finish",
    )(meta, *parts)


def together(*arrays):
    return lax.optimization_barrier(arrays)


CORE, X, Y, NEAR, FAR = 1, 2, 4, 8, 16
DEVICES = 32


def swap(array, mask):
    pairs = [(i, i ^ mask) for i in range(DEVICES)]
    return lax.ppermute(array, ("shard", "rep"), pairs)


def gather_z(piece):
    came = [swap(piece, mask) for mask in (FAR, NEAR, NEAR | FAR)]
    return jnp.stack([piece] + came)


def double(held, mask):
    return jnp.concatenate([held, swap(held, mask)], axis=0)


def gather_plane(held):
    by_y, by_x, across = (swap(held, mask) for mask in (Y, X, X | Y))
    low = jnp.concatenate([held, by_y], axis=0)
    return jnp.stack([low, jnp.concatenate([by_x, across], axis=0)])


def add(*terms):
    total = terms[0].astype(F32)
    for term in terms[1:]:
        total = total + term.astype(F32)
    return total.astype(BF16)


def sum_z(parts):
    return add(
        parts[0],
        *[swap(parts[i], mask) for i, mask in ((1, FAR), (2, NEAR), (3, NEAR | FAR))],
    )


def halve_z(parts, near):
    low = [add(parts[i], near[i]) for i in range(2)]
    return add(low[0], swap(low[1], FAR))


def plane_sends(kept, came):
    cut = BLOCKS // 2
    pick = lambda a, x, y: a[x, cut:] if y else a[x, :cut]
    parts = [[add(pick(kept, x, y), pick(came, x, y)) for y in range(2)] for x in range(2)]
    return [
        parts[0][0],
        swap(parts[0][1], Y),
        swap(parts[1][0], X),
        swap(parts[1][1], X | Y),
    ]


def plane_sum(terms):
    return [add(*[t[i] for t in terms]) for i in range(4)]


def share(piece):
    both = jnp.stack([piece, swap(piece, X)])
    return both, swap(both, CORE)


def local(
    fast,
    tokens,
    lengths,
    w_qkv,
    b_query,
    b_value,
    w_out,
    b_out,
    ln1_gain,
    ln1_bias,
    w_up,
    b_up,
    w_down,
    b_down,
    ln2_gain,
    ln2_bias,
    cotangent,
):
    seqs, seq_len, width = tokens.shape
    rows = seqs * seq_len
    hidden_width = w_up.shape[1]
    half = width // 2
    groups = GROUPS
    up_cut, out_cut = hidden_width // (2 * groups), half // groups
    vectors = (b_query, b_value, b_out, ln1_gain, ln1_bias, b_down, ln2_gain, ln2_bias, b_up)
    names = len(vectors)

    if fast:
        shard, rep = lax.axis_index("shard"), lax.axis_index("rep")
        x_at, core = rep // 2, rep % 2
    else:
        shard = rep = x_at = core = jnp.int32(0)
    block = width // BLOCKS
    quarter = block // 2
    meta = jnp.concatenate(
        [jnp.stack([shard, x_at, core]).astype(jnp.int32), lengths.astype(jnp.int32)]
    )

    def qkv_parts(w):
        return w.reshape(-1, 2, quarter, 3, 2, half)

    def up_parts(up, out):
        up = up.reshape(-1, 2, quarter, 2, groups, up_cut)
        out = out.reshape(-1, 2, quarter, 2, groups, out_cut)
        return jnp.concatenate([up, out], axis=-1)

    if fast:
        def piece(weight, columns, start):
            place = (x_at * quarter, start + core * columns)
            return lax.dynamic_slice(weight, place, (quarter, columns))

        qkv_piece = jnp.concatenate([piece(w_qkv, half, k * width) for k in range(3)], axis=1)
        up_piece, out_piece = piece(w_up, hidden_width // 2, 0), piece(w_out, half, 0)
        up_piece = jnp.concatenate(
            [
                part[:, g * cut : (g + 1) * cut]
                for g in range(groups)
                for part, cut in ((up_piece, up_cut), (out_piece, out_cut))
            ],
            axis=1,
        )
        down_rows = w_down.shape[0] // 4
        down_piece = lax.dynamic_slice(
            w_down, ((2 * core + x_at) * down_rows, 0), (down_rows, width)
        )
        extra = [jnp.pad(v[None], ((0, 0), (0, 3 * half - v.shape[0]))) for v in vectors]
        extra = jnp.concatenate(extra + [jnp.zeros((16 - names, 3 * half), BF16)], axis=0)
        qkv_piece = jnp.concatenate([qkv_piece, extra], axis=0)
        qkv_z, up_piece, down_piece = together(gather_z(qkv_piece), up_piece, down_piece)
        table = qkv_z[:, quarter : quarter + names, : vectors[-1].shape[0]]
        up_z = double(double(up_piece[None], FAR), NEAR)
        down_z = double(down_piece[None], FAR)
        qkv_mine, up_z, down_z, table = together(
            gather_plane(qkv_z[:, :quarter]), up_z, down_z, table
        )
        table = jnp.concatenate([table, swap(table, Y)], axis=0)
        qkv_w = qkv_mine, swap(qkv_mine, CORE)
        up_mine, down_z = gather_plane(up_z), double(down_z, NEAR)
        table = jnp.take(table, turned(jnp.arange(BLOCKS) ^ shard), axis=0)

    else:
        everything = lambda a: lax.all_gather(a, "shard", axis=0, tiled=True)
        table = None
        full = [everything(v) for v in vectors]
        order = [turned(p) for p in range(BLOCKS)]
        both = lambda a: (a[0][:, order], a[1][:, order])
        qkv_w = both(
            qkv_parts(everything(w_qkv))
            .transpose(4, 1, 0, 2, 3, 5)
            .reshape(2, 2, BLOCKS, quarter, 3 * half)
        )
        up_w = both(
            up_parts(everything(w_up), everything(w_out))
            .transpose(3, 1, 0, 2, 4, 5)
            .reshape(2, 2, BLOCKS, quarter, -1)
        )
        down_w = both(
            everything(w_down).reshape(BLOCKS, 2, 2, -1, width).transpose(1, 2, 0, 3, 4)
        )
    if fast:
        full = [table[:, i, : v.shape[0]].reshape(-1) for i, v in enumerate(vectors)]
    full = [v.astype(F32) for v in full]
    bias = jnp.stack(
        [full[0].reshape(2, half), jnp.zeros((2, half), F32), full[1].reshape(2, half)], axis=1
    ).reshape(2, 1, 3 * half)
    vec = jnp.stack(full[2:8] + [jnp.zeros_like(full[0])] * 2)

    if fast:
        bias = jnp.where(core == 0, bias, bias[::-1])
    x_rows = tokens.reshape(rows, width)
    x_t = x_rows.T
    heads = [attend(meta, tokens, qkv_w[0], bias[0]), None]
    if fast:
        qkv_other, up_mine, down_z, x_t, *heads[0] = together(
            qkv_w[1], up_mine, down_z, x_t, *heads[0]
        )
        qkv_w = qkv_mine, qkv_other
    heads[1] = attend(meta, tokens, qkv_w[1], bias[1])
    if fast:
        up_w = up_mine, swap(up_mine, CORE)
        down_mine, *heads[1] = together(gather_plane(down_z), *heads[1])
        down_w = down_mine, swap(down_mine, CORE)
    qkv, mixed, mixed_t, lse = zip(*heads)
    mixed_rows = [m.reshape(rows, half) for m in mixed]
    up_shape, out_shape, down_shape = (width, hidden_width), (width, width), (hidden_width, width)
    hat, scale, norm_t, active, active_t, slope = by_chunk(
        up_kernel,
        "feed_up",
        2 * rows * width * hidden_width,
        meta,
        (full[8].reshape(1, -1),),
        (x_rows, *mixed_rows, *up_w, vec),
        (),
        (
            ("whole", (rows, width), F32),
            ("whole", (rows, 128), F32),
            ("whole", (width, rows), BF16),
            ("cols", (rows, hidden_width), BF16),
            ("rows", (hidden_width, rows), BF16),
            ("cols", (rows, hidden_width), BF16),
        ),
        ((up_shape, BF16), (out_shape, BF16), ((rows, width), BF16)),
    )
    row, fixed = "row", "sum"
    layer_out, grad_second, vec_two = by_tile(
        functools.partial(down_kernel, seq_len),
        "feed_down",
        2 * rows * width * hidden_width,
        meta,
        (hat, active, cotangent.reshape(rows, width)),
        (*down_w, vec),
        (),
        ((row, width, BF16), (row, width, BF16), (fixed, (8, width), F32)),
        ((hidden_width, width),),
    )
    down_send = grad_down(1, meta, active_t, grad_second)
    down_keep = grad_down(0, meta, active_t, grad_second, down_send)
    gates = (down_keep,)
    if fast:
        down_plane = plane_sends(down_keep, swap(down_send, CORE))
        gates = (down_plane[0],)
    grad_hidden, grad_branch, *grad_mixed, vec_one, grad_b_up = by_chunk(
        rest_kernel,
        "feed_back",
        4 * rows * width * hidden_width,
        meta,
        (slope,),
        (grad_second, hat, scale, *up_w, *down_w, vec),
        gates,
        (
            ("cols", (rows, hidden_width), BF16),
            ("whole", (rows, width), BF16),
            ("whole", (rows, half), BF16),
            ("whole", (rows, half), BF16),
            ("whole", (8, width), F32),
            ("cols", (1, hidden_width), F32),
        ),
        (
            (up_shape, BF16),
            (out_shape, BF16),
            (down_shape, BF16),
            ((rows, width), F32),
        ),
    )
    gates = ()
    if fast:
        down_parts = plane_sum(down_plane)
        gates = tuple(down_parts)
    up_send = grad_up(1, meta, norm_t, mixed_t, grad_hidden, grad_branch, *gates)
    if fast:
        up_send, *down_parts = together(up_send, *down_parts)
    up_keep = grad_up(0, meta, norm_t, mixed_t, grad_hidden, grad_branch, up_send)
    gates = (up_keep,)
    if fast:
        up_plane = plane_sends(up_keep, swap(up_send, CORE))
        down_piece = sum_z(down_parts)
        gates = (up_plane[0],)
    grad_mixed = [g.reshape(seqs, seq_len, half) for g in grad_mixed]

    def back(i, *gates):
        return attend_back(meta, x_t, qkv[i], mixed_t[i], grad_mixed[i], lse[i], *gates)

    other_qkv, qkv_send, other_bias = back(1, *gates)
    gates = (qkv_send,)
    if fast:
        down_piece, qkv_send = together(down_piece, qkv_send)
        gates = (qkv_send, up_plane[1], up_plane[2])
    mine_qkv, qkv_keep, mine_bias = back(0, *gates)
    gates = (qkv_keep,)
    if fast:
        qkv_plane = plane_sends(qkv_keep, swap(qkv_send, CORE))
        down_piece, qkv_plane[0], *up_plane = together(down_piece, qkv_plane[0], *up_plane)
        down_both = jnp.stack([down_piece, swap(down_piece, X)])
        up_parts_sum = plane_sum(up_plane)
        up_near = swap(jnp.stack(up_parts_sum[2:]), NEAR)
        down_quarters = down_both, swap(down_both, CORE)
        gates = (qkv_plane[0], up_parts_sum[0])
    (input_grad,) = by_tile(
        input_kernel,
        "input_grad",
        6 * rows * width * width,
        meta,
        (grad_branch, mine_qkv.reshape(rows, -1), other_qkv.reshape(rows, -1)),
        qkv_w,
        gates,
        ((row, width, F32),),
        ((width, 3 * half), (width, 3 * half)),
    )

    bias_halves = jnp.stack([mine_bias, other_bias]).reshape(2, 3, half)
    bias_halves = jnp.where(core == 0, bias_halves, bias_halves[::-1])
    grad_vectors = [
        bias_halves[:, 0].reshape(-1),
        bias_halves[:, 2].reshape(-1),
        *[vec_one[i] for i in range(3)],
        *[vec_two[i] for i in range(3)],
        grad_b_up[0],
    ]
    if fast:
        total = jnp.concatenate([g.reshape(BLOCKS, -1) for g in grad_vectors], axis=1)
        total, input_grad, up_near, *qkv_plane = together(
            total, input_grad, up_near, *qkv_plane
        )
        for mask in (CORE, X, Y, NEAR, FAR):
            total = total + swap(total, mask)
        total = lax.dynamic_index_in_dim(total, shard, 0, keepdims=False)
        sums, start = [], 0
        for v in vectors:
            sums.append(total[start : start + v.shape[0]])
            start += v.shape[0]
        step = up_cut + out_cut
        up_moves = [
            move
            for g in range(groups)
            for move in (
                (slice(g * step, g * step + up_cut), 0, g * up_cut, hidden_width // 2),
                (slice(g * step + up_cut, (g + 1) * step), 1, g * out_cut, half),
            )
        ]
        qkv_moves = [(slice(k * half, (k + 1) * half), 0, k * width, half) for k in range(3)]
        up_quarters = share(halve_z(up_parts_sum, up_near))
        qkv_quarters = share(sum_z(plane_sum(qkv_plane)))
        (grad_w_down,) = finish(
            meta,
            down_quarters,
            [(slice(0, width), 0, 0, 0)],
            2 * down_rows,
            [w_down.shape],
        )
        grad_w_up, grad_w_out = finish(meta, up_quarters, up_moves, 0, [w_up.shape, w_out.shape])
        (grad_w_qkv,) = finish(meta, qkv_quarters, qkv_moves, 0, [w_qkv.shape])
    else:
        total_of = lambda a: lax.psum(
            lax.psum_scatter(a, "shard", scatter_dimension=0, tiled=True), "rep"
        )
        sums = [total_of(g) for g in grad_vectors]
        order = [turned(p) for p in range(BLOCKS)]
        down_keep, down_send, up_keep, up_send = (
            a[:, order] for a in (down_keep, down_send, up_keep, up_send)
        )
        down = jnp.stack([down_keep, down_send]).transpose(2, 0, 1, 3, 4)
        grad_w_down = total_of(down.reshape(hidden_width, width).astype(F32))
        up = jnp.stack([up_keep, up_send]).reshape(
            2, 2, BLOCKS, quarter, groups, up_cut + out_cut
        )
        up = up.transpose(2, 1, 3, 0, 4, 5)
        grad_w_up = total_of(up[..., :up_cut].reshape(width, hidden_width).astype(F32))
        grad_w_out = total_of(up[..., up_cut:].reshape(width, width).astype(F32))
        qkv_sum = jnp.stack([qkv_keep[:, order], qkv_send[:, order]])
        qkv_sum = qkv_sum.reshape(2, 2, BLOCKS, quarter, 3, half)
        qkv_sum = qkv_sum.transpose(2, 1, 3, 4, 0, 5).reshape(width, 3 * width)
        grad_w_qkv = total_of(qkv_sum.astype(F32))
    return (
        layer_out.reshape(seqs, seq_len, width),
        input_grad.reshape(seqs, seq_len, width),
        grad_w_qkv,
        sums[0],
        sums[1],
        grad_w_out,
        sums[2],
        sums[3],
        sums[4],
        grad_w_up,
        sums[8],
        grad_w_down,
        sums[5],
        sums[6],
        sums[7],
    )


def solution(mesh):
    fast = mesh.shape["shard"] == BLOCKS and mesh.shape["rep"] == 4
    by_seq = P(("shard", "rep"), None, None)
    one, two = P("shard"), P("shard", None)
    in_specs = (by_seq, P(("shard", "rep")), two, one, one, two, one, one, one)
    in_specs = in_specs + (two, one, two, one, one, one, by_seq)
    out_specs = (by_seq, by_seq, two, one, one, two, one, one, one, two, one, two, one, one, one)
    return jax.shard_map(
        functools.partial(local, fast),
        mesh=mesh,
        in_specs=in_specs,
        out_specs=out_specs,
        check_vma=False,
    )
```

```python
import functools

import jax
import jax.numpy as jnp
from jax import lax
from jax.experimental import pallas as pl
from jax.experimental.pallas import tpu as pltpu
from jax.sharding import PartitionSpec as P

HEADS = 12
EPS = 1e-05
F32 = jnp.float32
BF16 = jnp.bfloat16
BLOCKS = 8
GROUPS = 3
VMEM_LIMIT = 58 * 1024 * 1024


def dot_nn(a, b):
    return lax.dot_general(a, b, (((1,), (0,)), ((), ())), preferred_element_type=F32)


def dot_nt(a, b):
    return lax.dot_general(a, b, (((1,), (1,)), ((), ())), preferred_element_type=F32)


def dot_tn(a, b):
    return lax.dot_general(a, b, (((0,), (0,)), ((), ())), preferred_element_type=F32)


def params(grid_dims):
    return pltpu.CompilerParams(
        dimension_semantics=("arbitrary",) * grid_dims, vmem_limit_bytes=VMEM_LIMIT
    )


def cost(flops, nbytes, trans=0):
    return pl.CostEstimate(
        flops=int(flops), bytes_accessed=int(nbytes), transcendentals=int(trans)
    )


def gated(kernel, inputs, gates):
    def body(*refs):
        kernel(*refs[: inputs + 1], *refs[inputs + 1 + gates :])

    return body


def gate_specs(gates):
    return [pl.BlockSpec(memory_space=pl.ANY)] * len(gates)


def turned(place):
    return ((place & 1) << 2) | (place & 2) | ((place >> 2) & 1)


def place_rows(meta, source, target, columns, cut):
    rows = source.shape[2]
    for half in range(2):
        for block in range(BLOCKS):
            start = (meta[0] ^ turned(block)) * (2 * rows) + (meta[1] ^ half) * rows
            target[pl.ds(pl.multiple_of(start, 16), rows), cut] = source[half, block, :, columns]


def pack_kernel(groups, *refs):
    meta, w_qkv, w_up, w_out, w_down, *vectors, qkv_ref, up_ref, down_ref = refs
    rows, wide = up_ref.shape[0], qkv_ref.shape[1]
    half = wide // 3
    up_cut, out_cut = w_up.shape[1] // (2 * groups), w_out.shape[1] // (2 * groups)
    at = pl.ds(pl.multiple_of(meta[1] * rows, 16), rows)

    def columns(start, size):
        return pl.ds(pl.multiple_of(start, 128), size)

    for kind in range(3):
        start = (2 * kind + meta[2]) * half
        qkv_ref[:rows, kind * half : (kind + 1) * half] = w_qkv[at, columns(start, half)]
    for group in range(groups):
        base = group * (up_cut + out_cut)
        start = (meta[2] * groups + group) * up_cut
        up_ref[:, base : base + up_cut] = w_up[at, columns(start, up_cut)]
        start = (meta[2] * groups + group) * out_cut
        up_ref[:, base + up_cut : base + up_cut + out_cut] = w_out[at, columns(start, out_cut)]
    rows_down = down_ref.shape[0]
    start = (2 * meta[2] + meta[1]) * rows_down
    down_ref[...] = w_down[pl.ds(pl.multiple_of(start, 16), rows_down), :]
    *short, long = vectors
    extra = qkv_ref.shape[0] - rows
    small = short[0].shape[0]
    place = lax.broadcasted_iota(jnp.int32, (extra, small), 0)
    table = jnp.zeros((extra, small), F32)
    for i, v in enumerate(short):
        table = jnp.where(place == i, v[...].astype(F32).reshape(1, small), table)
    qkv_ref[rows:, :] = jnp.zeros((extra, wide), BF16)
    qkv_ref[rows:, :small] = table.astype(BF16)
    size = long.shape[0]
    wide_row = jnp.broadcast_to(long[...].astype(F32).reshape(1, size), (extra, size))
    qkv_ref[rows:, 128 : 128 + size] = wide_row.astype(BF16)


def pack(meta, w_qkv, w_up, w_out, w_down, vectors):
    rows = w_up.shape[0] // 2
    whole = lambda a: pl.BlockSpec(a.shape, lambda i, m: (0,) * a.ndim)
    shapes = [
        (rows + 16, w_qkv.shape[1] // 2),
        (rows, (w_up.shape[1] + w_out.shape[1]) // 2),
        (w_down.shape[0] // 4, w_down.shape[1]),
    ]
    outs = [jax.ShapeDtypeStruct(shape, BF16) for shape in shapes]
    operands = (w_qkv, w_up, w_out, w_down, *vectors)
    return pl.pallas_call(
        functools.partial(pack_kernel, GROUPS),
        grid_spec=pltpu.PrefetchScalarGridSpec(
            num_scalar_prefetch=1,
            grid=(1,),
            in_specs=[whole(a) for a in operands],
            out_specs=[whole(o) for o in outs],
        ),
        out_shape=outs,
        compiler_params=params(1),
        cost_estimate=cost(0, 4e6),
        name="pack",
    )(meta, *operands)


def attend_kernel(meta, x_ref, w_ref, bias_ref, qkv_ref, mixed_ref, mixed_t_ref, lse_ref, w_scr):
    seq = pl.program_id(0)
    wide = w_scr.shape[1]
    part = wide // 3

    @pl.when(seq == 0)
    def _():
        place_rows(meta, w_ref, w_scr, slice(None), slice(None))

    length = meta[3 + seq]
    qkv = (dot_nn(x_ref[0], w_scr[...]) + bias_ref[...]).astype(BF16)
    qkv_ref[0] = qkv
    rows = qkv.shape[0]
    lane = lax.broadcasted_iota(jnp.int32, (rows, 128), 1)
    key_ok = lax.broadcasted_iota(jnp.int32, (rows, rows), 0) < length
    for pair in range(part // 128):
        cut = pair * 128
        query = qkv[:, cut : cut + 128] * jnp.asarray(0.125, BF16)
        key = qkv[:, part + cut : part + cut + 128]
        value_t = qkv[:, 2 * part + cut : 2 * part + cut + 128].T
        outs = []
        for head in range(2):
            query_one = jnp.where((lane >= 64) == (head == 1), query, jnp.zeros_like(query))
            scores = jnp.where(key_ok, dot_nt(key, query_one), -1e30)
            top = jnp.max(scores, axis=0, keepdims=True)
            exp_scores = jnp.exp(scores - top)
            total = jnp.sum(exp_scores, axis=0, keepdims=True)
            lse_ref[0, 2 * pair + head] = top + jnp.log(total)
            out = dot_nn(value_t[64 * head : 64 * head + 64], exp_scores.astype(BF16))
            outs.append(out * (1.0 / total))
        mixed_t = jnp.concatenate(outs, axis=0)
        mixed_t_ref[cut : cut + 128, :] = mixed_t.astype(BF16)
        mixed_ref[0, :, cut : cut + 128] = mixed_t.T.astype(BF16)


def attend(meta, x, weight, bias):
    seqs, length, width = x.shape
    wide = weight.shape[3]
    part = wide // 3
    half_heads = HEADS // 2
    whole = lambda s, m: (0, 0, 0, 0)
    return pl.pallas_call(
        attend_kernel,
        grid_spec=pltpu.PrefetchScalarGridSpec(
            num_scalar_prefetch=1,
            grid=(seqs,),
            in_specs=[
                pl.BlockSpec((1, length, width), lambda s, m: (s, 0, 0)),
                pl.BlockSpec(weight.shape, whole, pipeline_mode=pl.Buffered(1)),
                pl.BlockSpec((1, wide), lambda s, m: (0, 0)),
            ],
            out_specs=[
                pl.BlockSpec((1, length, wide), lambda s, m: (s, 0, 0)),
                pl.BlockSpec((1, length, part), lambda s, m: (s, 0, 0)),
                pl.BlockSpec((part, length), lambda s, m: (0, s)),
                pl.BlockSpec((1, half_heads, 1, length), lambda s, m: (s, 0, 0, 0)),
            ],
            scratch_shapes=[pltpu.VMEM((width, wide), BF16)],
        ),
        out_shape=[
            jax.ShapeDtypeStruct((seqs, length, wide), BF16),
            jax.ShapeDtypeStruct((seqs, length, part), BF16),
            jax.ShapeDtypeStruct((part, seqs * length), BF16),
            jax.ShapeDtypeStruct((seqs, half_heads, 1, length), F32),
        ],
        compiler_params=params(1),
        cost_estimate=cost(
            2 * seqs * length * width * wide + 8 * seqs * length * length * width,
            10e6,
            seqs * length * length * half_heads,
        ),
        name="attend_forward",
    )(meta, x, weight, bias)


def gelu_and_slope(hidden):
    size = jnp.abs(hidden)
    bell = jnp.exp(-0.5 * hidden * hidden)
    t = 1.0 / (1.0 + (0.3275911 * 0.7071067811865476) * size)
    poly = t * (
        0.5 * 0.254829592
        + t
        * (
            0.5 * -0.284496736
            + t * (0.5 * 1.421413741 + t * (0.5 * -1.453152027 + t * (0.5 * 1.061405429)))
        )
    )
    tail = poly * bell
    phi = jnp.where(hidden < 0.0, tail, 1.0 - tail)
    return hidden * phi, phi + hidden * bell * 0.3989422804014327


def norm_forward(hidden):
    center = hidden - jnp.mean(hidden, axis=-1, keepdims=True)
    scale = lax.rsqrt(jnp.mean(center * center, axis=-1, keepdims=True) + EPS)
    return center * scale, scale


def norm_back(grad, hat, scale, gain):
    grad_hat = grad * gain
    shift = jnp.mean(grad_hat, axis=-1, keepdims=True)
    along = jnp.mean(grad_hat * hat, axis=-1, keepdims=True)
    return scale * (grad_hat - shift - hat * along)


def column_sum(rows):
    return jnp.sum(rows.astype(F32), axis=0, keepdims=True)


def place_up(meta, mine, other, w_up, w_out):
    hidden_width, width = w_up.shape[1], w_out.shape[1]
    up_cut, out_cut = hidden_width // (2 * GROUPS), width // (2 * GROUPS)
    for rel, source in enumerate((mine, other)):
        core = meta[2] ^ rel
        for group in range(GROUPS):
            base = group * (up_cut + out_cut)
            up_to = pl.multiple_of(core * (hidden_width // 2) + group * up_cut, 128)
            out_to = pl.multiple_of(core * (width // 2) + group * out_cut, 128)
            place_rows(meta, source, w_up, slice(base, base + up_cut), pl.ds(up_to, up_cut))
            place_rows(
                meta,
                source,
                w_out,
                slice(base + up_cut, base + up_cut + out_cut),
                pl.ds(out_to, out_cut),
            )


def place_down(meta, mine, other, w_down):
    rows = mine.shape[2]
    for rel, source in enumerate((mine, other)):
        for half in range(2):
            for block in range(BLOCKS):
                start = (
                    (meta[0] ^ turned(block)) * (4 * rows)
                    + (meta[2] ^ rel) * (2 * rows)
                    + (meta[1] ^ half) * rows
                )
                w_down[pl.ds(pl.multiple_of(start, 16), rows), :] = source[half, block]


def halves_of(meta, width):
    half = width // 2
    return (
        pl.ds(pl.multiple_of(meta[2] * half, 128), half),
        pl.ds(pl.multiple_of((1 - meta[2]) * half, 128), half),
    )


CHUNK = 512


def up_kernel(
    meta,
    x_ref,
    mixed_mine,
    mixed_other,
    up_mine,
    up_other,
    vec_ref,
    b_up_ref,
    hat_ref,
    scale_ref,
    norm_t_ref,
    active_ref,
    active_t_ref,
    slope_ref,
    w_up,
    w_out,
    normed_low,
):
    step = pl.program_id(0)
    width = w_out.shape[1]

    @pl.when(step == 0)
    def _():
        place_up(meta, up_mine, up_other, w_up, w_out)
        b_out, gain, shift = [vec_ref[i : i + 1, :] for i in range(3)]
        rows_mine, rows_other = halves_of(meta, width)
        branch = dot_nn(mixed_mine[...], w_out[rows_mine, :])
        branch = branch + dot_nn(mixed_other[...], w_out[rows_other, :])
        hat, scale = norm_forward(x_ref[...].astype(F32) + (branch + b_out))
        hat_ref[...] = hat
        scale_ref[...] = jnp.broadcast_to(scale, scale_ref.shape)
        normed_low[...] = (hat * gain + shift).astype(BF16)
        norm_t_ref[...] = normed_low[...].T

    cut = pl.ds(pl.multiple_of(step * CHUNK, CHUNK), CHUNK)
    hidden = dot_nn(normed_low[...], w_up[:, cut]) + b_up_ref[...]
    active, slope = gelu_and_slope(hidden)
    slope_ref[...] = slope.astype(BF16)
    active_low = active.astype(BF16)
    active_ref[...] = active_low
    active_t_ref[...] = active_low.T


def down_kernel(
    seq_len,
    meta,
    hat_ref,
    active_ref,
    cot_ref,
    down_mine,
    down_other,
    vec_ref,
    out_ref,
    grad_second_ref,
    grad_vec_ref,
    w_down,
):
    step = pl.program_id(0)
    tile = hat_ref.shape[0]

    @pl.when(step == 0)
    def _():
        grad_vec_ref[...] = jnp.zeros_like(grad_vec_ref)
        place_down(meta, down_mine, down_other, w_down)

    gain_one, shift_one, b_down, gain, shift = [vec_ref[i : i + 1, :] for i in range(1, 6)]
    seq = lax.div(step * tile, seq_len)
    place = lax.broadcasted_iota(jnp.int32, (tile, 1), 0) + lax.rem(step * tile, seq_len)
    valid = place < meta[3 + seq]
    second = dot_nn(active_ref[...], w_down[...])
    normed = hat_ref[...] * gain_one + shift_one
    hat, scale = norm_forward(normed + (second + b_down))
    out_ref[...] = jnp.where(valid, hat * gain + shift, 0.0).astype(BF16)
    grad_result = jnp.where(valid, cot_ref[...].astype(F32), 0.0)
    grad_second = norm_back(grad_result, hat, scale, gain).astype(BF16)
    grad_second_ref[...] = grad_second
    sums = column_sum(grad_second), column_sum(grad_result * hat), column_sum(grad_result)
    for i, total in enumerate(sums):
        grad_vec_ref[i : i + 1, :] += total


def rest_kernel(
    meta,
    grad_second_ref,
    hat_ref,
    scale_ref,
    w_out,
    vec_ref,
    w_down,
    w_up,
    slope_ref,
    grad_hidden_ref,
    grad_branch_ref,
    grad_mixed_mine,
    grad_mixed_other,
    grad_vec_ref,
    grad_b_up_ref,
    total,
):
    step = pl.program_id(0)
    width = w_out.shape[1]

    @pl.when(step == 0)
    def _():
        total[...] = grad_second_ref[...].astype(F32)

    grad_active = dot_nt(grad_second_ref[...], w_down[...])
    grad_hidden = (slope_ref[...].astype(F32) * grad_active).astype(BF16)
    grad_hidden_ref[...] = grad_hidden
    grad_b_up_ref[...] = column_sum(grad_hidden)
    total[...] += dot_nt(grad_hidden, w_up[...])

    @pl.when(step == pl.num_programs(0) - 1)
    def _():
        grad_normed, hat, gain = total[...], hat_ref[...], vec_ref[1:2, :]
        grad_branch = norm_back(grad_normed, hat, scale_ref[:, 0:1], gain).astype(BF16)
        grad_branch_ref[...] = grad_branch
        rows_mine, rows_other = halves_of(meta, width)
        grad_mixed_mine[...] = dot_nt(grad_branch, w_out[rows_mine, :]).astype(BF16)
        grad_mixed_other[...] = dot_nt(grad_branch, w_out[rows_other, :]).astype(BF16)
        grad_vec_ref[...] = jnp.zeros_like(grad_vec_ref)
        sums = column_sum(grad_branch), column_sum(grad_normed * hat), column_sum(grad_normed)
        for i, one in enumerate(sums):
            grad_vec_ref[i : i + 1, :] = one


def by_chunk(kernel, name, flops, meta, cut, wholes, gates, outs, scratch, cut_rows=()):
    hidden_width = cut[-1].shape[1]
    chunked = lambda shape: pl.BlockSpec((shape[0], CHUNK), lambda n, m: (0, n))
    whole = lambda shape: pl.BlockSpec(
        shape, lambda n, m: (0,) * len(shape), pipeline_mode=pl.Buffered(1)
    )
    spec_of = {
        "cols": chunked,
        "rows": lambda shape: pl.BlockSpec((CHUNK, shape[1]), lambda n, m: (n, 0)),
        "whole": lambda shape: pl.BlockSpec(shape, lambda n, m: (0,) * len(shape)),
    }
    return pl.pallas_call(
        gated(kernel, len(cut) + len(cut_rows) + len(wholes), len(gates)),
        grid_spec=pltpu.PrefetchScalarGridSpec(
            num_scalar_prefetch=1,
            grid=(hidden_width // CHUNK,),
            in_specs=[whole(a.shape) for a in wholes]
            + [spec_of["rows"](a.shape) for a in cut_rows]
            + [chunked(a.shape) for a in cut]
            + gate_specs(gates),
            out_specs=[spec_of[kind](shape) for kind, shape, _ in outs],
            scratch_shapes=[pltpu.VMEM(shape, dtype) for shape, dtype in scratch],
        ),
        out_shape=[jax.ShapeDtypeStruct(shape, dtype) for _, shape, dtype in outs],
        compiler_params=params(1),
        cost_estimate=cost(flops, 20e6),
        name=name,
    )(meta, *wholes, *cut_rows, *cut, *gates)


def by_tile(kernel, name, flops, meta, tiled, wholes, gates, outs, scratch, most=512):
    rows = tiled[0].shape[0]
    tile = min(most, rows)
    by_row = lambda cols: pl.BlockSpec((tile, cols), lambda i, m: (i, 0))
    whole = lambda a: pl.BlockSpec(
        a.shape, lambda i, m: (0,) * a.ndim, pipeline_mode=pl.Buffered(1)
    )
    specs, shapes = [], []
    for kind, size, dtype in outs:
        if kind == "row":
            specs.append(by_row(size))
            shapes.append(jax.ShapeDtypeStruct((rows, size), dtype))
        elif kind == "col":
            specs.append(pl.BlockSpec((size, tile), lambda i, m: (0, i)))
            shapes.append(jax.ShapeDtypeStruct((size, rows), dtype))
        else:
            specs.append(pl.BlockSpec(size, lambda i, m: (0, 0)))
            shapes.append(jax.ShapeDtypeStruct(size, dtype))
    return pl.pallas_call(
        gated(kernel, len(tiled) + len(wholes), len(gates)),
        grid_spec=pltpu.PrefetchScalarGridSpec(
            num_scalar_prefetch=1,
            grid=(rows // tile,),
            in_specs=[by_row(a.shape[1]) for a in tiled]
            + [whole(a) for a in wholes]
            + gate_specs(gates),
            out_specs=specs,
            scratch_shapes=[pltpu.VMEM(shape, BF16) for shape in scratch],
        ),
        out_shape=shapes,
        compiler_params=params(1),
        cost_estimate=cost(flops, 20e6),
        name=name,
    )(meta, *tiled, *wholes, *gates)


def store_blocks(meta, out_ref, value, cut, first=0):
    rows = out_ref.shape[2]
    for block in range(value.shape[0] // (2 * rows)):
        for half in range(2):
            start = (2 * block + half) * rows
            out_ref[meta[1] ^ half, turned(meta[0] ^ (first + block)), :, cut] = value[
                start : start + rows
            ].astype(BF16)


def grad_up_kernel(
    meta, norm_t_ref, mixed_mine, mixed_other, grad_hidden_ref, grad_branch_ref, out_ref
):
    up_cut = grad_hidden_ref.shape[1]
    store_blocks(meta, out_ref, dot_nn(norm_t_ref[...], grad_hidden_ref[...]), slice(0, up_cut))
    cut = slice(up_cut, out_ref.shape[3])
    few = BLOCKS // 2
    grad_branch = grad_branch_ref[...]
    store_blocks(meta, out_ref, dot_nn(mixed_mine[...], grad_branch), cut, meta[2] * few)
    store_blocks(meta, out_ref, dot_nn(mixed_other[...], grad_branch), cut, (1 - meta[2]) * few)


def grad_up(rel, meta, norm_t, mixed_t, grad_hidden, grad_branch, *gates):
    width, rows = norm_t.shape
    hidden_width = grad_hidden.shape[1]
    groups = 3
    up_cut, out_cut = hidden_width // (2 * groups), width // (2 * groups)
    block_rows = width // (2 * BLOCKS)
    whole = lambda tall: pl.BlockSpec(
        (tall, rows), lambda n, m: (0, 0), pipeline_mode=pl.Buffered(1)
    )
    turn = lambda n, m: (0, (m[2] ^ rel) * groups + n)
    return pl.pallas_call(
        gated(grad_up_kernel, 5, len(gates)),
        grid_spec=pltpu.PrefetchScalarGridSpec(
            num_scalar_prefetch=1,
            grid=(groups,),
            in_specs=[
                whole(width),
                whole(width // 2),
                whole(width // 2),
                pl.BlockSpec((rows, up_cut), turn),
                pl.BlockSpec((rows, out_cut), turn),
                *gate_specs(gates),
            ],
            out_specs=pl.BlockSpec(
                (2, BLOCKS, block_rows, up_cut + out_cut), lambda n, m: (0, 0, 0, n)
            ),
        ),
        out_shape=jax.ShapeDtypeStruct(
            (2, BLOCKS, block_rows, groups * (up_cut + out_cut)), BF16
        ),
        compiler_params=params(1),
        cost_estimate=cost(rows * width * (hidden_width + width), 12e6),
        name="grad_up",
    )(meta, norm_t, *mixed_t, grad_hidden, grad_branch, *gates)


def grad_down_kernel(meta, *refs):
    blocks, (grad_second_ref, out_ref) = refs[:-2], refs[-2:]
    rows = out_ref.shape[2]
    left = jnp.concatenate([b[...] for b in blocks], axis=0)
    value = dot_nn(left, grad_second_ref[...]).astype(BF16)
    for i in range(len(blocks)):
        for half in range(2):
            start = (2 * i + half) * rows
            out_ref[meta[1] ^ half, i] = value[start : start + rows]


def grad_down(rel, meta, active_t, grad_second, *gates):
    hidden_width, rows = active_t.shape
    width = grad_second.shape[1]
    block = hidden_width // (2 * BLOCKS)
    some = 4

    def spec(i):
        return pl.BlockSpec(
            (block, rows), lambda j, m: (2 * (m[0] ^ turned(some * j + i)) + (m[2] ^ rel), 0)
        )

    return pl.pallas_call(
        gated(grad_down_kernel, some + 1, len(gates)),
        grid_spec=pltpu.PrefetchScalarGridSpec(
            num_scalar_prefetch=1,
            grid=(BLOCKS // some,),
            in_specs=[spec(i) for i in range(some)]
            + [pl.BlockSpec((rows, width), lambda j, m: (0, 0), pipeline_mode=pl.Buffered(1))]
            + gate_specs(gates),
            out_specs=pl.BlockSpec((2, some, block // 2, width), lambda j, m: (0, j, 0, 0)),
        ),
        out_shape=jax.ShapeDtypeStruct((2, BLOCKS, block // 2, width), BF16),
        compiler_params=params(1),
        cost_estimate=cost(rows * hidden_width * width, 8e6),
        name="grad_down",
    )(meta, *[active_t] * some, grad_second, *gates)


def attend_back_kernel(
    meta,
    x_t_ref,
    qkv_ref,
    mixed_t_ref,
    grad_mixed_ref,
    lse_ref,
    grad_qkv_ref,
    grad_w_ref,
    grad_bias_ref,
    grad_scr,
):
    seq = pl.program_id(0)
    length = meta[3 + seq]
    rows, wide = qkv_ref.shape[1:]
    part = wide // 3
    lane = lax.broadcasted_iota(jnp.int32, (rows, 128), 1)
    key_ok = lax.broadcasted_iota(jnp.int32, (rows, rows), 0) < length
    start = pl.multiple_of(seq * rows, 128)

    @pl.when(seq == 0)
    def _():
        grad_bias_ref[...] = jnp.zeros_like(grad_bias_ref)

    for pair in range(part // 128):
        cut = pair * 128
        query = qkv_ref[0, :, cut : cut + 128] * jnp.asarray(0.125, BF16)
        key = qkv_ref[0, :, part + cut : part + cut + 128]
        value = qkv_ref[0, :, 2 * part + cut : 2 * part + cut + 128]
        grad_out = grad_mixed_ref[0, :, cut : cut + 128]
        product = grad_out.astype(F32).T * mixed_t_ref[cut : cut + 128, :].astype(F32)
        key_t = key.T
        grad_query, grad_key, grad_value = [], 0.0, 0.0
        for head in range(2):
            keep = (lane >= 64) == (head == 1)
            query_one = jnp.where(keep, query, jnp.zeros_like(query))
            grad_one = jnp.where(keep, grad_out, jnp.zeros_like(grad_out))
            inner = slice(64 * head, 64 * head + 64)
            delta = jnp.sum(product[inner], axis=0, keepdims=True)
            scores = jnp.where(key_ok, dot_nt(key, query_one), -1e30)
            prob = jnp.exp(scores - lse_ref[0, 2 * pair + head])
            grad_prob = dot_nt(value, grad_one)
            grad_scores = (prob * (grad_prob - delta)).astype(BF16)
            grad_value = grad_value + dot_nn(prob.astype(BF16), grad_one)
            grad_key = grad_key + dot_nn(grad_scores, query_one)
            grad_query.append(dot_nn(key_t[inner], grad_scores) * 0.125)
        grads = (jnp.concatenate(grad_query, axis=0).T, grad_key, grad_value)
        for kind, grad in enumerate(grads):
            grad = grad.astype(BF16)
            to = slice(kind * part + cut, kind * part + cut + 128)
            grad_scr[pl.ds(start, rows), to] = grad
            grad_qkv_ref[0, :, to] = grad
            grad_bias_ref[:, to] += column_sum(grad)

    @pl.when(seq == pl.num_programs(0) - 1)
    def _():
        store_blocks(meta, grad_w_ref, dot_nn(x_t_ref[...], grad_scr[...]), slice(None))


def attend_back(meta, x_t, qkv, mixed_t, grad_mixed, lse, *gates):
    seqs, length, wide = qkv.shape
    width, rows = x_t.shape
    part = wide // 3
    block_rows = width // (2 * BLOCKS)
    by_seq = lambda cols: pl.BlockSpec((1, length, cols), lambda s, m: (s, 0, 0))
    return pl.pallas_call(
        gated(attend_back_kernel, 5, len(gates)),
        grid_spec=pltpu.PrefetchScalarGridSpec(
            num_scalar_prefetch=1,
            grid=(seqs,),
            in_specs=[
                pl.BlockSpec((width, rows), lambda s, m: (0, 0), pipeline_mode=pl.Buffered(1)),
                by_seq(wide),
                pl.BlockSpec((part, length), lambda s, m: (0, s)),
                by_seq(part),
                pl.BlockSpec((1, HEADS // 2, 1, length), lambda s, m: (s, 0, 0, 0)),
                *gate_specs(gates),
            ],
            out_specs=[
                by_seq(wide),
                pl.BlockSpec((2, BLOCKS, block_rows, wide), lambda s, m: (0, 0, 0, 0)),
                pl.BlockSpec((1, wide), lambda s, m: (0, 0)),
            ],
            scratch_shapes=[pltpu.VMEM((rows, wide), BF16)],
        ),
        out_shape=[
            jax.ShapeDtypeStruct((seqs, length, wide), BF16),
            jax.ShapeDtypeStruct((2, BLOCKS, block_rows, wide), BF16),
            jax.ShapeDtypeStruct((1, wide), F32),
        ],
        compiler_params=params(1),
        cost_estimate=cost(
            2 * rows * width * wide + 10 * rows * length * 4 * part, 8e6, rows * length * 6
        ),
        name="attend_back",
    )(meta, x_t, qkv, mixed_t, grad_mixed, lse, *gates)


def input_kernel(
    meta, branch_ref, grad_mine, grad_other, w_mine, w_other, out_ref, scr_mine, scr_other
):
    @pl.when(pl.program_id(0) == 0)
    def _():
        place_rows(meta, w_mine, scr_mine, slice(None), slice(None))
        place_rows(meta, w_other, scr_other, slice(None), slice(None))

    total = branch_ref[...].astype(F32) + dot_nt(grad_mine[...], scr_mine[...])
    out_ref[...] = total + dot_nt(grad_other[...], scr_other[...])


def finish_kernel(moves, row_step, meta, *refs):
    parts, outs = refs[:2], refs[2:]
    for rel in range(4):
        part = parts[rel & 1].at[rel >> 1]
        x_at, core = meta[1] ^ (rel >> 1), meta[2] ^ (rel & 1)
        rows = part.shape[0]
        at = pl.ds(pl.multiple_of(x_at * rows + core * row_step, 16), rows)
        for columns, out, first, step in moves:
            size = columns.stop - columns.start
            to = pl.ds(pl.multiple_of(first + core * step, 128), size)
            outs[out][at, to] = part[:, columns].astype(F32)


def finish(meta, parts, moves, row_step, shapes):
    whole = lambda shape: pl.BlockSpec(shape, lambda i, m: (0,) * len(shape))
    return pl.pallas_call(
        functools.partial(finish_kernel, moves, row_step),
        grid_spec=pltpu.PrefetchScalarGridSpec(
            num_scalar_prefetch=1,
            grid=(1,),
            in_specs=[whole(p.shape) for p in parts],
            out_specs=[whole(shape) for shape in shapes],
        ),
        out_shape=[jax.ShapeDtypeStruct(shape, F32) for shape in shapes],
        compiler_params=params(1),
        cost_estimate=cost(0, 4e6),
        name="finish",
    )(meta, *parts)


def together(*arrays):
    return lax.optimization_barrier(arrays)


CORE, X, Y, NEAR, FAR = 1, 2, 4, 8, 16
DEVICES = 32


def swap(array, mask):
    pairs = [(i, i ^ mask) for i in range(DEVICES)]
    return lax.ppermute(array, ("shard", "rep"), pairs)


def gather_z(piece):
    came = [swap(piece, mask) for mask in (FAR, NEAR, NEAR | FAR)]
    return jnp.stack([piece] + came)


def double(held, mask):
    return jnp.concatenate([held, swap(held, mask)], axis=0)


def plane_hops(held):
    return [swap(held, mask) for mask in (Y, X, X | Y)]


def plane_join(held, by_y, by_x, across):
    low = jnp.concatenate([held, by_y], axis=0)
    return jnp.stack([low, jnp.concatenate([by_x, across], axis=0)])


def gather_plane(held):
    return plane_join(held, *plane_hops(held))


def add(*terms):
    total = terms[0].astype(F32)
    for term in terms[1:]:
        total = total + term.astype(F32)
    return total.astype(BF16)


def sum_z(parts):
    return add(
        parts[0],
        *[swap(parts[i], mask) for i, mask in ((1, FAR), (2, NEAR), (3, NEAR | FAR))],
    )


def halve_z(parts, near):
    low = [add(parts[i], near[i]) for i in range(2)]
    return add(low[0], swap(low[1], FAR))


def plane_sends(kept, came):
    cut = BLOCKS // 2
    pick = lambda a, x, y: a[x, cut:] if y else a[x, :cut]
    parts = [[add(pick(kept, x, y), pick(came, x, y)) for y in range(2)] for x in range(2)]
    return [
        parts[0][0],
        swap(parts[0][1], Y),
        swap(parts[1][0], X),
        swap(parts[1][1], X | Y),
    ]


def plane_sum(terms):
    return [add(*[t[i] for t in terms]) for i in range(4)]


def share(piece):
    both = jnp.stack([piece, swap(piece, X)])
    return both, swap(both, CORE)


def local(
    fast,
    tokens,
    lengths,
    w_qkv,
    b_query,
    b_value,
    w_out,
    b_out,
    ln1_gain,
    ln1_bias,
    w_up,
    b_up,
    w_down,
    b_down,
    ln2_gain,
    ln2_bias,
    cotangent,
):
    seqs, seq_len, width = tokens.shape
    rows = seqs * seq_len
    hidden_width = w_up.shape[1]
    half = width // 2
    groups = GROUPS
    up_cut, out_cut = hidden_width // (2 * groups), half // groups
    vectors = (b_query, b_value, b_out, ln1_gain, ln1_bias, b_down, ln2_gain, ln2_bias, b_up)

    if fast:
        shard, rep = lax.axis_index("shard"), lax.axis_index("rep")
        x_at, core = rep // 2, rep % 2
    else:
        shard = rep = x_at = core = jnp.int32(0)
    block = width // BLOCKS
    quarter = block // 2
    meta = jnp.concatenate(
        [jnp.stack([shard, x_at, core]).astype(jnp.int32), lengths.astype(jnp.int32)]
    )

    def qkv_parts(w):
        return w.reshape(-1, 2, quarter, 3, 2, half)

    def up_parts(up, out):
        up = up.reshape(-1, 2, quarter, 2, groups, up_cut)
        out = out.reshape(-1, 2, quarter, 2, groups, out_cut)
        return jnp.concatenate([up, out], axis=-1)

    if fast:
        qkv_piece, up_piece, down_piece = pack(meta, w_qkv, w_up, w_out, w_down, vectors)
        qkv_z, up_piece, down_piece = together(gather_z(qkv_piece), up_piece, down_piece)
        table = qkv_z[:, quarter:, : 128 + b_up.shape[0]]
        up_z = double(double(up_piece[None], FAR), NEAR)
        down_z = double(down_piece[None], FAR)
        qkv_mine, up_z, down_z, table = together(
            gather_plane(qkv_z[:, :quarter]), up_z, down_z, table
        )
        table = jnp.concatenate([table, swap(table, Y)], axis=0)
        qkv_w = qkv_mine, swap(qkv_mine, CORE)
        up_mine, down_z = gather_plane(up_z), double(down_z, NEAR)
        table = jnp.take(table, turned(jnp.arange(BLOCKS) ^ shard), axis=0)

    else:
        everything = lambda a: lax.all_gather(a, "shard", axis=0, tiled=True)
        table = None
        full = [everything(v) for v in vectors]
        order = [turned(p) for p in range(BLOCKS)]
        both = lambda a: (a[0][:, order], a[1][:, order])
        qkv_w = both(
            qkv_parts(everything(w_qkv))
            .transpose(4, 1, 0, 2, 3, 5)
            .reshape(2, 2, BLOCKS, quarter, 3 * half)
        )
        up_w = both(
            up_parts(everything(w_up), everything(w_out))
            .transpose(3, 1, 0, 2, 4, 5)
            .reshape(2, 2, BLOCKS, quarter, -1)
        )
        down_w = both(
            everything(w_down).reshape(BLOCKS, 2, 2, -1, width).transpose(1, 2, 0, 3, 4)
        )
    if fast:
        full = [table[:, i, :block].reshape(-1) for i in range(len(vectors) - 1)]
        full.append(table[:, 0, 128:].reshape(-1))
    full = [v.astype(F32) for v in full]
    bias = jnp.stack(
        [full[0].reshape(2, half), jnp.zeros((2, half), F32), full[1].reshape(2, half)], axis=1
    ).reshape(2, 1, 3 * half)
    vec = jnp.stack(full[2:8] + [jnp.zeros_like(full[0])] * 2)

    if fast:
        bias = jnp.where(core == 0, bias, bias[::-1])
    x_rows = tokens.reshape(rows, width)
    heads = [list(attend(meta, tokens, qkv_w[i], bias[i])) for i in range(2)]
    if fast:
        x_late, heads[0][0] = together(x_rows, heads[0][0])
        x_t = x_late.T
    else:
        x_t = x_rows.T
    if fast:
        up_mine, down_z, *outs = together(up_mine, down_z, *heads[0], *heads[1])
        heads = outs[:4], outs[4:]
        up_w = up_mine, swap(up_mine, CORE)
    qkv, mixed, mixed_t, lse = zip(*heads)
    mixed_rows = [m.reshape(rows, half) for m in mixed]
    up_shape, out_shape, down_shape = (width, hidden_width), (width, width), (hidden_width, width)
    hat, scale, norm_t, active, active_t, slope, up_full, out_full = by_chunk(
        up_kernel,
        "feed_up",
        2 * rows * width * hidden_width,
        meta,
        (full[8].reshape(1, -1),),
        (x_rows, *mixed_rows, *up_w, vec),
        (),
        (
            ("whole", (rows, width), F32),
            ("whole", (rows, 128), F32),
            ("whole", (width, rows), BF16),
            ("cols", (rows, hidden_width), BF16),
            ("rows", (hidden_width, rows), BF16),
            ("cols", (rows, hidden_width), BF16),
            ("whole", up_shape, BF16),
            ("whole", out_shape, BF16),
        ),
        (((rows, width), BF16),),
    )
    row, fixed = "row", "sum"
    if fast:
        active, *hops = together(active, *plane_hops(down_z))
        down_mine = plane_join(down_z, *hops)
        down_w = down_mine, swap(down_mine, CORE)
    layer_out, grad_second, vec_two, down_full = by_tile(
        functools.partial(down_kernel, seq_len),
        "feed_down",
        2 * rows * width * hidden_width,
        meta,
        (hat, active, cotangent.reshape(rows, width)),
        (*down_w, vec),
        (),
        (
            (row, width, BF16),
            (row, width, BF16),
            (fixed, (8, width), F32),
            (fixed, down_shape, BF16),
        ),
        (),
    )
    down_send = grad_down(1, meta, active_t, grad_second)
    down_keep = grad_down(0, meta, active_t, grad_second, down_send)
    gates = (down_keep,)
    if fast:
        down_plane = plane_sends(down_keep, swap(down_send, CORE))
        gates = (down_plane[0],)
    grad_hidden, grad_branch, *grad_mixed, vec_one, grad_b_up = by_chunk(
        rest_kernel,
        "feed_back",
        4 * rows * width * hidden_width,
        meta,
        (up_full, slope),
        (grad_second, hat, scale, out_full, vec),
        gates,
        (
            ("cols", (rows, hidden_width), BF16),
            ("whole", (rows, width), BF16),
            ("whole", (rows, half), BF16),
            ("whole", (rows, half), BF16),
            ("whole", (8, width), F32),
            ("cols", (1, hidden_width), F32),
        ),
        (((rows, width), F32),),
        (down_full,),
    )
    gates = ()
    if fast:
        down_parts = plane_sum(down_plane)
        gates = tuple(down_parts)
    up_send = grad_up(1, meta, norm_t, mixed_t, grad_hidden, grad_branch, *gates)
    if fast:
        up_send, *down_parts = together(up_send, *down_parts)
    up_keep = grad_up(0, meta, norm_t, mixed_t, grad_hidden, grad_branch, up_send)
    gates = (up_keep,)
    if fast:
        up_plane = plane_sends(up_keep, swap(up_send, CORE))
        down_piece = sum_z(down_parts)
        gates = (up_plane[0],)
    grad_mixed = [g.reshape(seqs, seq_len, half) for g in grad_mixed]

    def back(i, *gates):
        return attend_back(meta, x_t, qkv[i], mixed_t[i], grad_mixed[i], lse[i], *gates)

    other_qkv, qkv_send, other_bias = back(1, *gates)
    gates = (qkv_send,)
    if fast:
        down_piece, qkv_send = together(down_piece, qkv_send)
        gates = (qkv_send, up_plane[1], up_plane[2])
    mine_qkv, qkv_keep, mine_bias = back(0, *gates)
    gates = (qkv_keep,)
    if fast:
        qkv_plane = plane_sends(qkv_keep, swap(qkv_send, CORE))
        down_piece, qkv_plane[0], *up_plane = together(down_piece, qkv_plane[0], *up_plane)
        down_both = jnp.stack([down_piece, swap(down_piece, X)])
        up_parts_sum = plane_sum(up_plane)
        up_near = swap(jnp.stack(up_parts_sum[2:]), NEAR)
        down_quarters = down_both, swap(down_both, CORE)
        gates = (qkv_plane[0], up_parts_sum[0])
    (input_grad,) = by_tile(
        input_kernel,
        "input_grad",
        6 * rows * width * width,
        meta,
        (grad_branch, mine_qkv.reshape(rows, -1), other_qkv.reshape(rows, -1)),
        qkv_w,
        gates,
        ((row, width, F32),),
        ((width, 3 * half), (width, 3 * half)),
    )

    bias_halves = jnp.stack([mine_bias, other_bias]).reshape(2, 3, half)
    bias_halves = jnp.where(core == 0, bias_halves, bias_halves[::-1])
    grad_vectors = [
        bias_halves[:, 0].reshape(-1),
        bias_halves[:, 2].reshape(-1),
        *[vec_one[i] for i in range(3)],
        *[vec_two[i] for i in range(3)],
        grad_b_up[0],
    ]
    if fast:
        total = jnp.concatenate([g.reshape(BLOCKS, -1) for g in grad_vectors], axis=1)
        total, input_grad, up_near, *qkv_plane[1:3] = together(
            total, input_grad, up_near, *qkv_plane[1:3]
        )
        for mask in (CORE, X, Y, NEAR, FAR):
            total = total + swap(total, mask)
        total = lax.dynamic_index_in_dim(total, shard, 0, keepdims=False)
        sums, start = [], 0
        for v in vectors:
            sums.append(total[start : start + v.shape[0]])
            start += v.shape[0]
        step = up_cut + out_cut
        up_moves = [
            move
            for g in range(groups)
            for move in (
                (slice(g * step, g * step + up_cut), 0, g * up_cut, hidden_width // 2),
                (slice(g * step + up_cut, (g + 1) * step), 1, g * out_cut, half),
            )
        ]
        qkv_moves = [(slice(k * half, (k + 1) * half), 0, k * width, half) for k in range(3)]
        up_quarters = share(halve_z(up_parts_sum, up_near))
        qkv_quarters = share(sum_z(plane_sum(qkv_plane)))
        (grad_w_down,) = finish(
            meta,
            down_quarters,
            [(slice(0, width), 0, 0, 0)],
            w_down.shape[0] // 2,
            [w_down.shape],
        )
        grad_w_up, grad_w_out = finish(meta, up_quarters, up_moves, 0, [w_up.shape, w_out.shape])
        (grad_w_qkv,) = finish(meta, qkv_quarters, qkv_moves, 0, [w_qkv.shape])
    else:
        total_of = lambda a: lax.psum(
            lax.psum_scatter(a, "shard", scatter_dimension=0, tiled=True), "rep"
        )
        sums = [total_of(g) for g in grad_vectors]
        order = [turned(p) for p in range(BLOCKS)]
        down_keep, down_send, up_keep, up_send = (
            a[:, order] for a in (down_keep, down_send, up_keep, up_send)
        )
        down = jnp.stack([down_keep, down_send]).transpose(2, 0, 1, 3, 4)
        grad_w_down = total_of(down.reshape(hidden_width, width).astype(F32))
        up = jnp.stack([up_keep, up_send]).reshape(
            2, 2, BLOCKS, quarter, groups, up_cut + out_cut
        )
        up = up.transpose(2, 1, 3, 0, 4, 5)
        grad_w_up = total_of(up[..., :up_cut].reshape(width, hidden_width).astype(F32))
        grad_w_out = total_of(up[..., up_cut:].reshape(width, width).astype(F32))
        qkv_sum = jnp.stack([qkv_keep[:, order], qkv_send[:, order]])
        qkv_sum = qkv_sum.reshape(2, 2, BLOCKS, quarter, 3, half)
        qkv_sum = qkv_sum.transpose(2, 1, 3, 4, 0, 5).reshape(width, 3 * width)
        grad_w_qkv = total_of(qkv_sum.astype(F32))
    return (
        layer_out.reshape(seqs, seq_len, width),
        input_grad.reshape(seqs, seq_len, width),
        grad_w_qkv,
        sums[0],
        sums[1],
        grad_w_out,
        sums[2],
        sums[3],
        sums[4],
        grad_w_up,
        sums[8],
        grad_w_down,
        sums[5],
        sums[6],
        sums[7],
    )


def solution(mesh):
    fast = mesh.shape["shard"] == BLOCKS and mesh.shape["rep"] == 4
    by_seq = P(("shard", "rep"), None, None)
    one, two = P("shard"), P("shard", None)
    in_specs = (by_seq, P(("shard", "rep")), two, one, one, two, one, one, one)
    in_specs = in_specs + (two, one, two, one, one, one, by_seq)
    out_specs = (by_seq, by_seq, two, one, one, two, one, one, one, two, one, two, one, one, one)
    return jax.shard_map(
        functools.partial(local, fast),
        mesh=mesh,
        in_specs=in_specs,
        out_specs=out_specs,
        check_vma=False,
    )
```

```python
import functools

import jax
import jax.numpy as jnp
from jax import lax
from jax.experimental import pallas as pl
from jax.experimental.pallas import tpu as pltpu
from jax.sharding import PartitionSpec as P

HEADS = 12
EPS = 1e-05
F32 = jnp.float32
BF16 = jnp.bfloat16
BLOCKS = 8
GROUPS = 3
VMEM_LIMIT = 58 * 1024 * 1024


def dot_nn(a, b):
    return lax.dot_general(a, b, (((1,), (0,)), ((), ())), preferred_element_type=F32)


def dot_nt(a, b):
    return lax.dot_general(a, b, (((1,), (1,)), ((), ())), preferred_element_type=F32)


def dot_tn(a, b):
    return lax.dot_general(a, b, (((0,), (0,)), ((), ())), preferred_element_type=F32)


def params(grid_dims):
    return pltpu.CompilerParams(
        dimension_semantics=("arbitrary",) * grid_dims, vmem_limit_bytes=VMEM_LIMIT
    )


def cost(flops, nbytes, trans=0):
    return pl.CostEstimate(
        flops=int(flops), bytes_accessed=int(nbytes), transcendentals=int(trans)
    )


def gated(kernel, inputs, gates):
    def body(*refs):
        kernel(*refs[: inputs + 1], *refs[inputs + 1 + gates :])

    return body


def gate_specs(gates):
    return [pl.BlockSpec(memory_space=pl.ANY)] * len(gates)


def turned(place):
    return ((place & 1) << 2) | (place & 2) | ((place >> 2) & 1)


def place_rows(meta, source, target, columns, cut):
    rows = source.shape[2]
    for half in range(2):
        for block in range(BLOCKS):
            start = (meta[0] ^ turned(block)) * (2 * rows) + (meta[1] ^ half) * rows
            target[pl.ds(pl.multiple_of(start, 16), rows), cut] = source[half, block, :, columns]


def pack_kernel(groups, *refs):
    meta, w_qkv, w_up, w_out, w_down, *vectors, qkv_ref, up_ref, down_ref = refs
    rows, wide = up_ref.shape[0], qkv_ref.shape[1]
    half = wide // 3
    up_cut, out_cut = w_up.shape[1] // (2 * groups), w_out.shape[1] // (2 * groups)
    at = pl.ds(pl.multiple_of(meta[1] * rows, 16), rows)

    def columns(start, size):
        return pl.ds(pl.multiple_of(start, 128), size)

    for kind in range(3):
        start = (2 * kind + meta[2]) * half
        qkv_ref[:rows, kind * half : (kind + 1) * half] = w_qkv[at, columns(start, half)]
    for group in range(groups):
        base = group * (up_cut + out_cut)
        start = (meta[2] * groups + group) * up_cut
        up_ref[:, base : base + up_cut] = w_up[at, columns(start, up_cut)]
        start = (meta[2] * groups + group) * out_cut
        up_ref[:, base + up_cut : base + up_cut + out_cut] = w_out[at, columns(start, out_cut)]
    rows_down = down_ref.shape[0]
    start = (2 * meta[2] + meta[1]) * rows_down
    down_ref[...] = w_down[pl.ds(pl.multiple_of(start, 16), rows_down), :]
    *short, long = vectors
    extra = qkv_ref.shape[0] - rows
    small = short[0].shape[0]
    place = lax.broadcasted_iota(jnp.int32, (extra, small), 0)
    table = jnp.zeros((extra, small), F32)
    for i, v in enumerate(short):
        table = jnp.where(place == i, v[...].astype(F32).reshape(1, small), table)
    qkv_ref[rows:, :] = jnp.zeros((extra, wide), BF16)
    qkv_ref[rows:, :small] = table.astype(BF16)
    size = long.shape[0]
    wide_row = jnp.broadcast_to(long[...].astype(F32).reshape(1, size), (extra, size))
    qkv_ref[rows:, 128 : 128 + size] = wide_row.astype(BF16)


def pack(meta, w_qkv, w_up, w_out, w_down, vectors):
    rows = w_up.shape[0] // 2
    whole = lambda a: pl.BlockSpec(a.shape, lambda i, m: (0,) * a.ndim)
    shapes = [
        (rows + 16, w_qkv.shape[1] // 2),
        (rows, (w_up.shape[1] + w_out.shape[1]) // 2),
        (w_down.shape[0] // 4, w_down.shape[1]),
    ]
    outs = [jax.ShapeDtypeStruct(shape, BF16) for shape in shapes]
    operands = (w_qkv, w_up, w_out, w_down, *vectors)
    return pl.pallas_call(
        functools.partial(pack_kernel, GROUPS),
        grid_spec=pltpu.PrefetchScalarGridSpec(
            num_scalar_prefetch=1,
            grid=(1,),
            in_specs=[whole(a) for a in operands],
            out_specs=[whole(o) for o in outs],
        ),
        out_shape=outs,
        compiler_params=params(1),
        cost_estimate=cost(0, 4e6),
        name="pack",
    )(meta, *operands)


def shard_columns(shard, block, width, lanes):
    lane = lax.broadcasted_iota(jnp.int32, (lanes, width), 0)
    column = lax.broadcasted_iota(jnp.int32, (lanes, width), 1)
    return (lane < block) & (column == lane + shard * block)


def unpack_kernel(block, meta, near_ref, far_ref, vec_ref, b_up_ref, mine_ref, other_ref, scr):
    width = vec_ref.shape[1]
    half, size = width // 2, b_up_ref.shape[1] // BLOCKS
    total = jnp.zeros(scr.shape, F32)
    for place in range(BLOCKS):
        source = (near_ref, far_ref)[place // 4]
        rows = source[place % 4]
        shard = meta[0] ^ turned(place)
        spread = shard_columns(shard, block, width, 128).astype(F32).astype(BF16)
        total = total + dot_nn(rows[:, :128], spread)
        to = pl.ds(pl.multiple_of(shard * size, 128), size)
        b_up_ref[:, to] = rows[:1, 128 : 128 + size].astype(F32)
    scr[...] = total
    vec_ref[...] = jnp.zeros_like(vec_ref)
    vec_ref[0:6, :] = total[2:8]
    for rel, out in enumerate((mine_ref, other_ref)):
        cut = pl.ds(pl.multiple_of((meta[2] ^ rel) * half, 128), half)
        out[...] = jnp.zeros_like(out)
        out[:, :half] = scr[0:1, cut]
        out[:, 2 * half :] = scr[1:2, cut]


def small_call(kernel, name, meta, operands, shapes, scratch=()):
    whole = lambda a: pl.BlockSpec(a.shape, lambda i, m: (0,) * len(a.shape))
    outs = [jax.ShapeDtypeStruct(shape, F32) for shape in shapes]
    return pl.pallas_call(
        kernel,
        grid_spec=pltpu.PrefetchScalarGridSpec(
            num_scalar_prefetch=1,
            grid=(1,),
            in_specs=[whole(a) for a in operands],
            out_specs=[whole(o) for o in outs],
            scratch_shapes=[pltpu.VMEM(shape, F32) for shape in scratch],
        ),
        out_shape=outs,
        compiler_params=params(1),
        cost_estimate=cost(0, 4e6),
        name=name,
    )(meta, *operands)


def sums_kernel(meta, vec_one, vec_two, b_up, bias_mine, bias_other, out_ref):
    width = out_ref.shape[1]
    half = width // 2
    out_ref[...] = jnp.zeros_like(out_ref)
    for rel, source in enumerate((bias_mine, bias_other)):
        to = pl.ds(pl.multiple_of((meta[2] ^ rel) * half, 128), half)
        out_ref[0:1, to] = source[:, :half]
        out_ref[1:2, to] = source[:, 2 * half :]
    out_ref[2:5, :] = vec_one[0:3, :]
    out_ref[5:8, :] = vec_two[0:3, :]
    for i in range(b_up.shape[1] // width):
        out_ref[8 + i : 9 + i, :] = b_up[:, i * width : (i + 1) * width]


def own_sums_kernel(block, meta, sum_ref, own_ref, b_up_ref):
    width, size = sum_ref.shape[1], b_up_ref.shape[1]
    pick = shard_columns(meta[0], block, width, 128).astype(F32)
    own_ref[...] = lax.dot_general(
        sum_ref[0:8, :],
        pick,
        (((1,), (1,)), ((), ())),
        precision=lax.Precision.HIGHEST,
        preferred_element_type=F32,
    )
    each = width // size
    cut = pl.ds(pl.multiple_of(lax.rem(meta[0], each) * size, 128), size)
    b_up_ref[...] = sum_ref[pl.ds(8 + lax.div(meta[0], each), 1), cut]


def attend_kernel(meta, x_ref, w_ref, bias_ref, qkv_ref, mixed_ref, mixed_t_ref, lse_ref, w_scr):
    seq = pl.program_id(0)
    wide = w_scr.shape[1]
    part = wide // 3

    @pl.when(seq == 0)
    def _():
        place_rows(meta, w_ref, w_scr, slice(None), slice(None))

    length = meta[3 + seq]
    qkv = (dot_nn(x_ref[0], w_scr[...]) + bias_ref[...]).astype(BF16)
    qkv_ref[0] = qkv
    rows = qkv.shape[0]
    lane = lax.broadcasted_iota(jnp.int32, (rows, 128), 1)
    key_ok = lax.broadcasted_iota(jnp.int32, (rows, rows), 0) < length
    for pair in range(part // 128):
        cut = pair * 128
        query = qkv[:, cut : cut + 128] * jnp.asarray(0.125, BF16)
        key = qkv[:, part + cut : part + cut + 128]
        value_t = qkv[:, 2 * part + cut : 2 * part + cut + 128].T
        outs = []
        for head in range(2):
            query_one = jnp.where((lane >= 64) == (head == 1), query, jnp.zeros_like(query))
            scores = jnp.where(key_ok, dot_nt(key, query_one), -1e30)
            top = jnp.max(scores, axis=0, keepdims=True)
            exp_scores = jnp.exp(scores - top)
            total = jnp.sum(exp_scores, axis=0, keepdims=True)
            lse_ref[0, 2 * pair + head] = top + jnp.log(total)
            out = dot_nn(value_t[64 * head : 64 * head + 64], exp_scores.astype(BF16))
            outs.append(out * (1.0 / total))
        mixed_t = jnp.concatenate(outs, axis=0)
        mixed_t_ref[cut : cut + 128, :] = mixed_t.astype(BF16)
        mixed_ref[0, :, cut : cut + 128] = mixed_t.T.astype(BF16)


def attend(meta, x, weight, bias):
    seqs, length, width = x.shape
    wide = weight.shape[3]
    part = wide // 3
    half_heads = HEADS // 2
    whole = lambda s, m: (0, 0, 0, 0)
    return pl.pallas_call(
        attend_kernel,
        grid_spec=pltpu.PrefetchScalarGridSpec(
            num_scalar_prefetch=1,
            grid=(seqs,),
            in_specs=[
                pl.BlockSpec((1, length, width), lambda s, m: (s, 0, 0)),
                pl.BlockSpec(weight.shape, whole, pipeline_mode=pl.Buffered(1)),
                pl.BlockSpec((1, wide), lambda s, m: (0, 0)),
            ],
            out_specs=[
                pl.BlockSpec((1, length, wide), lambda s, m: (s, 0, 0)),
                pl.BlockSpec((1, length, part), lambda s, m: (s, 0, 0)),
                pl.BlockSpec((part, length), lambda s, m: (0, s)),
                pl.BlockSpec((1, half_heads, 1, length), lambda s, m: (s, 0, 0, 0)),
            ],
            scratch_shapes=[pltpu.VMEM((width, wide), BF16)],
        ),
        out_shape=[
            jax.ShapeDtypeStruct((seqs, length, wide), BF16),
            jax.ShapeDtypeStruct((seqs, length, part), BF16),
            jax.ShapeDtypeStruct((part, seqs * length), BF16),
            jax.ShapeDtypeStruct((seqs, half_heads, 1, length), F32),
        ],
        compiler_params=params(1),
        cost_estimate=cost(
            2 * seqs * length * width * wide + 8 * seqs * length * length * width,
            10e6,
            seqs * length * length * half_heads,
        ),
        name="attend_forward",
    )(meta, x, weight, bias)


def gelu_and_slope(hidden):
    size = jnp.abs(hidden)
    bell = jnp.exp(-0.5 * hidden * hidden)
    t = 1.0 / (1.0 + (0.3275911 * 0.7071067811865476) * size)
    poly = t * (
        0.5 * 0.254829592
        + t
        * (
            0.5 * -0.284496736
            + t * (0.5 * 1.421413741 + t * (0.5 * -1.453152027 + t * (0.5 * 1.061405429)))
        )
    )
    tail = poly * bell
    phi = jnp.where(hidden < 0.0, tail, 1.0 - tail)
    return hidden * phi, phi + hidden * bell * 0.3989422804014327


def norm_forward(hidden):
    center = hidden - jnp.mean(hidden, axis=-1, keepdims=True)
    scale = lax.rsqrt(jnp.mean(center * center, axis=-1, keepdims=True) + EPS)
    return center * scale, scale


def norm_back(grad, hat, scale, gain):
    grad_hat = grad * gain
    shift = jnp.mean(grad_hat, axis=-1, keepdims=True)
    along = jnp.mean(grad_hat * hat, axis=-1, keepdims=True)
    return scale * (grad_hat - shift - hat * along)


def column_sum(rows):
    return jnp.sum(rows.astype(F32), axis=0, keepdims=True)


def place_up(meta, mine, other, w_up, w_out):
    hidden_width, width = w_up.shape[1], w_out.shape[1]
    up_cut, out_cut = hidden_width // (2 * GROUPS), width // (2 * GROUPS)
    for rel, source in enumerate((mine, other)):
        core = meta[2] ^ rel
        for group in range(GROUPS):
            base = group * (up_cut + out_cut)
            up_to = pl.multiple_of(core * (hidden_width // 2) + group * up_cut, 128)
            out_to = pl.multiple_of(core * (width // 2) + group * out_cut, 128)
            place_rows(meta, source, w_up, slice(base, base + up_cut), pl.ds(up_to, up_cut))
            place_rows(
                meta,
                source,
                w_out,
                slice(base + up_cut, base + up_cut + out_cut),
                pl.ds(out_to, out_cut),
            )


def place_down(meta, mine, other, w_down):
    rows = mine.shape[2]
    for rel, source in enumerate((mine, other)):
        for half in range(2):
            for block in range(BLOCKS):
                start = (
                    (meta[0] ^ turned(block)) * (4 * rows)
                    + (meta[2] ^ rel) * (2 * rows)
                    + (meta[1] ^ half) * rows
                )
                w_down[pl.ds(pl.multiple_of(start, 16), rows), :] = source[half, block]


def halves_of(meta, width):
    half = width // 2
    return (
        pl.ds(pl.multiple_of(meta[2] * half, 128), half),
        pl.ds(pl.multiple_of((1 - meta[2]) * half, 128), half),
    )


CHUNK = 512


def up_kernel(
    meta,
    x_ref,
    mixed_mine,
    mixed_other,
    up_mine,
    up_other,
    vec_ref,
    b_up_ref,
    hat_ref,
    scale_ref,
    norm_t_ref,
    active_ref,
    active_t_ref,
    slope_ref,
    w_up,
    w_out,
    normed_low,
):
    step = pl.program_id(0)
    width = w_out.shape[1]

    @pl.when(step == 0)
    def _():
        place_up(meta, up_mine, up_other, w_up, w_out)
        b_out, gain, shift = [vec_ref[i : i + 1, :] for i in range(3)]
        rows_mine, rows_other = halves_of(meta, width)
        branch = dot_nn(mixed_mine[...], w_out[rows_mine, :])
        branch = branch + dot_nn(mixed_other[...], w_out[rows_other, :])
        hat, scale = norm_forward(x_ref[...].astype(F32) + (branch + b_out))
        hat_ref[...] = hat
        scale_ref[...] = jnp.broadcast_to(scale, scale_ref.shape)
        normed_low[...] = (hat * gain + shift).astype(BF16)
        norm_t_ref[...] = normed_low[...].T

    cut = pl.ds(pl.multiple_of(step * CHUNK, CHUNK), CHUNK)
    hidden = dot_nn(normed_low[...], w_up[:, cut]) + b_up_ref[...]
    active, slope = gelu_and_slope(hidden)
    slope_ref[...] = slope.astype(BF16)
    active_low = active.astype(BF16)
    active_ref[...] = active_low
    active_t_ref[...] = active_low.T


def down_kernel(
    seq_len,
    meta,
    hat_ref,
    active_ref,
    cot_ref,
    down_mine,
    down_other,
    vec_ref,
    out_ref,
    grad_second_ref,
    grad_vec_ref,
    w_down,
):
    step = pl.program_id(0)
    tile = hat_ref.shape[0]

    @pl.when(step == 0)
    def _():
        grad_vec_ref[...] = jnp.zeros_like(grad_vec_ref)
        place_down(meta, down_mine, down_other, w_down)

    gain_one, shift_one, b_down, gain, shift = [vec_ref[i : i + 1, :] for i in range(1, 6)]
    seq = lax.div(step * tile, seq_len)
    place = lax.broadcasted_iota(jnp.int32, (tile, 1), 0) + lax.rem(step * tile, seq_len)
    valid = place < meta[3 + seq]
    second = dot_nn(active_ref[...], w_down[...])
    normed = hat_ref[...] * gain_one + shift_one
    hat, scale = norm_forward(normed + (second + b_down))
    out_ref[...] = jnp.where(valid, hat * gain + shift, 0.0).astype(BF16)
    grad_result = jnp.where(valid, cot_ref[...].astype(F32), 0.0)
    grad_second = norm_back(grad_result, hat, scale, gain).astype(BF16)
    grad_second_ref[...] = grad_second
    sums = column_sum(grad_second), column_sum(grad_result * hat), column_sum(grad_result)
    for i, total in enumerate(sums):
        grad_vec_ref[i : i + 1, :] += total


def rest_kernel(
    meta,
    grad_second_ref,
    hat_ref,
    scale_ref,
    w_out,
    vec_ref,
    w_down,
    w_up,
    slope_ref,
    grad_hidden_ref,
    grad_branch_ref,
    grad_mixed_mine,
    grad_mixed_other,
    grad_vec_ref,
    grad_b_up_ref,
    total,
):
    step = pl.program_id(0)
    width = w_out.shape[1]

    @pl.when(step == 0)
    def _():
        total[...] = grad_second_ref[...].astype(F32)

    grad_active = dot_nt(grad_second_ref[...], w_down[...])
    grad_hidden = (slope_ref[...].astype(F32) * grad_active).astype(BF16)
    grad_hidden_ref[...] = grad_hidden
    grad_b_up_ref[...] = column_sum(grad_hidden)
    total[...] += dot_nt(grad_hidden, w_up[...])

    @pl.when(step == pl.num_programs(0) - 1)
    def _():
        grad_normed, hat, gain = total[...], hat_ref[...], vec_ref[1:2, :]
        grad_branch = norm_back(grad_normed, hat, scale_ref[:, 0:1], gain).astype(BF16)
        grad_branch_ref[...] = grad_branch
        rows_mine, rows_other = halves_of(meta, width)
        grad_mixed_mine[...] = dot_nt(grad_branch, w_out[rows_mine, :]).astype(BF16)
        grad_mixed_other[...] = dot_nt(grad_branch, w_out[rows_other, :]).astype(BF16)
        grad_vec_ref[...] = jnp.zeros_like(grad_vec_ref)
        sums = column_sum(grad_branch), column_sum(grad_normed * hat), column_sum(grad_normed)
        for i, one in enumerate(sums):
            grad_vec_ref[i : i + 1, :] = one


def by_chunk(kernel, name, flops, meta, cut, wholes, gates, outs, scratch, cut_rows=()):
    hidden_width = cut[-1].shape[1]
    chunked = lambda shape: pl.BlockSpec((shape[0], CHUNK), lambda n, m: (0, n))
    whole = lambda shape: pl.BlockSpec(
        shape, lambda n, m: (0,) * len(shape), pipeline_mode=pl.Buffered(1)
    )
    spec_of = {
        "cols": chunked,
        "rows": lambda shape: pl.BlockSpec((CHUNK, shape[1]), lambda n, m: (n, 0)),
        "whole": lambda shape: pl.BlockSpec(shape, lambda n, m: (0,) * len(shape)),
    }
    return pl.pallas_call(
        gated(kernel, len(cut) + len(cut_rows) + len(wholes), len(gates)),
        grid_spec=pltpu.PrefetchScalarGridSpec(
            num_scalar_prefetch=1,
            grid=(hidden_width // CHUNK,),
            in_specs=[whole(a.shape) for a in wholes]
            + [spec_of["rows"](a.shape) for a in cut_rows]
            + [chunked(a.shape) for a in cut]
            + gate_specs(gates),
            out_specs=[spec_of[kind](shape) for kind, shape, _ in outs],
            scratch_shapes=[pltpu.VMEM(shape, dtype) for shape, dtype in scratch],
        ),
        out_shape=[jax.ShapeDtypeStruct(shape, dtype) for _, shape, dtype in outs],
        compiler_params=params(1),
        cost_estimate=cost(flops, 20e6),
        name=name,
    )(meta, *wholes, *cut_rows, *cut, *gates)


def by_tile(kernel, name, flops, meta, tiled, wholes, gates, outs, scratch, most=512):
    rows = tiled[0].shape[0]
    tile = min(most, rows)
    by_row = lambda cols: pl.BlockSpec((tile, cols), lambda i, m: (i, 0))
    whole = lambda a: pl.BlockSpec(
        a.shape, lambda i, m: (0,) * a.ndim, pipeline_mode=pl.Buffered(1)
    )
    specs, shapes = [], []
    for kind, size, dtype in outs:
        if kind == "row":
            specs.append(by_row(size))
            shapes.append(jax.ShapeDtypeStruct((rows, size), dtype))
        elif kind == "col":
            specs.append(pl.BlockSpec((size, tile), lambda i, m: (0, i)))
            shapes.append(jax.ShapeDtypeStruct((size, rows), dtype))
        else:
            specs.append(pl.BlockSpec(size, lambda i, m: (0, 0)))
            shapes.append(jax.ShapeDtypeStruct(size, dtype))
    return pl.pallas_call(
        gated(kernel, len(tiled) + len(wholes), len(gates)),
        grid_spec=pltpu.PrefetchScalarGridSpec(
            num_scalar_prefetch=1,
            grid=(rows // tile,),
            in_specs=[by_row(a.shape[1]) for a in tiled]
            + [whole(a) for a in wholes]
            + gate_specs(gates),
            out_specs=specs,
            scratch_shapes=[pltpu.VMEM(shape, BF16) for shape in scratch],
        ),
        out_shape=shapes,
        compiler_params=params(1),
        cost_estimate=cost(flops, 20e6),
        name=name,
    )(meta, *tiled, *wholes, *gates)


def store_blocks(meta, out_ref, value, cut, first=0):
    rows = out_ref.shape[2]
    for block in range(value.shape[0] // (2 * rows)):
        for half in range(2):
            start = (2 * block + half) * rows
            out_ref[meta[1] ^ half, turned(meta[0] ^ (first + block)), :, cut] = value[
                start : start + rows
            ].astype(BF16)


def grad_up_kernel(
    meta, norm_t_ref, mixed_mine, mixed_other, grad_hidden_ref, grad_branch_ref, out_ref
):
    up_cut = grad_hidden_ref.shape[1]
    store_blocks(meta, out_ref, dot_nn(norm_t_ref[...], grad_hidden_ref[...]), slice(0, up_cut))
    cut = slice(up_cut, out_ref.shape[3])
    few = BLOCKS // 2
    grad_branch = grad_branch_ref[...]
    store_blocks(meta, out_ref, dot_nn(mixed_mine[...], grad_branch), cut, meta[2] * few)
    store_blocks(meta, out_ref, dot_nn(mixed_other[...], grad_branch), cut, (1 - meta[2]) * few)


def grad_up(rel, meta, norm_t, mixed_t, grad_hidden, grad_branch, *gates):
    width, rows = norm_t.shape
    hidden_width = grad_hidden.shape[1]
    groups = 3
    up_cut, out_cut = hidden_width // (2 * groups), width // (2 * groups)
    block_rows = width // (2 * BLOCKS)
    whole = lambda tall: pl.BlockSpec(
        (tall, rows), lambda n, m: (0, 0), pipeline_mode=pl.Buffered(1)
    )
    turn = lambda n, m: (0, (m[2] ^ rel) * groups + n)
    return pl.pallas_call(
        gated(grad_up_kernel, 5, len(gates)),
        grid_spec=pltpu.PrefetchScalarGridSpec(
            num_scalar_prefetch=1,
            grid=(groups,),
            in_specs=[
                whole(width),
                whole(width // 2),
                whole(width // 2),
                pl.BlockSpec((rows, up_cut), turn),
                pl.BlockSpec((rows, out_cut), turn),
                *gate_specs(gates),
            ],
            out_specs=pl.BlockSpec(
                (2, BLOCKS, block_rows, up_cut + out_cut), lambda n, m: (0, 0, 0, n)
            ),
        ),
        out_shape=jax.ShapeDtypeStruct(
            (2, BLOCKS, block_rows, groups * (up_cut + out_cut)), BF16
        ),
        compiler_params=params(1),
        cost_estimate=cost(rows * width * (hidden_width + width), 12e6),
        name="grad_up",
    )(meta, norm_t, *mixed_t, grad_hidden, grad_branch, *gates)


def grad_down_kernel(meta, *refs):
    blocks, (grad_second_ref, out_ref) = refs[:-2], refs[-2:]
    rows = out_ref.shape[2]
    left = jnp.concatenate([b[...] for b in blocks], axis=0)
    value = dot_nn(left, grad_second_ref[...]).astype(BF16)
    for i in range(len(blocks)):
        for half in range(2):
            start = (2 * i + half) * rows
            out_ref[meta[1] ^ half, i] = value[start : start + rows]


def grad_down(rel, meta, active_t, grad_second, *gates):
    hidden_width, rows = active_t.shape
    width = grad_second.shape[1]
    block = hidden_width // (2 * BLOCKS)
    some = 4

    def spec(i):
        return pl.BlockSpec(
            (block, rows), lambda j, m: (2 * (m[0] ^ turned(some * j + i)) + (m[2] ^ rel), 0)
        )

    return pl.pallas_call(
        gated(grad_down_kernel, some + 1, len(gates)),
        grid_spec=pltpu.PrefetchScalarGridSpec(
            num_scalar_prefetch=1,
            grid=(BLOCKS // some,),
            in_specs=[spec(i) for i in range(some)]
            + [pl.BlockSpec((rows, width), lambda j, m: (0, 0), pipeline_mode=pl.Buffered(1))]
            + gate_specs(gates),
            out_specs=pl.BlockSpec((2, some, block // 2, width), lambda j, m: (0, j, 0, 0)),
        ),
        out_shape=jax.ShapeDtypeStruct((2, BLOCKS, block // 2, width), BF16),
        compiler_params=params(1),
        cost_estimate=cost(rows * hidden_width * width, 8e6),
        name="grad_down",
    )(meta, *[active_t] * some, grad_second, *gates)


def attend_back_kernel(
    meta,
    x_t_ref,
    qkv_ref,
    mixed_t_ref,
    grad_mixed_ref,
    lse_ref,
    grad_qkv_ref,
    grad_w_ref,
    grad_bias_ref,
    grad_scr,
):
    seq = pl.program_id(0)
    length = meta[3 + seq]
    rows, wide = qkv_ref.shape[1:]
    part = wide // 3
    lane = lax.broadcasted_iota(jnp.int32, (rows, 128), 1)
    key_ok = lax.broadcasted_iota(jnp.int32, (rows, rows), 0) < length
    start = pl.multiple_of(seq * rows, 128)

    @pl.when(seq == 0)
    def _():
        grad_bias_ref[...] = jnp.zeros_like(grad_bias_ref)

    for pair in range(part // 128):
        cut = pair * 128
        query = qkv_ref[0, :, cut : cut + 128] * jnp.asarray(0.125, BF16)
        key = qkv_ref[0, :, part + cut : part + cut + 128]
        value = qkv_ref[0, :, 2 * part + cut : 2 * part + cut + 128]
        grad_out = grad_mixed_ref[0, :, cut : cut + 128]
        product = grad_out.astype(F32).T * mixed_t_ref[cut : cut + 128, :].astype(F32)
        key_t = key.T
        grad_query, grad_key, grad_value = [], 0.0, 0.0
        for head in range(2):
            keep = (lane >= 64) == (head == 1)
            query_one = jnp.where(keep, query, jnp.zeros_like(query))
            grad_one = jnp.where(keep, grad_out, jnp.zeros_like(grad_out))
            inner = slice(64 * head, 64 * head + 64)
            delta = jnp.sum(product[inner], axis=0, keepdims=True)
            scores = jnp.where(key_ok, dot_nt(key, query_one), -1e30)
            prob = jnp.exp(scores - lse_ref[0, 2 * pair + head])
            grad_prob = dot_nt(value, grad_one)
            grad_scores = (prob * (grad_prob - delta)).astype(BF16)
            grad_value = grad_value + dot_nn(prob.astype(BF16), grad_one)
            grad_key = grad_key + dot_nn(grad_scores, query_one)
            grad_query.append(dot_nn(key_t[inner], grad_scores) * 0.125)
        grads = (jnp.concatenate(grad_query, axis=0).T, grad_key, grad_value)
        for kind, grad in enumerate(grads):
            grad = grad.astype(BF16)
            to = slice(kind * part + cut, kind * part + cut + 128)
            grad_scr[pl.ds(start, rows), to] = grad
            grad_qkv_ref[0, :, to] = grad
            grad_bias_ref[:, to] += column_sum(grad)

    @pl.when(seq == pl.num_programs(0) - 1)
    def _():
        store_blocks(meta, grad_w_ref, dot_nn(x_t_ref[...], grad_scr[...]), slice(None))


def attend_back(meta, x_t, qkv, mixed_t, grad_mixed, lse, *gates):
    seqs, length, wide = qkv.shape
    width, rows = x_t.shape
    part = wide // 3
    block_rows = width // (2 * BLOCKS)
    by_seq = lambda cols: pl.BlockSpec((1, length, cols), lambda s, m: (s, 0, 0))
    return pl.pallas_call(
        gated(attend_back_kernel, 5, len(gates)),
        grid_spec=pltpu.PrefetchScalarGridSpec(
            num_scalar_prefetch=1,
            grid=(seqs,),
            in_specs=[
                pl.BlockSpec((width, rows), lambda s, m: (0, 0), pipeline_mode=pl.Buffered(1)),
                by_seq(wide),
                pl.BlockSpec((part, length), lambda s, m: (0, s)),
                by_seq(part),
                pl.BlockSpec((1, HEADS // 2, 1, length), lambda s, m: (s, 0, 0, 0)),
                *gate_specs(gates),
            ],
            out_specs=[
                by_seq(wide),
                pl.BlockSpec((2, BLOCKS, block_rows, wide), lambda s, m: (0, 0, 0, 0)),
                pl.BlockSpec((1, wide), lambda s, m: (0, 0)),
            ],
            scratch_shapes=[pltpu.VMEM((rows, wide), BF16)],
        ),
        out_shape=[
            jax.ShapeDtypeStruct((seqs, length, wide), BF16),
            jax.ShapeDtypeStruct((2, BLOCKS, block_rows, wide), BF16),
            jax.ShapeDtypeStruct((1, wide), F32),
        ],
        compiler_params=params(1),
        cost_estimate=cost(
            2 * rows * width * wide + 10 * rows * length * 4 * part, 8e6, rows * length * 6
        ),
        name="attend_back",
    )(meta, x_t, qkv, mixed_t, grad_mixed, lse, *gates)


def input_kernel(
    meta, branch_ref, grad_mine, grad_other, w_mine, w_other, out_ref, scr_mine, scr_other
):
    @pl.when(pl.program_id(0) == 0)
    def _():
        place_rows(meta, w_mine, scr_mine, slice(None), slice(None))
        place_rows(meta, w_other, scr_other, slice(None), slice(None))

    total = branch_ref[...].astype(F32) + dot_nt(grad_mine[...], scr_mine[...])
    out_ref[...] = total + dot_nt(grad_other[...], scr_other[...])


def finish_kernel(moves, row_step, meta, *refs):
    parts, outs = refs[:2], refs[2:]
    for rel in range(4):
        part = parts[rel & 1].at[rel >> 1]
        x_at, core = meta[1] ^ (rel >> 1), meta[2] ^ (rel & 1)
        rows = part.shape[0]
        at = pl.ds(pl.multiple_of(x_at * rows + core * row_step, 16), rows)
        for columns, out, first, step in moves:
            size = columns.stop - columns.start
            to = pl.ds(pl.multiple_of(first + core * step, 128), size)
            outs[out][at, to] = part[:, columns].astype(F32)


def finish(meta, parts, moves, row_step, shapes):
    whole = lambda shape: pl.BlockSpec(shape, lambda i, m: (0,) * len(shape))
    return pl.pallas_call(
        functools.partial(finish_kernel, moves, row_step),
        grid_spec=pltpu.PrefetchScalarGridSpec(
            num_scalar_prefetch=1,
            grid=(1,),
            in_specs=[whole(p.shape) for p in parts],
            out_specs=[whole(shape) for shape in shapes],
        ),
        out_shape=[jax.ShapeDtypeStruct(shape, F32) for shape in shapes],
        compiler_params=params(1),
        cost_estimate=cost(0, 4e6),
        name="finish",
    )(meta, *parts)


def together(*arrays):
    return lax.optimization_barrier(arrays)


CORE, X, Y, NEAR, FAR = 1, 2, 4, 8, 16
DEVICES = 32


def swap(array, mask):
    pairs = [(i, i ^ mask) for i in range(DEVICES)]
    return lax.ppermute(array, ("shard", "rep"), pairs)


def gather_z(piece):
    came = [swap(piece, mask) for mask in (FAR, NEAR, NEAR | FAR)]
    return jnp.stack([piece] + came)


def double(held, mask):
    return jnp.concatenate([held, swap(held, mask)], axis=0)


def plane_hops(held):
    return [swap(held, mask) for mask in (Y, X, X | Y)]


def plane_join(held, by_y, by_x, across):
    low = jnp.concatenate([held, by_y], axis=0)
    return jnp.stack([low, jnp.concatenate([by_x, across], axis=0)])


def gather_plane(held):
    return plane_join(held, *plane_hops(held))


def add(*terms):
    total = terms[0].astype(F32)
    for term in terms[1:]:
        total = total + term.astype(F32)
    return total.astype(BF16)


def sum_z(parts):
    return add(
        parts[0],
        *[swap(parts[i], mask) for i, mask in ((1, FAR), (2, NEAR), (3, NEAR | FAR))],
    )


def plane_sends(kept, came):
    cut = BLOCKS // 2
    pick = lambda a, x, y: a[x, cut:] if y else a[x, :cut]
    parts = [[add(pick(kept, x, y), pick(came, x, y)) for y in range(2)] for x in range(2)]
    return [
        parts[0][0],
        swap(parts[0][1], Y),
        swap(parts[1][0], X),
        swap(parts[1][1], X | Y),
    ]


def plane_sum(terms):
    return [add(*[t[i] for t in terms]) for i in range(4)]


def share(piece):
    both = jnp.stack([piece, swap(piece, X)])
    return both, swap(both, CORE)


def local(
    fast,
    tokens,
    lengths,
    w_qkv,
    b_query,
    b_value,
    w_out,
    b_out,
    ln1_gain,
    ln1_bias,
    w_up,
    b_up,
    w_down,
    b_down,
    ln2_gain,
    ln2_bias,
    cotangent,
):
    seqs, seq_len, width = tokens.shape
    rows = seqs * seq_len
    hidden_width = w_up.shape[1]
    half = width // 2
    groups = GROUPS
    up_cut, out_cut = hidden_width // (2 * groups), half // groups
    vectors = (b_query, b_value, b_out, ln1_gain, ln1_bias, b_down, ln2_gain, ln2_bias, b_up)

    if fast:
        shard, rep = lax.axis_index("shard"), lax.axis_index("rep")
        x_at, core = rep // 2, rep % 2
    else:
        shard = rep = x_at = core = jnp.int32(0)
    block = width // BLOCKS
    quarter = block // 2
    meta = jnp.concatenate(
        [jnp.stack([shard, x_at, core]).astype(jnp.int32), lengths.astype(jnp.int32)]
    )

    def qkv_parts(w):
        return w.reshape(-1, 2, quarter, 3, 2, half)

    def up_parts(up, out):
        up = up.reshape(-1, 2, quarter, 2, groups, up_cut)
        out = out.reshape(-1, 2, quarter, 2, groups, out_cut)
        return jnp.concatenate([up, out], axis=-1)

    if fast:
        qkv_piece, up_piece, down_piece = pack(meta, w_qkv, w_up, w_out, w_down, vectors)
        qkv_z, up_piece, down_piece = together(gather_z(qkv_piece), up_piece, down_piece)
        table = qkv_z[:, quarter:, : 128 + b_up.shape[0]]
        up_z = double(double(up_piece[None], FAR), NEAR)
        down_z = double(down_piece[None], FAR)
        qkv_mine, up_z, down_z, table = together(
            gather_plane(qkv_z[:, :quarter]), up_z, down_z, table
        )
        vec, b_up_row, *bias = small_call(
            functools.partial(unpack_kernel, block),
            "unpack",
            meta,
            (table, swap(table, Y)),
            ((8, width), (1, hidden_width), (1, 3 * half), (1, 3 * half)),
            ((16, width),),
        )
        qkv_w = qkv_mine, swap(qkv_mine, CORE)
        up_hops, down_z = plane_hops(up_z), double(down_z, NEAR)
    else:
        everything = lambda a: lax.all_gather(a, "shard", axis=0, tiled=True)
        full = [everything(v) for v in vectors]
        order = [turned(p) for p in range(BLOCKS)]
        both = lambda a: (a[0][:, order], a[1][:, order])
        qkv_w = both(
            qkv_parts(everything(w_qkv))
            .transpose(4, 1, 0, 2, 3, 5)
            .reshape(2, 2, BLOCKS, quarter, 3 * half)
        )
        up_w = both(
            up_parts(everything(w_up), everything(w_out))
            .transpose(3, 1, 0, 2, 4, 5)
            .reshape(2, 2, BLOCKS, quarter, -1)
        )
        down_w = both(
            everything(w_down).reshape(BLOCKS, 2, 2, -1, width).transpose(1, 2, 0, 3, 4)
        )
        full = [v.astype(F32) for v in full]
        bias = jnp.stack(
            [full[0].reshape(2, half), jnp.zeros((2, half), F32), full[1].reshape(2, half)], axis=1
        ).reshape(2, 1, 3 * half)
        vec = jnp.stack(full[2:8] + [jnp.zeros_like(full[0])] * 2)
        b_up_row = full[8].reshape(1, -1)
    x_rows = tokens.reshape(rows, width)
    heads = [list(attend(meta, tokens, qkv_w[i], bias[i])) for i in range(2)]
    if fast:
        x_late, heads[0][0] = together(x_rows, heads[0][0])
        x_t = x_late.T
    else:
        x_t = x_rows.T
    if fast:
        *up_hops, down_z, heads[1][0], heads[1][1] = together(
            *up_hops, down_z, heads[1][0], heads[1][1]
        )
        up_mine = plane_join(up_z, *up_hops)
        up_w = up_mine, swap(up_mine, CORE)
    qkv, mixed, mixed_t, lse = zip(*heads)
    mixed_rows = [m.reshape(rows, half) for m in mixed]
    up_shape, out_shape, down_shape = (width, hidden_width), (width, width), (hidden_width, width)
    hat, scale, norm_t, active, active_t, slope, up_full, out_full = by_chunk(
        up_kernel,
        "feed_up",
        2 * rows * width * hidden_width,
        meta,
        (b_up_row,),
        (x_rows, *mixed_rows, *up_w, vec),
        (),
        (
            ("whole", (rows, width), F32),
            ("whole", (rows, 128), F32),
            ("whole", (width, rows), BF16),
            ("cols", (rows, hidden_width), BF16),
            ("rows", (hidden_width, rows), BF16),
            ("cols", (rows, hidden_width), BF16),
            ("whole", up_shape, BF16),
            ("whole", out_shape, BF16),
        ),
        (((rows, width), BF16),),
    )
    row, fixed = "row", "sum"
    if fast:
        active, *hops = together(active, *plane_hops(down_z))
        down_mine = plane_join(down_z, *hops)
        down_w = down_mine, swap(down_mine, CORE)
    layer_out, grad_second, vec_two, down_full = by_tile(
        functools.partial(down_kernel, seq_len),
        "feed_down",
        2 * rows * width * hidden_width,
        meta,
        (hat, active, cotangent.reshape(rows, width)),
        (*down_w, vec),
        (),
        (
            (row, width, BF16),
            (row, width, BF16),
            (fixed, (8, width), F32),
            (fixed, down_shape, BF16),
        ),
        (),
    )
    down_send = grad_down(1, meta, active_t, grad_second)
    down_keep = grad_down(0, meta, active_t, grad_second, down_send)
    gates = (down_keep,)
    if fast:
        down_plane = plane_sends(down_keep, swap(down_send, CORE))
        gates = (down_plane[0],)
    grad_hidden, grad_branch, *grad_mixed, vec_one, grad_b_up = by_chunk(
        rest_kernel,
        "feed_back",
        4 * rows * width * hidden_width,
        meta,
        (up_full, slope),
        (grad_second, hat, scale, out_full, vec),
        gates,
        (
            ("cols", (rows, hidden_width), BF16),
            ("whole", (rows, width), BF16),
            ("whole", (rows, half), BF16),
            ("whole", (rows, half), BF16),
            ("whole", (8, width), F32),
            ("cols", (1, hidden_width), F32),
        ),
        (((rows, width), F32),),
        (down_full,),
    )
    gates = ()
    if fast:
        down_parts = plane_sum(down_plane)
        gates = tuple(down_parts)
    up_send = grad_up(1, meta, norm_t, mixed_t, grad_hidden, grad_branch, *gates)
    if fast:
        up_send, *down_parts = together(up_send, *down_parts)
    up_keep = grad_up(0, meta, norm_t, mixed_t, grad_hidden, grad_branch, up_send)
    gates = (up_keep,)
    if fast:
        up_plane = plane_sends(up_keep, swap(up_send, CORE))
        down_piece = sum_z(down_parts)
        gates = (up_plane[0],)
    grad_mixed = [g.reshape(seqs, seq_len, half) for g in grad_mixed]

    def back(i, *gates):
        return attend_back(meta, x_t, qkv[i], mixed_t[i], grad_mixed[i], lse[i], *gates)

    other_qkv, qkv_send, other_bias = back(1, *gates)
    gates = (qkv_send,)
    if fast:
        down_piece, qkv_send = together(down_piece, qkv_send)
        gates = (qkv_send, up_plane[1], up_plane[2])
    mine_qkv, qkv_keep, mine_bias = back(0, *gates)
    gates = (qkv_keep,)
    if fast:
        qkv_plane = plane_sends(qkv_keep, swap(qkv_send, CORE))
        down_piece, qkv_plane[0], *up_plane = together(down_piece, qkv_plane[0], *up_plane)
        down_both = jnp.stack([down_piece, swap(down_piece, X)])
        up_parts_sum = plane_sum(up_plane)
        up_near = swap(jnp.stack(up_parts_sum[2:]), NEAR)
        down_quarters = down_both, swap(down_both, CORE)
        gates = (qkv_plane[0], up_parts_sum[0])
    (input_grad,) = by_tile(
        input_kernel,
        "input_grad",
        6 * rows * width * width,
        meta,
        (grad_branch, mine_qkv.reshape(rows, -1), other_qkv.reshape(rows, -1)),
        qkv_w,
        gates,
        ((row, width, F32),),
        ((width, 3 * half), (width, 3 * half)),
    )

    (total,) = small_call(
        sums_kernel,
        "sums",
        meta,
        (vec_one, vec_two, grad_b_up, mine_bias, other_bias),
        ((16, width),),
    )
    if fast:
        total, input_grad, up_near, *qkv_plane[1:3] = together(
            total, input_grad, up_near, *qkv_plane[1:3]
        )
        up_low = [add(up_parts_sum[i], up_near[i]) for i in range(2)]
        up_far, qkv_plane[3] = together(swap(up_low[1], FAR), qkv_plane[3])
        up_piece = add(up_low[0], up_far)
        qkv_parts_sum = plane_sum(qkv_plane)
        qkv_hops = [swap(qkv_parts_sum[i], m) for i, m in ((1, FAR), (2, NEAR), (3, NEAR | FAR))]
        up_x, *qkv_hops = together(swap(up_piece, X), *qkv_hops)
        up_both = jnp.stack([up_piece, up_x])
        up_quarters = up_both, swap(up_both, CORE)
        qkv_quarters = share(add(qkv_parts_sum[0], *qkv_hops))
        for mask in (CORE, X, Y, NEAR, FAR):
            total = total + swap(total, mask)
        own, own_b_up = small_call(
            functools.partial(own_sums_kernel, block),
            "own_sums",
            meta,
            (total,),
            ((8, 128), (1, b_up.shape[0])),
        )
        sums = [own[i, :block] for i in range(8)] + [own_b_up[0]]
        step = up_cut + out_cut
        up_moves = [
            move
            for g in range(groups)
            for move in (
                (slice(g * step, g * step + up_cut), 0, g * up_cut, hidden_width // 2),
                (slice(g * step + up_cut, (g + 1) * step), 1, g * out_cut, half),
            )
        ]
        qkv_moves = [(slice(k * half, (k + 1) * half), 0, k * width, half) for k in range(3)]
        (grad_w_down,) = finish(
            meta,
            down_quarters,
            [(slice(0, width), 0, 0, 0)],
            w_down.shape[0] // 2,
            [w_down.shape],
        )
        grad_w_up, grad_w_out = finish(meta, up_quarters, up_moves, 0, [w_up.shape, w_out.shape])
        (grad_w_qkv,) = finish(meta, qkv_quarters, qkv_moves, 0, [w_qkv.shape])
    else:
        total_of = lambda a: lax.psum(
            lax.psum_scatter(a, "shard", scatter_dimension=0, tiled=True), "rep"
        )
        sums = [total_of(g) for g in (*total[:8], total[8:12].reshape(-1))]
        order = [turned(p) for p in range(BLOCKS)]
        down_keep, down_send, up_keep, up_send = (
            a[:, order] for a in (down_keep, down_send, up_keep, up_send)
        )
        down = jnp.stack([down_keep, down_send]).transpose(2, 0, 1, 3, 4)
        grad_w_down = total_of(down.reshape(hidden_width, width).astype(F32))
        up = jnp.stack([up_keep, up_send]).reshape(
            2, 2, BLOCKS, quarter, groups, up_cut + out_cut
        )
        up = up.transpose(2, 1, 3, 0, 4, 5)
        grad_w_up = total_of(up[..., :up_cut].reshape(width, hidden_width).astype(F32))
        grad_w_out = total_of(up[..., up_cut:].reshape(width, width).astype(F32))
        qkv_sum = jnp.stack([qkv_keep[:, order], qkv_send[:, order]])
        qkv_sum = qkv_sum.reshape(2, 2, BLOCKS, quarter, 3, half)
        qkv_sum = qkv_sum.transpose(2, 1, 3, 4, 0, 5).reshape(width, 3 * width)
        grad_w_qkv = total_of(qkv_sum.astype(F32))
    return (
        layer_out.reshape(seqs, seq_len, width),
        input_grad.reshape(seqs, seq_len, width),
        grad_w_qkv,
        sums[0],
        sums[1],
        grad_w_out,
        sums[2],
        sums[3],
        sums[4],
        grad_w_up,
        sums[8],
        grad_w_down,
        sums[5],
        sums[6],
        sums[7],
    )


def solution(mesh):
    fast = mesh.shape["shard"] == BLOCKS and mesh.shape["rep"] == 4
    by_seq = P(("shard", "rep"), None, None)
    one, two = P("shard"), P("shard", None)
    in_specs = (by_seq, P(("shard", "rep")), two, one, one, two, one, one, one)
    in_specs = in_specs + (two, one, two, one, one, one, by_seq)
    out_specs = (by_seq, by_seq, two, one, one, two, one, one, one, two, one, two, one, one, one)
    return jax.shard_map(
        functools.partial(local, fast),
        mesh=mesh,
        in_specs=in_specs,
        out_specs=out_specs,
        check_vma=False,
    )
```

```python
import functools

import jax
import jax.numpy as jnp
from jax import lax
from jax.experimental import pallas as pl
from jax.experimental.pallas import tpu as pltpu
from jax.sharding import PartitionSpec as P

HEADS = 12
EPS = 1e-05
F32 = jnp.float32
BF16 = jnp.bfloat16
BLOCKS = 8
GROUPS = 3
VMEM_LIMIT = 58 * 1024 * 1024


def dot_nn(a, b):
    return lax.dot_general(a, b, (((1,), (0,)), ((), ())), preferred_element_type=F32)


def dot_nt(a, b):
    return lax.dot_general(a, b, (((1,), (1,)), ((), ())), preferred_element_type=F32)


def dot_tn(a, b):
    return lax.dot_general(a, b, (((0,), (0,)), ((), ())), preferred_element_type=F32)


def params(grid_dims):
    return pltpu.CompilerParams(
        dimension_semantics=("arbitrary",) * grid_dims, vmem_limit_bytes=VMEM_LIMIT
    )


def cost(micros):
    return pl.CostEstimate(flops=int(micros * 1.15e9), bytes_accessed=1 << 20, transcendentals=0)


def gated(kernel, inputs, gates):
    def body(*refs):
        kernel(*refs[: inputs + 1], *refs[inputs + 1 + gates :])

    return body


def gate_specs(gates):
    return [pl.BlockSpec(memory_space=pl.ANY)] * len(gates)


def turned(place):
    return ((place & 1) << 2) | (place & 2) | ((place >> 2) & 1)


def place_rows(meta, source, target, columns, cut):
    rows = source.shape[2]
    for half in range(2):
        for block in range(BLOCKS):
            start = (meta[0] ^ turned(block)) * (2 * rows) + (meta[1] ^ half) * rows
            target[pl.ds(pl.multiple_of(start, 16), rows), cut] = source[half, block, :, columns]


def pack_kernel(groups, *refs):
    meta, w_qkv, w_up, w_out, w_down, *vectors, qkv_ref, up_ref, down_ref = refs
    rows, wide = up_ref.shape[0], qkv_ref.shape[1]
    half = wide // 3
    up_cut, out_cut = w_up.shape[1] // (2 * groups), w_out.shape[1] // (2 * groups)
    at = pl.ds(pl.multiple_of(meta[1] * rows, 16), rows)

    def columns(start, size):
        return pl.ds(pl.multiple_of(start, 128), size)

    for kind in range(3):
        start = (2 * kind + meta[2]) * half
        qkv_ref[:rows, kind * half : (kind + 1) * half] = w_qkv[at, columns(start, half)]
    for group in range(groups):
        base = group * (up_cut + out_cut)
        start = (meta[2] * groups + group) * up_cut
        up_ref[:, base : base + up_cut] = w_up[at, columns(start, up_cut)]
        start = (meta[2] * groups + group) * out_cut
        up_ref[:, base + up_cut : base + up_cut + out_cut] = w_out[at, columns(start, out_cut)]
    rows_down = down_ref.shape[0]
    start = (2 * meta[2] + meta[1]) * rows_down
    down_ref[...] = w_down[pl.ds(pl.multiple_of(start, 16), rows_down), :]
    *short, long = vectors
    extra = qkv_ref.shape[0] - rows
    small = short[0].shape[0]
    place = lax.broadcasted_iota(jnp.int32, (extra, small), 0)
    table = jnp.zeros((extra, small), F32)
    for i, v in enumerate(short):
        table = jnp.where(place == i, v[...].astype(F32).reshape(1, small), table)
    qkv_ref[rows:, :] = jnp.zeros((extra, wide), BF16)
    qkv_ref[rows:, :small] = table.astype(BF16)
    size = long.shape[0]
    wide_row = jnp.broadcast_to(long[...].astype(F32).reshape(1, size), (extra, size))
    qkv_ref[rows:, 128 : 128 + size] = wide_row.astype(BF16)


def pack(meta, w_qkv, w_up, w_out, w_down, vectors):
    rows = w_up.shape[0] // 2
    whole = lambda a: pl.BlockSpec(a.shape, lambda i, m: (0,) * a.ndim)
    shapes = [
        (rows + 16, w_qkv.shape[1] // 2),
        (rows, (w_up.shape[1] + w_out.shape[1]) // 2),
        (w_down.shape[0] // 4, w_down.shape[1]),
    ]
    outs = [jax.ShapeDtypeStruct(shape, BF16) for shape in shapes]
    operands = (w_qkv, w_up, w_out, w_down, *vectors)
    return pl.pallas_call(
        functools.partial(pack_kernel, GROUPS),
        grid_spec=pltpu.PrefetchScalarGridSpec(
            num_scalar_prefetch=1,
            grid=(1,),
            in_specs=[whole(a) for a in operands],
            out_specs=[whole(o) for o in outs],
        ),
        out_shape=outs,
        compiler_params=params(1),
        cost_estimate=cost(2),
        name="pack",
    )(meta, *operands)


def shard_columns(shard, block, width, lanes):
    lane = lax.broadcasted_iota(jnp.int32, (lanes, width), 0)
    column = lax.broadcasted_iota(jnp.int32, (lanes, width), 1)
    return (lane < block) & (column == lane + shard * block)


def unpack_kernel(block, meta, near_ref, far_ref, vec_ref, b_up_ref, mine_ref, other_ref, scr):
    width = vec_ref.shape[1]
    half, size = width // 2, b_up_ref.shape[1] // BLOCKS
    total = jnp.zeros(scr.shape, F32)
    for place in range(BLOCKS):
        source = (near_ref, far_ref)[place // 4]
        rows = source[place % 4]
        shard = meta[0] ^ turned(place)
        spread = shard_columns(shard, block, width, 128).astype(F32).astype(BF16)
        total = total + dot_nn(rows[:, :128], spread)
        to = pl.ds(pl.multiple_of(shard * size, 128), size)
        b_up_ref[:, to] = rows[:1, 128 : 128 + size].astype(F32)
    scr[...] = total
    vec_ref[...] = jnp.zeros_like(vec_ref)
    vec_ref[0:6, :] = total[2:8]
    for rel, out in enumerate((mine_ref, other_ref)):
        cut = pl.ds(pl.multiple_of((meta[2] ^ rel) * half, 128), half)
        out[...] = jnp.zeros_like(out)
        out[:, :half] = scr[0:1, cut]
        out[:, 2 * half :] = scr[1:2, cut]


def small_call(kernel, name, meta, operands, shapes, scratch=()):
    whole = lambda a: pl.BlockSpec(a.shape, lambda i, m: (0,) * len(a.shape))
    outs = [jax.ShapeDtypeStruct(shape, F32) for shape in shapes]
    return pl.pallas_call(
        kernel,
        grid_spec=pltpu.PrefetchScalarGridSpec(
            num_scalar_prefetch=1,
            grid=(1,),
            in_specs=[whole(a) for a in operands],
            out_specs=[whole(o) for o in outs],
            scratch_shapes=[pltpu.VMEM(shape, F32) for shape in scratch],
        ),
        out_shape=outs,
        compiler_params=params(1),
        cost_estimate=cost(2),
        name=name,
    )(meta, *operands)


def sums_kernel(meta, vec_one, vec_two, b_up, bias_mine, bias_other, out_ref):
    width = out_ref.shape[1]
    half = width // 2
    out_ref[...] = jnp.zeros_like(out_ref)
    for rel, source in enumerate((bias_mine, bias_other)):
        to = pl.ds(pl.multiple_of((meta[2] ^ rel) * half, 128), half)
        out_ref[0:1, to] = source[:, :half]
        out_ref[1:2, to] = source[:, 2 * half :]
    out_ref[2:5, :] = vec_one[0:3, :]
    out_ref[5:8, :] = vec_two[0:3, :]
    for i in range(b_up.shape[1] // width):
        out_ref[8 + i : 9 + i, :] = b_up[:, i * width : (i + 1) * width]


def own_sums_kernel(block, meta, sum_ref, own_ref, b_up_ref):
    width, size = sum_ref.shape[1], b_up_ref.shape[1]
    pick = shard_columns(meta[0], block, width, 128).astype(F32)
    own_ref[...] = lax.dot_general(
        sum_ref[0:8, :],
        pick,
        (((1,), (1,)), ((), ())),
        precision=lax.Precision.HIGHEST,
        preferred_element_type=F32,
    )
    each = width // size
    cut = pl.ds(pl.multiple_of(lax.rem(meta[0], each) * size, 128), size)
    b_up_ref[...] = sum_ref[pl.ds(8 + lax.div(meta[0], each), 1), cut]


def attend_kernel(meta, x_ref, w_ref, bias_ref, qkv_ref, mixed_ref, mixed_t_ref, lse_ref, w_scr):
    seq = pl.program_id(0)
    wide = w_scr.shape[1]
    part = wide // 3

    @pl.when(seq == 0)
    def _():
        place_rows(meta, w_ref, w_scr, slice(None), slice(None))

    length = meta[3 + seq]
    qkv = (dot_nn(x_ref[0], w_scr[...]) + bias_ref[...]).astype(BF16)
    qkv_ref[0] = qkv
    rows = qkv.shape[0]
    lane = lax.broadcasted_iota(jnp.int32, (rows, 128), 1)
    key_ok = lax.broadcasted_iota(jnp.int32, (rows, rows), 0) < length
    for pair in range(part // 128):
        cut = pair * 128
        query = qkv[:, cut : cut + 128] * jnp.asarray(0.125, BF16)
        key = qkv[:, part + cut : part + cut + 128]
        value_t = qkv[:, 2 * part + cut : 2 * part + cut + 128].T
        outs = []
        for head in range(2):
            query_one = jnp.where((lane >= 64) == (head == 1), query, jnp.zeros_like(query))
            scores = jnp.where(key_ok, dot_nt(key, query_one), -1e30)
            top = jnp.max(scores, axis=0, keepdims=True)
            exp_scores = jnp.exp(scores - top)
            total = jnp.sum(exp_scores, axis=0, keepdims=True)
            lse_ref[0, 2 * pair + head] = top + jnp.log(total)
            out = dot_nn(value_t[64 * head : 64 * head + 64], exp_scores.astype(BF16))
            outs.append(out * (1.0 / total))
        mixed_t = jnp.concatenate(outs, axis=0)
        mixed_t_ref[cut : cut + 128, :] = mixed_t.astype(BF16)
        mixed_ref[0, :, cut : cut + 128] = mixed_t.T.astype(BF16)


def attend(meta, x, weight, bias):
    seqs, length, width = x.shape
    wide = weight.shape[3]
    part = wide // 3
    half_heads = HEADS // 2
    whole = lambda s, m: (0, 0, 0, 0)
    return pl.pallas_call(
        attend_kernel,
        grid_spec=pltpu.PrefetchScalarGridSpec(
            num_scalar_prefetch=1,
            grid=(seqs,),
            in_specs=[
                pl.BlockSpec((1, length, width), lambda s, m: (s, 0, 0)),
                pl.BlockSpec(weight.shape, whole, pipeline_mode=pl.Buffered(1)),
                pl.BlockSpec((1, wide), lambda s, m: (0, 0)),
            ],
            out_specs=[
                pl.BlockSpec((1, length, wide), lambda s, m: (s, 0, 0)),
                pl.BlockSpec((1, length, part), lambda s, m: (s, 0, 0)),
                pl.BlockSpec((part, length), lambda s, m: (0, s)),
                pl.BlockSpec((1, half_heads, 1, length), lambda s, m: (s, 0, 0, 0)),
            ],
            scratch_shapes=[pltpu.VMEM((width, wide), BF16)],
        ),
        out_shape=[
            jax.ShapeDtypeStruct((seqs, length, wide), BF16),
            jax.ShapeDtypeStruct((seqs, length, part), BF16),
            jax.ShapeDtypeStruct((part, seqs * length), BF16),
            jax.ShapeDtypeStruct((seqs, half_heads, 1, length), F32),
        ],
        compiler_params=params(1),
        cost_estimate=cost(11),
        name="attend_forward",
    )(meta, x, weight, bias)


def gelu_and_slope(hidden):
    size = jnp.abs(hidden)
    bell = jnp.exp2(hidden * hidden * -0.7213475204444817)
    t = 1.0 / (1.0 + (0.3275911 * 0.7071067811865476) * size)
    poly = t * (
        0.5 * 0.254829592
        + t
        * (
            0.5 * -0.284496736
            + t * (0.5 * 1.421413741 + t * (0.5 * -1.453152027 + t * (0.5 * 1.061405429)))
        )
    )
    tail = poly * bell
    phi = jnp.where(hidden < 0.0, tail, 1.0 - tail)
    return hidden * phi, phi + hidden * bell * 0.3989422804014327


def norm_forward(hidden):
    center = hidden - jnp.mean(hidden, axis=-1, keepdims=True)
    scale = lax.rsqrt(jnp.mean(center * center, axis=-1, keepdims=True) + EPS)
    return center * scale, scale


def norm_back(grad, hat, scale, gain):
    grad_hat = grad * gain
    shift = jnp.mean(grad_hat, axis=-1, keepdims=True)
    along = jnp.mean(grad_hat * hat, axis=-1, keepdims=True)
    return scale * (grad_hat - shift - hat * along)


def column_sum(rows):
    return jnp.sum(rows.astype(F32), axis=0, keepdims=True)


def place_up(meta, mine, other, w_up, w_out):
    hidden_width, width = w_up.shape[1], w_out.shape[1]
    up_cut, out_cut = hidden_width // (2 * GROUPS), width // (2 * GROUPS)
    for rel, source in enumerate((mine, other)):
        core = meta[2] ^ rel
        for group in range(GROUPS):
            base = group * (up_cut + out_cut)
            up_to = pl.multiple_of(core * (hidden_width // 2) + group * up_cut, 128)
            out_to = pl.multiple_of(core * (width // 2) + group * out_cut, 128)
            place_rows(meta, source, w_up, slice(base, base + up_cut), pl.ds(up_to, up_cut))
            place_rows(
                meta,
                source,
                w_out,
                slice(base + up_cut, base + up_cut + out_cut),
                pl.ds(out_to, out_cut),
            )


def place_down(meta, mine, other, w_down):
    rows = mine.shape[2]
    for rel, source in enumerate((mine, other)):
        for half in range(2):
            for block in range(BLOCKS):
                start = (
                    (meta[0] ^ turned(block)) * (4 * rows)
                    + (meta[2] ^ rel) * (2 * rows)
                    + (meta[1] ^ half) * rows
                )
                w_down[pl.ds(pl.multiple_of(start, 16), rows), :] = source[half, block]


def halves_of(meta, width):
    half = width // 2
    return (
        pl.ds(pl.multiple_of(meta[2] * half, 128), half),
        pl.ds(pl.multiple_of((1 - meta[2]) * half, 128), half),
    )


CHUNK = 512


def up_kernel(
    meta,
    x_ref,
    mixed_mine,
    mixed_other,
    up_mine,
    up_other,
    vec_ref,
    b_up_ref,
    hat_ref,
    scale_ref,
    norm_t_ref,
    active_ref,
    active_t_ref,
    slope_ref,
    w_up,
    w_out,
    normed_low,
):
    step = pl.program_id(0)
    width = w_out.shape[1]

    @pl.when(step == 0)
    def _():
        place_up(meta, up_mine, up_other, w_up, w_out)
        b_out, gain, shift = [vec_ref[i : i + 1, :] for i in range(3)]
        rows_mine, rows_other = halves_of(meta, width)
        branch = dot_nn(mixed_mine[...], w_out[rows_mine, :])
        branch = branch + dot_nn(mixed_other[...], w_out[rows_other, :])
        hat, scale = norm_forward(x_ref[...].astype(F32) + (branch + b_out))
        hat_ref[...] = hat
        scale_ref[...] = jnp.broadcast_to(scale, scale_ref.shape)
        normed_low[...] = (hat * gain + shift).astype(BF16)
        norm_t_ref[...] = normed_low[...].T

    cut = pl.ds(pl.multiple_of(step * CHUNK, CHUNK), CHUNK)
    hidden = dot_nn(normed_low[...], w_up[:, cut]) + b_up_ref[...]
    active, slope = gelu_and_slope(hidden)
    slope_ref[...] = slope.astype(BF16)
    active_low = active.astype(BF16)
    active_ref[...] = active_low
    active_t_ref[...] = active_low.T


def down_kernel(
    seq_len,
    meta,
    hat_ref,
    active_ref,
    cot_ref,
    down_mine,
    down_other,
    vec_ref,
    out_ref,
    grad_second_ref,
    grad_vec_ref,
    w_down,
):
    step = pl.program_id(0)
    tile = hat_ref.shape[0]

    @pl.when(step == 0)
    def _():
        grad_vec_ref[...] = jnp.zeros_like(grad_vec_ref)
        place_down(meta, down_mine, down_other, w_down)

    gain_one, shift_one, b_down, gain, shift = [vec_ref[i : i + 1, :] for i in range(1, 6)]
    seq = lax.div(step * tile, seq_len)
    place = lax.broadcasted_iota(jnp.int32, (tile, 1), 0) + lax.rem(step * tile, seq_len)
    valid = place < meta[3 + seq]
    second = dot_nn(active_ref[...], w_down[...])
    normed = hat_ref[...] * gain_one + shift_one
    hat, scale = norm_forward(normed + (second + b_down))
    out_ref[...] = jnp.where(valid, hat * gain + shift, 0.0).astype(BF16)
    grad_result = jnp.where(valid, cot_ref[...].astype(F32), 0.0)
    grad_second = norm_back(grad_result, hat, scale, gain).astype(BF16)
    grad_second_ref[...] = grad_second
    sums = column_sum(grad_second), column_sum(grad_result * hat), column_sum(grad_result)
    for i, total in enumerate(sums):
        grad_vec_ref[i : i + 1, :] += total


def rest_kernel(
    meta,
    grad_second_ref,
    hat_ref,
    scale_ref,
    w_out,
    vec_ref,
    w_down,
    w_up,
    slope_ref,
    grad_hidden_ref,
    grad_branch_ref,
    grad_mixed_mine,
    grad_mixed_other,
    grad_vec_ref,
    grad_b_up_ref,
    total,
):
    step = pl.program_id(0)
    width = w_out.shape[1]

    @pl.when(step == 0)
    def _():
        total[...] = grad_second_ref[...].astype(F32)

    grad_active = dot_nt(grad_second_ref[...], w_down[...])
    grad_hidden = (slope_ref[...].astype(F32) * grad_active).astype(BF16)
    grad_hidden_ref[...] = grad_hidden
    grad_b_up_ref[...] = column_sum(grad_hidden)
    total[...] += dot_nt(grad_hidden, w_up[...])

    @pl.when(step == pl.num_programs(0) - 1)
    def _():
        grad_normed, hat, gain = total[...], hat_ref[...], vec_ref[1:2, :]
        grad_branch = norm_back(grad_normed, hat, scale_ref[:, 0:1], gain).astype(BF16)
        grad_branch_ref[...] = grad_branch
        rows_mine, rows_other = halves_of(meta, width)
        grad_mixed_mine[...] = dot_nt(grad_branch, w_out[rows_mine, :]).astype(BF16)
        grad_mixed_other[...] = dot_nt(grad_branch, w_out[rows_other, :]).astype(BF16)
        grad_vec_ref[...] = jnp.zeros_like(grad_vec_ref)
        sums = column_sum(grad_branch), column_sum(grad_normed * hat), column_sum(grad_normed)
        for i, one in enumerate(sums):
            grad_vec_ref[i : i + 1, :] = one


def by_chunk(kernel, name, micros, meta, cut, wholes, gates, outs, scratch, cut_rows=()):
    hidden_width = cut[-1].shape[1]
    chunked = lambda shape: pl.BlockSpec((shape[0], CHUNK), lambda n, m: (0, n))
    whole = lambda shape: pl.BlockSpec(
        shape, lambda n, m: (0,) * len(shape), pipeline_mode=pl.Buffered(1)
    )
    spec_of = {
        "cols": chunked,
        "rows": lambda shape: pl.BlockSpec((CHUNK, shape[1]), lambda n, m: (n, 0)),
        "whole": lambda shape: pl.BlockSpec(shape, lambda n, m: (0,) * len(shape)),
    }
    return pl.pallas_call(
        gated(kernel, len(cut) + len(cut_rows) + len(wholes), len(gates)),
        grid_spec=pltpu.PrefetchScalarGridSpec(
            num_scalar_prefetch=1,
            grid=(hidden_width // CHUNK,),
            in_specs=[whole(a.shape) for a in wholes]
            + [spec_of["rows"](a.shape) for a in cut_rows]
            + [chunked(a.shape) for a in cut]
            + gate_specs(gates),
            out_specs=[spec_of[kind](shape) for kind, shape, _ in outs],
            scratch_shapes=[pltpu.VMEM(shape, dtype) for shape, dtype in scratch],
        ),
        out_shape=[jax.ShapeDtypeStruct(shape, dtype) for _, shape, dtype in outs],
        compiler_params=params(1),
        cost_estimate=cost(micros),
        name=name,
    )(meta, *wholes, *cut_rows, *cut, *gates)


def by_tile(kernel, name, micros, meta, tiled, wholes, gates, outs, scratch, most=512):
    rows = tiled[0].shape[0]
    tile = min(most, rows)
    by_row = lambda cols: pl.BlockSpec((tile, cols), lambda i, m: (i, 0))
    whole = lambda a: pl.BlockSpec(
        a.shape, lambda i, m: (0,) * a.ndim, pipeline_mode=pl.Buffered(1)
    )
    specs, shapes = [], []
    for kind, size, dtype in outs:
        if kind == "row":
            specs.append(by_row(size))
            shapes.append(jax.ShapeDtypeStruct((rows, size), dtype))
        elif kind == "col":
            specs.append(pl.BlockSpec((size, tile), lambda i, m: (0, i)))
            shapes.append(jax.ShapeDtypeStruct((size, rows), dtype))
        else:
            specs.append(pl.BlockSpec(size, lambda i, m: (0, 0)))
            shapes.append(jax.ShapeDtypeStruct(size, dtype))
    return pl.pallas_call(
        gated(kernel, len(tiled) + len(wholes), len(gates)),
        grid_spec=pltpu.PrefetchScalarGridSpec(
            num_scalar_prefetch=1,
            grid=(rows // tile,),
            in_specs=[by_row(a.shape[1]) for a in tiled]
            + [whole(a) for a in wholes]
            + gate_specs(gates),
            out_specs=specs,
            scratch_shapes=[pltpu.VMEM(shape, BF16) for shape in scratch],
        ),
        out_shape=shapes,
        compiler_params=params(1),
        cost_estimate=cost(micros),
        name=name,
    )(meta, *tiled, *wholes, *gates)


def store_blocks(meta, out_ref, value, cut, first=0):
    rows = out_ref.shape[2]
    for block in range(value.shape[0] // (2 * rows)):
        for half in range(2):
            start = (2 * block + half) * rows
            out_ref[meta[1] ^ half, turned(meta[0] ^ (first + block)), :, cut] = value[
                start : start + rows
            ].astype(BF16)


def grad_up_kernel(
    meta, norm_t_ref, mixed_mine, mixed_other, grad_hidden_ref, grad_branch_ref, out_ref
):
    up_cut = grad_hidden_ref.shape[1]
    store_blocks(meta, out_ref, dot_nn(norm_t_ref[...], grad_hidden_ref[...]), slice(0, up_cut))
    cut = slice(up_cut, out_ref.shape[3])
    few = BLOCKS // 2
    grad_branch = grad_branch_ref[...]
    store_blocks(meta, out_ref, dot_nn(mixed_mine[...], grad_branch), cut, meta[2] * few)
    store_blocks(meta, out_ref, dot_nn(mixed_other[...], grad_branch), cut, (1 - meta[2]) * few)


def grad_up(rel, meta, norm_t, mixed_t, grad_hidden, grad_branch, *gates):
    width, rows = norm_t.shape
    hidden_width = grad_hidden.shape[1]
    groups = 3
    up_cut, out_cut = hidden_width // (2 * groups), width // (2 * groups)
    block_rows = width // (2 * BLOCKS)
    whole = lambda tall: pl.BlockSpec(
        (tall, rows), lambda n, m: (0, 0), pipeline_mode=pl.Buffered(1)
    )
    turn = lambda n, m: (0, (m[2] ^ rel) * groups + n)
    return pl.pallas_call(
        gated(grad_up_kernel, 5, len(gates)),
        grid_spec=pltpu.PrefetchScalarGridSpec(
            num_scalar_prefetch=1,
            grid=(groups,),
            in_specs=[
                whole(width),
                whole(width // 2),
                whole(width // 2),
                pl.BlockSpec((rows, up_cut), turn),
                pl.BlockSpec((rows, out_cut), turn),
                *gate_specs(gates),
            ],
            out_specs=pl.BlockSpec(
                (2, BLOCKS, block_rows, up_cut + out_cut), lambda n, m: (0, 0, 0, n)
            ),
        ),
        out_shape=jax.ShapeDtypeStruct(
            (2, BLOCKS, block_rows, groups * (up_cut + out_cut)), BF16
        ),
        compiler_params=params(1),
        cost_estimate=cost(8),
        name="grad_up",
    )(meta, norm_t, *mixed_t, grad_hidden, grad_branch, *gates)


def grad_down_kernel(meta, *refs):
    blocks, (grad_second_ref, out_ref) = refs[:-2], refs[-2:]
    rows = out_ref.shape[2]
    left = jnp.concatenate([b[...] for b in blocks], axis=0)
    value = dot_nn(left, grad_second_ref[...]).astype(BF16)
    for i in range(len(blocks)):
        for half in range(2):
            start = (2 * i + half) * rows
            out_ref[meta[1] ^ half, i] = value[start : start + rows]


def grad_down(rel, meta, active_t, grad_second, *gates):
    hidden_width, rows = active_t.shape
    width = grad_second.shape[1]
    block = hidden_width // (2 * BLOCKS)
    some = 4

    def spec(i):
        return pl.BlockSpec(
            (block, rows), lambda j, m: (2 * (m[0] ^ turned(some * j + i)) + (m[2] ^ rel), 0)
        )

    return pl.pallas_call(
        gated(grad_down_kernel, some + 1, len(gates)),
        grid_spec=pltpu.PrefetchScalarGridSpec(
            num_scalar_prefetch=1,
            grid=(BLOCKS // some,),
            in_specs=[spec(i) for i in range(some)]
            + [pl.BlockSpec((rows, width), lambda j, m: (0, 0), pipeline_mode=pl.Buffered(1))]
            + gate_specs(gates),
            out_specs=pl.BlockSpec((2, some, block // 2, width), lambda j, m: (0, j, 0, 0)),
        ),
        out_shape=jax.ShapeDtypeStruct((2, BLOCKS, block // 2, width), BF16),
        compiler_params=params(1),
        cost_estimate=cost(6),
        name="grad_down",
    )(meta, *[active_t] * some, grad_second, *gates)


def attend_back_kernel(
    meta,
    x_t_ref,
    qkv_ref,
    mixed_t_ref,
    grad_mixed_ref,
    lse_ref,
    grad_qkv_ref,
    grad_w_ref,
    grad_bias_ref,
    grad_scr,
):
    seq = pl.program_id(0)
    length = meta[3 + seq]
    rows, wide = qkv_ref.shape[1:]
    part = wide // 3
    lane = lax.broadcasted_iota(jnp.int32, (rows, 128), 1)
    key_ok = lax.broadcasted_iota(jnp.int32, (rows, rows), 0) < length
    start = pl.multiple_of(seq * rows, 128)

    @pl.when(seq == 0)
    def _():
        grad_bias_ref[...] = jnp.zeros_like(grad_bias_ref)

    for pair in range(part // 128):
        cut = pair * 128
        query = qkv_ref[0, :, cut : cut + 128] * jnp.asarray(0.125, BF16)
        key = qkv_ref[0, :, part + cut : part + cut + 128]
        value = qkv_ref[0, :, 2 * part + cut : 2 * part + cut + 128]
        grad_out = grad_mixed_ref[0, :, cut : cut + 128]
        product = grad_out.astype(F32).T * mixed_t_ref[cut : cut + 128, :].astype(F32)
        key_t = key.T
        grad_query, grad_key, grad_value = [], 0.0, 0.0
        for head in range(2):
            keep = (lane >= 64) == (head == 1)
            query_one = jnp.where(keep, query, jnp.zeros_like(query))
            grad_one = jnp.where(keep, grad_out, jnp.zeros_like(grad_out))
            inner = slice(64 * head, 64 * head + 64)
            delta = jnp.sum(product[inner], axis=0, keepdims=True)
            scores = jnp.where(key_ok, dot_nt(key, query_one), -1e30)
            prob = jnp.exp(scores - lse_ref[0, 2 * pair + head])
            grad_prob = dot_nt(value, grad_one)
            grad_scores = (prob * (grad_prob - delta)).astype(BF16)
            grad_value = grad_value + dot_nn(prob.astype(BF16), grad_one)
            grad_key = grad_key + dot_nn(grad_scores, query_one)
            grad_query.append(dot_nn(key_t[inner], grad_scores) * 0.125)
        grads = (jnp.concatenate(grad_query, axis=0).T, grad_key, grad_value)
        for kind, grad in enumerate(grads):
            grad = grad.astype(BF16)
            to = slice(kind * part + cut, kind * part + cut + 128)
            grad_scr[pl.ds(start, rows), to] = grad
            grad_qkv_ref[0, :, to] = grad
            grad_bias_ref[:, to] += column_sum(grad)

    @pl.when(seq == pl.num_programs(0) - 1)
    def _():
        store_blocks(meta, grad_w_ref, dot_nn(x_t_ref[...], grad_scr[...]), slice(None))


def attend_back(meta, x_t, qkv, mixed_t, grad_mixed, lse, *gates):
    seqs, length, wide = qkv.shape
    width, rows = x_t.shape
    part = wide // 3
    block_rows = width // (2 * BLOCKS)
    by_seq = lambda cols: pl.BlockSpec((1, length, cols), lambda s, m: (s, 0, 0))
    return pl.pallas_call(
        gated(attend_back_kernel, 5, len(gates)),
        grid_spec=pltpu.PrefetchScalarGridSpec(
            num_scalar_prefetch=1,
            grid=(seqs,),
            in_specs=[
                pl.BlockSpec((width, rows), lambda s, m: (0, 0), pipeline_mode=pl.Buffered(1)),
                by_seq(wide),
                pl.BlockSpec((part, length), lambda s, m: (0, s)),
                by_seq(part),
                pl.BlockSpec((1, HEADS // 2, 1, length), lambda s, m: (s, 0, 0, 0)),
                *gate_specs(gates),
            ],
            out_specs=[
                by_seq(wide),
                pl.BlockSpec((2, BLOCKS, block_rows, wide), lambda s, m: (0, 0, 0, 0)),
                pl.BlockSpec((1, wide), lambda s, m: (0, 0)),
            ],
            scratch_shapes=[pltpu.VMEM((rows, wide), BF16)],
        ),
        out_shape=[
            jax.ShapeDtypeStruct((seqs, length, wide), BF16),
            jax.ShapeDtypeStruct((2, BLOCKS, block_rows, wide), BF16),
            jax.ShapeDtypeStruct((1, wide), F32),
        ],
        compiler_params=params(1),
        cost_estimate=cost(16),
        name="attend_back",
    )(meta, x_t, qkv, mixed_t, grad_mixed, lse, *gates)


def input_kernel(
    meta, branch_ref, grad_mine, grad_other, w_mine, w_other, out_ref, scr_mine, scr_other
):
    @pl.when(pl.program_id(0) == 0)
    def _():
        place_rows(meta, w_mine, scr_mine, slice(None), slice(None))
        place_rows(meta, w_other, scr_other, slice(None), slice(None))

    total = branch_ref[...].astype(F32) + dot_nt(grad_mine[...], scr_mine[...])
    out_ref[...] = total + dot_nt(grad_other[...], scr_other[...])


def finish_kernel(moves, row_step, meta, *refs):
    parts, outs = refs[:2], refs[2:]
    for rel in range(4):
        part = parts[rel & 1].at[rel >> 1]
        x_at, core = meta[1] ^ (rel >> 1), meta[2] ^ (rel & 1)
        rows = part.shape[0]
        at = pl.ds(pl.multiple_of(x_at * rows + core * row_step, 16), rows)
        for columns, out, first, step in moves:
            size = columns.stop - columns.start
            to = pl.ds(pl.multiple_of(first + core * step, 128), size)
            outs[out][at, to] = part[:, columns].astype(F32)


def finish(meta, parts, moves, row_step, shapes):
    whole = lambda shape: pl.BlockSpec(shape, lambda i, m: (0,) * len(shape))
    return pl.pallas_call(
        functools.partial(finish_kernel, moves, row_step),
        grid_spec=pltpu.PrefetchScalarGridSpec(
            num_scalar_prefetch=1,
            grid=(1,),
            in_specs=[whole(p.shape) for p in parts],
            out_specs=[whole(shape) for shape in shapes],
        ),
        out_shape=[jax.ShapeDtypeStruct(shape, F32) for shape in shapes],
        compiler_params=params(1),
        cost_estimate=cost(2),
        name="finish",
    )(meta, *parts)


def together(*arrays):
    return lax.optimization_barrier(arrays)


CORE, X, Y, NEAR, FAR = 1, 2, 4, 8, 16
DEVICES = 32


def swap(array, mask):
    pairs = [(i, i ^ mask) for i in range(DEVICES)]
    return lax.ppermute(array, ("shard", "rep"), pairs)


def gather_z(piece):
    came = [swap(piece, mask) for mask in (FAR, NEAR, NEAR | FAR)]
    return jnp.stack([piece] + came)


def double(held, mask):
    return jnp.concatenate([held, swap(held, mask)], axis=0)


def plane_hops(held):
    return [swap(held, mask) for mask in (Y, X, X | Y)]


def plane_join(held, by_y, by_x, across):
    low = jnp.concatenate([held, by_y], axis=0)
    return jnp.stack([low, jnp.concatenate([by_x, across], axis=0)])


def gather_plane(held):
    return plane_join(held, *plane_hops(held))


def add(*terms):
    total = terms[0].astype(F32)
    for term in terms[1:]:
        total = total + term.astype(F32)
    return total.astype(BF16)


def sum_z(parts):
    return add(
        parts[0],
        *[swap(parts[i], mask) for i, mask in ((1, FAR), (2, NEAR), (3, NEAR | FAR))],
    )


def plane_sends(kept, came):
    cut = BLOCKS // 2
    pick = lambda a, x, y: a[x, cut:] if y else a[x, :cut]
    parts = [[add(pick(kept, x, y), pick(came, x, y)) for y in range(2)] for x in range(2)]
    return [
        parts[0][0],
        swap(parts[0][1], Y),
        swap(parts[1][0], X),
        swap(parts[1][1], X | Y),
    ]


def plane_sum(terms):
    return [add(*[t[i] for t in terms]) for i in range(4)]


def local(
    fast,
    tokens,
    lengths,
    w_qkv,
    b_query,
    b_value,
    w_out,
    b_out,
    ln1_gain,
    ln1_bias,
    w_up,
    b_up,
    w_down,
    b_down,
    ln2_gain,
    ln2_bias,
    cotangent,
):
    seqs, seq_len, width = tokens.shape
    rows = seqs * seq_len
    hidden_width = w_up.shape[1]
    half = width // 2
    groups = GROUPS
    up_cut, out_cut = hidden_width // (2 * groups), half // groups
    vectors = (b_query, b_value, b_out, ln1_gain, ln1_bias, b_down, ln2_gain, ln2_bias, b_up)

    if fast:
        shard, rep = lax.axis_index("shard"), lax.axis_index("rep")
        x_at, core = rep // 2, rep % 2
    else:
        shard = rep = x_at = core = jnp.int32(0)
    block = width // BLOCKS
    quarter = block // 2
    meta = jnp.concatenate(
        [jnp.stack([shard, x_at, core]).astype(jnp.int32), lengths.astype(jnp.int32)]
    )

    def qkv_parts(w):
        return w.reshape(-1, 2, quarter, 3, 2, half)

    def up_parts(up, out):
        up = up.reshape(-1, 2, quarter, 2, groups, up_cut)
        out = out.reshape(-1, 2, quarter, 2, groups, out_cut)
        return jnp.concatenate([up, out], axis=-1)

    if fast:
        qkv_piece, up_piece, down_piece = pack(meta, w_qkv, w_up, w_out, w_down, vectors)
        qkv_z, up_piece, down_piece = together(gather_z(qkv_piece), up_piece, down_piece)
        table = qkv_z[:, quarter:, : 128 + b_up.shape[0]]
        up_z = double(double(up_piece[None], FAR), NEAR)
        down_z = double(down_piece[None], FAR)
        qkv_mine, up_z, down_z, table = together(
            gather_plane(qkv_z[:, :quarter]), up_z, down_z, table
        )
        vec, b_up_row, *bias = small_call(
            functools.partial(unpack_kernel, block),
            "unpack",
            meta,
            (table, swap(table, Y)),
            ((8, width), (1, hidden_width), (1, 3 * half), (1, 3 * half)),
            ((16, width),),
        )
        qkv_w = qkv_mine, swap(qkv_mine, CORE)
        up_hops, down_z = plane_hops(up_z), double(down_z, NEAR)
    else:
        everything = lambda a: lax.all_gather(a, "shard", axis=0, tiled=True)
        full = [everything(v) for v in vectors]
        order = [turned(p) for p in range(BLOCKS)]
        both = lambda a: (a[0][:, order], a[1][:, order])
        qkv_w = both(
            qkv_parts(everything(w_qkv))
            .transpose(4, 1, 0, 2, 3, 5)
            .reshape(2, 2, BLOCKS, quarter, 3 * half)
        )
        up_w = both(
            up_parts(everything(w_up), everything(w_out))
            .transpose(3, 1, 0, 2, 4, 5)
            .reshape(2, 2, BLOCKS, quarter, -1)
        )
        down_w = both(
            everything(w_down).reshape(BLOCKS, 2, 2, -1, width).transpose(1, 2, 0, 3, 4)
        )
        full = [v.astype(F32) for v in full]
        bias = jnp.stack(
            [full[0].reshape(2, half), jnp.zeros((2, half), F32), full[1].reshape(2, half)], axis=1
        ).reshape(2, 1, 3 * half)
        vec = jnp.stack(full[2:8] + [jnp.zeros_like(full[0])] * 2)
        b_up_row = full[8].reshape(1, -1)
    x_rows = tokens.reshape(rows, width)
    heads = [list(attend(meta, tokens, qkv_w[i], bias[i])) for i in range(2)]
    if fast:
        x_late, heads[0][0] = together(x_rows, heads[0][0])
        x_t = x_late.T
    else:
        x_t = x_rows.T
    if fast:
        *up_hops, down_z, heads[1][0], heads[1][1] = together(
            *up_hops, down_z, heads[1][0], heads[1][1]
        )
        up_mine = plane_join(up_z, *up_hops)
        up_w = up_mine, swap(up_mine, CORE)
    qkv, mixed, mixed_t, lse = zip(*heads)
    mixed_rows = [m.reshape(rows, half) for m in mixed]
    up_shape, out_shape, down_shape = (width, hidden_width), (width, width), (hidden_width, width)
    hat, scale, norm_t, active, active_t, slope, up_full, out_full = by_chunk(
        up_kernel,
        "feed_up",
        26,
        meta,
        (b_up_row,),
        (x_rows, *mixed_rows, *up_w, vec),
        (),
        (
            ("whole", (rows, width), F32),
            ("whole", (rows, 128), F32),
            ("whole", (width, rows), BF16),
            ("cols", (rows, hidden_width), BF16),
            ("rows", (hidden_width, rows), BF16),
            ("cols", (rows, hidden_width), BF16),
            ("whole", up_shape, BF16),
            ("whole", out_shape, BF16),
        ),
        (((rows, width), BF16),),
    )
    row, fixed = "row", "sum"
    if fast:
        active, x_t, *hops = together(active, x_t, *plane_hops(down_z))
        down_mine = plane_join(down_z, *hops)
        down_w = down_mine, swap(down_mine, CORE)
    layer_out, grad_second, vec_two, down_full = by_tile(
        functools.partial(down_kernel, seq_len),
        "feed_down",
        14,
        meta,
        (hat, active, cotangent.reshape(rows, width)),
        (*down_w, vec),
        (),
        (
            (row, width, BF16),
            (row, width, BF16),
            (fixed, (8, width), F32),
            (fixed, down_shape, BF16),
        ),
        (),
    )
    down_send = grad_down(1, meta, active_t, grad_second)
    down_keep = grad_down(0, meta, active_t, grad_second, down_send)
    gates = (down_keep,)
    if fast:
        down_plane = plane_sends(down_keep, swap(down_send, CORE))
        gates = (down_plane[0],)
    grad_hidden, grad_branch, *grad_mixed, vec_one, grad_b_up = by_chunk(
        rest_kernel,
        "feed_back",
        22,
        meta,
        (up_full, slope),
        (grad_second, hat, scale, out_full, vec),
        gates,
        (
            ("cols", (rows, hidden_width), BF16),
            ("whole", (rows, width), BF16),
            ("whole", (rows, half), BF16),
            ("whole", (rows, half), BF16),
            ("whole", (8, width), F32),
            ("cols", (1, hidden_width), F32),
        ),
        (((rows, width), F32),),
        (down_full,),
    )
    gates = ()
    if fast:
        down_parts = plane_sum(down_plane)
        gates = tuple(down_parts)
    up_send = grad_up(1, meta, norm_t, mixed_t, grad_hidden, grad_branch, *gates)
    if fast:
        up_send, *down_parts = together(up_send, *down_parts)
    up_keep = grad_up(0, meta, norm_t, mixed_t, grad_hidden, grad_branch, up_send)
    gates = (up_keep,)
    if fast:
        up_plane = plane_sends(up_keep, swap(up_send, CORE))
        down_piece = sum_z(down_parts)
        gates = (up_plane[0],)
    grad_mixed = [g.reshape(seqs, seq_len, half) for g in grad_mixed]

    def back(i, *gates):
        return attend_back(meta, x_t, qkv[i], mixed_t[i], grad_mixed[i], lse[i], *gates)

    other_qkv, qkv_send, other_bias = back(1, *gates)
    gates = (qkv_send,)
    if fast:
        down_piece, qkv_send = together(down_piece, qkv_send)
        gates = (qkv_send, up_plane[1], up_plane[2])
    mine_qkv, qkv_keep, mine_bias = back(0, *gates)
    gates = (qkv_keep,)
    if fast:
        qkv_plane = plane_sends(qkv_keep, swap(qkv_send, CORE))
        down_piece, qkv_plane[0], *up_plane = together(down_piece, qkv_plane[0], *up_plane)
        down_both = jnp.stack([down_piece, swap(down_piece, X)])
        up_parts_sum = plane_sum(up_plane)
        up_near = swap(jnp.stack(up_parts_sum[2:]), NEAR)
        down_quarters = down_both, swap(down_both, CORE)
        gates = (qkv_plane[0], up_parts_sum[0])
    (input_grad,) = by_tile(
        input_kernel,
        "input_grad",
        10,
        meta,
        (grad_branch, mine_qkv.reshape(rows, -1), other_qkv.reshape(rows, -1)),
        qkv_w,
        gates,
        ((row, width, F32),),
        ((width, 3 * half), (width, 3 * half)),
    )

    (total,) = small_call(
        sums_kernel,
        "sums",
        meta,
        (vec_one, vec_two, grad_b_up, mine_bias, other_bias),
        ((16, width),),
    )
    if fast:
        came, input_grad, up_near, *qkv_plane[1:3] = together(
            swap(total, CORE), input_grad, up_near, *qkv_plane[1:3]
        )
        total = total + came
        up_low = [add(up_parts_sum[i], up_near[i]) for i in range(2)]
        came, up_far, qkv_plane[3] = together(
            swap(total, X), swap(up_low[1], FAR), qkv_plane[3]
        )
        total = total + came
        up_piece = add(up_low[0], up_far)
        qkv_parts_sum = plane_sum(qkv_plane)
        qkv_hops = [swap(qkv_parts_sum[i], m) for i, m in ((1, FAR), (2, NEAR), (3, NEAR | FAR))]
        came, up_x, *qkv_hops = together(swap(total, Y), swap(up_piece, X), *qkv_hops)
        total = total + came
        up_both = jnp.stack([up_piece, up_x])
        qkv_piece = add(qkv_parts_sum[0], *qkv_hops)
        came, up_core, qkv_x = together(
            swap(total, NEAR), swap(up_both, CORE), swap(qkv_piece, X)
        )
        total = total + came
        total = total + swap(total, FAR)
        up_quarters = up_both, up_core
        qkv_both = jnp.stack([qkv_piece, qkv_x])
        qkv_quarters = qkv_both, swap(qkv_both, CORE)
        own, own_b_up = small_call(
            functools.partial(own_sums_kernel, block),
            "own_sums",
            meta,
            (total,),
            ((8, 128), (1, b_up.shape[0])),
        )
        sums = [own[i, :block] for i in range(8)] + [own_b_up[0]]
        step = up_cut + out_cut
        up_moves = [
            move
            for g in range(groups)
            for move in (
                (slice(g * step, g * step + up_cut), 0, g * up_cut, hidden_width // 2),
                (slice(g * step + up_cut, (g + 1) * step), 1, g * out_cut, half),
            )
        ]
        qkv_moves = [(slice(k * half, (k + 1) * half), 0, k * width, half) for k in range(3)]
        (grad_w_down,) = finish(
            meta,
            down_quarters,
            [(slice(0, width), 0, 0, 0)],
            w_down.shape[0] // 2,
            [w_down.shape],
        )
        grad_w_up, grad_w_out = finish(meta, up_quarters, up_moves, 0, [w_up.shape, w_out.shape])
        (grad_w_qkv,) = finish(meta, qkv_quarters, qkv_moves, 0, [w_qkv.shape])
    else:
        total_of = lambda a: lax.psum(
            lax.psum_scatter(a, "shard", scatter_dimension=0, tiled=True), "rep"
        )
        sums = [total_of(g) for g in (*total[:8], total[8:12].reshape(-1))]
        order = [turned(p) for p in range(BLOCKS)]
        down_keep, down_send, up_keep, up_send = (
            a[:, order] for a in (down_keep, down_send, up_keep, up_send)
        )
        down = jnp.stack([down_keep, down_send]).transpose(2, 0, 1, 3, 4)
        grad_w_down = total_of(down.reshape(hidden_width, width).astype(F32))
        up = jnp.stack([up_keep, up_send]).reshape(
            2, 2, BLOCKS, quarter, groups, up_cut + out_cut
        )
        up = up.transpose(2, 1, 3, 0, 4, 5)
        grad_w_up = total_of(up[..., :up_cut].reshape(width, hidden_width).astype(F32))
        grad_w_out = total_of(up[..., up_cut:].reshape(width, width).astype(F32))
        qkv_sum = jnp.stack([qkv_keep[:, order], qkv_send[:, order]])
        qkv_sum = qkv_sum.reshape(2, 2, BLOCKS, quarter, 3, half)
        qkv_sum = qkv_sum.transpose(2, 1, 3, 4, 0, 5).reshape(width, 3 * width)
        grad_w_qkv = total_of(qkv_sum.astype(F32))
    return (
        layer_out.reshape(seqs, seq_len, width),
        input_grad.reshape(seqs, seq_len, width),
        grad_w_qkv,
        sums[0],
        sums[1],
        grad_w_out,
        sums[2],
        sums[3],
        sums[4],
        grad_w_up,
        sums[8],
        grad_w_down,
        sums[5],
        sums[6],
        sums[7],
    )


def solution(mesh):
    fast = mesh.shape["shard"] == BLOCKS and mesh.shape["rep"] == 4
    by_seq = P(("shard", "rep"), None, None)
    one, two = P("shard"), P("shard", None)
    in_specs = (by_seq, P(("shard", "rep")), two, one, one, two, one, one, one)
    in_specs = in_specs + (two, one, two, one, one, one, by_seq)
    out_specs = (by_seq, by_seq, two, one, one, two, one, one, one, two, one, two, one, one, one)
    return jax.shard_map(
        functools.partial(local, fast),
        mesh=mesh,
        in_specs=in_specs,
        out_specs=out_specs,
        check_vma=False,
    )
```

```python
import functools

import jax
import jax.numpy as jnp
from jax import lax
from jax.experimental import pallas as pl
from jax.experimental.pallas import tpu as pltpu
from jax.sharding import PartitionSpec as P

HEADS = 12
EPS = 1e-05
F32 = jnp.float32
BF16 = jnp.bfloat16
BLOCKS = 8
GROUPS = 3
VMEM_LIMIT = 58 * 1024 * 1024


def dot_nn(a, b):
    return lax.dot_general(a, b, (((1,), (0,)), ((), ())), preferred_element_type=F32)


def dot_nt(a, b):
    return lax.dot_general(a, b, (((1,), (1,)), ((), ())), preferred_element_type=F32)


def dot_tn(a, b):
    return lax.dot_general(a, b, (((0,), (0,)), ((), ())), preferred_element_type=F32)


def params(grid_dims):
    return pltpu.CompilerParams(
        dimension_semantics=("arbitrary",) * grid_dims, vmem_limit_bytes=VMEM_LIMIT
    )


def cost(micros):
    return pl.CostEstimate(flops=int(micros * 1.15e9), bytes_accessed=1 << 20, transcendentals=0)


def gated(kernel, inputs, gates):
    def body(*refs):
        kernel(*refs[: inputs + 1], *refs[inputs + 1 + gates :])

    return body


def gate_specs(gates):
    return [pl.BlockSpec(memory_space=pl.ANY)] * len(gates)


def turned(place):
    return ((place & 1) << 2) | (place & 2) | ((place >> 2) & 1)


def place_rows(meta, source, target, columns, cut):
    rows = source.shape[2]
    for half in range(2):
        for block in range(BLOCKS):
            start = (meta[0] ^ turned(block)) * (2 * rows) + (meta[1] ^ half) * rows
            target[pl.ds(pl.multiple_of(start, 16), rows), cut] = source[half, block, :, columns]


def pack_kernel(groups, *refs):
    meta, w_qkv, w_up, w_out, w_down, *vectors, qkv_ref, up_ref, down_ref = refs
    rows, wide = up_ref.shape[0], qkv_ref.shape[1]
    half = wide // 3
    up_cut, out_cut = w_up.shape[1] // (2 * groups), w_out.shape[1] // (2 * groups)
    at = pl.ds(pl.multiple_of(meta[1] * rows, 16), rows)

    def columns(start, size):
        return pl.ds(pl.multiple_of(start, 128), size)

    for kind in range(3):
        start = (2 * kind + meta[2]) * half
        qkv_ref[:rows, kind * half : (kind + 1) * half] = w_qkv[at, columns(start, half)]
    for group in range(groups):
        base = group * (up_cut + out_cut)
        start = (meta[2] * groups + group) * up_cut
        up_ref[:, base : base + up_cut] = w_up[at, columns(start, up_cut)]
        start = (meta[2] * groups + group) * out_cut
        up_ref[:, base + up_cut : base + up_cut + out_cut] = w_out[at, columns(start, out_cut)]
    rows_down = down_ref.shape[0]
    start = (2 * meta[2] + meta[1]) * rows_down
    down_ref[...] = w_down[pl.ds(pl.multiple_of(start, 16), rows_down), :]
    *short, long = vectors
    extra = qkv_ref.shape[0] - rows
    small = short[0].shape[0]
    place = lax.broadcasted_iota(jnp.int32, (extra, small), 0)
    table = jnp.zeros((extra, small), F32)
    for i, v in enumerate(short):
        table = jnp.where(place == i, v[...].astype(F32).reshape(1, small), table)
    qkv_ref[rows:, :] = jnp.zeros((extra, wide), BF16)
    qkv_ref[rows:, :small] = table.astype(BF16)
    size = long.shape[0]
    wide_row = jnp.broadcast_to(long[...].astype(F32).reshape(1, size), (extra, size))
    qkv_ref[rows:, 128 : 128 + size] = wide_row.astype(BF16)


def pack(meta, w_qkv, w_up, w_out, w_down, vectors):
    rows = w_up.shape[0] // 2
    whole = lambda a: pl.BlockSpec(a.shape, lambda i, m: (0,) * a.ndim)
    shapes = [
        (rows + 16, w_qkv.shape[1] // 2),
        (rows, (w_up.shape[1] + w_out.shape[1]) // 2),
        (w_down.shape[0] // 4, w_down.shape[1]),
    ]
    outs = [jax.ShapeDtypeStruct(shape, BF16) for shape in shapes]
    operands = (w_qkv, w_up, w_out, w_down, *vectors)
    return pl.pallas_call(
        functools.partial(pack_kernel, GROUPS),
        grid_spec=pltpu.PrefetchScalarGridSpec(
            num_scalar_prefetch=1,
            grid=(1,),
            in_specs=[whole(a) for a in operands],
            out_specs=[whole(o) for o in outs],
        ),
        out_shape=outs,
        compiler_params=params(1),
        cost_estimate=cost(2),
        name="pack",
    )(meta, *operands)


def shard_columns(shard, block, width, lanes):
    lane = lax.broadcasted_iota(jnp.int32, (lanes, width), 0)
    column = lax.broadcasted_iota(jnp.int32, (lanes, width), 1)
    return (lane < block) & (column == lane + shard * block)


def unpack_kernel(block, meta, near_ref, far_ref, vec_ref, b_up_ref, mine_ref, other_ref, scr):
    width = vec_ref.shape[1]
    half, size = width // 2, b_up_ref.shape[1] // BLOCKS
    total = jnp.zeros(scr.shape, F32)
    for place in range(BLOCKS):
        source = (near_ref, far_ref)[place // 4]
        rows = source[place % 4]
        shard = meta[0] ^ turned(place)
        spread = shard_columns(shard, block, width, 128).astype(F32).astype(BF16)
        total = total + dot_nn(rows[:, :128], spread)
        to = pl.ds(pl.multiple_of(shard * size, 128), size)
        b_up_ref[:, to] = rows[:1, 128 : 128 + size].astype(F32)
    scr[...] = total
    vec_ref[...] = jnp.zeros_like(vec_ref)
    vec_ref[0:6, :] = total[2:8]
    for rel, out in enumerate((mine_ref, other_ref)):
        cut = pl.ds(pl.multiple_of((meta[2] ^ rel) * half, 128), half)
        out[...] = jnp.zeros_like(out)
        out[:, :half] = scr[0:1, cut]
        out[:, 2 * half :] = scr[1:2, cut]


def small_call(kernel, name, meta, operands, shapes, scratch=(), gates=()):
    whole = lambda a: pl.BlockSpec(a.shape, lambda i, m: (0,) * len(a.shape))
    outs = [jax.ShapeDtypeStruct(shape, F32) for shape in shapes]
    return pl.pallas_call(
        gated(kernel, len(operands), len(gates)),
        grid_spec=pltpu.PrefetchScalarGridSpec(
            num_scalar_prefetch=1,
            grid=(1,),
            in_specs=[whole(a) for a in operands] + gate_specs(gates),
            out_specs=[whole(o) for o in outs],
            scratch_shapes=[pltpu.VMEM(shape, F32) for shape in scratch],
        ),
        out_shape=outs,
        compiler_params=params(1),
        cost_estimate=cost(2),
        name=name,
    )(meta, *operands, *gates)


def sums_kernel(meta, vec_one, vec_two, b_up, bias_mine, bias_other, out_ref):
    width = out_ref.shape[1]
    half = width // 2
    out_ref[...] = jnp.zeros_like(out_ref)
    for rel, source in enumerate((bias_mine, bias_other)):
        to = pl.ds(pl.multiple_of((meta[2] ^ rel) * half, 128), half)
        out_ref[0:1, to] = source[:, :half]
        out_ref[1:2, to] = source[:, 2 * half :]
    out_ref[2:5, :] = vec_one[0:3, :]
    out_ref[5:8, :] = vec_two[0:3, :]
    for i in range(b_up.shape[1] // width):
        out_ref[8 + i : 9 + i, :] = b_up[:, i * width : (i + 1) * width]


def own_sums_kernel(block, meta, sum_ref, *outs):
    *short, b_up_ref = outs
    width, size = sum_ref.shape[1], b_up_ref.shape[0]
    pick = shard_columns(meta[0], block, width, 128).astype(F32)
    own = lax.dot_general(
        sum_ref[0:8, :],
        pick,
        (((1,), (1,)), ((), ())),
        precision=lax.Precision.HIGHEST,
        preferred_element_type=F32,
    )
    each = width // size
    cut = pl.ds(pl.multiple_of(lax.rem(meta[0], each) * size, 128), size)
    b_up_ref[...] = sum_ref[pl.ds(8 + lax.div(meta[0], each), 1), cut].reshape(size)
    for i, out in enumerate(short):
        out[...] = own[i : i + 1, :block].reshape(block)


def attend_kernel(meta, x_ref, w_ref, bias_ref, qkv_ref, mixed_ref, mixed_t_ref, lse_ref, w_scr):
    seq = pl.program_id(0)
    wide = w_scr.shape[1]
    part = wide // 3

    @pl.when(seq == 0)
    def _():
        place_rows(meta, w_ref, w_scr, slice(None), slice(None))

    length = meta[3 + seq]
    qkv = (dot_nn(x_ref[0], w_scr[...]) + bias_ref[...]).astype(BF16)
    qkv_ref[0] = qkv
    rows = qkv.shape[0]
    lane = lax.broadcasted_iota(jnp.int32, (rows, 128), 1)
    key_ok = lax.broadcasted_iota(jnp.int32, (rows, rows), 0) < length
    for pair in range(part // 128):
        cut = pair * 128
        query = qkv[:, cut : cut + 128] * jnp.asarray(0.125, BF16)
        key = qkv[:, part + cut : part + cut + 128]
        value_t = qkv[:, 2 * part + cut : 2 * part + cut + 128].T
        outs = []
        for head in range(2):
            query_one = jnp.where((lane >= 64) == (head == 1), query, jnp.zeros_like(query))
            scores = jnp.where(key_ok, dot_nt(key, query_one), -1e30)
            top = jnp.max(scores, axis=0, keepdims=True)
            exp_scores = jnp.exp(scores - top)
            total = jnp.sum(exp_scores, axis=0, keepdims=True)
            lse_ref[0, 2 * pair + head] = top + jnp.log(total)
            out = dot_nn(value_t[64 * head : 64 * head + 64], exp_scores.astype(BF16))
            outs.append(out * (1.0 / total))
        mixed_t = jnp.concatenate(outs, axis=0)
        mixed_t_ref[cut : cut + 128, :] = mixed_t.astype(BF16)
        mixed_ref[0, :, cut : cut + 128] = mixed_t.T.astype(BF16)


def attend(meta, x, weight, bias):
    seqs, length, width = x.shape
    wide = weight.shape[3]
    part = wide // 3
    half_heads = HEADS // 2
    whole = lambda s, m: (0, 0, 0, 0)
    return pl.pallas_call(
        attend_kernel,
        grid_spec=pltpu.PrefetchScalarGridSpec(
            num_scalar_prefetch=1,
            grid=(seqs,),
            in_specs=[
                pl.BlockSpec((1, length, width), lambda s, m: (s, 0, 0)),
                pl.BlockSpec(weight.shape, whole, pipeline_mode=pl.Buffered(1)),
                pl.BlockSpec((1, wide), lambda s, m: (0, 0)),
            ],
            out_specs=[
                pl.BlockSpec((1, length, wide), lambda s, m: (s, 0, 0)),
                pl.BlockSpec((1, length, part), lambda s, m: (s, 0, 0)),
                pl.BlockSpec((part, length), lambda s, m: (0, s)),
                pl.BlockSpec((1, half_heads, 1, length), lambda s, m: (s, 0, 0, 0)),
            ],
            scratch_shapes=[pltpu.VMEM((width, wide), BF16)],
        ),
        out_shape=[
            jax.ShapeDtypeStruct((seqs, length, wide), BF16),
            jax.ShapeDtypeStruct((seqs, length, part), BF16),
            jax.ShapeDtypeStruct((part, seqs * length), BF16),
            jax.ShapeDtypeStruct((seqs, half_heads, 1, length), F32),
        ],
        compiler_params=params(1),
        cost_estimate=cost(11),
        name="attend_forward",
    )(meta, x, weight, bias)


def gelu_and_slope(hidden):
    size = jnp.abs(hidden)
    bell = jnp.exp2(hidden * hidden * -0.7213475204444817)
    t = 1.0 / (1.0 + (0.3275911 * 0.7071067811865476) * size)
    poly = t * (
        0.5 * 0.254829592
        + t
        * (
            0.5 * -0.284496736
            + t * (0.5 * 1.421413741 + t * (0.5 * -1.453152027 + t * (0.5 * 1.061405429)))
        )
    )
    tail = poly * bell
    phi = jnp.where(hidden < 0.0, tail, 1.0 - tail)
    return hidden * phi, phi + hidden * bell * 0.3989422804014327


def norm_forward(hidden):
    center = hidden - jnp.mean(hidden, axis=-1, keepdims=True)
    scale = lax.rsqrt(jnp.mean(center * center, axis=-1, keepdims=True) + EPS)
    return center * scale, scale


def norm_back(grad, hat, scale, gain):
    grad_hat = grad * gain
    shift = jnp.mean(grad_hat, axis=-1, keepdims=True)
    along = jnp.mean(grad_hat * hat, axis=-1, keepdims=True)
    return scale * (grad_hat - shift - hat * along)


def column_sum(rows):
    return jnp.sum(rows.astype(F32), axis=0, keepdims=True)


def place_up(meta, mine, other, w_up, w_out):
    hidden_width, width = w_up.shape[1], w_out.shape[1]
    up_cut, out_cut = hidden_width // (2 * GROUPS), width // (2 * GROUPS)
    for rel, source in enumerate((mine, other)):
        core = meta[2] ^ rel
        for group in range(GROUPS):
            base = group * (up_cut + out_cut)
            up_to = pl.multiple_of(core * (hidden_width // 2) + group * up_cut, 128)
            out_to = pl.multiple_of(core * (width // 2) + group * out_cut, 128)
            place_rows(meta, source, w_up, slice(base, base + up_cut), pl.ds(up_to, up_cut))
            place_rows(
                meta,
                source,
                w_out,
                slice(base + up_cut, base + up_cut + out_cut),
                pl.ds(out_to, out_cut),
            )


def place_down(meta, mine, other, w_down):
    rows = mine.shape[2]
    for rel, source in enumerate((mine, other)):
        for half in range(2):
            for block in range(BLOCKS):
                start = (
                    (meta[0] ^ turned(block)) * (4 * rows)
                    + (meta[2] ^ rel) * (2 * rows)
                    + (meta[1] ^ half) * rows
                )
                w_down[pl.ds(pl.multiple_of(start, 16), rows), :] = source[half, block]


def halves_of(meta, width):
    half = width // 2
    return (
        pl.ds(pl.multiple_of(meta[2] * half, 128), half),
        pl.ds(pl.multiple_of((1 - meta[2]) * half, 128), half),
    )


CHUNK = 512


def up_kernel(
    meta,
    x_ref,
    mixed_mine,
    mixed_other,
    up_mine,
    up_other,
    vec_ref,
    b_up_ref,
    hat_ref,
    scale_ref,
    norm_t_ref,
    active_ref,
    active_t_ref,
    slope_ref,
    w_up,
    w_out,
    normed_low,
):
    step = pl.program_id(0)
    width = w_out.shape[1]

    @pl.when(step == 0)
    def _():
        place_up(meta, up_mine, up_other, w_up, w_out)
        b_out, gain, shift = [vec_ref[i : i + 1, :] for i in range(3)]
        rows_mine, rows_other = halves_of(meta, width)
        branch = dot_nn(mixed_mine[...], w_out[rows_mine, :])
        branch = branch + dot_nn(mixed_other[...], w_out[rows_other, :])
        hat, scale = norm_forward(x_ref[...].astype(F32) + (branch + b_out))
        hat_ref[...] = hat
        scale_ref[...] = jnp.broadcast_to(scale, scale_ref.shape)
        normed_low[...] = (hat * gain + shift).astype(BF16)
        norm_t_ref[...] = normed_low[...].T

    cut = pl.ds(pl.multiple_of(step * CHUNK, CHUNK), CHUNK)
    hidden = dot_nn(normed_low[...], w_up[:, cut]) + b_up_ref[...]
    active, slope = gelu_and_slope(hidden)
    slope_ref[...] = slope.astype(BF16)
    active_low = active.astype(BF16)
    active_ref[...] = active_low
    active_t_ref[...] = active_low.T


def down_kernel(
    seq_len,
    meta,
    hat_ref,
    active_ref,
    cot_ref,
    down_mine,
    down_other,
    vec_ref,
    out_ref,
    grad_second_ref,
    grad_vec_ref,
    w_down,
):
    step = pl.program_id(0)
    tile = hat_ref.shape[0]

    @pl.when(step == 0)
    def _():
        grad_vec_ref[...] = jnp.zeros_like(grad_vec_ref)
        place_down(meta, down_mine, down_other, w_down)

    gain_one, shift_one, b_down, gain, shift = [vec_ref[i : i + 1, :] for i in range(1, 6)]
    seq = lax.div(step * tile, seq_len)
    place = lax.broadcasted_iota(jnp.int32, (tile, 1), 0) + lax.rem(step * tile, seq_len)
    valid = place < meta[3 + seq]
    second = dot_nn(active_ref[...], w_down[...])
    normed = hat_ref[...] * gain_one + shift_one
    hat, scale = norm_forward(normed + (second + b_down))
    out_ref[...] = jnp.where(valid, hat * gain + shift, 0.0).astype(BF16)
    grad_result = jnp.where(valid, cot_ref[...].astype(F32), 0.0)
    grad_second = norm_back(grad_result, hat, scale, gain).astype(BF16)
    grad_second_ref[...] = grad_second
    sums = column_sum(grad_second), column_sum(grad_result * hat), column_sum(grad_result)
    for i, total in enumerate(sums):
        grad_vec_ref[i : i + 1, :] += total


def rest_kernel(
    meta,
    grad_second_ref,
    hat_ref,
    scale_ref,
    w_out,
    vec_ref,
    w_down,
    w_up,
    slope_ref,
    grad_hidden_ref,
    grad_branch_ref,
    grad_mixed_mine,
    grad_mixed_other,
    grad_vec_ref,
    grad_b_up_ref,
    total,
):
    step = pl.program_id(0)
    width = w_out.shape[1]

    @pl.when(step == 0)
    def _():
        total[...] = grad_second_ref[...].astype(F32)

    grad_active = dot_nt(grad_second_ref[...], w_down[...])
    grad_hidden = (slope_ref[...].astype(F32) * grad_active).astype(BF16)
    grad_hidden_ref[...] = grad_hidden
    grad_b_up_ref[...] = column_sum(grad_hidden)
    total[...] += dot_nt(grad_hidden, w_up[...])

    @pl.when(step == pl.num_programs(0) - 1)
    def _():
        grad_normed, hat, gain = total[...], hat_ref[...], vec_ref[1:2, :]
        grad_branch = norm_back(grad_normed, hat, scale_ref[:, 0:1], gain).astype(BF16)
        grad_branch_ref[...] = grad_branch
        rows_mine, rows_other = halves_of(meta, width)
        grad_mixed_mine[...] = dot_nt(grad_branch, w_out[rows_mine, :]).astype(BF16)
        grad_mixed_other[...] = dot_nt(grad_branch, w_out[rows_other, :]).astype(BF16)
        grad_vec_ref[...] = jnp.zeros_like(grad_vec_ref)
        sums = column_sum(grad_branch), column_sum(grad_normed * hat), column_sum(grad_normed)
        for i, one in enumerate(sums):
            grad_vec_ref[i : i + 1, :] = one


def by_chunk(kernel, name, micros, meta, cut, wholes, gates, outs, scratch, cut_rows=()):
    hidden_width = cut[-1].shape[1]
    chunked = lambda shape: pl.BlockSpec((shape[0], CHUNK), lambda n, m: (0, n))
    whole = lambda shape: pl.BlockSpec(
        shape, lambda n, m: (0,) * len(shape), pipeline_mode=pl.Buffered(1)
    )
    spec_of = {
        "cols": chunked,
        "rows": lambda shape: pl.BlockSpec((CHUNK, shape[1]), lambda n, m: (n, 0)),
        "whole": lambda shape: pl.BlockSpec(shape, lambda n, m: (0,) * len(shape)),
    }
    return pl.pallas_call(
        gated(kernel, len(cut) + len(cut_rows) + len(wholes), len(gates)),
        grid_spec=pltpu.PrefetchScalarGridSpec(
            num_scalar_prefetch=1,
            grid=(hidden_width // CHUNK,),
            in_specs=[whole(a.shape) for a in wholes]
            + [spec_of["rows"](a.shape) for a in cut_rows]
            + [chunked(a.shape) for a in cut]
            + gate_specs(gates),
            out_specs=[spec_of[kind](shape) for kind, shape, _ in outs],
            scratch_shapes=[pltpu.VMEM(shape, dtype) for shape, dtype in scratch],
        ),
        out_shape=[jax.ShapeDtypeStruct(shape, dtype) for _, shape, dtype in outs],
        compiler_params=params(1),
        cost_estimate=cost(micros),
        name=name,
    )(meta, *wholes, *cut_rows, *cut, *gates)


def by_tile(kernel, name, micros, meta, tiled, wholes, gates, outs, scratch, most=512):
    rows = tiled[0].shape[0]
    tile = min(most, rows)
    by_row = lambda cols: pl.BlockSpec((tile, cols), lambda i, m: (i, 0))
    whole = lambda a: pl.BlockSpec(
        a.shape, lambda i, m: (0,) * a.ndim, pipeline_mode=pl.Buffered(1)
    )
    specs, shapes = [], []
    for kind, size, dtype in outs:
        if kind == "row":
            specs.append(by_row(size))
            shapes.append(jax.ShapeDtypeStruct((rows, size), dtype))
        elif kind == "col":
            specs.append(pl.BlockSpec((size, tile), lambda i, m: (0, i)))
            shapes.append(jax.ShapeDtypeStruct((size, rows), dtype))
        else:
            specs.append(pl.BlockSpec(size, lambda i, m: (0, 0)))
            shapes.append(jax.ShapeDtypeStruct(size, dtype))
    return pl.pallas_call(
        gated(kernel, len(tiled) + len(wholes), len(gates)),
        grid_spec=pltpu.PrefetchScalarGridSpec(
            num_scalar_prefetch=1,
            grid=(rows // tile,),
            in_specs=[by_row(a.shape[1]) for a in tiled]
            + [whole(a) for a in wholes]
            + gate_specs(gates),
            out_specs=specs,
            scratch_shapes=[pltpu.VMEM(shape, BF16) for shape in scratch],
        ),
        out_shape=shapes,
        compiler_params=params(1),
        cost_estimate=cost(micros),
        name=name,
    )(meta, *tiled, *wholes, *gates)


def store_blocks(meta, out_ref, value, cut, first=0):
    rows = out_ref.shape[2]
    for block in range(value.shape[0] // (2 * rows)):
        for half in range(2):
            start = (2 * block + half) * rows
            out_ref[meta[1] ^ half, turned(meta[0] ^ (first + block)), :, cut] = value[
                start : start + rows
            ].astype(BF16)


def grad_up_kernel(
    meta, norm_t_ref, mixed_mine, mixed_other, grad_hidden_ref, grad_branch_ref, out_ref
):
    up_cut = grad_hidden_ref.shape[1]
    store_blocks(meta, out_ref, dot_nn(norm_t_ref[...], grad_hidden_ref[...]), slice(0, up_cut))
    cut = slice(up_cut, out_ref.shape[3])
    few = BLOCKS // 2
    grad_branch = grad_branch_ref[...]
    store_blocks(meta, out_ref, dot_nn(mixed_mine[...], grad_branch), cut, meta[2] * few)
    store_blocks(meta, out_ref, dot_nn(mixed_other[...], grad_branch), cut, (1 - meta[2]) * few)


def grad_up(rel, meta, norm_t, mixed_t, grad_hidden, grad_branch, *gates):
    width, rows = norm_t.shape
    hidden_width = grad_hidden.shape[1]
    groups = 3
    up_cut, out_cut = hidden_width // (2 * groups), width // (2 * groups)
    block_rows = width // (2 * BLOCKS)
    whole = lambda tall: pl.BlockSpec(
        (tall, rows), lambda n, m: (0, 0), pipeline_mode=pl.Buffered(1)
    )
    turn = lambda n, m: (0, (m[2] ^ rel) * groups + n)
    return pl.pallas_call(
        gated(grad_up_kernel, 5, len(gates)),
        grid_spec=pltpu.PrefetchScalarGridSpec(
            num_scalar_prefetch=1,
            grid=(groups,),
            in_specs=[
                whole(width),
                whole(width // 2),
                whole(width // 2),
                pl.BlockSpec((rows, up_cut), turn),
                pl.BlockSpec((rows, out_cut), turn),
                *gate_specs(gates),
            ],
            out_specs=pl.BlockSpec(
                (2, BLOCKS, block_rows, up_cut + out_cut), lambda n, m: (0, 0, 0, n)
            ),
        ),
        out_shape=jax.ShapeDtypeStruct(
            (2, BLOCKS, block_rows, groups * (up_cut + out_cut)), BF16
        ),
        compiler_params=params(1),
        cost_estimate=cost(8),
        name="grad_up",
    )(meta, norm_t, *mixed_t, grad_hidden, grad_branch, *gates)


def grad_down_kernel(meta, *refs):
    blocks, (grad_second_ref, out_ref) = refs[:-2], refs[-2:]
    rows = out_ref.shape[2]
    left = jnp.concatenate([b[...] for b in blocks], axis=0)
    value = dot_nn(left, grad_second_ref[...]).astype(BF16)
    for i in range(len(blocks)):
        for half in range(2):
            start = (2 * i + half) * rows
            out_ref[meta[1] ^ half, i] = value[start : start + rows]


def grad_down(rel, meta, active_t, grad_second, *gates):
    hidden_width, rows = active_t.shape
    width = grad_second.shape[1]
    block = hidden_width // (2 * BLOCKS)
    some = 4

    def spec(i):
        return pl.BlockSpec(
            (block, rows), lambda j, m: (2 * (m[0] ^ turned(some * j + i)) + (m[2] ^ rel), 0)
        )

    return pl.pallas_call(
        gated(grad_down_kernel, some + 1, len(gates)),
        grid_spec=pltpu.PrefetchScalarGridSpec(
            num_scalar_prefetch=1,
            grid=(BLOCKS // some,),
            in_specs=[spec(i) for i in range(some)]
            + [pl.BlockSpec((rows, width), lambda j, m: (0, 0), pipeline_mode=pl.Buffered(1))]
            + gate_specs(gates),
            out_specs=pl.BlockSpec((2, some, block // 2, width), lambda j, m: (0, j, 0, 0)),
        ),
        out_shape=jax.ShapeDtypeStruct((2, BLOCKS, block // 2, width), BF16),
        compiler_params=params(1),
        cost_estimate=cost(6),
        name="grad_down",
    )(meta, *[active_t] * some, grad_second, *gates)


def attend_back_kernel(
    meta,
    x_t_ref,
    qkv_ref,
    mixed_t_ref,
    grad_mixed_ref,
    lse_ref,
    grad_qkv_ref,
    grad_w_ref,
    grad_bias_ref,
    grad_scr,
):
    seq = pl.program_id(0)
    length = meta[3 + seq]
    rows, wide = qkv_ref.shape[1:]
    part = wide // 3
    lane = lax.broadcasted_iota(jnp.int32, (rows, 128), 1)
    key_ok = lax.broadcasted_iota(jnp.int32, (rows, rows), 0) < length
    start = pl.multiple_of(seq * rows, 128)

    @pl.when(seq == 0)
    def _():
        grad_bias_ref[...] = jnp.zeros_like(grad_bias_ref)

    for pair in range(part // 128):
        cut = pair * 128
        query = qkv_ref[0, :, cut : cut + 128] * jnp.asarray(0.125, BF16)
        key = qkv_ref[0, :, part + cut : part + cut + 128]
        value = qkv_ref[0, :, 2 * part + cut : 2 * part + cut + 128]
        grad_out = grad_mixed_ref[0, :, cut : cut + 128]
        product = grad_out.astype(F32).T * mixed_t_ref[cut : cut + 128, :].astype(F32)
        key_t = key.T
        grad_query, grad_key, grad_value = [], 0.0, 0.0
        for head in range(2):
            keep = (lane >= 64) == (head == 1)
            query_one = jnp.where(keep, query, jnp.zeros_like(query))
            grad_one = jnp.where(keep, grad_out, jnp.zeros_like(grad_out))
            inner = slice(64 * head, 64 * head + 64)
            delta = jnp.sum(product[inner], axis=0, keepdims=True)
            scores = jnp.where(key_ok, dot_nt(key, query_one), -1e30)
            prob = jnp.exp(scores - lse_ref[0, 2 * pair + head])
            grad_prob = dot_nt(value, grad_one)
            grad_scores = (prob * (grad_prob - delta)).astype(BF16)
            grad_value = grad_value + dot_nn(prob.astype(BF16), grad_one)
            grad_key = grad_key + dot_nn(grad_scores, query_one)
            grad_query.append(dot_nn(key_t[inner], grad_scores) * 0.125)
        grads = (jnp.concatenate(grad_query, axis=0).T, grad_key, grad_value)
        for kind, grad in enumerate(grads):
            grad = grad.astype(BF16)
            to = slice(kind * part + cut, kind * part + cut + 128)
            grad_scr[pl.ds(start, rows), to] = grad
            grad_qkv_ref[0, :, to] = grad
            grad_bias_ref[:, to] += column_sum(grad)

    @pl.when(seq == pl.num_programs(0) - 1)
    def _():
        store_blocks(meta, grad_w_ref, dot_nn(x_t_ref[...], grad_scr[...]), slice(None))


def attend_back(meta, x_t, qkv, mixed_t, grad_mixed, lse, *gates):
    seqs, length, wide = qkv.shape
    width, rows = x_t.shape
    part = wide // 3
    block_rows = width // (2 * BLOCKS)
    by_seq = lambda cols: pl.BlockSpec((1, length, cols), lambda s, m: (s, 0, 0))
    return pl.pallas_call(
        gated(attend_back_kernel, 5, len(gates)),
        grid_spec=pltpu.PrefetchScalarGridSpec(
            num_scalar_prefetch=1,
            grid=(seqs,),
            in_specs=[
                pl.BlockSpec((width, rows), lambda s, m: (0, 0), pipeline_mode=pl.Buffered(1)),
                by_seq(wide),
                pl.BlockSpec((part, length), lambda s, m: (0, s)),
                by_seq(part),
                pl.BlockSpec((1, HEADS // 2, 1, length), lambda s, m: (s, 0, 0, 0)),
                *gate_specs(gates),
            ],
            out_specs=[
                by_seq(wide),
                pl.BlockSpec((2, BLOCKS, block_rows, wide), lambda s, m: (0, 0, 0, 0)),
                pl.BlockSpec((1, wide), lambda s, m: (0, 0)),
            ],
            scratch_shapes=[pltpu.VMEM((rows, wide), BF16)],
        ),
        out_shape=[
            jax.ShapeDtypeStruct((seqs, length, wide), BF16),
            jax.ShapeDtypeStruct((2, BLOCKS, block_rows, wide), BF16),
            jax.ShapeDtypeStruct((1, wide), F32),
        ],
        compiler_params=params(1),
        cost_estimate=cost(16),
        name="attend_back",
    )(meta, x_t, qkv, mixed_t, grad_mixed, lse, *gates)


def input_kernel(
    meta, branch_ref, grad_mine, grad_other, w_mine, w_other, out_ref, scr_mine, scr_other
):
    @pl.when(pl.program_id(0) == 0)
    def _():
        place_rows(meta, w_mine, scr_mine, slice(None), slice(None))
        place_rows(meta, w_other, scr_other, slice(None), slice(None))

    total = branch_ref[...].astype(F32) + dot_nt(grad_mine[...], scr_mine[...])
    out_ref[...] = total + dot_nt(grad_other[...], scr_other[...])


def finish_kernel(moves, row_step, meta, *refs):
    parts, outs = refs[:2], refs[2:]
    for rel in range(4):
        part = parts[rel & 1].at[rel >> 1]
        x_at, core = meta[1] ^ (rel >> 1), meta[2] ^ (rel & 1)
        rows = part.shape[0]
        at = pl.ds(pl.multiple_of(x_at * rows + core * row_step, 16), rows)
        for columns, out, first, step in moves:
            size = columns.stop - columns.start
            to = pl.ds(pl.multiple_of(first + core * step, 128), size)
            outs[out][at, to] = part[:, columns].astype(F32)


def finish(meta, parts, moves, row_step, shapes):
    whole = lambda shape: pl.BlockSpec(shape, lambda i, m: (0,) * len(shape))
    return pl.pallas_call(
        functools.partial(finish_kernel, moves, row_step),
        grid_spec=pltpu.PrefetchScalarGridSpec(
            num_scalar_prefetch=1,
            grid=(1,),
            in_specs=[whole(p.shape) for p in parts],
            out_specs=[whole(shape) for shape in shapes],
        ),
        out_shape=[jax.ShapeDtypeStruct(shape, F32) for shape in shapes],
        compiler_params=params(1),
        cost_estimate=cost(2),
        name="finish",
    )(meta, *parts)


def together(*arrays):
    return lax.optimization_barrier(arrays)


CORE, X, Y, NEAR, FAR = 1, 2, 4, 8, 16
DEVICES = 32


def swap(array, mask):
    pairs = [(i, i ^ mask) for i in range(DEVICES)]
    return lax.ppermute(array, ("shard", "rep"), pairs)


def gather_z(piece):
    came = [swap(piece, mask) for mask in (FAR, NEAR, NEAR | FAR)]
    return jnp.stack([piece] + came)


def double(held, mask):
    return jnp.concatenate([held, swap(held, mask)], axis=0)


def plane_hops(held):
    return [swap(held, mask) for mask in (Y, X, X | Y)]


def plane_join(held, by_y, by_x, across):
    low = jnp.concatenate([held, by_y], axis=0)
    return jnp.stack([low, jnp.concatenate([by_x, across], axis=0)])


def gather_plane(held):
    return plane_join(held, *plane_hops(held))


def add(*terms):
    total = terms[0].astype(F32)
    for term in terms[1:]:
        total = total + term.astype(F32)
    return total.astype(BF16)


def sum_z(parts):
    return add(
        parts[0],
        *[swap(parts[i], mask) for i, mask in ((1, FAR), (2, NEAR), (3, NEAR | FAR))],
    )


def plane_sends(kept, came):
    cut = BLOCKS // 2
    pick = lambda a, x, y: a[x, cut:] if y else a[x, :cut]
    parts = [[add(pick(kept, x, y), pick(came, x, y)) for y in range(2)] for x in range(2)]
    return [
        parts[0][0],
        swap(parts[0][1], Y),
        swap(parts[1][0], X),
        swap(parts[1][1], X | Y),
    ]


def plane_sum(terms):
    return [add(*[t[i] for t in terms]) for i in range(4)]


def local(
    fast,
    tokens,
    lengths,
    w_qkv,
    b_query,
    b_value,
    w_out,
    b_out,
    ln1_gain,
    ln1_bias,
    w_up,
    b_up,
    w_down,
    b_down,
    ln2_gain,
    ln2_bias,
    cotangent,
):
    seqs, seq_len, width = tokens.shape
    rows = seqs * seq_len
    hidden_width = w_up.shape[1]
    half = width // 2
    groups = GROUPS
    up_cut, out_cut = hidden_width // (2 * groups), half // groups
    vectors = (b_query, b_value, b_out, ln1_gain, ln1_bias, b_down, ln2_gain, ln2_bias, b_up)

    if fast:
        shard, rep = lax.axis_index("shard"), lax.axis_index("rep")
        x_at, core = rep // 2, rep % 2
    else:
        shard = rep = x_at = core = jnp.int32(0)
    block = width // BLOCKS
    quarter = block // 2
    meta = jnp.concatenate(
        [jnp.stack([shard, x_at, core]).astype(jnp.int32), lengths.astype(jnp.int32)]
    )

    def qkv_parts(w):
        return w.reshape(-1, 2, quarter, 3, 2, half)

    def up_parts(up, out):
        up = up.reshape(-1, 2, quarter, 2, groups, up_cut)
        out = out.reshape(-1, 2, quarter, 2, groups, out_cut)
        return jnp.concatenate([up, out], axis=-1)

    if fast:
        qkv_piece, up_piece, down_piece = pack(meta, w_qkv, w_up, w_out, w_down, vectors)
        qkv_z, up_piece, down_piece = together(gather_z(qkv_piece), up_piece, down_piece)
        table = qkv_z[:, quarter:, : 128 + b_up.shape[0]]
        up_z = double(double(up_piece[None], FAR), NEAR)
        down_z = double(down_piece[None], FAR)
        qkv_mine, up_z, down_z, table, table_y = together(
            gather_plane(qkv_z[:, :quarter]), up_z, down_z, table, swap(table, Y)
        )
        vec, b_up_row, *bias = small_call(
            functools.partial(unpack_kernel, block),
            "unpack",
            meta,
            (table, table_y),
            ((8, width), (1, hidden_width), (1, 3 * half), (1, 3 * half)),
            ((16, width),),
        )
        qkv_w = qkv_mine, swap(qkv_mine, CORE)
        up_hops, down_z = plane_hops(up_z), double(down_z, NEAR)
    else:
        everything = lambda a: lax.all_gather(a, "shard", axis=0, tiled=True)
        full = [everything(v) for v in vectors]
        order = [turned(p) for p in range(BLOCKS)]
        both = lambda a: (a[0][:, order], a[1][:, order])
        qkv_w = both(
            qkv_parts(everything(w_qkv))
            .transpose(4, 1, 0, 2, 3, 5)
            .reshape(2, 2, BLOCKS, quarter, 3 * half)
        )
        up_w = both(
            up_parts(everything(w_up), everything(w_out))
            .transpose(3, 1, 0, 2, 4, 5)
            .reshape(2, 2, BLOCKS, quarter, -1)
        )
        down_w = both(
            everything(w_down).reshape(BLOCKS, 2, 2, -1, width).transpose(1, 2, 0, 3, 4)
        )
        full = [v.astype(F32) for v in full]
        bias = jnp.stack(
            [full[0].reshape(2, half), jnp.zeros((2, half), F32), full[1].reshape(2, half)], axis=1
        ).reshape(2, 1, 3 * half)
        vec = jnp.stack(full[2:8] + [jnp.zeros_like(full[0])] * 2)
        b_up_row = full[8].reshape(1, -1)
    x_rows = tokens.reshape(rows, width)
    heads = [list(attend(meta, tokens, qkv_w[i], bias[i])) for i in range(2)]
    if fast:
        x_late, heads[0][0] = together(x_rows, heads[0][0])
        x_t = x_late.T
    else:
        x_t = x_rows.T
    if fast:
        *up_hops, down_z, heads[0][1], heads[1][1] = together(
            *up_hops, down_z, heads[0][1], heads[1][1]
        )
        up_mine = plane_join(up_z, *up_hops)
        up_w = up_mine, swap(up_mine, CORE)
    qkv, mixed, mixed_t, lse = zip(*heads)
    mixed_rows = [m.reshape(rows, half) for m in mixed]
    up_shape, out_shape, down_shape = (width, hidden_width), (width, width), (hidden_width, width)
    hat, scale, norm_t, active, active_t, slope, up_full, out_full = by_chunk(
        up_kernel,
        "feed_up",
        26,
        meta,
        (b_up_row,),
        (x_rows, *mixed_rows, *up_w, vec),
        (),
        (
            ("whole", (rows, width), F32),
            ("whole", (rows, 128), F32),
            ("whole", (width, rows), BF16),
            ("cols", (rows, hidden_width), BF16),
            ("rows", (hidden_width, rows), BF16),
            ("cols", (rows, hidden_width), BF16),
            ("whole", up_shape, BF16),
            ("whole", out_shape, BF16),
        ),
        (((rows, width), BF16),),
    )
    row, fixed = "row", "sum"
    if fast:
        active, x_t, *hops = together(active, x_t, *plane_hops(down_z))
        down_mine = plane_join(down_z, *hops)
        down_w = down_mine, swap(down_mine, CORE)
    layer_out, grad_second, vec_two, down_full = by_tile(
        functools.partial(down_kernel, seq_len),
        "feed_down",
        14,
        meta,
        (hat, active, cotangent.reshape(rows, width)),
        (*down_w, vec),
        (),
        (
            (row, width, BF16),
            (row, width, BF16),
            (fixed, (8, width), F32),
            (fixed, down_shape, BF16),
        ),
        (),
    )
    down_send = grad_down(1, meta, active_t, grad_second)
    down_keep = grad_down(0, meta, active_t, grad_second, down_send)
    gates = (down_keep,)
    if fast:
        down_plane = plane_sends(down_keep, swap(down_send, CORE))
        gates = (down_plane[0],)
    grad_hidden, grad_branch, *grad_mixed, vec_one, grad_b_up = by_chunk(
        rest_kernel,
        "feed_back",
        22,
        meta,
        (up_full, slope),
        (grad_second, hat, scale, out_full, vec),
        gates,
        (
            ("cols", (rows, hidden_width), BF16),
            ("whole", (rows, width), BF16),
            ("whole", (rows, half), BF16),
            ("whole", (rows, half), BF16),
            ("whole", (8, width), F32),
            ("cols", (1, hidden_width), F32),
        ),
        (((rows, width), F32),),
        (down_full,),
    )
    gates = ()
    if fast:
        down_parts = plane_sum(down_plane)
        gates = tuple(down_parts)
    up_send = grad_up(1, meta, norm_t, mixed_t, grad_hidden, grad_branch, *gates)
    if fast:
        up_send, *down_parts = together(up_send, *down_parts)
    up_keep = grad_up(0, meta, norm_t, mixed_t, grad_hidden, grad_branch, up_send)
    gates = (up_keep,)
    if fast:
        up_plane = plane_sends(up_keep, swap(up_send, CORE))
        down_piece = sum_z(down_parts)
        gates = (up_plane[0],)
    grad_mixed = [g.reshape(seqs, seq_len, half) for g in grad_mixed]

    def back(i, *gates):
        return attend_back(meta, x_t, qkv[i], mixed_t[i], grad_mixed[i], lse[i], *gates)

    other_qkv, qkv_send, other_bias = back(1, *gates)
    gates = (qkv_send,)
    if fast:
        down_piece, qkv_send = together(down_piece, qkv_send)
        gates = (qkv_send, up_plane[1], up_plane[2])
    mine_qkv, qkv_keep, mine_bias = back(0, *gates)
    gates = (qkv_keep,)
    if fast:
        qkv_plane = plane_sends(qkv_keep, swap(qkv_send, CORE))
        down_piece, qkv_plane[0], *up_plane = together(down_piece, qkv_plane[0], *up_plane)
        down_both = jnp.stack([down_piece, swap(down_piece, X)])
        up_parts_sum = plane_sum(up_plane)
        up_near = swap(jnp.stack(up_parts_sum[2:]), NEAR)
        down_quarters = down_both, swap(down_both, CORE)
        gates = (qkv_plane[0], up_parts_sum[0])
    (input_grad,) = by_tile(
        input_kernel,
        "input_grad",
        10,
        meta,
        (grad_branch, mine_qkv.reshape(rows, -1), other_qkv.reshape(rows, -1)),
        qkv_w,
        gates,
        ((row, width, F32),),
        ((width, 3 * half), (width, 3 * half)),
    )

    (total,) = small_call(
        sums_kernel,
        "sums",
        meta,
        (vec_one, vec_two, grad_b_up, mine_bias, other_bias),
        ((16, width),),
        gates=gates[:1],
    )
    if fast:
        came, input_grad, up_near, *qkv_plane[1:3] = together(
            swap(total, CORE), input_grad, up_near, *qkv_plane[1:3]
        )
        total = total + came
        up_low = [add(up_parts_sum[i], up_near[i]) for i in range(2)]
        came, up_far, qkv_plane[3] = together(
            swap(total, X), swap(up_low[1], FAR), qkv_plane[3]
        )
        total = total + came
        up_piece = add(up_low[0], up_far)
        qkv_parts_sum = plane_sum(qkv_plane)
        qkv_hops = [swap(qkv_parts_sum[i], m) for i, m in ((1, FAR), (2, NEAR), (3, NEAR | FAR))]
        came, up_x, *qkv_hops = together(swap(total, Y), swap(up_piece, X), *qkv_hops)
        total = total + came
        up_both = jnp.stack([up_piece, up_x])
        qkv_piece = add(qkv_parts_sum[0], *qkv_hops)
        came, up_core, qkv_x = together(
            swap(total, NEAR), swap(up_both, CORE), swap(qkv_piece, X)
        )
        total = total + came
        total = total + swap(total, FAR)
        up_quarters = up_both, up_core
        qkv_both = jnp.stack([qkv_piece, qkv_x])
        qkv_quarters = qkv_both, swap(qkv_both, CORE)
        sums = small_call(
            functools.partial(own_sums_kernel, block),
            "own_sums",
            meta,
            (total,),
            ((block,),) * 8 + (b_up.shape,),
        )
        step = up_cut + out_cut
        up_moves = [
            move
            for g in range(groups)
            for move in (
                (slice(g * step, g * step + up_cut), 0, g * up_cut, hidden_width // 2),
                (slice(g * step + up_cut, (g + 1) * step), 1, g * out_cut, half),
            )
        ]
        qkv_moves = [(slice(k * half, (k + 1) * half), 0, k * width, half) for k in range(3)]
        (grad_w_down,) = finish(
            meta,
            down_quarters,
            [(slice(0, width), 0, 0, 0)],
            w_down.shape[0] // 2,
            [w_down.shape],
        )
        grad_w_up, grad_w_out = finish(meta, up_quarters, up_moves, 0, [w_up.shape, w_out.shape])
        (grad_w_qkv,) = finish(meta, qkv_quarters, qkv_moves, 0, [w_qkv.shape])
    else:
        total_of = lambda a: lax.psum(
            lax.psum_scatter(a, "shard", scatter_dimension=0, tiled=True), "rep"
        )
        sums = [total_of(g) for g in (*total[:8], total[8:12].reshape(-1))]
        order = [turned(p) for p in range(BLOCKS)]
        down_keep, down_send, up_keep, up_send = (
            a[:, order] for a in (down_keep, down_send, up_keep, up_send)
        )
        down = jnp.stack([down_keep, down_send]).transpose(2, 0, 1, 3, 4)
        grad_w_down = total_of(down.reshape(hidden_width, width).astype(F32))
        up = jnp.stack([up_keep, up_send]).reshape(
            2, 2, BLOCKS, quarter, groups, up_cut + out_cut
        )
        up = up.transpose(2, 1, 3, 0, 4, 5)
        grad_w_up = total_of(up[..., :up_cut].reshape(width, hidden_width).astype(F32))
        grad_w_out = total_of(up[..., up_cut:].reshape(width, width).astype(F32))
        qkv_sum = jnp.stack([qkv_keep[:, order], qkv_send[:, order]])
        qkv_sum = qkv_sum.reshape(2, 2, BLOCKS, quarter, 3, half)
        qkv_sum = qkv_sum.transpose(2, 1, 3, 4, 0, 5).reshape(width, 3 * width)
        grad_w_qkv = total_of(qkv_sum.astype(F32))
    return (
        layer_out.reshape(seqs, seq_len, width),
        input_grad.reshape(seqs, seq_len, width),
        grad_w_qkv,
        sums[0],
        sums[1],
        grad_w_out,
        sums[2],
        sums[3],
        sums[4],
        grad_w_up,
        sums[8],
        grad_w_down,
        sums[5],
        sums[6],
        sums[7],
    )


def solution(mesh):
    fast = mesh.shape["shard"] == BLOCKS and mesh.shape["rep"] == 4
    by_seq = P(("shard", "rep"), None, None)
    one, two = P("shard"), P("shard", None)
    in_specs = (by_seq, P(("shard", "rep")), two, one, one, two, one, one, one)
    in_specs = in_specs + (two, one, two, one, one, one, by_seq)
    out_specs = (by_seq, by_seq, two, one, one, two, one, one, one, two, one, two, one, one, one)
    return jax.shard_map(
        functools.partial(local, fast),
        mesh=mesh,
        in_specs=in_specs,
        out_specs=out_specs,
        check_vma=False,
    )
```

```python
import functools

import jax
import jax.numpy as jnp
from jax import lax
from jax.experimental import pallas as pl
from jax.experimental.pallas import tpu as pltpu
from jax.sharding import PartitionSpec as P

HEADS = 12
EPS = 1e-05
F32 = jnp.float32
BF16 = jnp.bfloat16
BLOCKS = 8
GROUPS = 3
VMEM_LIMIT = 58 * 1024 * 1024


def dot_nn(a, b):
    return lax.dot_general(a, b, (((1,), (0,)), ((), ())), preferred_element_type=F32)


def dot_nt(a, b):
    return lax.dot_general(a, b, (((1,), (1,)), ((), ())), preferred_element_type=F32)


def dot_tn(a, b):
    return lax.dot_general(a, b, (((0,), (0,)), ((), ())), preferred_element_type=F32)


def params(grid_dims):
    return pltpu.CompilerParams(
        dimension_semantics=("arbitrary",) * grid_dims, vmem_limit_bytes=VMEM_LIMIT
    )


def cost(micros):
    return pl.CostEstimate(flops=int(micros * 1.15e9), bytes_accessed=1 << 20, transcendentals=0)


def gated(kernel, inputs, gates):
    def body(*refs):
        kernel(*refs[: inputs + 1], *refs[inputs + 1 + gates :])

    return body


def gate_specs(gates):
    return [pl.BlockSpec(memory_space=pl.ANY)] * len(gates)


def turned(place):
    return ((place & 1) << 2) | (place & 2) | ((place >> 2) & 1)


def place_rows(meta, source, target, columns, cut):
    rows = source.shape[2]
    for half in range(2):
        for block in range(BLOCKS):
            start = (meta[0] ^ turned(block)) * (2 * rows) + (meta[1] ^ half) * rows
            target[pl.ds(pl.multiple_of(start, 16), rows), cut] = source[half, block, :, columns]


def pack_kernel(groups, *refs):
    meta, w_qkv, w_up, w_out, w_down, *vectors, qkv_ref, up_ref, down_ref = refs
    rows, wide = up_ref.shape[0], qkv_ref.shape[1]
    half = wide // 3
    up_cut, out_cut = w_up.shape[1] // (2 * groups), w_out.shape[1] // (2 * groups)
    at = pl.ds(pl.multiple_of(meta[1] * rows, 16), rows)

    def columns(start, size):
        return pl.ds(pl.multiple_of(start, 128), size)

    for kind in range(3):
        start = (2 * kind + meta[2]) * half
        qkv_ref[:rows, kind * half : (kind + 1) * half] = w_qkv[at, columns(start, half)]
    for group in range(groups):
        base = group * (up_cut + out_cut)
        start = (meta[2] * groups + group) * up_cut
        up_ref[:, base : base + up_cut] = w_up[at, columns(start, up_cut)]
        start = (meta[2] * groups + group) * out_cut
        up_ref[:, base + up_cut : base + up_cut + out_cut] = w_out[at, columns(start, out_cut)]
    rows_down = down_ref.shape[0]
    start = (2 * meta[2] + meta[1]) * rows_down
    down_ref[...] = w_down[pl.ds(pl.multiple_of(start, 16), rows_down), :]
    *short, long = vectors
    extra = qkv_ref.shape[0] - rows
    small = short[0].shape[0]
    place = lax.broadcasted_iota(jnp.int32, (extra, small), 0)
    table = jnp.zeros((extra, small), F32)
    for i, v in enumerate(short):
        table = jnp.where(place == i, v[...].astype(F32).reshape(1, small), table)
    qkv_ref[rows:, :] = jnp.zeros((extra, wide), BF16)
    qkv_ref[rows:, :small] = table.astype(BF16)
    size = long.shape[0]
    wide_row = jnp.broadcast_to(long[...].astype(F32).reshape(1, size), (extra, size))
    qkv_ref[rows:, 128 : 128 + size] = wide_row.astype(BF16)


def pack(meta, w_qkv, w_up, w_out, w_down, vectors):
    rows = w_up.shape[0] // 2
    whole = lambda a: pl.BlockSpec(a.shape, lambda i, m: (0,) * a.ndim)
    shapes = [
        (rows + 16, w_qkv.shape[1] // 2),
        (rows, (w_up.shape[1] + w_out.shape[1]) // 2),
        (w_down.shape[0] // 4, w_down.shape[1]),
    ]
    outs = [jax.ShapeDtypeStruct(shape, BF16) for shape in shapes]
    operands = (w_qkv, w_up, w_out, w_down, *vectors)
    return pl.pallas_call(
        functools.partial(pack_kernel, GROUPS),
        grid_spec=pltpu.PrefetchScalarGridSpec(
            num_scalar_prefetch=1,
            grid=(1,),
            in_specs=[whole(a) for a in operands],
            out_specs=[whole(o) for o in outs],
        ),
        out_shape=outs,
        compiler_params=params(1),
        cost_estimate=cost(2),
        name="pack",
    )(meta, *operands)


def shard_columns(shard, block, width, lanes):
    lane = lax.broadcasted_iota(jnp.int32, (lanes, width), 0)
    column = lax.broadcasted_iota(jnp.int32, (lanes, width), 1)
    return (lane < block) & (column == lane + shard * block)


def unpack_kernel(block, meta, near_ref, far_ref, vec_ref, b_up_ref, mine_ref, other_ref, scr):
    width = vec_ref.shape[1]
    half, size = width // 2, b_up_ref.shape[1] // BLOCKS
    total = jnp.zeros(scr.shape, F32)
    for place in range(BLOCKS):
        source = (near_ref, far_ref)[place // 4]
        rows = source[place % 4]
        shard = meta[0] ^ turned(place)
        spread = shard_columns(shard, block, width, 128).astype(F32).astype(BF16)
        total = total + dot_nn(rows[:, :128], spread)
        to = pl.ds(pl.multiple_of(shard * size, 128), size)
        b_up_ref[:, to] = rows[:1, 128 : 128 + size].astype(F32)
    scr[...] = total
    vec_ref[...] = jnp.zeros_like(vec_ref)
    vec_ref[0:6, :] = total[2:8]
    for rel, out in enumerate((mine_ref, other_ref)):
        cut = pl.ds(pl.multiple_of((meta[2] ^ rel) * half, 128), half)
        out[...] = jnp.zeros_like(out)
        out[:, :half] = scr[0:1, cut]
        out[:, 2 * half :] = scr[1:2, cut]


def small_call(kernel, name, meta, operands, shapes, scratch=(), gates=()):
    whole = lambda a: pl.BlockSpec(a.shape, lambda i, m: (0,) * len(a.shape))
    outs = [jax.ShapeDtypeStruct(shape, F32) for shape in shapes]
    return pl.pallas_call(
        gated(kernel, len(operands), len(gates)),
        grid_spec=pltpu.PrefetchScalarGridSpec(
            num_scalar_prefetch=1,
            grid=(1,),
            in_specs=[whole(a) for a in operands] + gate_specs(gates),
            out_specs=[whole(o) for o in outs],
            scratch_shapes=[pltpu.VMEM(shape, F32) for shape in scratch],
        ),
        out_shape=outs,
        compiler_params=params(1),
        cost_estimate=cost(2),
        name=name,
    )(meta, *operands, *gates)


def sums_kernel(meta, vec_one, vec_two, b_up, bias_mine, bias_other, out_ref):
    width = out_ref.shape[1]
    half = width // 2
    out_ref[...] = jnp.zeros_like(out_ref)
    for rel, source in enumerate((bias_mine, bias_other)):
        to = pl.ds(pl.multiple_of((meta[2] ^ rel) * half, 128), half)
        out_ref[0:1, to] = source[:, :half]
        out_ref[1:2, to] = source[:, 2 * half :]
    out_ref[2:5, :] = vec_one[0:3, :]
    out_ref[5:8, :] = vec_two[0:3, :]
    for i in range(b_up.shape[1] // width):
        out_ref[8 + i : 9 + i, :] = b_up[:, i * width : (i + 1) * width]


def own_sums_kernel(block, meta, sum_ref, *outs):
    *short, b_up_ref = outs
    width, size = sum_ref.shape[1], b_up_ref.shape[0]
    pick = shard_columns(meta[0], block, width, 128).astype(F32)
    own = lax.dot_general(
        sum_ref[0:8, :],
        pick,
        (((1,), (1,)), ((), ())),
        precision=lax.Precision.HIGHEST,
        preferred_element_type=F32,
    )
    each = width // size
    cut = pl.ds(pl.multiple_of(lax.rem(meta[0], each) * size, 128), size)
    b_up_ref[...] = sum_ref[pl.ds(8 + lax.div(meta[0], each), 1), cut].reshape(size)
    for i, out in enumerate(short):
        out[...] = own[i : i + 1, :block].reshape(block)


def attend_kernel(meta, x_ref, w_ref, bias_ref, qkv_ref, mixed_ref, mixed_t_ref, lse_ref, x_t_ref, w_scr):
    seq = pl.program_id(0)
    wide = w_scr.shape[1]
    part = wide // 3

    @pl.when(seq == 0)
    def _():
        place_rows(meta, w_ref, w_scr, slice(None), slice(None))

    length = meta[3 + seq]
    x_t_ref[...] = x_ref[0].T
    qkv = (dot_nn(x_ref[0], w_scr[...]) + bias_ref[...]).astype(BF16)
    qkv_ref[0] = qkv
    rows = qkv.shape[0]
    lane = lax.broadcasted_iota(jnp.int32, (rows, 128), 1)
    key_ok = lax.broadcasted_iota(jnp.int32, (rows, rows), 0) < length
    for pair in range(part // 128):
        cut = pair * 128
        query = qkv[:, cut : cut + 128] * jnp.asarray(0.125, BF16)
        key = qkv[:, part + cut : part + cut + 128]
        value_t = qkv[:, 2 * part + cut : 2 * part + cut + 128].T
        outs = []
        for head in range(2):
            query_one = jnp.where((lane >= 64) == (head == 1), query, jnp.zeros_like(query))
            scores = jnp.where(key_ok, dot_nt(key, query_one), -1e30)
            top = jnp.max(scores, axis=0, keepdims=True)
            exp_scores = jnp.exp(scores - top)
            total = jnp.sum(exp_scores, axis=0, keepdims=True)
            lse_ref[0, 2 * pair + head] = top + jnp.log(total)
            out = dot_nn(value_t[64 * head : 64 * head + 64], exp_scores.astype(BF16))
            outs.append(out * (1.0 / total))
        mixed_t = jnp.concatenate(outs, axis=0)
        mixed_t_ref[cut : cut + 128, :] = mixed_t.astype(BF16)
        mixed_ref[0, :, cut : cut + 128] = mixed_t.T.astype(BF16)


def attend(meta, x, weight, bias):
    seqs, length, width = x.shape
    wide = weight.shape[3]
    part = wide // 3
    half_heads = HEADS // 2
    whole = lambda s, m: (0, 0, 0, 0)
    return pl.pallas_call(
        attend_kernel,
        grid_spec=pltpu.PrefetchScalarGridSpec(
            num_scalar_prefetch=1,
            grid=(seqs,),
            in_specs=[
                pl.BlockSpec((1, length, width), lambda s, m: (s, 0, 0)),
                pl.BlockSpec(weight.shape, whole, pipeline_mode=pl.Buffered(1)),
                pl.BlockSpec((1, wide), lambda s, m: (0, 0)),
            ],
            out_specs=[
                pl.BlockSpec((1, length, wide), lambda s, m: (s, 0, 0)),
                pl.BlockSpec((1, length, part), lambda s, m: (s, 0, 0)),
                pl.BlockSpec((part, length), lambda s, m: (0, s)),
                pl.BlockSpec((1, half_heads, 1, length), lambda s, m: (s, 0, 0, 0)),
                pl.BlockSpec((width, length), lambda s, m: (0, s)),
            ],
            scratch_shapes=[pltpu.VMEM((width, wide), BF16)],
        ),
        out_shape=[
            jax.ShapeDtypeStruct((seqs, length, wide), BF16),
            jax.ShapeDtypeStruct((seqs, length, part), BF16),
            jax.ShapeDtypeStruct((part, seqs * length), BF16),
            jax.ShapeDtypeStruct((seqs, half_heads, 1, length), F32),
            jax.ShapeDtypeStruct((width, seqs * length), BF16),
        ],
        compiler_params=params(1),
        cost_estimate=cost(11),
        name="attend_forward",
    )(meta, x, weight, bias)


def gelu_and_slope(hidden):
    size = jnp.abs(hidden)
    bell = jnp.exp2(hidden * hidden * -0.7213475204444817)
    t = 1.0 / (1.0 + (0.3275911 * 0.7071067811865476) * size)
    poly = t * (
        0.5 * 0.254829592
        + t
        * (
            0.5 * -0.284496736
            + t * (0.5 * 1.421413741 + t * (0.5 * -1.453152027 + t * (0.5 * 1.061405429)))
        )
    )
    tail = poly * bell
    phi = jnp.where(hidden < 0.0, tail, 1.0 - tail)
    return hidden * phi, phi + hidden * bell * 0.3989422804014327


def norm_forward(hidden):
    center = hidden - jnp.mean(hidden, axis=-1, keepdims=True)
    scale = lax.rsqrt(jnp.mean(center * center, axis=-1, keepdims=True) + EPS)
    return center * scale, scale


def norm_back(grad, hat, scale, gain):
    grad_hat = grad * gain
    shift = jnp.mean(grad_hat, axis=-1, keepdims=True)
    along = jnp.mean(grad_hat * hat, axis=-1, keepdims=True)
    return scale * (grad_hat - shift - hat * along)


def column_sum(rows):
    return jnp.sum(rows.astype(F32), axis=0, keepdims=True)


def place_up(meta, mine, other, w_up, w_out):
    hidden_width, width = w_up.shape[1], w_out.shape[1]
    up_cut, out_cut = hidden_width // (2 * GROUPS), width // (2 * GROUPS)
    for rel, source in enumerate((mine, other)):
        core = meta[2] ^ rel
        for group in range(GROUPS):
            base = group * (up_cut + out_cut)
            up_to = pl.multiple_of(core * (hidden_width // 2) + group * up_cut, 128)
            out_to = pl.multiple_of(core * (width // 2) + group * out_cut, 128)
            place_rows(meta, source, w_up, slice(base, base + up_cut), pl.ds(up_to, up_cut))
            place_rows(
                meta,
                source,
                w_out,
                slice(base + up_cut, base + up_cut + out_cut),
                pl.ds(out_to, out_cut),
            )


def place_down(meta, mine, other, w_down):
    rows = mine.shape[2]
    for rel, source in enumerate((mine, other)):
        for half in range(2):
            for block in range(BLOCKS):
                start = (
                    (meta[0] ^ turned(block)) * (4 * rows)
                    + (meta[2] ^ rel) * (2 * rows)
                    + (meta[1] ^ half) * rows
                )
                w_down[pl.ds(pl.multiple_of(start, 16), rows), :] = source[half, block]


def halves_of(meta, width):
    half = width // 2
    return (
        pl.ds(pl.multiple_of(meta[2] * half, 128), half),
        pl.ds(pl.multiple_of((1 - meta[2]) * half, 128), half),
    )


CHUNK = 512


def up_kernel(
    meta,
    x_ref,
    mixed_mine,
    mixed_other,
    up_mine,
    up_other,
    vec_ref,
    b_up_ref,
    hat_ref,
    scale_ref,
    norm_t_ref,
    active_ref,
    active_t_ref,
    slope_ref,
    w_up,
    w_out,
    normed_low,
):
    step = pl.program_id(0)
    width = w_out.shape[1]

    @pl.when(step == 0)
    def _():
        place_up(meta, up_mine, up_other, w_up, w_out)
        b_out, gain, shift = [vec_ref[i : i + 1, :] for i in range(3)]
        rows_mine, rows_other = halves_of(meta, width)
        branch = dot_nn(mixed_mine[...], w_out[rows_mine, :])
        branch = branch + dot_nn(mixed_other[...], w_out[rows_other, :])
        hat, scale = norm_forward(x_ref[...].astype(F32) + (branch + b_out))
        hat_ref[...] = hat
        scale_ref[...] = jnp.broadcast_to(scale, scale_ref.shape)
        normed_low[...] = (hat * gain + shift).astype(BF16)
        norm_t_ref[...] = normed_low[...].T

    cut = pl.ds(pl.multiple_of(step * CHUNK, CHUNK), CHUNK)
    hidden = dot_nn(normed_low[...], w_up[:, cut]) + b_up_ref[...]
    active, slope = gelu_and_slope(hidden)
    slope_ref[...] = slope.astype(BF16)
    active_low = active.astype(BF16)
    active_ref[...] = active_low
    active_t_ref[...] = active_low.T


def down_kernel(
    seq_len,
    meta,
    hat_ref,
    active_ref,
    cot_ref,
    down_mine,
    down_other,
    vec_ref,
    out_ref,
    grad_second_ref,
    grad_vec_ref,
    w_down,
):
    step = pl.program_id(0)
    tile = hat_ref.shape[0]

    @pl.when(step == 0)
    def _():
        grad_vec_ref[...] = jnp.zeros_like(grad_vec_ref)
        place_down(meta, down_mine, down_other, w_down)

    gain_one, shift_one, b_down, gain, shift = [vec_ref[i : i + 1, :] for i in range(1, 6)]
    seq = lax.div(step * tile, seq_len)
    place = lax.broadcasted_iota(jnp.int32, (tile, 1), 0) + lax.rem(step * tile, seq_len)
    valid = place < meta[3 + seq]
    second = dot_nn(active_ref[...], w_down[...])
    normed = hat_ref[...] * gain_one + shift_one
    hat, scale = norm_forward(normed + (second + b_down))
    out_ref[...] = jnp.where(valid, hat * gain + shift, 0.0).astype(BF16)
    grad_result = jnp.where(valid, cot_ref[...].astype(F32), 0.0)
    grad_second = norm_back(grad_result, hat, scale, gain).astype(BF16)
    grad_second_ref[...] = grad_second
    sums = column_sum(grad_second), column_sum(grad_result * hat), column_sum(grad_result)
    for i, total in enumerate(sums):
        grad_vec_ref[i : i + 1, :] += total


def rest_kernel(
    meta,
    grad_second_ref,
    hat_ref,
    scale_ref,
    w_out,
    vec_ref,
    w_down,
    w_up,
    slope_ref,
    grad_hidden_ref,
    grad_branch_ref,
    grad_mixed_mine,
    grad_mixed_other,
    grad_vec_ref,
    grad_b_up_ref,
    total,
):
    step = pl.program_id(0)
    width = w_out.shape[1]

    @pl.when(step == 0)
    def _():
        total[...] = grad_second_ref[...].astype(F32)

    grad_active = dot_nt(grad_second_ref[...], w_down[...])
    grad_hidden = (slope_ref[...].astype(F32) * grad_active).astype(BF16)
    grad_hidden_ref[...] = grad_hidden
    grad_b_up_ref[...] = column_sum(grad_hidden)
    total[...] += dot_nt(grad_hidden, w_up[...])

    @pl.when(step == pl.num_programs(0) - 1)
    def _():
        grad_normed, hat, gain = total[...], hat_ref[...], vec_ref[1:2, :]
        grad_branch = norm_back(grad_normed, hat, scale_ref[:, 0:1], gain).astype(BF16)
        grad_branch_ref[...] = grad_branch
        rows_mine, rows_other = halves_of(meta, width)
        grad_mixed_mine[...] = dot_nt(grad_branch, w_out[rows_mine, :]).astype(BF16)
        grad_mixed_other[...] = dot_nt(grad_branch, w_out[rows_other, :]).astype(BF16)
        grad_vec_ref[...] = jnp.zeros_like(grad_vec_ref)
        sums = column_sum(grad_branch), column_sum(grad_normed * hat), column_sum(grad_normed)
        for i, one in enumerate(sums):
            grad_vec_ref[i : i + 1, :] = one


def by_chunk(kernel, name, micros, meta, cut, wholes, gates, outs, scratch, cut_rows=()):
    hidden_width = cut[-1].shape[1]
    chunked = lambda shape: pl.BlockSpec((shape[0], CHUNK), lambda n, m: (0, n))
    whole = lambda shape: pl.BlockSpec(
        shape, lambda n, m: (0,) * len(shape), pipeline_mode=pl.Buffered(1)
    )
    spec_of = {
        "cols": chunked,
        "rows": lambda shape: pl.BlockSpec((CHUNK, shape[1]), lambda n, m: (n, 0)),
        "whole": lambda shape: pl.BlockSpec(shape, lambda n, m: (0,) * len(shape)),
    }
    return pl.pallas_call(
        gated(kernel, len(cut) + len(cut_rows) + len(wholes), len(gates)),
        grid_spec=pltpu.PrefetchScalarGridSpec(
            num_scalar_prefetch=1,
            grid=(hidden_width // CHUNK,),
            in_specs=[whole(a.shape) for a in wholes]
            + [spec_of["rows"](a.shape) for a in cut_rows]
            + [chunked(a.shape) for a in cut]
            + gate_specs(gates),
            out_specs=[spec_of[kind](shape) for kind, shape, _ in outs],
            scratch_shapes=[pltpu.VMEM(shape, dtype) for shape, dtype in scratch],
        ),
        out_shape=[jax.ShapeDtypeStruct(shape, dtype) for _, shape, dtype in outs],
        compiler_params=params(1),
        cost_estimate=cost(micros),
        name=name,
    )(meta, *wholes, *cut_rows, *cut, *gates)


def by_tile(kernel, name, micros, meta, tiled, wholes, gates, outs, scratch, most=512):
    rows = tiled[0].shape[0]
    tile = min(most, rows)
    by_row = lambda cols: pl.BlockSpec((tile, cols), lambda i, m: (i, 0))
    whole = lambda a: pl.BlockSpec(
        a.shape, lambda i, m: (0,) * a.ndim, pipeline_mode=pl.Buffered(1)
    )
    specs, shapes = [], []
    for kind, size, dtype in outs:
        if kind == "row":
            specs.append(by_row(size))
            shapes.append(jax.ShapeDtypeStruct((rows, size), dtype))
        elif kind == "col":
            specs.append(pl.BlockSpec((size, tile), lambda i, m: (0, i)))
            shapes.append(jax.ShapeDtypeStruct((size, rows), dtype))
        else:
            specs.append(pl.BlockSpec(size, lambda i, m: (0, 0)))
            shapes.append(jax.ShapeDtypeStruct(size, dtype))
    return pl.pallas_call(
        gated(kernel, len(tiled) + len(wholes), len(gates)),
        grid_spec=pltpu.PrefetchScalarGridSpec(
            num_scalar_prefetch=1,
            grid=(rows // tile,),
            in_specs=[by_row(a.shape[1]) for a in tiled]
            + [whole(a) for a in wholes]
            + gate_specs(gates),
            out_specs=specs,
            scratch_shapes=[pltpu.VMEM(shape, BF16) for shape in scratch],
        ),
        out_shape=shapes,
        compiler_params=params(1),
        cost_estimate=cost(micros),
        name=name,
    )(meta, *tiled, *wholes, *gates)


def store_blocks(meta, out_ref, value, cut, first=0):
    rows = out_ref.shape[2]
    for block in range(value.shape[0] // (2 * rows)):
        for half in range(2):
            start = (2 * block + half) * rows
            out_ref[meta[1] ^ half, turned(meta[0] ^ (first + block)), :, cut] = value[
                start : start + rows
            ].astype(BF16)


def grad_up_kernel(
    meta, norm_t_ref, mixed_mine, mixed_other, grad_hidden_ref, grad_branch_ref, out_ref
):
    up_cut = grad_hidden_ref.shape[1]
    store_blocks(meta, out_ref, dot_nn(norm_t_ref[...], grad_hidden_ref[...]), slice(0, up_cut))
    cut = slice(up_cut, out_ref.shape[3])
    few = BLOCKS // 2
    grad_branch = grad_branch_ref[...]
    store_blocks(meta, out_ref, dot_nn(mixed_mine[...], grad_branch), cut, meta[2] * few)
    store_blocks(meta, out_ref, dot_nn(mixed_other[...], grad_branch), cut, (1 - meta[2]) * few)


def grad_up(rel, meta, norm_t, mixed_t, grad_hidden, grad_branch, *gates):
    width, rows = norm_t.shape
    hidden_width = grad_hidden.shape[1]
    groups = 3
    up_cut, out_cut = hidden_width // (2 * groups), width // (2 * groups)
    block_rows = width // (2 * BLOCKS)
    whole = lambda tall: pl.BlockSpec(
        (tall, rows), lambda n, m: (0, 0), pipeline_mode=pl.Buffered(1)
    )
    turn = lambda n, m: (0, (m[2] ^ rel) * groups + n)
    return pl.pallas_call(
        gated(grad_up_kernel, 5, len(gates)),
        grid_spec=pltpu.PrefetchScalarGridSpec(
            num_scalar_prefetch=1,
            grid=(groups,),
            in_specs=[
                whole(width),
                whole(width // 2),
                whole(width // 2),
                pl.BlockSpec((rows, up_cut), turn),
                pl.BlockSpec((rows, out_cut), turn),
                *gate_specs(gates),
            ],
            out_specs=pl.BlockSpec(
                (2, BLOCKS, block_rows, up_cut + out_cut), lambda n, m: (0, 0, 0, n)
            ),
        ),
        out_shape=jax.ShapeDtypeStruct(
            (2, BLOCKS, block_rows, groups * (up_cut + out_cut)), BF16
        ),
        compiler_params=params(1),
        cost_estimate=cost(8),
        name="grad_up",
    )(meta, norm_t, *mixed_t, grad_hidden, grad_branch, *gates)


def grad_down_kernel(meta, *refs):
    blocks, (grad_second_ref, out_ref) = refs[:-2], refs[-2:]
    rows = out_ref.shape[2]
    left = jnp.concatenate([b[...] for b in blocks], axis=0)
    value = dot_nn(left, grad_second_ref[...]).astype(BF16)
    for i in range(len(blocks)):
        for half in range(2):
            start = (2 * i + half) * rows
            out_ref[meta[1] ^ half, i] = value[start : start + rows]


def grad_down(rel, meta, active_t, grad_second, *gates):
    hidden_width, rows = active_t.shape
    width = grad_second.shape[1]
    block = hidden_width // (2 * BLOCKS)
    some = 4

    def spec(i):
        return pl.BlockSpec(
            (block, rows), lambda j, m: (2 * (m[0] ^ turned(some * j + i)) + (m[2] ^ rel), 0)
        )

    return pl.pallas_call(
        gated(grad_down_kernel, some + 1, len(gates)),
        grid_spec=pltpu.PrefetchScalarGridSpec(
            num_scalar_prefetch=1,
            grid=(BLOCKS // some,),
            in_specs=[spec(i) for i in range(some)]
            + [pl.BlockSpec((rows, width), lambda j, m: (0, 0), pipeline_mode=pl.Buffered(1))]
            + gate_specs(gates),
            out_specs=pl.BlockSpec((2, some, block // 2, width), lambda j, m: (0, j, 0, 0)),
        ),
        out_shape=jax.ShapeDtypeStruct((2, BLOCKS, block // 2, width), BF16),
        compiler_params=params(1),
        cost_estimate=cost(6),
        name="grad_down",
    )(meta, *[active_t] * some, grad_second, *gates)


def attend_back_kernel(
    meta,
    x_t_ref,
    qkv_ref,
    mixed_t_ref,
    grad_mixed_ref,
    lse_ref,
    grad_qkv_ref,
    grad_w_ref,
    grad_bias_ref,
    grad_scr,
):
    seq = pl.program_id(0)
    length = meta[3 + seq]
    rows, wide = qkv_ref.shape[1:]
    part = wide // 3
    lane = lax.broadcasted_iota(jnp.int32, (rows, 128), 1)
    key_ok = lax.broadcasted_iota(jnp.int32, (rows, rows), 0) < length
    start = pl.multiple_of(seq * rows, 128)

    @pl.when(seq == 0)
    def _():
        grad_bias_ref[...] = jnp.zeros_like(grad_bias_ref)

    for pair in range(part // 128):
        cut = pair * 128
        query = qkv_ref[0, :, cut : cut + 128] * jnp.asarray(0.125, BF16)
        key = qkv_ref[0, :, part + cut : part + cut + 128]
        value = qkv_ref[0, :, 2 * part + cut : 2 * part + cut + 128]
        grad_out = grad_mixed_ref[0, :, cut : cut + 128]
        product = grad_out.astype(F32).T * mixed_t_ref[cut : cut + 128, :].astype(F32)
        key_t = key.T
        grad_query, grad_key, grad_value = [], 0.0, 0.0
        for head in range(2):
            keep = (lane >= 64) == (head == 1)
            query_one = jnp.where(keep, query, jnp.zeros_like(query))
            grad_one = jnp.where(keep, grad_out, jnp.zeros_like(grad_out))
            inner = slice(64 * head, 64 * head + 64)
            delta = jnp.sum(product[inner], axis=0, keepdims=True)
            scores = jnp.where(key_ok, dot_nt(key, query_one), -1e30)
            prob = jnp.exp(scores - lse_ref[0, 2 * pair + head])
            grad_prob = dot_nt(value, grad_one)
            grad_scores = (prob * (grad_prob - delta)).astype(BF16)
            grad_value = grad_value + dot_nn(prob.astype(BF16), grad_one)
            grad_key = grad_key + dot_nn(grad_scores, query_one)
            grad_query.append(dot_nn(key_t[inner], grad_scores) * 0.125)
        grads = (jnp.concatenate(grad_query, axis=0).T, grad_key, grad_value)
        for kind, grad in enumerate(grads):
            grad = grad.astype(BF16)
            to = slice(kind * part + cut, kind * part + cut + 128)
            grad_scr[pl.ds(start, rows), to] = grad
            grad_qkv_ref[0, :, to] = grad
            grad_bias_ref[:, to] += column_sum(grad)

    @pl.when(seq == pl.num_programs(0) - 1)
    def _():
        store_blocks(meta, grad_w_ref, dot_nn(x_t_ref[...], grad_scr[...]), slice(None))


def attend_back(meta, x_t, qkv, mixed_t, grad_mixed, lse, *gates):
    seqs, length, wide = qkv.shape
    width, rows = x_t.shape
    part = wide // 3
    block_rows = width // (2 * BLOCKS)
    by_seq = lambda cols: pl.BlockSpec((1, length, cols), lambda s, m: (s, 0, 0))
    return pl.pallas_call(
        gated(attend_back_kernel, 5, len(gates)),
        grid_spec=pltpu.PrefetchScalarGridSpec(
            num_scalar_prefetch=1,
            grid=(seqs,),
            in_specs=[
                pl.BlockSpec((width, rows), lambda s, m: (0, 0), pipeline_mode=pl.Buffered(1)),
                by_seq(wide),
                pl.BlockSpec((part, length), lambda s, m: (0, s)),
                by_seq(part),
                pl.BlockSpec((1, HEADS // 2, 1, length), lambda s, m: (s, 0, 0, 0)),
                *gate_specs(gates),
            ],
            out_specs=[
                by_seq(wide),
                pl.BlockSpec((2, BLOCKS, block_rows, wide), lambda s, m: (0, 0, 0, 0)),
                pl.BlockSpec((1, wide), lambda s, m: (0, 0)),
            ],
            scratch_shapes=[pltpu.VMEM((rows, wide), BF16)],
        ),
        out_shape=[
            jax.ShapeDtypeStruct((seqs, length, wide), BF16),
            jax.ShapeDtypeStruct((2, BLOCKS, block_rows, wide), BF16),
            jax.ShapeDtypeStruct((1, wide), F32),
        ],
        compiler_params=params(1),
        cost_estimate=cost(16),
        name="attend_back",
    )(meta, x_t, qkv, mixed_t, grad_mixed, lse, *gates)


def input_kernel(
    meta, branch_ref, grad_mine, grad_other, w_mine, w_other, out_ref, scr_mine, scr_other
):
    @pl.when(pl.program_id(0) == 0)
    def _():
        place_rows(meta, w_mine, scr_mine, slice(None), slice(None))
        place_rows(meta, w_other, scr_other, slice(None), slice(None))

    total = branch_ref[...].astype(F32) + dot_nt(grad_mine[...], scr_mine[...])
    out_ref[...] = total + dot_nt(grad_other[...], scr_other[...])


def finish_kernel(moves, row_step, meta, *refs):
    parts, outs = refs[:2], refs[2:]
    for rel in range(4):
        part = parts[rel & 1].at[rel >> 1]
        x_at, core = meta[1] ^ (rel >> 1), meta[2] ^ (rel & 1)
        rows = part.shape[0]
        at = pl.ds(pl.multiple_of(x_at * rows + core * row_step, 16), rows)
        for columns, out, first, step in moves:
            size = columns.stop - columns.start
            to = pl.ds(pl.multiple_of(first + core * step, 128), size)
            outs[out][at, to] = part[:, columns].astype(F32)


def finish(meta, parts, moves, row_step, shapes):
    whole = lambda shape: pl.BlockSpec(shape, lambda i, m: (0,) * len(shape))
    return pl.pallas_call(
        functools.partial(finish_kernel, moves, row_step),
        grid_spec=pltpu.PrefetchScalarGridSpec(
            num_scalar_prefetch=1,
            grid=(1,),
            in_specs=[whole(p.shape) for p in parts],
            out_specs=[whole(shape) for shape in shapes],
        ),
        out_shape=[jax.ShapeDtypeStruct(shape, F32) for shape in shapes],
        compiler_params=params(1),
        cost_estimate=cost(2),
        name="finish",
    )(meta, *parts)


def together(*arrays):
    return lax.optimization_barrier(arrays)


CORE, X, Y, NEAR, FAR = 1, 2, 4, 8, 16
DEVICES = 32


def swap(array, mask):
    pairs = [(i, i ^ mask) for i in range(DEVICES)]
    return lax.ppermute(array, ("shard", "rep"), pairs)


def gather_z(piece):
    came = [swap(piece, mask) for mask in (FAR, NEAR, NEAR | FAR)]
    return jnp.stack([piece] + came)


def double(held, mask):
    return jnp.concatenate([held, swap(held, mask)], axis=0)


def plane_hops(held):
    return [swap(held, mask) for mask in (Y, X, X | Y)]


def plane_join(held, by_y, by_x, across):
    low = jnp.concatenate([held, by_y], axis=0)
    return jnp.stack([low, jnp.concatenate([by_x, across], axis=0)])


def gather_plane(held):
    return plane_join(held, *plane_hops(held))


def add(*terms):
    total = terms[0].astype(F32)
    for term in terms[1:]:
        total = total + term.astype(F32)
    return total.astype(BF16)


def sum_z(parts):
    return add(
        parts[0],
        *[swap(parts[i], mask) for i, mask in ((1, FAR), (2, NEAR), (3, NEAR | FAR))],
    )


def plane_sends(kept, came):
    cut = BLOCKS // 2
    pick = lambda a, x, y: a[x, cut:] if y else a[x, :cut]
    parts = [[add(pick(kept, x, y), pick(came, x, y)) for y in range(2)] for x in range(2)]
    return [
        parts[0][0],
        swap(parts[0][1], Y),
        swap(parts[1][0], X),
        swap(parts[1][1], X | Y),
    ]


def plane_sum(terms):
    return [add(*[t[i] for t in terms]) for i in range(4)]


def local(
    fast,
    tokens,
    lengths,
    w_qkv,
    b_query,
    b_value,
    w_out,
    b_out,
    ln1_gain,
    ln1_bias,
    w_up,
    b_up,
    w_down,
    b_down,
    ln2_gain,
    ln2_bias,
    cotangent,
):
    seqs, seq_len, width = tokens.shape
    rows = seqs * seq_len
    hidden_width = w_up.shape[1]
    half = width // 2
    groups = GROUPS
    up_cut, out_cut = hidden_width // (2 * groups), half // groups
    vectors = (b_query, b_value, b_out, ln1_gain, ln1_bias, b_down, ln2_gain, ln2_bias, b_up)

    if fast:
        shard, rep = lax.axis_index("shard"), lax.axis_index("rep")
        x_at, core = rep // 2, rep % 2
    else:
        shard = rep = x_at = core = jnp.int32(0)
    block = width // BLOCKS
    quarter = block // 2
    meta = jnp.concatenate(
        [jnp.stack([shard, x_at, core]).astype(jnp.int32), lengths.astype(jnp.int32)]
    )

    def qkv_parts(w):
        return w.reshape(-1, 2, quarter, 3, 2, half)

    def up_parts(up, out):
        up = up.reshape(-1, 2, quarter, 2, groups, up_cut)
        out = out.reshape(-1, 2, quarter, 2, groups, out_cut)
        return jnp.concatenate([up, out], axis=-1)

    if fast:
        qkv_piece, up_piece, down_piece = pack(meta, w_qkv, w_up, w_out, w_down, vectors)
        qkv_z, up_piece, down_piece = together(gather_z(qkv_piece), up_piece, down_piece)
        table = qkv_z[:, quarter:, : 128 + b_up.shape[0]]
        up_z = double(double(up_piece[None], FAR), NEAR)
        down_z = double(down_piece[None], FAR)
        qkv_mine, up_z, down_z, table, table_y = together(
            gather_plane(qkv_z[:, :quarter]), up_z, down_z, table, swap(table, Y)
        )
        vec, b_up_row, *bias = small_call(
            functools.partial(unpack_kernel, block),
            "unpack",
            meta,
            (table, table_y),
            ((8, width), (1, hidden_width), (1, 3 * half), (1, 3 * half)),
            ((16, width),),
        )
        qkv_w = qkv_mine, swap(qkv_mine, CORE)
        up_hops, down_z = plane_hops(up_z), double(down_z, NEAR)
    else:
        everything = lambda a: lax.all_gather(a, "shard", axis=0, tiled=True)
        full = [everything(v) for v in vectors]
        order = [turned(p) for p in range(BLOCKS)]
        both = lambda a: (a[0][:, order], a[1][:, order])
        qkv_w = both(
            qkv_parts(everything(w_qkv))
            .transpose(4, 1, 0, 2, 3, 5)
            .reshape(2, 2, BLOCKS, quarter, 3 * half)
        )
        up_w = both(
            up_parts(everything(w_up), everything(w_out))
            .transpose(3, 1, 0, 2, 4, 5)
            .reshape(2, 2, BLOCKS, quarter, -1)
        )
        down_w = both(
            everything(w_down).reshape(BLOCKS, 2, 2, -1, width).transpose(1, 2, 0, 3, 4)
        )
        full = [v.astype(F32) for v in full]
        bias = jnp.stack(
            [full[0].reshape(2, half), jnp.zeros((2, half), F32), full[1].reshape(2, half)], axis=1
        ).reshape(2, 1, 3 * half)
        vec = jnp.stack(full[2:8] + [jnp.zeros_like(full[0])] * 2)
        b_up_row = full[8].reshape(1, -1)
    x_rows = tokens.reshape(rows, width)
    heads = [list(attend(meta, tokens, qkv_w[i], bias[i])) for i in range(2)]
    if fast:
        *up_hops, down_z, heads[0][1], heads[1][1] = together(
            *up_hops, down_z, heads[0][1], heads[1][1]
        )
        up_mine = plane_join(up_z, *up_hops)
        up_w = up_mine, swap(up_mine, CORE)
    qkv, mixed, mixed_t, lse, (x_t, _) = zip(*heads)
    mixed_rows = [m.reshape(rows, half) for m in mixed]
    up_shape, out_shape, down_shape = (width, hidden_width), (width, width), (hidden_width, width)
    hat, scale, norm_t, active, active_t, slope, up_full, out_full = by_chunk(
        up_kernel,
        "feed_up",
        26,
        meta,
        (b_up_row,),
        (x_rows, *mixed_rows, *up_w, vec),
        (),
        (
            ("whole", (rows, width), F32),
            ("whole", (rows, 128), F32),
            ("whole", (width, rows), BF16),
            ("cols", (rows, hidden_width), BF16),
            ("rows", (hidden_width, rows), BF16),
            ("cols", (rows, hidden_width), BF16),
            ("whole", up_shape, BF16),
            ("whole", out_shape, BF16),
        ),
        (((rows, width), BF16),),
    )
    row, fixed = "row", "sum"
    if fast:
        active, *hops = together(active, *plane_hops(down_z))
        down_mine = plane_join(down_z, *hops)
        down_w = down_mine, swap(down_mine, CORE)
    layer_out, grad_second, vec_two, down_full = by_tile(
        functools.partial(down_kernel, seq_len),
        "feed_down",
        14,
        meta,
        (hat, active, cotangent.reshape(rows, width)),
        (*down_w, vec),
        (),
        (
            (row, width, BF16),
            (row, width, BF16),
            (fixed, (8, width), F32),
            (fixed, down_shape, BF16),
        ),
        (),
    )
    down_send = grad_down(1, meta, active_t, grad_second)
    down_keep = grad_down(0, meta, active_t, grad_second, down_send)
    gates = (down_keep,)
    if fast:
        down_plane = plane_sends(down_keep, swap(down_send, CORE))
        gates = (down_plane[0],)
    grad_hidden, grad_branch, *grad_mixed, vec_one, grad_b_up = by_chunk(
        rest_kernel,
        "feed_back",
        22,
        meta,
        (up_full, slope),
        (grad_second, hat, scale, out_full, vec),
        gates,
        (
            ("cols", (rows, hidden_width), BF16),
            ("whole", (rows, width), BF16),
            ("whole", (rows, half), BF16),
            ("whole", (rows, half), BF16),
            ("whole", (8, width), F32),
            ("cols", (1, hidden_width), F32),
        ),
        (((rows, width), F32),),
        (down_full,),
    )
    gates = ()
    if fast:
        down_parts = plane_sum(down_plane)
        gates = tuple(down_parts)
    up_send = grad_up(1, meta, norm_t, mixed_t, grad_hidden, grad_branch, *gates)
    if fast:
        up_send, *down_parts = together(up_send, *down_parts)
    up_keep = grad_up(0, meta, norm_t, mixed_t, grad_hidden, grad_branch, up_send)
    gates = (up_keep,)
    if fast:
        up_plane = plane_sends(up_keep, swap(up_send, CORE))
        down_piece = sum_z(down_parts)
        gates = (up_plane[0],)
    grad_mixed = [g.reshape(seqs, seq_len, half) for g in grad_mixed]

    def back(i, *gates):
        return attend_back(meta, x_t, qkv[i], mixed_t[i], grad_mixed[i], lse[i], *gates)

    other_qkv, qkv_send, other_bias = back(1, *gates)
    gates = (qkv_send,)
    if fast:
        down_piece, qkv_send = together(down_piece, qkv_send)
        gates = (qkv_send, up_plane[1], up_plane[2])
    mine_qkv, qkv_keep, mine_bias = back(0, *gates)
    gates = (qkv_keep,)
    if fast:
        qkv_plane = plane_sends(qkv_keep, swap(qkv_send, CORE))
        down_piece, qkv_plane[0], *up_plane = together(down_piece, qkv_plane[0], *up_plane)
        down_both = jnp.stack([down_piece, swap(down_piece, X)])
        up_parts_sum = plane_sum(up_plane)
        up_near = swap(jnp.stack(up_parts_sum[2:]), NEAR)
        down_quarters = down_both, swap(down_both, CORE)
        gates = (qkv_plane[0], up_parts_sum[0])
    (input_grad,) = by_tile(
        input_kernel,
        "input_grad",
        10,
        meta,
        (grad_branch, mine_qkv.reshape(rows, -1), other_qkv.reshape(rows, -1)),
        qkv_w,
        gates,
        ((row, width, F32),),
        ((width, 3 * half), (width, 3 * half)),
    )

    (total,) = small_call(
        sums_kernel,
        "sums",
        meta,
        (vec_one, vec_two, grad_b_up, mine_bias, other_bias),
        ((16, width),),
        gates=(input_grad,),
    )
    if fast:
        input_grad, up_near, *qkv_plane[1:3] = together(input_grad, up_near, *qkv_plane[1:3])
        up_low = [add(up_parts_sum[i], up_near[i]) for i in range(2)]
        came, qkv_plane[3] = together(swap(total, CORE), qkv_plane[3])
        total = total + came
        qkv_parts_sum = plane_sum(qkv_plane)
        qkv_hops = [swap(qkv_parts_sum[i], m) for i, m in ((1, FAR), (2, NEAR), (3, NEAR | FAR))]
        came, up_far, *qkv_hops = together(swap(total, X), swap(up_low[1], FAR), *qkv_hops)
        total = total + came
        up_piece = add(up_low[0], up_far)
        qkv_piece = add(qkv_parts_sum[0], *qkv_hops)
        came, up_x, qkv_x = together(swap(total, Y), swap(up_piece, X), swap(qkv_piece, X))
        total = total + came
        total = total + swap(total, NEAR)
        total = total + swap(total, FAR)
        up_both = jnp.stack([up_piece, up_x])
        up_core = swap(up_both, CORE)
        up_quarters = up_both, up_core
        qkv_both = jnp.stack([qkv_piece, qkv_x])
        qkv_quarters = qkv_both, swap(qkv_both, CORE)
        sums = small_call(
            functools.partial(own_sums_kernel, block),
            "own_sums",
            meta,
            (total,),
            ((block,),) * 8 + (b_up.shape,),
        )
        step = up_cut + out_cut
        up_moves = [
            move
            for g in range(groups)
            for move in (
                (slice(g * step, g * step + up_cut), 0, g * up_cut, hidden_width // 2),
                (slice(g * step + up_cut, (g + 1) * step), 1, g * out_cut, half),
            )
        ]
        qkv_moves = [(slice(k * half, (k + 1) * half), 0, k * width, half) for k in range(3)]
        (grad_w_down,) = finish(
            meta,
            down_quarters,
            [(slice(0, width), 0, 0, 0)],
            w_down.shape[0] // 2,
            [w_down.shape],
        )
        grad_w_up, grad_w_out = finish(meta, up_quarters, up_moves, 0, [w_up.shape, w_out.shape])
        (grad_w_qkv,) = finish(meta, qkv_quarters, qkv_moves, 0, [w_qkv.shape])
    else:
        total_of = lambda a: lax.psum(
            lax.psum_scatter(a, "shard", scatter_dimension=0, tiled=True), "rep"
        )
        sums = [total_of(g) for g in (*total[:8], total[8:12].reshape(-1))]
        order = [turned(p) for p in range(BLOCKS)]
        down_keep, down_send, up_keep, up_send = (
            a[:, order] for a in (down_keep, down_send, up_keep, up_send)
        )
        down = jnp.stack([down_keep, down_send]).transpose(2, 0, 1, 3, 4)
        grad_w_down = total_of(down.reshape(hidden_width, width).astype(F32))
        up = jnp.stack([up_keep, up_send]).reshape(
            2, 2, BLOCKS, quarter, groups, up_cut + out_cut
        )
        up = up.transpose(2, 1, 3, 0, 4, 5)
        grad_w_up = total_of(up[..., :up_cut].reshape(width, hidden_width).astype(F32))
        grad_w_out = total_of(up[..., up_cut:].reshape(width, width).astype(F32))
        qkv_sum = jnp.stack([qkv_keep[:, order], qkv_send[:, order]])
        qkv_sum = qkv_sum.reshape(2, 2, BLOCKS, quarter, 3, half)
        qkv_sum = qkv_sum.transpose(2, 1, 3, 4, 0, 5).reshape(width, 3 * width)
        grad_w_qkv = total_of(qkv_sum.astype(F32))
    return (
        layer_out.reshape(seqs, seq_len, width),
        input_grad.reshape(seqs, seq_len, width),
        grad_w_qkv,
        sums[0],
        sums[1],
        grad_w_out,
        sums[2],
        sums[3],
        sums[4],
        grad_w_up,
        sums[8],
        grad_w_down,
        sums[5],
        sums[6],
        sums[7],
    )


def solution(mesh):
    fast = mesh.shape["shard"] == BLOCKS and mesh.shape["rep"] == 4
    by_seq = P(("shard", "rep"), None, None)
    one, two = P("shard"), P("shard", None)
    in_specs = (by_seq, P(("shard", "rep")), two, one, one, two, one, one, one)
    in_specs = in_specs + (two, one, two, one, one, one, by_seq)
    out_specs = (by_seq, by_seq, two, one, one, two, one, one, one, two, one, two, one, one, one)
    return jax.shard_map(
        functools.partial(local, fast),
        mesh=mesh,
        in_specs=in_specs,
        out_specs=out_specs,
        check_vma=False,
    )
```

```python
import functools

import jax
import jax.numpy as jnp
from jax import lax
from jax.experimental import pallas as pl
from jax.experimental.pallas import tpu as pltpu
from jax.sharding import PartitionSpec as P

HEADS = 12
EPS = 1e-05
F32 = jnp.float32
BF16 = jnp.bfloat16
BLOCKS = 8
GROUPS = 3
VMEM_LIMIT = 58 * 1024 * 1024


def dot_nn(a, b):
    return lax.dot_general(a, b, (((1,), (0,)), ((), ())), preferred_element_type=F32)


def dot_nt(a, b):
    return lax.dot_general(a, b, (((1,), (1,)), ((), ())), preferred_element_type=F32)


def dot_tn(a, b):
    return lax.dot_general(a, b, (((0,), (0,)), ((), ())), preferred_element_type=F32)


def params(grid_dims):
    return pltpu.CompilerParams(
        dimension_semantics=("arbitrary",) * grid_dims, vmem_limit_bytes=VMEM_LIMIT
    )


def cost(micros):
    return pl.CostEstimate(flops=int(micros * 1.15e9), bytes_accessed=1 << 20, transcendentals=0)


def gated(kernel, inputs, gates):
    def body(*refs):
        kernel(*refs[: inputs + 1], *refs[inputs + 1 + gates :])

    return body


def gate_specs(gates):
    return [pl.BlockSpec(memory_space=pl.ANY)] * len(gates)


def turned(place):
    return ((place & 1) << 2) | (place & 2) | ((place >> 2) & 1)


def place_rows(meta, source, target, columns, cut):
    rows = source.shape[2]
    for half in range(2):
        for block in range(BLOCKS):
            start = (meta[0] ^ turned(block)) * (2 * rows) + (meta[1] ^ half) * rows
            target[pl.ds(pl.multiple_of(start, 16), rows), cut] = source[half, block, :, columns]


def pack_kernel(groups, *refs):
    meta, w_qkv, w_up, w_out, w_down, *vectors, qkv_ref, up_ref, down_ref = refs
    rows, wide = up_ref.shape[0], qkv_ref.shape[1]
    half = wide // 3
    up_cut, out_cut = w_up.shape[1] // (2 * groups), w_out.shape[1] // (2 * groups)
    at = pl.ds(pl.multiple_of(meta[1] * rows, 16), rows)

    def columns(start, size):
        return pl.ds(pl.multiple_of(start, 128), size)

    for kind in range(3):
        start = (2 * kind + meta[2]) * half
        qkv_ref[:rows, kind * half : (kind + 1) * half] = w_qkv[at, columns(start, half)]
    for group in range(groups):
        base = group * (up_cut + out_cut)
        start = (meta[2] * groups + group) * up_cut
        up_ref[:, base : base + up_cut] = w_up[at, columns(start, up_cut)]
        start = (meta[2] * groups + group) * out_cut
        up_ref[:, base + up_cut : base + up_cut + out_cut] = w_out[at, columns(start, out_cut)]
    rows_down = down_ref.shape[0]
    start = (2 * meta[2] + meta[1]) * rows_down
    down_ref[...] = w_down[pl.ds(pl.multiple_of(start, 16), rows_down), :]
    *short, long = vectors
    extra = qkv_ref.shape[0] - rows
    small = short[0].shape[0]
    place = lax.broadcasted_iota(jnp.int32, (extra, small), 0)
    table = jnp.zeros((extra, small), F32)
    for i, v in enumerate(short):
        table = jnp.where(place == i, v[...].astype(F32).reshape(1, small), table)
    qkv_ref[rows:, :] = jnp.zeros((extra, wide), BF16)
    qkv_ref[rows:, :small] = table.astype(BF16)
    size = long.shape[0]
    wide_row = jnp.broadcast_to(long[...].astype(F32).reshape(1, size), (extra, size))
    qkv_ref[rows:, 128 : 128 + size] = wide_row.astype(BF16)


def pack(meta, w_qkv, w_up, w_out, w_down, vectors):
    rows = w_up.shape[0] // 2
    whole = lambda a: pl.BlockSpec(a.shape, lambda i, m: (0,) * a.ndim)
    shapes = [
        (rows + 16, w_qkv.shape[1] // 2),
        (rows, (w_up.shape[1] + w_out.shape[1]) // 2),
        (w_down.shape[0] // 4, w_down.shape[1]),
    ]
    outs = [jax.ShapeDtypeStruct(shape, BF16) for shape in shapes]
    operands = (w_qkv, w_up, w_out, w_down, *vectors)
    return pl.pallas_call(
        functools.partial(pack_kernel, GROUPS),
        grid_spec=pltpu.PrefetchScalarGridSpec(
            num_scalar_prefetch=1,
            grid=(1,),
            in_specs=[whole(a) for a in operands],
            out_specs=[whole(o) for o in outs],
        ),
        out_shape=outs,
        compiler_params=params(1),
        cost_estimate=cost(2),
        name="pack",
    )(meta, *operands)


def shard_columns(shard, block, width, lanes):
    lane = lax.broadcasted_iota(jnp.int32, (lanes, width), 0)
    column = lax.broadcasted_iota(jnp.int32, (lanes, width), 1)
    return (lane < block) & (column == lane + shard * block)


def unpack_kernel(block, meta, near_ref, far_ref, vec_ref, b_up_ref, mine_ref, other_ref, scr):
    width = vec_ref.shape[1]
    half, size = width // 2, b_up_ref.shape[1] // BLOCKS
    total = jnp.zeros(scr.shape, F32)
    for place in range(BLOCKS):
        source = (near_ref, far_ref)[place // 4]
        rows = source[place % 4]
        shard = meta[0] ^ turned(place)
        spread = shard_columns(shard, block, width, 128).astype(F32).astype(BF16)
        total = total + dot_nn(rows[:, :128], spread)
        to = pl.ds(pl.multiple_of(shard * size, 128), size)
        b_up_ref[:, to] = rows[:1, 128 : 128 + size].astype(F32)
    scr[...] = total
    vec_ref[...] = jnp.zeros_like(vec_ref)
    vec_ref[0:6, :] = total[2:8]
    for rel, out in enumerate((mine_ref, other_ref)):
        cut = pl.ds(pl.multiple_of((meta[2] ^ rel) * half, 128), half)
        out[...] = jnp.zeros_like(out)
        out[:, :half] = scr[0:1, cut]
        out[:, 2 * half :] = scr[1:2, cut]


def small_call(kernel, name, meta, operands, shapes, scratch=(), gates=()):
    whole = lambda a: pl.BlockSpec(a.shape, lambda i, m: (0,) * len(a.shape))
    outs = [jax.ShapeDtypeStruct(shape, F32) for shape in shapes]
    return pl.pallas_call(
        gated(kernel, len(operands), len(gates)),
        grid_spec=pltpu.PrefetchScalarGridSpec(
            num_scalar_prefetch=1,
            grid=(1,),
            in_specs=[whole(a) for a in operands] + gate_specs(gates),
            out_specs=[whole(o) for o in outs],
            scratch_shapes=[pltpu.VMEM(shape, F32) for shape in scratch],
        ),
        out_shape=outs,
        compiler_params=params(1),
        cost_estimate=cost(2),
        name=name,
    )(meta, *operands, *gates)


def sums_kernel(meta, vec_one, vec_two, b_up, bias_mine, bias_other, out_ref):
    width = out_ref.shape[1]
    half = width // 2
    out_ref[...] = jnp.zeros_like(out_ref)
    for rel, source in enumerate((bias_mine, bias_other)):
        to = pl.ds(pl.multiple_of((meta[2] ^ rel) * half, 128), half)
        out_ref[0:1, to] = source[:, :half]
        out_ref[1:2, to] = source[:, 2 * half :]
    out_ref[2:5, :] = vec_one[0:3, :]
    out_ref[5:8, :] = vec_two[0:3, :]
    for i in range(b_up.shape[1] // width):
        out_ref[8 + i : 9 + i, :] = b_up[:, i * width : (i + 1) * width]


def own_sums_kernel(block, meta, sum_ref, *outs):
    *short, b_up_ref = outs
    width, size = sum_ref.shape[1], b_up_ref.shape[0]
    pick = shard_columns(meta[0], block, width, 128).astype(F32)
    own = lax.dot_general(
        sum_ref[0:8, :],
        pick,
        (((1,), (1,)), ((), ())),
        precision=lax.Precision.HIGHEST,
        preferred_element_type=F32,
    )
    each = width // size
    cut = pl.ds(pl.multiple_of(lax.rem(meta[0], each) * size, 128), size)
    b_up_ref[...] = sum_ref[pl.ds(8 + lax.div(meta[0], each), 1), cut].reshape(size)
    for i, out in enumerate(short):
        out[...] = own[i : i + 1, :block].reshape(block)


def attend_kernel(meta, x_ref, w_ref, bias_ref, qkv_ref, mixed_ref, mixed_t_ref, lse_ref, x_t_ref, w_scr):
    seq = pl.program_id(0)
    wide = w_scr.shape[1]
    part = wide // 3

    @pl.when(seq == 0)
    def _():
        place_rows(meta, w_ref, w_scr, slice(None), slice(None))

    length = meta[3 + seq]
    x_t_ref[...] = x_ref[0].T
    qkv = (dot_nn(x_ref[0], w_scr[...]) + bias_ref[...]).astype(BF16)
    qkv_ref[0] = qkv
    rows = qkv.shape[0]
    lane = lax.broadcasted_iota(jnp.int32, (rows, 128), 1)
    key_ok = lax.broadcasted_iota(jnp.int32, (rows, rows), 0) < length
    for pair in range(part // 128):
        cut = pair * 128
        query = qkv[:, cut : cut + 128] * jnp.asarray(0.125, BF16)
        key = qkv[:, part + cut : part + cut + 128]
        value_t = qkv[:, 2 * part + cut : 2 * part + cut + 128].T
        outs = []
        for head in range(2):
            query_one = jnp.where((lane >= 64) == (head == 1), query, jnp.zeros_like(query))
            scores = jnp.where(key_ok, dot_nt(key, query_one), -1e30)
            top = jnp.max(scores, axis=0, keepdims=True)
            exp_scores = jnp.exp(scores - top)
            total = jnp.sum(exp_scores, axis=0, keepdims=True)
            lse_ref[0, 2 * pair + head] = top + jnp.log(total)
            out = dot_nn(value_t[64 * head : 64 * head + 64], exp_scores.astype(BF16))
            outs.append(out * (1.0 / total))
        mixed_t = jnp.concatenate(outs, axis=0)
        mixed_t_ref[cut : cut + 128, :] = mixed_t.astype(BF16)
        mixed_ref[0, :, cut : cut + 128] = mixed_t.T.astype(BF16)


def attend(meta, x, weight, bias):
    seqs, length, width = x.shape
    wide = weight.shape[3]
    part = wide // 3
    half_heads = HEADS // 2
    whole = lambda s, m: (0, 0, 0, 0)
    return pl.pallas_call(
        attend_kernel,
        grid_spec=pltpu.PrefetchScalarGridSpec(
            num_scalar_prefetch=1,
            grid=(seqs,),
            in_specs=[
                pl.BlockSpec((1, length, width), lambda s, m: (s, 0, 0)),
                pl.BlockSpec(weight.shape, whole, pipeline_mode=pl.Buffered(1)),
                pl.BlockSpec((1, wide), lambda s, m: (0, 0)),
            ],
            out_specs=[
                pl.BlockSpec((1, length, wide), lambda s, m: (s, 0, 0)),
                pl.BlockSpec((1, length, part), lambda s, m: (s, 0, 0)),
                pl.BlockSpec((part, length), lambda s, m: (0, s)),
                pl.BlockSpec((1, half_heads, 1, length), lambda s, m: (s, 0, 0, 0)),
                pl.BlockSpec((width, length), lambda s, m: (0, s)),
            ],
            scratch_shapes=[pltpu.VMEM((width, wide), BF16)],
        ),
        out_shape=[
            jax.ShapeDtypeStruct((seqs, length, wide), BF16),
            jax.ShapeDtypeStruct((seqs, length, part), BF16),
            jax.ShapeDtypeStruct((part, seqs * length), BF16),
            jax.ShapeDtypeStruct((seqs, half_heads, 1, length), F32),
            jax.ShapeDtypeStruct((width, seqs * length), BF16),
        ],
        compiler_params=params(1),
        cost_estimate=cost(11),
        name="attend_forward",
    )(meta, x, weight, bias)


def gelu_and_slope(hidden):
    size = jnp.abs(hidden)
    bell = jnp.exp2(hidden * hidden * -0.7213475204444817)
    t = 1.0 / (1.0 + (0.3275911 * 0.7071067811865476) * size)
    poly = t * (
        0.5 * 0.254829592
        + t
        * (
            0.5 * -0.284496736
            + t * (0.5 * 1.421413741 + t * (0.5 * -1.453152027 + t * (0.5 * 1.061405429)))
        )
    )
    tail = poly * bell
    phi = jnp.where(hidden < 0.0, tail, 1.0 - tail)
    return hidden * phi, phi + hidden * bell * 0.3989422804014327


def norm_forward(hidden):
    center = hidden - jnp.mean(hidden, axis=-1, keepdims=True)
    scale = lax.rsqrt(jnp.mean(center * center, axis=-1, keepdims=True) + EPS)
    return center * scale, scale


def norm_back(grad, hat, scale, gain):
    grad_hat = grad * gain
    shift = jnp.mean(grad_hat, axis=-1, keepdims=True)
    along = jnp.mean(grad_hat * hat, axis=-1, keepdims=True)
    return scale * (grad_hat - shift - hat * along)


def column_sum(rows):
    return jnp.sum(rows.astype(F32), axis=0, keepdims=True)


def place_up(meta, mine, other, w_up, w_out):
    hidden_width, width = w_up.shape[1], w_out.shape[1]
    up_cut, out_cut = hidden_width // (2 * GROUPS), width // (2 * GROUPS)
    for rel, source in enumerate((mine, other)):
        core = meta[2] ^ rel
        for group in range(GROUPS):
            base = group * (up_cut + out_cut)
            up_to = pl.multiple_of(core * (hidden_width // 2) + group * up_cut, 128)
            out_to = pl.multiple_of(core * (width // 2) + group * out_cut, 128)
            place_rows(meta, source, w_up, slice(base, base + up_cut), pl.ds(up_to, up_cut))
            place_rows(
                meta,
                source,
                w_out,
                slice(base + up_cut, base + up_cut + out_cut),
                pl.ds(out_to, out_cut),
            )


def place_down(meta, mine, other, w_down):
    rows = mine.shape[2]
    for rel, source in enumerate((mine, other)):
        for half in range(2):
            for block in range(BLOCKS):
                start = (
                    (meta[0] ^ turned(block)) * (4 * rows)
                    + (meta[2] ^ rel) * (2 * rows)
                    + (meta[1] ^ half) * rows
                )
                w_down[pl.ds(pl.multiple_of(start, 16), rows), :] = source[half, block]


def halves_of(meta, width):
    half = width // 2
    return (
        pl.ds(pl.multiple_of(meta[2] * half, 128), half),
        pl.ds(pl.multiple_of((1 - meta[2]) * half, 128), half),
    )


CHUNK = 512


def up_kernel(
    meta,
    x_ref,
    mixed_mine,
    mixed_other,
    up_mine,
    up_other,
    vec_ref,
    b_up_ref,
    hat_ref,
    scale_ref,
    norm_t_ref,
    active_ref,
    active_t_ref,
    slope_ref,
    w_up,
    w_out,
    normed_low,
):
    step = pl.program_id(0)
    width = w_out.shape[1]

    @pl.when(step == 0)
    def _():
        place_up(meta, up_mine, up_other, w_up, w_out)
        b_out, gain, shift = [vec_ref[i : i + 1, :] for i in range(3)]
        rows_mine, rows_other = halves_of(meta, width)
        branch = dot_nn(mixed_mine[...], w_out[rows_mine, :])
        branch = branch + dot_nn(mixed_other[...], w_out[rows_other, :])
        hat, scale = norm_forward(x_ref[...].astype(F32) + (branch + b_out))
        hat_ref[...] = hat
        scale_ref[...] = jnp.broadcast_to(scale, scale_ref.shape)
        normed_low[...] = (hat * gain + shift).astype(BF16)
        norm_t_ref[...] = normed_low[...].T

    cut = pl.ds(pl.multiple_of(step * CHUNK, CHUNK), CHUNK)
    hidden = dot_nn(normed_low[...], w_up[:, cut]) + b_up_ref[...]
    active, slope = gelu_and_slope(hidden)
    slope_ref[...] = slope.astype(BF16)
    active_low = active.astype(BF16)
    active_ref[...] = active_low
    active_t_ref[...] = active_low.T


def down_kernel(
    seq_len,
    meta,
    hat_ref,
    active_ref,
    cot_ref,
    down_mine,
    down_other,
    vec_ref,
    out_ref,
    grad_second_ref,
    grad_vec_ref,
    w_down,
):
    step = pl.program_id(0)
    tile = hat_ref.shape[0]

    @pl.when(step == 0)
    def _():
        grad_vec_ref[...] = jnp.zeros_like(grad_vec_ref)
        place_down(meta, down_mine, down_other, w_down)

    gain_one, shift_one, b_down, gain, shift = [vec_ref[i : i + 1, :] for i in range(1, 6)]
    seq = lax.div(step * tile, seq_len)
    place = lax.broadcasted_iota(jnp.int32, (tile, 1), 0) + lax.rem(step * tile, seq_len)
    valid = place < meta[3 + seq]
    second = dot_nn(active_ref[...], w_down[...])
    normed = hat_ref[...] * gain_one + shift_one
    hat, scale = norm_forward(normed + (second + b_down))
    out_ref[...] = jnp.where(valid, hat * gain + shift, 0.0).astype(BF16)
    grad_result = jnp.where(valid, cot_ref[...].astype(F32), 0.0)
    grad_second = norm_back(grad_result, hat, scale, gain).astype(BF16)
    grad_second_ref[...] = grad_second
    sums = column_sum(grad_second), column_sum(grad_result * hat), column_sum(grad_result)
    for i, total in enumerate(sums):
        grad_vec_ref[i : i + 1, :] += total


def rest_kernel(
    meta,
    grad_second_ref,
    hat_ref,
    scale_ref,
    w_out,
    vec_ref,
    w_down,
    w_up,
    slope_ref,
    grad_hidden_ref,
    grad_branch_ref,
    grad_mixed_mine,
    grad_mixed_other,
    grad_vec_ref,
    grad_b_up_ref,
    total,
):
    step = pl.program_id(0)
    width = w_out.shape[1]

    @pl.when(step == 0)
    def _():
        total[...] = grad_second_ref[...].astype(F32)

    grad_active = dot_nt(grad_second_ref[...], w_down[...])
    grad_hidden = (slope_ref[...].astype(F32) * grad_active).astype(BF16)
    grad_hidden_ref[...] = grad_hidden
    grad_b_up_ref[...] = column_sum(grad_hidden)
    total[...] += dot_nt(grad_hidden, w_up[...])

    @pl.when(step == pl.num_programs(0) - 1)
    def _():
        grad_normed, hat, gain = total[...], hat_ref[...], vec_ref[1:2, :]
        grad_branch = norm_back(grad_normed, hat, scale_ref[:, 0:1], gain).astype(BF16)
        grad_branch_ref[...] = grad_branch
        rows_mine, rows_other = halves_of(meta, width)
        grad_mixed_mine[...] = dot_nt(grad_branch, w_out[rows_mine, :]).astype(BF16)
        grad_mixed_other[...] = dot_nt(grad_branch, w_out[rows_other, :]).astype(BF16)
        grad_vec_ref[...] = jnp.zeros_like(grad_vec_ref)
        sums = column_sum(grad_branch), column_sum(grad_normed * hat), column_sum(grad_normed)
        for i, one in enumerate(sums):
            grad_vec_ref[i : i + 1, :] = one


def by_chunk(kernel, name, micros, meta, cut, wholes, gates, outs, scratch, cut_rows=()):
    hidden_width = cut[-1].shape[1]
    chunked = lambda shape: pl.BlockSpec((shape[0], CHUNK), lambda n, m: (0, n))
    whole = lambda shape: pl.BlockSpec(
        shape, lambda n, m: (0,) * len(shape), pipeline_mode=pl.Buffered(1)
    )
    spec_of = {
        "cols": chunked,
        "rows": lambda shape: pl.BlockSpec((CHUNK, shape[1]), lambda n, m: (n, 0)),
        "whole": lambda shape: pl.BlockSpec(shape, lambda n, m: (0,) * len(shape)),
    }
    return pl.pallas_call(
        gated(kernel, len(cut) + len(cut_rows) + len(wholes), len(gates)),
        grid_spec=pltpu.PrefetchScalarGridSpec(
            num_scalar_prefetch=1,
            grid=(hidden_width // CHUNK,),
            in_specs=[whole(a.shape) for a in wholes]
            + [spec_of["rows"](a.shape) for a in cut_rows]
            + [chunked(a.shape) for a in cut]
            + gate_specs(gates),
            out_specs=[spec_of[kind](shape) for kind, shape, _ in outs],
            scratch_shapes=[pltpu.VMEM(shape, dtype) for shape, dtype in scratch],
        ),
        out_shape=[jax.ShapeDtypeStruct(shape, dtype) for _, shape, dtype in outs],
        compiler_params=params(1),
        cost_estimate=cost(micros),
        name=name,
    )(meta, *wholes, *cut_rows, *cut, *gates)


def by_tile(kernel, name, micros, meta, tiled, wholes, gates, outs, scratch, most=512):
    rows = tiled[0].shape[0]
    tile = min(most, rows)
    by_row = lambda cols: pl.BlockSpec((tile, cols), lambda i, m: (i, 0))
    whole = lambda a: pl.BlockSpec(
        a.shape, lambda i, m: (0,) * a.ndim, pipeline_mode=pl.Buffered(1)
    )
    specs, shapes = [], []
    for kind, size, dtype in outs:
        if kind == "row":
            specs.append(by_row(size))
            shapes.append(jax.ShapeDtypeStruct((rows, size), dtype))
        elif kind == "col":
            specs.append(pl.BlockSpec((size, tile), lambda i, m: (0, i)))
            shapes.append(jax.ShapeDtypeStruct((size, rows), dtype))
        else:
            specs.append(pl.BlockSpec(size, lambda i, m: (0, 0)))
            shapes.append(jax.ShapeDtypeStruct(size, dtype))
    return pl.pallas_call(
        gated(kernel, len(tiled) + len(wholes), len(gates)),
        grid_spec=pltpu.PrefetchScalarGridSpec(
            num_scalar_prefetch=1,
            grid=(rows // tile,),
            in_specs=[by_row(a.shape[1]) for a in tiled]
            + [whole(a) for a in wholes]
            + gate_specs(gates),
            out_specs=specs,
            scratch_shapes=[pltpu.VMEM(shape, BF16) for shape in scratch],
        ),
        out_shape=shapes,
        compiler_params=params(1),
        cost_estimate=cost(micros),
        name=name,
    )(meta, *tiled, *wholes, *gates)


def store_blocks(meta, out_ref, value, cut, first=0):
    rows = out_ref.shape[2]
    for block in range(value.shape[0] // (2 * rows)):
        for half in range(2):
            start = (2 * block + half) * rows
            out_ref[meta[1] ^ half, turned(meta[0] ^ (first + block)), :, cut] = value[
                start : start + rows
            ].astype(BF16)


def grad_up_kernel(
    meta, norm_t_ref, mixed_mine, mixed_other, grad_hidden_ref, grad_branch_ref, out_ref
):
    up_cut = grad_hidden_ref.shape[1]
    store_blocks(meta, out_ref, dot_nn(norm_t_ref[...], grad_hidden_ref[...]), slice(0, up_cut))
    cut = slice(up_cut, out_ref.shape[3])
    few = BLOCKS // 2
    grad_branch = grad_branch_ref[...]
    store_blocks(meta, out_ref, dot_nn(mixed_mine[...], grad_branch), cut, meta[2] * few)
    store_blocks(meta, out_ref, dot_nn(mixed_other[...], grad_branch), cut, (1 - meta[2]) * few)


def grad_up(rel, meta, norm_t, mixed_t, grad_hidden, grad_branch, *gates):
    width, rows = norm_t.shape
    hidden_width = grad_hidden.shape[1]
    groups = 3
    up_cut, out_cut = hidden_width // (2 * groups), width // (2 * groups)
    block_rows = width // (2 * BLOCKS)
    whole = lambda tall: pl.BlockSpec(
        (tall, rows), lambda n, m: (0, 0), pipeline_mode=pl.Buffered(1)
    )
    turn = lambda n, m: (0, (m[2] ^ rel) * groups + n)
    return pl.pallas_call(
        gated(grad_up_kernel, 5, len(gates)),
        grid_spec=pltpu.PrefetchScalarGridSpec(
            num_scalar_prefetch=1,
            grid=(groups,),
            in_specs=[
                whole(width),
                whole(width // 2),
                whole(width // 2),
                pl.BlockSpec((rows, up_cut), turn),
                pl.BlockSpec((rows, out_cut), turn),
                *gate_specs(gates),
            ],
            out_specs=pl.BlockSpec(
                (2, BLOCKS, block_rows, up_cut + out_cut), lambda n, m: (0, 0, 0, n)
            ),
        ),
        out_shape=jax.ShapeDtypeStruct(
            (2, BLOCKS, block_rows, groups * (up_cut + out_cut)), BF16
        ),
        compiler_params=params(1),
        cost_estimate=cost(8),
        name="grad_up",
    )(meta, norm_t, *mixed_t, grad_hidden, grad_branch, *gates)


def grad_down_kernel(meta, *refs):
    blocks, (grad_second_ref, out_ref) = refs[:-2], refs[-2:]
    rows = out_ref.shape[2]
    left = jnp.concatenate([b[...] for b in blocks], axis=0)
    value = dot_nn(left, grad_second_ref[...]).astype(BF16)
    for i in range(len(blocks)):
        for half in range(2):
            start = (2 * i + half) * rows
            out_ref[meta[1] ^ half, i] = value[start : start + rows]


def grad_down(rel, meta, active_t, grad_second, *gates):
    hidden_width, rows = active_t.shape
    width = grad_second.shape[1]
    block = hidden_width // (2 * BLOCKS)
    some = 4

    def spec(i):
        return pl.BlockSpec(
            (block, rows), lambda j, m: (2 * (m[0] ^ turned(some * j + i)) + (m[2] ^ rel), 0)
        )

    return pl.pallas_call(
        gated(grad_down_kernel, some + 1, len(gates)),
        grid_spec=pltpu.PrefetchScalarGridSpec(
            num_scalar_prefetch=1,
            grid=(BLOCKS // some,),
            in_specs=[spec(i) for i in range(some)]
            + [pl.BlockSpec((rows, width), lambda j, m: (0, 0), pipeline_mode=pl.Buffered(1))]
            + gate_specs(gates),
            out_specs=pl.BlockSpec((2, some, block // 2, width), lambda j, m: (0, j, 0, 0)),
        ),
        out_shape=jax.ShapeDtypeStruct((2, BLOCKS, block // 2, width), BF16),
        compiler_params=params(1),
        cost_estimate=cost(6),
        name="grad_down",
    )(meta, *[active_t] * some, grad_second, *gates)


def attend_back_kernel(
    meta,
    x_t_ref,
    qkv_ref,
    mixed_t_ref,
    grad_mixed_ref,
    lse_ref,
    grad_qkv_ref,
    grad_w_ref,
    grad_bias_ref,
    grad_scr,
):
    seq = pl.program_id(0)
    length = meta[3 + seq]
    rows, wide = qkv_ref.shape[1:]
    part = wide // 3
    lane = lax.broadcasted_iota(jnp.int32, (rows, 128), 1)
    key_ok = lax.broadcasted_iota(jnp.int32, (rows, rows), 0) < length
    start = pl.multiple_of(seq * rows, 128)

    @pl.when(seq == 0)
    def _():
        grad_bias_ref[...] = jnp.zeros_like(grad_bias_ref)

    for pair in range(part // 128):
        cut = pair * 128
        query = qkv_ref[0, :, cut : cut + 128] * jnp.asarray(0.125, BF16)
        key = qkv_ref[0, :, part + cut : part + cut + 128]
        value = qkv_ref[0, :, 2 * part + cut : 2 * part + cut + 128]
        grad_out = grad_mixed_ref[0, :, cut : cut + 128]
        product = grad_out.astype(F32).T * mixed_t_ref[cut : cut + 128, :].astype(F32)
        key_t = key.T
        grad_query, grad_key, grad_value = [], 0.0, 0.0
        for head in range(2):
            keep = (lane >= 64) == (head == 1)
            query_one = jnp.where(keep, query, jnp.zeros_like(query))
            grad_one = jnp.where(keep, grad_out, jnp.zeros_like(grad_out))
            inner = slice(64 * head, 64 * head + 64)
            delta = jnp.sum(product[inner], axis=0, keepdims=True)
            scores = jnp.where(key_ok, dot_nt(key, query_one), -1e30)
            prob = jnp.exp(scores - lse_ref[0, 2 * pair + head])
            grad_prob = dot_nt(value, grad_one)
            grad_scores = (prob * (grad_prob - delta)).astype(BF16)
            grad_value = grad_value + dot_nn(prob.astype(BF16), grad_one)
            grad_key = grad_key + dot_nn(grad_scores, query_one)
            grad_query.append(dot_nn(key_t[inner], grad_scores) * 0.125)
        grads = (jnp.concatenate(grad_query, axis=0).T, grad_key, grad_value)
        for kind, grad in enumerate(grads):
            grad = grad.astype(BF16)
            to = slice(kind * part + cut, kind * part + cut + 128)
            grad_scr[pl.ds(start, rows), to] = grad
            grad_qkv_ref[0, :, to] = grad
            grad_bias_ref[:, to] += column_sum(grad)

    @pl.when(seq == pl.num_programs(0) - 1)
    def _():
        store_blocks(meta, grad_w_ref, dot_nn(x_t_ref[...], grad_scr[...]), slice(None))


def attend_back(meta, x_t, qkv, mixed_t, grad_mixed, lse, *gates):
    seqs, length, wide = qkv.shape
    width, rows = x_t.shape
    part = wide // 3
    block_rows = width // (2 * BLOCKS)
    by_seq = lambda cols: pl.BlockSpec((1, length, cols), lambda s, m: (s, 0, 0))
    return pl.pallas_call(
        gated(attend_back_kernel, 5, len(gates)),
        grid_spec=pltpu.PrefetchScalarGridSpec(
            num_scalar_prefetch=1,
            grid=(seqs,),
            in_specs=[
                pl.BlockSpec((width, rows), lambda s, m: (0, 0), pipeline_mode=pl.Buffered(1)),
                by_seq(wide),
                pl.BlockSpec((part, length), lambda s, m: (0, s)),
                by_seq(part),
                pl.BlockSpec((1, HEADS // 2, 1, length), lambda s, m: (s, 0, 0, 0)),
                *gate_specs(gates),
            ],
            out_specs=[
                by_seq(wide),
                pl.BlockSpec((2, BLOCKS, block_rows, wide), lambda s, m: (0, 0, 0, 0)),
                pl.BlockSpec((1, wide), lambda s, m: (0, 0)),
            ],
            scratch_shapes=[pltpu.VMEM((rows, wide), BF16)],
        ),
        out_shape=[
            jax.ShapeDtypeStruct((seqs, length, wide), BF16),
            jax.ShapeDtypeStruct((2, BLOCKS, block_rows, wide), BF16),
            jax.ShapeDtypeStruct((1, wide), F32),
        ],
        compiler_params=params(1),
        cost_estimate=cost(16),
        name="attend_back",
    )(meta, x_t, qkv, mixed_t, grad_mixed, lse, *gates)


def input_kernel(
    meta, branch_ref, grad_mine, grad_other, w_mine, w_other, out_ref, scr_mine, scr_other
):
    @pl.when(pl.program_id(0) == 0)
    def _():
        place_rows(meta, w_mine, scr_mine, slice(None), slice(None))
        place_rows(meta, w_other, scr_other, slice(None), slice(None))

    total = branch_ref[...].astype(F32) + dot_nt(grad_mine[...], scr_mine[...])
    out_ref[...] = total + dot_nt(grad_other[...], scr_other[...])


def finish_kernel(moves, row_step, meta, *refs):
    parts, outs = refs[:2], refs[2:]
    for rel in range(4):
        part = parts[rel & 1].at[rel >> 1]
        x_at, core = meta[1] ^ (rel >> 1), meta[2] ^ (rel & 1)
        rows = part.shape[0]
        at = pl.ds(pl.multiple_of(x_at * rows + core * row_step, 16), rows)
        for columns, out, first, step in moves:
            size = columns.stop - columns.start
            to = pl.ds(pl.multiple_of(first + core * step, 128), size)
            outs[out][at, to] = part[:, columns].astype(F32)


def finish(meta, parts, moves, row_step, shapes):
    whole = lambda shape: pl.BlockSpec(shape, lambda i, m: (0,) * len(shape))
    return pl.pallas_call(
        functools.partial(finish_kernel, moves, row_step),
        grid_spec=pltpu.PrefetchScalarGridSpec(
            num_scalar_prefetch=1,
            grid=(1,),
            in_specs=[whole(p.shape) for p in parts],
            out_specs=[whole(shape) for shape in shapes],
        ),
        out_shape=[jax.ShapeDtypeStruct(shape, F32) for shape in shapes],
        compiler_params=params(1),
        cost_estimate=cost(2),
        name="finish",
    )(meta, *parts)


def together(*arrays):
    return lax.optimization_barrier(arrays)


CORE, X, Y, NEAR, FAR = 1, 2, 4, 8, 16
DEVICES = 32


def swap(array, mask):
    pairs = [(i, i ^ mask) for i in range(DEVICES)]
    return lax.ppermute(array, ("shard", "rep"), pairs)


def gather_z(piece):
    came = [swap(piece, mask) for mask in (FAR, NEAR, NEAR | FAR)]
    return jnp.stack([piece] + came)


def double(held, mask):
    return jnp.concatenate([held, swap(held, mask)], axis=0)


def plane_hops(held):
    return [swap(held, mask) for mask in (Y, X, X | Y)]


def plane_join(held, by_y, by_x, across):
    low = jnp.concatenate([held, by_y], axis=0)
    return jnp.stack([low, jnp.concatenate([by_x, across], axis=0)])


def gather_plane(held):
    return plane_join(held, *plane_hops(held))


def add(*terms):
    total = terms[0].astype(F32)
    for term in terms[1:]:
        total = total + term.astype(F32)
    return total.astype(BF16)


def sum_z(parts):
    return add(
        parts[0],
        *[swap(parts[i], mask) for i, mask in ((1, FAR), (2, NEAR), (3, NEAR | FAR))],
    )


def plane_sends(kept, came):
    cut = BLOCKS // 2
    pick = lambda a, x, y: a[x, cut:] if y else a[x, :cut]
    parts = [[add(pick(kept, x, y), pick(came, x, y)) for y in range(2)] for x in range(2)]
    return [
        parts[0][0],
        swap(parts[0][1], Y),
        swap(parts[1][0], X),
        swap(parts[1][1], X | Y),
    ]


def plane_sum(terms):
    return [add(*[t[i] for t in terms]) for i in range(4)]


def local(
    fast,
    tokens,
    lengths,
    w_qkv,
    b_query,
    b_value,
    w_out,
    b_out,
    ln1_gain,
    ln1_bias,
    w_up,
    b_up,
    w_down,
    b_down,
    ln2_gain,
    ln2_bias,
    cotangent,
):
    seqs, seq_len, width = tokens.shape
    rows = seqs * seq_len
    hidden_width = w_up.shape[1]
    half = width // 2
    groups = GROUPS
    up_cut, out_cut = hidden_width // (2 * groups), half // groups
    vectors = (b_query, b_value, b_out, ln1_gain, ln1_bias, b_down, ln2_gain, ln2_bias, b_up)

    if fast:
        shard, rep = lax.axis_index("shard"), lax.axis_index("rep")
        x_at, core = rep // 2, rep % 2
    else:
        shard = rep = x_at = core = jnp.int32(0)
    block = width // BLOCKS
    quarter = block // 2
    meta = jnp.concatenate(
        [jnp.stack([shard, x_at, core]).astype(jnp.int32), lengths.astype(jnp.int32)]
    )

    def qkv_parts(w):
        return w.reshape(-1, 2, quarter, 3, 2, half)

    def up_parts(up, out):
        up = up.reshape(-1, 2, quarter, 2, groups, up_cut)
        out = out.reshape(-1, 2, quarter, 2, groups, out_cut)
        return jnp.concatenate([up, out], axis=-1)

    if fast:
        qkv_piece, up_piece, down_piece = pack(meta, w_qkv, w_up, w_out, w_down, vectors)
        qkv_z, up_piece, down_piece = together(gather_z(qkv_piece), up_piece, down_piece)
        table = qkv_z[:, quarter:, : 128 + b_up.shape[0]]
        up_z = double(double(up_piece[None], FAR), NEAR)
        down_z = double(down_piece[None], FAR)
        qkv_mine, up_z, down_z, table, table_y = together(
            gather_plane(qkv_z[:, :quarter]), up_z, down_z, table, swap(table, Y)
        )
        vec, b_up_row, *bias = small_call(
            functools.partial(unpack_kernel, block),
            "unpack",
            meta,
            (table, table_y),
            ((8, width), (1, hidden_width), (1, 3 * half), (1, 3 * half)),
            ((16, width),),
        )
        qkv_w = qkv_mine, swap(qkv_mine, CORE)
        up_hops, down_z = plane_hops(up_z), double(down_z, NEAR)
    else:
        everything = lambda a: lax.all_gather(a, "shard", axis=0, tiled=True)
        full = [everything(v) for v in vectors]
        order = [turned(p) for p in range(BLOCKS)]
        both = lambda a: (a[0][:, order], a[1][:, order])
        qkv_w = both(
            qkv_parts(everything(w_qkv))
            .transpose(4, 1, 0, 2, 3, 5)
            .reshape(2, 2, BLOCKS, quarter, 3 * half)
        )
        up_w = both(
            up_parts(everything(w_up), everything(w_out))
            .transpose(3, 1, 0, 2, 4, 5)
            .reshape(2, 2, BLOCKS, quarter, -1)
        )
        down_w = both(
            everything(w_down).reshape(BLOCKS, 2, 2, -1, width).transpose(1, 2, 0, 3, 4)
        )
        full = [v.astype(F32) for v in full]
        bias = jnp.stack(
            [full[0].reshape(2, half), jnp.zeros((2, half), F32), full[1].reshape(2, half)], axis=1
        ).reshape(2, 1, 3 * half)
        vec = jnp.stack(full[2:8] + [jnp.zeros_like(full[0])] * 2)
        b_up_row = full[8].reshape(1, -1)
    x_rows = tokens.reshape(rows, width)
    heads = [list(attend(meta, tokens, qkv_w[i], bias[i])) for i in range(2)]
    if fast:
        *up_hops, down_z, heads[0][1], heads[1][1] = together(
            *up_hops, down_z, heads[0][1], heads[1][1]
        )
        up_mine = plane_join(up_z, *up_hops)
        up_w = up_mine, swap(up_mine, CORE)
    qkv, mixed, mixed_t, lse, (x_t, _) = zip(*heads)
    mixed_rows = [m.reshape(rows, half) for m in mixed]
    up_shape, out_shape, down_shape = (width, hidden_width), (width, width), (hidden_width, width)
    hat, scale, norm_t, active, active_t, slope, up_full, out_full = by_chunk(
        up_kernel,
        "feed_up",
        26,
        meta,
        (b_up_row,),
        (x_rows, *mixed_rows, *up_w, vec),
        (),
        (
            ("whole", (rows, width), F32),
            ("whole", (rows, 128), F32),
            ("whole", (width, rows), BF16),
            ("cols", (rows, hidden_width), BF16),
            ("rows", (hidden_width, rows), BF16),
            ("cols", (rows, hidden_width), BF16),
            ("whole", up_shape, BF16),
            ("whole", out_shape, BF16),
        ),
        (((rows, width), BF16),),
    )
    row, fixed = "row", "sum"
    if fast:
        active, *hops = together(active, *plane_hops(down_z))
        down_mine = plane_join(down_z, *hops)
        down_w = down_mine, swap(down_mine, CORE)
    layer_out, grad_second, vec_two, down_full = by_tile(
        functools.partial(down_kernel, seq_len),
        "feed_down",
        14,
        meta,
        (hat, active, cotangent.reshape(rows, width)),
        (*down_w, vec),
        (),
        (
            (row, width, BF16),
            (row, width, BF16),
            (fixed, (8, width), F32),
            (fixed, down_shape, BF16),
        ),
        (),
    )
    down_send = grad_down(1, meta, active_t, grad_second)
    down_keep = grad_down(0, meta, active_t, grad_second, down_send)
    gates = (down_keep,)
    if fast:
        down_plane = plane_sends(down_keep, swap(down_send, CORE))
        gates = (down_plane[0],)
    grad_hidden, grad_branch, *grad_mixed, vec_one, grad_b_up = by_chunk(
        rest_kernel,
        "feed_back",
        22,
        meta,
        (up_full, slope),
        (grad_second, hat, scale, out_full, vec),
        gates,
        (
            ("cols", (rows, hidden_width), BF16),
            ("whole", (rows, width), BF16),
            ("whole", (rows, half), BF16),
            ("whole", (rows, half), BF16),
            ("whole", (8, width), F32),
            ("cols", (1, hidden_width), F32),
        ),
        (((rows, width), F32),),
        (down_full,),
    )
    gates = ()
    if fast:
        down_parts = plane_sum(down_plane)
        gates = tuple(down_parts)
    up_send = grad_up(1, meta, norm_t, mixed_t, grad_hidden, grad_branch, *gates)
    if fast:
        up_send, *down_parts = together(up_send, *down_parts)
    up_keep = grad_up(0, meta, norm_t, mixed_t, grad_hidden, grad_branch, up_send)
    gates = (up_keep,)
    if fast:
        up_plane = plane_sends(up_keep, swap(up_send, CORE))
        down_piece = sum_z(down_parts)
        gates = (up_plane[0],)
    grad_mixed = [g.reshape(seqs, seq_len, half) for g in grad_mixed]

    def back(i, *gates):
        return attend_back(meta, x_t, qkv[i], mixed_t[i], grad_mixed[i], lse[i], *gates)

    other_qkv, qkv_send, other_bias = back(1, *gates)
    gates = (qkv_send,)
    if fast:
        down_piece, qkv_send = together(down_piece, qkv_send)
        gates = (qkv_send, up_plane[1], up_plane[2])
    mine_qkv, qkv_keep, mine_bias = back(0, *gates)
    gates = (qkv_keep,)
    if fast:
        qkv_plane = plane_sends(qkv_keep, swap(qkv_send, CORE))
        down_x, qkv_plane[0], *up_plane = together(
            swap(down_piece, X), qkv_plane[0], *up_plane
        )
        down_both = jnp.stack([down_piece, down_x])
        up_parts_sum = plane_sum(up_plane)
        up_near = swap(jnp.stack(up_parts_sum[2:]), NEAR)
        down_quarters = down_both, swap(down_both, CORE)
        gates = (qkv_plane[0], up_parts_sum[0])
    (input_grad,) = by_tile(
        input_kernel,
        "input_grad",
        10,
        meta,
        (grad_branch, mine_qkv.reshape(rows, -1), other_qkv.reshape(rows, -1)),
        qkv_w,
        gates,
        ((row, width, F32),),
        ((width, 3 * half), (width, 3 * half)),
    )

    (total,) = small_call(
        sums_kernel,
        "sums",
        meta,
        (vec_one, vec_two, grad_b_up, mine_bias, other_bias),
        ((16, width),),
        gates=gates[:1],
    )
    if fast:
        came, input_grad, up_near, *qkv_plane[1:3] = together(
            swap(total, CORE), input_grad, up_near, *qkv_plane[1:3]
        )
        up_low = [add(up_parts_sum[i], up_near[i]) for i in range(2)]
        total = total + came
        came, qkv_plane[3] = together(swap(total, X), qkv_plane[3])
        total = total + came
        qkv_parts_sum = plane_sum(qkv_plane)
        qkv_hops = [swap(qkv_parts_sum[i], m) for i, m in ((1, FAR), (2, NEAR), (3, NEAR | FAR))]
        came, up_far, *qkv_hops = together(swap(total, Y), swap(up_low[1], FAR), *qkv_hops)
        total = total + came
        up_piece = add(up_low[0], up_far)
        qkv_piece = add(qkv_parts_sum[0], *qkv_hops)
        came, up_x, qkv_x = together(swap(total, NEAR), swap(up_piece, X), swap(qkv_piece, X))
        total = total + came
        total = total + swap(total, FAR)
        up_both = jnp.stack([up_piece, up_x])
        up_core = swap(up_both, CORE)
        up_quarters = up_both, up_core
        qkv_both = jnp.stack([qkv_piece, qkv_x])
        qkv_quarters = qkv_both, swap(qkv_both, CORE)
        sums = small_call(
            functools.partial(own_sums_kernel, block),
            "own_sums",
            meta,
            (total,),
            ((block,),) * 8 + (b_up.shape,),
        )
        step = up_cut + out_cut
        up_moves = [
            move
            for g in range(groups)
            for move in (
                (slice(g * step, g * step + up_cut), 0, g * up_cut, hidden_width // 2),
                (slice(g * step + up_cut, (g + 1) * step), 1, g * out_cut, half),
            )
        ]
        qkv_moves = [(slice(k * half, (k + 1) * half), 0, k * width, half) for k in range(3)]
        (grad_w_down,) = finish(
            meta,
            down_quarters,
            [(slice(0, width), 0, 0, 0)],
            w_down.shape[0] // 2,
            [w_down.shape],
        )
        grad_w_up, grad_w_out = finish(meta, up_quarters, up_moves, 0, [w_up.shape, w_out.shape])
        (grad_w_qkv,) = finish(meta, qkv_quarters, qkv_moves, 0, [w_qkv.shape])
    else:
        total_of = lambda a: lax.psum(
            lax.psum_scatter(a, "shard", scatter_dimension=0, tiled=True), "rep"
        )
        sums = [total_of(g) for g in (*total[:8], total[8:12].reshape(-1))]
        order = [turned(p) for p in range(BLOCKS)]
        down_keep, down_send, up_keep, up_send = (
            a[:, order] for a in (down_keep, down_send, up_keep, up_send)
        )
        down = jnp.stack([down_keep, down_send]).transpose(2, 0, 1, 3, 4)
        grad_w_down = total_of(down.reshape(hidden_width, width).astype(F32))
        up = jnp.stack([up_keep, up_send]).reshape(
            2, 2, BLOCKS, quarter, groups, up_cut + out_cut
        )
        up = up.transpose(2, 1, 3, 0, 4, 5)
        grad_w_up = total_of(up[..., :up_cut].reshape(width, hidden_width).astype(F32))
        grad_w_out = total_of(up[..., up_cut:].reshape(width, width).astype(F32))
        qkv_sum = jnp.stack([qkv_keep[:, order], qkv_send[:, order]])
        qkv_sum = qkv_sum.reshape(2, 2, BLOCKS, quarter, 3, half)
        qkv_sum = qkv_sum.transpose(2, 1, 3, 4, 0, 5).reshape(width, 3 * width)
        grad_w_qkv = total_of(qkv_sum.astype(F32))
    return (
        layer_out.reshape(seqs, seq_len, width),
        input_grad.reshape(seqs, seq_len, width),
        grad_w_qkv,
        sums[0],
        sums[1],
        grad_w_out,
        sums[2],
        sums[3],
        sums[4],
        grad_w_up,
        sums[8],
        grad_w_down,
        sums[5],
        sums[6],
        sums[7],
    )


def solution(mesh):
    fast = mesh.shape["shard"] == BLOCKS and mesh.shape["rep"] == 4
    by_seq = P(("shard", "rep"), None, None)
    one, two = P("shard"), P("shard", None)
    in_specs = (by_seq, P(("shard", "rep")), two, one, one, two, one, one, one)
    in_specs = in_specs + (two, one, two, one, one, one, by_seq)
    out_specs = (by_seq, by_seq, two, one, one, two, one, one, one, two, one, two, one, one, one)
    return jax.shard_map(
        functools.partial(local, fast),
        mesh=mesh,
        in_specs=in_specs,
        out_specs=out_specs,
        check_vma=False,
    )
```

```python
import functools

import jax
import jax.numpy as jnp
from jax import lax
from jax.experimental import pallas as pl
from jax.experimental.pallas import tpu as pltpu
from jax.sharding import PartitionSpec as P

HEADS = 12
EPS = 1e-05
F32 = jnp.float32
BF16 = jnp.bfloat16
BLOCKS = 8
GROUPS = 3
VMEM_LIMIT = 58 * 1024 * 1024


def dot_nn(a, b):
    return lax.dot_general(a, b, (((1,), (0,)), ((), ())), preferred_element_type=F32)


def dot_nt(a, b):
    return lax.dot_general(a, b, (((1,), (1,)), ((), ())), preferred_element_type=F32)


def dot_tn(a, b):
    return lax.dot_general(a, b, (((0,), (0,)), ((), ())), preferred_element_type=F32)


def params(grid_dims):
    return pltpu.CompilerParams(
        dimension_semantics=("arbitrary",) * grid_dims, vmem_limit_bytes=VMEM_LIMIT
    )


def cost(micros):
    return pl.CostEstimate(flops=int(micros * 1.15e9), bytes_accessed=1 << 20, transcendentals=0)


def gated(kernel, inputs, gates):
    def body(*refs):
        kernel(*refs[: inputs + 1], *refs[inputs + 1 + gates :])

    return body


def gate_specs(gates):
    return [pl.BlockSpec(memory_space=pl.ANY)] * len(gates)


def turned(place):
    return ((place & 1) << 2) | (place & 2) | ((place >> 2) & 1)


def place_rows(meta, source, target, columns, cut):
    rows = source.shape[2]
    for half in range(2):
        for block in range(BLOCKS):
            start = (meta[0] ^ turned(block)) * (2 * rows) + (meta[1] ^ half) * rows
            target[pl.ds(pl.multiple_of(start, 16), rows), cut] = source[half, block, :, columns]


def pack_kernel(groups, *refs):
    meta, w_qkv, w_up, w_out, w_down, *vectors, qkv_ref, up_ref, down_ref = refs
    rows, wide = up_ref.shape[0], qkv_ref.shape[1]
    half = wide // 3
    up_cut, out_cut = w_up.shape[1] // (2 * groups), w_out.shape[1] // (2 * groups)
    at = pl.ds(pl.multiple_of(meta[1] * rows, 16), rows)

    def columns(start, size):
        return pl.ds(pl.multiple_of(start, 128), size)

    for kind in range(3):
        start = (2 * kind + meta[2]) * half
        qkv_ref[:rows, kind * half : (kind + 1) * half] = w_qkv[at, columns(start, half)]
    for group in range(groups):
        base = group * (up_cut + out_cut)
        start = (meta[2] * groups + group) * up_cut
        up_ref[:, base : base + up_cut] = w_up[at, columns(start, up_cut)]
        start = (meta[2] * groups + group) * out_cut
        up_ref[:, base + up_cut : base + up_cut + out_cut] = w_out[at, columns(start, out_cut)]
    rows_down = down_ref.shape[0]
    start = (2 * meta[2] + meta[1]) * rows_down
    down_ref[...] = w_down[pl.ds(pl.multiple_of(start, 16), rows_down), :]
    *short, long = vectors
    extra = qkv_ref.shape[0] - rows
    small = short[0].shape[0]
    place = lax.broadcasted_iota(jnp.int32, (extra, small), 0)
    table = jnp.zeros((extra, small), F32)
    for i, v in enumerate(short):
        table = jnp.where(place == i, v[...].astype(F32).reshape(1, small), table)
    qkv_ref[rows:, :] = jnp.zeros((extra, wide), BF16)
    qkv_ref[rows:, :small] = table.astype(BF16)
    size = long.shape[0]
    wide_row = jnp.broadcast_to(long[...].astype(F32).reshape(1, size), (extra, size))
    qkv_ref[rows:, 128 : 128 + size] = wide_row.astype(BF16)


def pack(meta, w_qkv, w_up, w_out, w_down, vectors):
    rows = w_up.shape[0] // 2
    whole = lambda a: pl.BlockSpec(a.shape, lambda i, m: (0,) * a.ndim)
    shapes = [
        (rows + 16, w_qkv.shape[1] // 2),
        (rows, (w_up.shape[1] + w_out.shape[1]) // 2),
        (w_down.shape[0] // 4, w_down.shape[1]),
    ]
    outs = [jax.ShapeDtypeStruct(shape, BF16) for shape in shapes]
    operands = (w_qkv, w_up, w_out, w_down, *vectors)
    return pl.pallas_call(
        functools.partial(pack_kernel, GROUPS),
        grid_spec=pltpu.PrefetchScalarGridSpec(
            num_scalar_prefetch=1,
            grid=(1,),
            in_specs=[whole(a) for a in operands],
            out_specs=[whole(o) for o in outs],
        ),
        out_shape=outs,
        compiler_params=params(1),
        cost_estimate=cost(2),
        name="pack",
    )(meta, *operands)


def shard_columns(shard, block, width, lanes):
    lane = lax.broadcasted_iota(jnp.int32, (lanes, width), 0)
    column = lax.broadcasted_iota(jnp.int32, (lanes, width), 1)
    return (lane < block) & (column == lane + shard * block)


def unpack_kernel(block, meta, near_ref, far_ref, vec_ref, b_up_ref, mine_ref, other_ref, scr):
    width = vec_ref.shape[1]
    half, size = width // 2, b_up_ref.shape[1] // BLOCKS
    total = jnp.zeros(scr.shape, F32)
    for place in range(BLOCKS):
        source = (near_ref, far_ref)[place // 4]
        rows = source[place % 4]
        shard = meta[0] ^ turned(place)
        spread = shard_columns(shard, block, width, 128).astype(F32).astype(BF16)
        total = total + dot_nn(rows[:, :128], spread)
        to = pl.ds(pl.multiple_of(shard * size, 128), size)
        b_up_ref[:, to] = rows[:1, 128 : 128 + size].astype(F32)
    scr[...] = total
    vec_ref[...] = jnp.zeros_like(vec_ref)
    vec_ref[0:6, :] = total[2:8]
    for rel, out in enumerate((mine_ref, other_ref)):
        cut = pl.ds(pl.multiple_of((meta[2] ^ rel) * half, 128), half)
        out[...] = jnp.zeros_like(out)
        out[:, :half] = scr[0:1, cut]
        out[:, 2 * half :] = scr[1:2, cut]


def small_call(kernel, name, meta, operands, shapes, scratch=(), gates=()):
    whole = lambda a: pl.BlockSpec(a.shape, lambda i, m: (0,) * len(a.shape))
    outs = [jax.ShapeDtypeStruct(shape, F32) for shape in shapes]
    return pl.pallas_call(
        gated(kernel, len(operands), len(gates)),
        grid_spec=pltpu.PrefetchScalarGridSpec(
            num_scalar_prefetch=1,
            grid=(1,),
            in_specs=[whole(a) for a in operands] + gate_specs(gates),
            out_specs=[whole(o) for o in outs],
            scratch_shapes=[pltpu.VMEM(shape, F32) for shape in scratch],
        ),
        out_shape=outs,
        compiler_params=params(1),
        cost_estimate=cost(2),
        name=name,
    )(meta, *operands, *gates)


def sums_kernel(meta, vec_one, vec_two, b_up, bias_mine, bias_other, out_ref):
    width = out_ref.shape[1]
    half = width // 2
    out_ref[...] = jnp.zeros_like(out_ref)
    for rel, source in enumerate((bias_mine, bias_other)):
        to = pl.ds(pl.multiple_of((meta[2] ^ rel) * half, 128), half)
        out_ref[0:1, to] = source[:, :half]
        out_ref[1:2, to] = source[:, 2 * half :]
    out_ref[2:5, :] = vec_one[0:3, :]
    out_ref[5:8, :] = vec_two[0:3, :]
    for i in range(b_up.shape[1] // width):
        out_ref[8 + i : 9 + i, :] = b_up[:, i * width : (i + 1) * width]


def own_sums_kernel(block, meta, sum_ref, *outs):
    *short, b_up_ref = outs
    width, size = sum_ref.shape[1], b_up_ref.shape[0]
    pick = shard_columns(meta[0], block, width, 128).astype(F32)
    own = lax.dot_general(
        sum_ref[0:8, :],
        pick,
        (((1,), (1,)), ((), ())),
        precision=lax.Precision.HIGHEST,
        preferred_element_type=F32,
    )
    each = width // size
    cut = pl.ds(pl.multiple_of(lax.rem(meta[0], each) * size, 128), size)
    b_up_ref[...] = sum_ref[pl.ds(8 + lax.div(meta[0], each), 1), cut].reshape(size)
    for i, out in enumerate(short):
        out[...] = own[i : i + 1, :block].reshape(block)


def attend_kernel(meta, x_ref, w_ref, bias_ref, qkv_ref, mixed_ref, mixed_t_ref, lse_ref, w_scr):
    seq = pl.program_id(0)
    wide = w_scr.shape[1]
    part = wide // 3

    @pl.when(seq == 0)
    def _():
        place_rows(meta, w_ref, w_scr, slice(None), slice(None))

    length = meta[3 + seq]
    qkv = (dot_nn(x_ref[0], w_scr[...]) + bias_ref[...]).astype(BF16)
    qkv_ref[0] = qkv
    rows = qkv.shape[0]
    lane = lax.broadcasted_iota(jnp.int32, (rows, 128), 1)
    key_ok = lax.broadcasted_iota(jnp.int32, (rows, rows), 0) < length
    for pair in range(part // 128):
        cut = pair * 128
        query = qkv[:, cut : cut + 128] * jnp.asarray(0.125, BF16)
        key = qkv[:, part + cut : part + cut + 128]
        value_t = qkv[:, 2 * part + cut : 2 * part + cut + 128].T
        outs = []
        for head in range(2):
            query_one = jnp.where((lane >= 64) == (head == 1), query, jnp.zeros_like(query))
            scores = jnp.where(key_ok, dot_nt(key, query_one), -1e30)
            top = jnp.max(scores, axis=0, keepdims=True)
            exp_scores = jnp.exp(scores - top)
            total = jnp.sum(exp_scores, axis=0, keepdims=True)
            lse_ref[0, 2 * pair + head] = top + jnp.log(total)
            out = dot_nn(value_t[64 * head : 64 * head + 64], exp_scores.astype(BF16))
            outs.append(out * (1.0 / total))
        mixed_t = jnp.concatenate(outs, axis=0)
        mixed_t_ref[cut : cut + 128, :] = mixed_t.astype(BF16)
        mixed_ref[0, :, cut : cut + 128] = mixed_t.T.astype(BF16)


def attend(meta, x, weight, bias):
    seqs, length, width = x.shape
    wide = weight.shape[3]
    part = wide // 3
    half_heads = HEADS // 2
    whole = lambda s, m: (0, 0, 0, 0)
    return pl.pallas_call(
        attend_kernel,
        grid_spec=pltpu.PrefetchScalarGridSpec(
            num_scalar_prefetch=1,
            grid=(seqs,),
            in_specs=[
                pl.BlockSpec((1, length, width), lambda s, m: (s, 0, 0)),
                pl.BlockSpec(weight.shape, whole, pipeline_mode=pl.Buffered(1)),
                pl.BlockSpec((1, wide), lambda s, m: (0, 0)),
            ],
            out_specs=[
                pl.BlockSpec((1, length, wide), lambda s, m: (s, 0, 0)),
                pl.BlockSpec((1, length, part), lambda s, m: (s, 0, 0)),
                pl.BlockSpec((part, length), lambda s, m: (0, s)),
                pl.BlockSpec((1, half_heads, 1, length), lambda s, m: (s, 0, 0, 0)),
            ],
            scratch_shapes=[pltpu.VMEM((width, wide), BF16)],
        ),
        out_shape=[
            jax.ShapeDtypeStruct((seqs, length, wide), BF16),
            jax.ShapeDtypeStruct((seqs, length, part), BF16),
            jax.ShapeDtypeStruct((part, seqs * length), BF16),
            jax.ShapeDtypeStruct((seqs, half_heads, 1, length), F32),
        ],
        compiler_params=params(1),
        cost_estimate=cost(11),
        name="attend_forward",
    )(meta, x, weight, bias)


def gelu_and_slope(hidden):
    size = jnp.abs(hidden)
    bell = jnp.exp2(hidden * hidden * -0.7213475204444817)
    t = 1.0 / (1.0 + (0.3275911 * 0.7071067811865476) * size)
    poly = t * (
        0.5 * 0.254829592
        + t
        * (
            0.5 * -0.284496736
            + t * (0.5 * 1.421413741 + t * (0.5 * -1.453152027 + t * (0.5 * 1.061405429)))
        )
    )
    tail = poly * bell
    phi = jnp.where(hidden < 0.0, tail, 1.0 - tail)
    return hidden * phi, phi + hidden * bell * 0.3989422804014327


def norm_forward(hidden):
    center = hidden - jnp.mean(hidden, axis=-1, keepdims=True)
    scale = lax.rsqrt(jnp.mean(center * center, axis=-1, keepdims=True) + EPS)
    return center * scale, scale


def norm_back(grad, hat, scale, gain):
    grad_hat = grad * gain
    shift = jnp.mean(grad_hat, axis=-1, keepdims=True)
    along = jnp.mean(grad_hat * hat, axis=-1, keepdims=True)
    return scale * (grad_hat - shift - hat * along)


def column_sum(rows):
    return jnp.sum(rows.astype(F32), axis=0, keepdims=True)


def place_up(meta, mine, other, w_up, w_out):
    hidden_width, width = w_up.shape[1], w_out.shape[1]
    up_cut, out_cut = hidden_width // (2 * GROUPS), width // (2 * GROUPS)
    for rel, source in enumerate((mine, other)):
        core = meta[2] ^ rel
        for group in range(GROUPS):
            base = group * (up_cut + out_cut)
            up_to = pl.multiple_of(core * (hidden_width // 2) + group * up_cut, 128)
            out_to = pl.multiple_of(core * (width // 2) + group * out_cut, 128)
            place_rows(meta, source, w_up, slice(base, base + up_cut), pl.ds(up_to, up_cut))
            place_rows(
                meta,
                source,
                w_out,
                slice(base + up_cut, base + up_cut + out_cut),
                pl.ds(out_to, out_cut),
            )


def place_down(meta, mine, other, w_down):
    rows = mine.shape[2]
    for rel, source in enumerate((mine, other)):
        for half in range(2):
            for block in range(BLOCKS):
                start = (
                    (meta[0] ^ turned(block)) * (4 * rows)
                    + (meta[2] ^ rel) * (2 * rows)
                    + (meta[1] ^ half) * rows
                )
                w_down[pl.ds(pl.multiple_of(start, 16), rows), :] = source[half, block]


def halves_of(meta, width):
    half = width // 2
    return (
        pl.ds(pl.multiple_of(meta[2] * half, 128), half),
        pl.ds(pl.multiple_of((1 - meta[2]) * half, 128), half),
    )


CHUNK = 512


def up_kernel(
    meta,
    x_ref,
    mixed_mine,
    mixed_other,
    up_mine,
    up_other,
    vec_ref,
    b_up_ref,
    hat_ref,
    scale_ref,
    norm_t_ref,
    active_ref,
    active_t_ref,
    slope_ref,
    w_up,
    w_out,
    normed_low,
):
    step = pl.program_id(0)
    width = w_out.shape[1]

    @pl.when(step == 0)
    def _():
        place_up(meta, up_mine, up_other, w_up, w_out)
        b_out, gain, shift = [vec_ref[i : i + 1, :] for i in range(3)]
        rows_mine, rows_other = halves_of(meta, width)
        branch = dot_nn(mixed_mine[...], w_out[rows_mine, :])
        branch = branch + dot_nn(mixed_other[...], w_out[rows_other, :])
        hat, scale = norm_forward(x_ref[...].astype(F32) + (branch + b_out))
        hat_ref[...] = hat
        scale_ref[...] = jnp.broadcast_to(scale, scale_ref.shape)
        normed_low[...] = (hat * gain + shift).astype(BF16)
        norm_t_ref[...] = normed_low[...].T

    cut = pl.ds(pl.multiple_of(step * CHUNK, CHUNK), CHUNK)
    hidden = dot_nn(normed_low[...], w_up[:, cut]) + b_up_ref[...]
    active, slope = gelu_and_slope(hidden)
    slope_ref[...] = slope.astype(BF16)
    active_low = active.astype(BF16)
    active_ref[...] = active_low
    active_t_ref[...] = active_low.T


def down_kernel(
    seq_len,
    meta,
    hat_ref,
    active_ref,
    cot_ref,
    down_mine,
    down_other,
    vec_ref,
    out_ref,
    grad_second_ref,
    grad_vec_ref,
    w_down,
):
    step = pl.program_id(0)
    tile = hat_ref.shape[0]

    @pl.when(step == 0)
    def _():
        grad_vec_ref[...] = jnp.zeros_like(grad_vec_ref)
        place_down(meta, down_mine, down_other, w_down)

    gain_one, shift_one, b_down, gain, shift = [vec_ref[i : i + 1, :] for i in range(1, 6)]
    seq = lax.div(step * tile, seq_len)
    place = lax.broadcasted_iota(jnp.int32, (tile, 1), 0) + lax.rem(step * tile, seq_len)
    valid = place < meta[3 + seq]
    second = dot_nn(active_ref[...], w_down[...])
    normed = hat_ref[...] * gain_one + shift_one
    hat, scale = norm_forward(normed + (second + b_down))
    out_ref[...] = jnp.where(valid, hat * gain + shift, 0.0).astype(BF16)
    grad_result = jnp.where(valid, cot_ref[...].astype(F32), 0.0)
    grad_second = norm_back(grad_result, hat, scale, gain).astype(BF16)
    grad_second_ref[...] = grad_second
    sums = column_sum(grad_second), column_sum(grad_result * hat), column_sum(grad_result)
    for i, total in enumerate(sums):
        grad_vec_ref[i : i + 1, :] += total


def rest_kernel(
    meta,
    grad_second_ref,
    hat_ref,
    scale_ref,
    w_out,
    vec_ref,
    w_down,
    w_up,
    slope_ref,
    grad_hidden_ref,
    grad_branch_ref,
    grad_mixed_mine,
    grad_mixed_other,
    grad_vec_ref,
    grad_b_up_ref,
    total,
):
    step = pl.program_id(0)
    width = w_out.shape[1]

    @pl.when(step == 0)
    def _():
        total[...] = grad_second_ref[...].astype(F32)

    grad_active = dot_nt(grad_second_ref[...], w_down[...])
    grad_hidden = (slope_ref[...].astype(F32) * grad_active).astype(BF16)
    grad_hidden_ref[...] = grad_hidden
    grad_b_up_ref[...] = column_sum(grad_hidden)
    total[...] += dot_nt(grad_hidden, w_up[...])

    @pl.when(step == pl.num_programs(0) - 1)
    def _():
        grad_normed, hat, gain = total[...], hat_ref[...], vec_ref[1:2, :]
        grad_branch = norm_back(grad_normed, hat, scale_ref[:, 0:1], gain).astype(BF16)
        grad_branch_ref[...] = grad_branch
        rows_mine, rows_other = halves_of(meta, width)
        grad_mixed_mine[...] = dot_nt(grad_branch, w_out[rows_mine, :]).astype(BF16)
        grad_mixed_other[...] = dot_nt(grad_branch, w_out[rows_other, :]).astype(BF16)
        grad_vec_ref[...] = jnp.zeros_like(grad_vec_ref)
        sums = column_sum(grad_branch), column_sum(grad_normed * hat), column_sum(grad_normed)
        for i, one in enumerate(sums):
            grad_vec_ref[i : i + 1, :] = one


def by_chunk(kernel, name, micros, meta, cut, wholes, gates, outs, scratch, cut_rows=()):
    hidden_width = cut[-1].shape[1]
    chunked = lambda shape: pl.BlockSpec((shape[0], CHUNK), lambda n, m: (0, n))
    whole = lambda shape: pl.BlockSpec(
        shape, lambda n, m: (0,) * len(shape), pipeline_mode=pl.Buffered(1)
    )
    spec_of = {
        "cols": chunked,
        "rows": lambda shape: pl.BlockSpec((CHUNK, shape[1]), lambda n, m: (n, 0)),
        "whole": lambda shape: pl.BlockSpec(shape, lambda n, m: (0,) * len(shape)),
    }
    return pl.pallas_call(
        gated(kernel, len(cut) + len(cut_rows) + len(wholes), len(gates)),
        grid_spec=pltpu.PrefetchScalarGridSpec(
            num_scalar_prefetch=1,
            grid=(hidden_width // CHUNK,),
            in_specs=[whole(a.shape) for a in wholes]
            + [spec_of["rows"](a.shape) for a in cut_rows]
            + [chunked(a.shape) for a in cut]
            + gate_specs(gates),
            out_specs=[spec_of[kind](shape) for kind, shape, _ in outs],
            scratch_shapes=[pltpu.VMEM(shape, dtype) for shape, dtype in scratch],
        ),
        out_shape=[jax.ShapeDtypeStruct(shape, dtype) for _, shape, dtype in outs],
        compiler_params=params(1),
        cost_estimate=cost(micros),
        name=name,
    )(meta, *wholes, *cut_rows, *cut, *gates)


def by_tile(kernel, name, micros, meta, tiled, wholes, gates, outs, scratch, most=512):
    rows = tiled[0].shape[0]
    tile = min(most, rows)
    by_row = lambda cols: pl.BlockSpec((tile, cols), lambda i, m: (i, 0))
    whole = lambda a: pl.BlockSpec(
        a.shape, lambda i, m: (0,) * a.ndim, pipeline_mode=pl.Buffered(1)
    )
    specs, shapes = [], []
    for kind, size, dtype in outs:
        if kind == "row":
            specs.append(by_row(size))
            shapes.append(jax.ShapeDtypeStruct((rows, size), dtype))
        elif kind == "col":
            specs.append(pl.BlockSpec((size, tile), lambda i, m: (0, i)))
            shapes.append(jax.ShapeDtypeStruct((size, rows), dtype))
        else:
            specs.append(pl.BlockSpec(size, lambda i, m: (0, 0)))
            shapes.append(jax.ShapeDtypeStruct(size, dtype))
    return pl.pallas_call(
        gated(kernel, len(tiled) + len(wholes), len(gates)),
        grid_spec=pltpu.PrefetchScalarGridSpec(
            num_scalar_prefetch=1,
            grid=(rows // tile,),
            in_specs=[by_row(a.shape[1]) for a in tiled]
            + [whole(a) for a in wholes]
            + gate_specs(gates),
            out_specs=specs,
            scratch_shapes=[pltpu.VMEM(shape, BF16) for shape in scratch],
        ),
        out_shape=shapes,
        compiler_params=params(1),
        cost_estimate=cost(micros),
        name=name,
    )(meta, *tiled, *wholes, *gates)


def store_blocks(meta, out_ref, value, cut, first=0):
    rows = out_ref.shape[2]
    for block in range(value.shape[0] // (2 * rows)):
        for half in range(2):
            start = (2 * block + half) * rows
            out_ref[meta[1] ^ half, turned(meta[0] ^ (first + block)), :, cut] = value[
                start : start + rows
            ].astype(BF16)


def grad_up_kernel(
    meta, norm_t_ref, mixed_mine, mixed_other, grad_hidden_ref, grad_branch_ref, out_ref
):
    up_cut = grad_hidden_ref.shape[1]
    store_blocks(meta, out_ref, dot_nn(norm_t_ref[...], grad_hidden_ref[...]), slice(0, up_cut))
    cut = slice(up_cut, out_ref.shape[3])
    few = BLOCKS // 2
    grad_branch = grad_branch_ref[...]
    store_blocks(meta, out_ref, dot_nn(mixed_mine[...], grad_branch), cut, meta[2] * few)
    store_blocks(meta, out_ref, dot_nn(mixed_other[...], grad_branch), cut, (1 - meta[2]) * few)


def grad_up(rel, meta, norm_t, mixed_t, grad_hidden, grad_branch, *gates):
    width, rows = norm_t.shape
    hidden_width = grad_hidden.shape[1]
    groups = 3
    up_cut, out_cut = hidden_width // (2 * groups), width // (2 * groups)
    block_rows = width // (2 * BLOCKS)
    whole = lambda tall: pl.BlockSpec(
        (tall, rows), lambda n, m: (0, 0), pipeline_mode=pl.Buffered(1)
    )
    turn = lambda n, m: (0, (m[2] ^ rel) * groups + n)
    return pl.pallas_call(
        gated(grad_up_kernel, 5, len(gates)),
        grid_spec=pltpu.PrefetchScalarGridSpec(
            num_scalar_prefetch=1,
            grid=(groups,),
            in_specs=[
                whole(width),
                whole(width // 2),
                whole(width // 2),
                pl.BlockSpec((rows, up_cut), turn),
                pl.BlockSpec((rows, out_cut), turn),
                *gate_specs(gates),
            ],
            out_specs=pl.BlockSpec(
                (2, BLOCKS, block_rows, up_cut + out_cut), lambda n, m: (0, 0, 0, n)
            ),
        ),
        out_shape=jax.ShapeDtypeStruct(
            (2, BLOCKS, block_rows, groups * (up_cut + out_cut)), BF16
        ),
        compiler_params=params(1),
        cost_estimate=cost(8),
        name="grad_up",
    )(meta, norm_t, *mixed_t, grad_hidden, grad_branch, *gates)


def grad_down_kernel(meta, *refs):
    blocks, (grad_second_ref, out_ref) = refs[:-2], refs[-2:]
    rows = out_ref.shape[2]
    left = jnp.concatenate([b[...] for b in blocks], axis=0)
    value = dot_nn(left, grad_second_ref[...]).astype(BF16)
    for i in range(len(blocks)):
        for half in range(2):
            start = (2 * i + half) * rows
            out_ref[meta[1] ^ half, i] = value[start : start + rows]


def grad_down(rel, meta, active_t, grad_second, *gates):
    hidden_width, rows = active_t.shape
    width = grad_second.shape[1]
    block = hidden_width // (2 * BLOCKS)
    some = 4

    def spec(i):
        return pl.BlockSpec(
            (block, rows), lambda j, m: (2 * (m[0] ^ turned(some * j + i)) + (m[2] ^ rel), 0)
        )

    return pl.pallas_call(
        gated(grad_down_kernel, some + 1, len(gates)),
        grid_spec=pltpu.PrefetchScalarGridSpec(
            num_scalar_prefetch=1,
            grid=(BLOCKS // some,),
            in_specs=[spec(i) for i in range(some)]
            + [pl.BlockSpec((rows, width), lambda j, m: (0, 0), pipeline_mode=pl.Buffered(1))]
            + gate_specs(gates),
            out_specs=pl.BlockSpec((2, some, block // 2, width), lambda j, m: (0, j, 0, 0)),
        ),
        out_shape=jax.ShapeDtypeStruct((2, BLOCKS, block // 2, width), BF16),
        compiler_params=params(1),
        cost_estimate=cost(6),
        name="grad_down",
    )(meta, *[active_t] * some, grad_second, *gates)


def attend_back_kernel(
    meta,
    x_t_ref,
    qkv_ref,
    mixed_t_ref,
    grad_mixed_ref,
    lse_ref,
    grad_qkv_ref,
    grad_w_ref,
    grad_bias_ref,
    grad_scr,
):
    seq = pl.program_id(0)
    length = meta[3 + seq]
    rows, wide = qkv_ref.shape[1:]
    part = wide // 3
    lane = lax.broadcasted_iota(jnp.int32, (rows, 128), 1)
    key_ok = lax.broadcasted_iota(jnp.int32, (rows, rows), 0) < length
    start = pl.multiple_of(seq * rows, 128)

    @pl.when(seq == 0)
    def _():
        grad_bias_ref[...] = jnp.zeros_like(grad_bias_ref)

    for pair in range(part // 128):
        cut = pair * 128
        query = qkv_ref[0, :, cut : cut + 128] * jnp.asarray(0.125, BF16)
        key = qkv_ref[0, :, part + cut : part + cut + 128]
        value = qkv_ref[0, :, 2 * part + cut : 2 * part + cut + 128]
        grad_out = grad_mixed_ref[0, :, cut : cut + 128]
        product = grad_out.astype(F32).T * mixed_t_ref[cut : cut + 128, :].astype(F32)
        key_t = key.T
        grad_query, grad_key, grad_value = [], 0.0, 0.0
        for head in range(2):
            keep = (lane >= 64) == (head == 1)
            query_one = jnp.where(keep, query, jnp.zeros_like(query))
            grad_one = jnp.where(keep, grad_out, jnp.zeros_like(grad_out))
            inner = slice(64 * head, 64 * head + 64)
            delta = jnp.sum(product[inner], axis=0, keepdims=True)
            scores = jnp.where(key_ok, dot_nt(key, query_one), -1e30)
            prob = jnp.exp(scores - lse_ref[0, 2 * pair + head])
            grad_prob = dot_nt(value, grad_one)
            grad_scores = (prob * (grad_prob - delta)).astype(BF16)
            grad_value = grad_value + dot_nn(prob.astype(BF16), grad_one)
            grad_key = grad_key + dot_nn(grad_scores, query_one)
            grad_query.append(dot_nn(key_t[inner], grad_scores) * 0.125)
        grads = (jnp.concatenate(grad_query, axis=0).T, grad_key, grad_value)
        for kind, grad in enumerate(grads):
            grad = grad.astype(BF16)
            to = slice(kind * part + cut, kind * part + cut + 128)
            grad_scr[pl.ds(start, rows), to] = grad
            grad_qkv_ref[0, :, to] = grad
            grad_bias_ref[:, to] += column_sum(grad)

    @pl.when(seq == pl.num_programs(0) - 1)
    def _():
        store_blocks(meta, grad_w_ref, dot_nn(x_t_ref[...], grad_scr[...]), slice(None))


def attend_back(meta, x_t, qkv, mixed_t, grad_mixed, lse, *gates):
    seqs, length, wide = qkv.shape
    width, rows = x_t.shape
    part = wide // 3
    block_rows = width // (2 * BLOCKS)
    by_seq = lambda cols: pl.BlockSpec((1, length, cols), lambda s, m: (s, 0, 0))
    return pl.pallas_call(
        gated(attend_back_kernel, 5, len(gates)),
        grid_spec=pltpu.PrefetchScalarGridSpec(
            num_scalar_prefetch=1,
            grid=(seqs,),
            in_specs=[
                pl.BlockSpec((width, rows), lambda s, m: (0, 0), pipeline_mode=pl.Buffered(1)),
                by_seq(wide),
                pl.BlockSpec((part, length), lambda s, m: (0, s)),
                by_seq(part),
                pl.BlockSpec((1, HEADS // 2, 1, length), lambda s, m: (s, 0, 0, 0)),
                *gate_specs(gates),
            ],
            out_specs=[
                by_seq(wide),
                pl.BlockSpec((2, BLOCKS, block_rows, wide), lambda s, m: (0, 0, 0, 0)),
                pl.BlockSpec((1, wide), lambda s, m: (0, 0)),
            ],
            scratch_shapes=[pltpu.VMEM((rows, wide), BF16)],
        ),
        out_shape=[
            jax.ShapeDtypeStruct((seqs, length, wide), BF16),
            jax.ShapeDtypeStruct((2, BLOCKS, block_rows, wide), BF16),
            jax.ShapeDtypeStruct((1, wide), F32),
        ],
        compiler_params=params(1),
        cost_estimate=cost(16),
        name="attend_back",
    )(meta, x_t, qkv, mixed_t, grad_mixed, lse, *gates)


def input_kernel(
    meta, branch_ref, grad_mine, grad_other, w_mine, w_other, out_ref, scr_mine, scr_other
):
    @pl.when(pl.program_id(0) == 0)
    def _():
        place_rows(meta, w_mine, scr_mine, slice(None), slice(None))
        place_rows(meta, w_other, scr_other, slice(None), slice(None))

    total = branch_ref[...].astype(F32) + dot_nt(grad_mine[...], scr_mine[...])
    out_ref[...] = total + dot_nt(grad_other[...], scr_other[...])


def finish_kernel(moves, row_step, meta, *refs):
    parts, outs = refs[:2], refs[2:]
    for rel in range(4):
        part = parts[rel & 1].at[rel >> 1]
        x_at, core = meta[1] ^ (rel >> 1), meta[2] ^ (rel & 1)
        rows = part.shape[0]
        at = pl.ds(pl.multiple_of(x_at * rows + core * row_step, 16), rows)
        for columns, out, first, step in moves:
            size = columns.stop - columns.start
            to = pl.ds(pl.multiple_of(first + core * step, 128), size)
            outs[out][at, to] = part[:, columns].astype(F32)


def finish(meta, parts, moves, row_step, shapes):
    whole = lambda shape: pl.BlockSpec(shape, lambda i, m: (0,) * len(shape))
    return pl.pallas_call(
        functools.partial(finish_kernel, moves, row_step),
        grid_spec=pltpu.PrefetchScalarGridSpec(
            num_scalar_prefetch=1,
            grid=(1,),
            in_specs=[whole(p.shape) for p in parts],
            out_specs=[whole(shape) for shape in shapes],
        ),
        out_shape=[jax.ShapeDtypeStruct(shape, F32) for shape in shapes],
        compiler_params=params(1),
        cost_estimate=cost(2),
        name="finish",
    )(meta, *parts)


def together(*arrays):
    return lax.optimization_barrier(arrays)


CORE, X, Y, NEAR, FAR = 1, 2, 4, 8, 16
DEVICES = 32


def swap(array, mask):
    pairs = [(i, i ^ mask) for i in range(DEVICES)]
    return lax.ppermute(array, ("shard", "rep"), pairs)


def gather_z(piece):
    came = [swap(piece, mask) for mask in (FAR, NEAR, NEAR | FAR)]
    return jnp.stack([piece] + came)


def double(held, mask):
    return jnp.concatenate([held, swap(held, mask)], axis=0)


def plane_hops(held):
    return [swap(held, mask) for mask in (Y, X, X | Y)]


def plane_join(held, by_y, by_x, across):
    low = jnp.concatenate([held, by_y], axis=0)
    return jnp.stack([low, jnp.concatenate([by_x, across], axis=0)])


def gather_plane(held):
    return plane_join(held, *plane_hops(held))


def add(*terms):
    total = terms[0].astype(F32)
    for term in terms[1:]:
        total = total + term.astype(F32)
    return total.astype(BF16)


def sum_z(parts):
    return add(
        parts[0],
        *[swap(parts[i], mask) for i, mask in ((1, FAR), (2, NEAR), (3, NEAR | FAR))],
    )


def plane_sends(kept, came):
    cut = BLOCKS // 2
    pick = lambda a, x, y: a[x, cut:] if y else a[x, :cut]
    parts = [[add(pick(kept, x, y), pick(came, x, y)) for y in range(2)] for x in range(2)]
    return [
        parts[0][0],
        swap(parts[0][1], Y),
        swap(parts[1][0], X),
        swap(parts[1][1], X | Y),
    ]


def plane_sum(terms):
    return [add(*[t[i] for t in terms]) for i in range(4)]


def local(
    fast,
    tokens,
    lengths,
    w_qkv,
    b_query,
    b_value,
    w_out,
    b_out,
    ln1_gain,
    ln1_bias,
    w_up,
    b_up,
    w_down,
    b_down,
    ln2_gain,
    ln2_bias,
    cotangent,
):
    seqs, seq_len, width = tokens.shape
    rows = seqs * seq_len
    hidden_width = w_up.shape[1]
    half = width // 2
    groups = GROUPS
    up_cut, out_cut = hidden_width // (2 * groups), half // groups
    vectors = (b_query, b_value, b_out, ln1_gain, ln1_bias, b_down, ln2_gain, ln2_bias, b_up)

    if fast:
        shard, rep = lax.axis_index("shard"), lax.axis_index("rep")
        x_at, core = rep // 2, rep % 2
    else:
        shard = rep = x_at = core = jnp.int32(0)
    block = width // BLOCKS
    quarter = block // 2
    meta = jnp.concatenate(
        [jnp.stack([shard, x_at, core]).astype(jnp.int32), lengths.astype(jnp.int32)]
    )

    def qkv_parts(w):
        return w.reshape(-1, 2, quarter, 3, 2, half)

    def up_parts(up, out):
        up = up.reshape(-1, 2, quarter, 2, groups, up_cut)
        out = out.reshape(-1, 2, quarter, 2, groups, out_cut)
        return jnp.concatenate([up, out], axis=-1)

    if fast:
        qkv_piece, up_piece, down_piece = pack(meta, w_qkv, w_up, w_out, w_down, vectors)
        qkv_z, up_piece, down_piece = together(gather_z(qkv_piece), up_piece, down_piece)
        table = qkv_z[:, quarter:, : 128 + b_up.shape[0]]
        up_z = double(double(up_piece[None], FAR), NEAR)
        down_z = double(down_piece[None], FAR)
        qkv_mine, up_z, down_z, table, table_y = together(
            gather_plane(qkv_z[:, :quarter]), up_z, down_z, table, swap(table, Y)
        )
        vec, b_up_row, *bias = small_call(
            functools.partial(unpack_kernel, block),
            "unpack",
            meta,
            (table, table_y),
            ((8, width), (1, hidden_width), (1, 3 * half), (1, 3 * half)),
            ((16, width),),
        )
        qkv_w = qkv_mine, swap(qkv_mine, CORE)
        up_hops, down_z = plane_hops(up_z), double(down_z, NEAR)
    else:
        everything = lambda a: lax.all_gather(a, "shard", axis=0, tiled=True)
        full = [everything(v) for v in vectors]
        order = [turned(p) for p in range(BLOCKS)]
        both = lambda a: (a[0][:, order], a[1][:, order])
        qkv_w = both(
            qkv_parts(everything(w_qkv))
            .transpose(4, 1, 0, 2, 3, 5)
            .reshape(2, 2, BLOCKS, quarter, 3 * half)
        )
        up_w = both(
            up_parts(everything(w_up), everything(w_out))
            .transpose(3, 1, 0, 2, 4, 5)
            .reshape(2, 2, BLOCKS, quarter, -1)
        )
        down_w = both(
            everything(w_down).reshape(BLOCKS, 2, 2, -1, width).transpose(1, 2, 0, 3, 4)
        )
        full = [v.astype(F32) for v in full]
        bias = jnp.stack(
            [full[0].reshape(2, half), jnp.zeros((2, half), F32), full[1].reshape(2, half)], axis=1
        ).reshape(2, 1, 3 * half)
        vec = jnp.stack(full[2:8] + [jnp.zeros_like(full[0])] * 2)
        b_up_row = full[8].reshape(1, -1)
    x_rows = tokens.reshape(rows, width)
    heads = [list(attend(meta, tokens, qkv_w[i], bias[i])) for i in range(2)]
    if fast:
        x_late, heads[0][0] = together(x_rows, heads[0][0])
        x_t = x_late.T
    else:
        x_t = x_rows.T
    if fast:
        *up_hops, down_z, heads[0][1], heads[1][1] = together(
            *up_hops, down_z, heads[0][1], heads[1][1]
        )
        up_mine = plane_join(up_z, *up_hops)
        up_w = up_mine, swap(up_mine, CORE)
    qkv, mixed, mixed_t, lse = zip(*heads)
    mixed_rows = [m.reshape(rows, half) for m in mixed]
    up_shape, out_shape, down_shape = (width, hidden_width), (width, width), (hidden_width, width)
    hat, scale, norm_t, active, active_t, slope, up_full, out_full = by_chunk(
        up_kernel,
        "feed_up",
        26,
        meta,
        (b_up_row,),
        (x_rows, *mixed_rows, *up_w, vec),
        (),
        (
            ("whole", (rows, width), F32),
            ("whole", (rows, 128), F32),
            ("whole", (width, rows), BF16),
            ("cols", (rows, hidden_width), BF16),
            ("rows", (hidden_width, rows), BF16),
            ("cols", (rows, hidden_width), BF16),
            ("whole", up_shape, BF16),
            ("whole", out_shape, BF16),
        ),
        (((rows, width), BF16),),
    )
    row, fixed = "row", "sum"
    if fast:
        active, x_t, *hops = together(active, x_t, *plane_hops(down_z))
        down_mine = plane_join(down_z, *hops)
        down_w = down_mine, swap(down_mine, CORE)
    layer_out, grad_second, vec_two, down_full = by_tile(
        functools.partial(down_kernel, seq_len),
        "feed_down",
        14,
        meta,
        (hat, active, cotangent.reshape(rows, width)),
        (*down_w, vec),
        (),
        (
            (row, width, BF16),
            (row, width, BF16),
            (fixed, (8, width), F32),
            (fixed, down_shape, BF16),
        ),
        (),
    )
    down_send = grad_down(1, meta, active_t, grad_second)
    down_keep = grad_down(0, meta, active_t, grad_second, down_send)
    gates = (down_keep,)
    if fast:
        down_plane = plane_sends(down_keep, swap(down_send, CORE))
        gates = (down_plane[0],)
    grad_hidden, grad_branch, *grad_mixed, vec_one, grad_b_up = by_chunk(
        rest_kernel,
        "feed_back",
        22,
        meta,
        (up_full, slope),
        (grad_second, hat, scale, out_full, vec),
        gates,
        (
            ("cols", (rows, hidden_width), BF16),
            ("whole", (rows, width), BF16),
            ("whole", (rows, half), BF16),
            ("whole", (rows, half), BF16),
            ("whole", (8, width), F32),
            ("cols", (1, hidden_width), F32),
        ),
        (((rows, width), F32),),
        (down_full,),
    )
    gates = ()
    if fast:
        down_parts = plane_sum(down_plane)
        gates = tuple(down_parts)
    up_send = grad_up(1, meta, norm_t, mixed_t, grad_hidden, grad_branch, *gates)
    if fast:
        up_send, *down_parts = together(up_send, *down_parts)
    up_keep = grad_up(0, meta, norm_t, mixed_t, grad_hidden, grad_branch, up_send)
    gates = (up_keep,)
    if fast:
        up_plane = plane_sends(up_keep, swap(up_send, CORE))
        down_piece = sum_z(down_parts)
        gates = (up_plane[0],)
    grad_mixed = [g.reshape(seqs, seq_len, half) for g in grad_mixed]

    def back(i, *gates):
        return attend_back(meta, x_t, qkv[i], mixed_t[i], grad_mixed[i], lse[i], *gates)

    other_qkv, qkv_send, other_bias = back(1, *gates)
    gates = (qkv_send,)
    if fast:
        down_piece, qkv_send = together(down_piece, qkv_send)
        gates = (qkv_send, up_plane[1], up_plane[2])
    mine_qkv, qkv_keep, mine_bias = back(0, *gates)
    gates = (qkv_keep,)
    if fast:
        qkv_plane = plane_sends(qkv_keep, swap(qkv_send, CORE))
        down_x, qkv_plane[0], *up_plane = together(
            swap(down_piece, X), qkv_plane[0], *up_plane
        )
        down_both = jnp.stack([down_piece, down_x])
        up_parts_sum = plane_sum(up_plane)
        up_near = swap(jnp.stack(up_parts_sum[2:]), NEAR)
        down_quarters = down_both, swap(down_both, CORE)
        gates = (qkv_plane[0], up_parts_sum[0])
    (input_grad,) = by_tile(
        input_kernel,
        "input_grad",
        10,
        meta,
        (grad_branch, mine_qkv.reshape(rows, -1), other_qkv.reshape(rows, -1)),
        qkv_w,
        gates,
        ((row, width, F32),),
        ((width, 3 * half), (width, 3 * half)),
    )

    (total,) = small_call(
        sums_kernel,
        "sums",
        meta,
        (vec_one, vec_two, grad_b_up, mine_bias, other_bias),
        ((16, width),),
        gates=gates[:1],
    )
    if fast:
        came, input_grad, up_near, *qkv_plane[1:3] = together(
            swap(total, CORE), input_grad, up_near, *qkv_plane[1:3]
        )
        total = total + came
        up_low = [add(up_parts_sum[i], up_near[i]) for i in range(2)]
        came, up_far, qkv_plane[3] = together(
            swap(total, X), swap(up_low[1], FAR), qkv_plane[3]
        )
        total = total + came
        up_piece = add(up_low[0], up_far)
        qkv_parts_sum = plane_sum(qkv_plane)
        qkv_hops = [swap(qkv_parts_sum[i], m) for i, m in ((1, FAR), (2, NEAR), (3, NEAR | FAR))]
        came, up_x, *qkv_hops = together(swap(total, Y), swap(up_piece, X), *qkv_hops)
        total = total + came
        up_both = jnp.stack([up_piece, up_x])
        qkv_piece = add(qkv_parts_sum[0], *qkv_hops)
        came, up_core, qkv_x = together(
            swap(total, NEAR), swap(up_both, CORE), swap(qkv_piece, X)
        )
        total = total + came
        total = total + swap(total, FAR)
        up_quarters = up_both, up_core
        qkv_both = jnp.stack([qkv_piece, qkv_x])
        qkv_quarters = qkv_both, swap(qkv_both, CORE)
        sums = small_call(
            functools.partial(own_sums_kernel, block),
            "own_sums",
            meta,
            (total,),
            ((block,),) * 8 + (b_up.shape,),
        )
        step = up_cut + out_cut
        up_moves = [
            move
            for g in range(groups)
            for move in (
                (slice(g * step, g * step + up_cut), 0, g * up_cut, hidden_width // 2),
                (slice(g * step + up_cut, (g + 1) * step), 1, g * out_cut, half),
            )
        ]
        qkv_moves = [(slice(k * half, (k + 1) * half), 0, k * width, half) for k in range(3)]
        (grad_w_down,) = finish(
            meta,
            down_quarters,
            [(slice(0, width), 0, 0, 0)],
            w_down.shape[0] // 2,
            [w_down.shape],
        )
        grad_w_up, grad_w_out = finish(meta, up_quarters, up_moves, 0, [w_up.shape, w_out.shape])
        (grad_w_qkv,) = finish(meta, qkv_quarters, qkv_moves, 0, [w_qkv.shape])
    else:
        total_of = lambda a: lax.psum(
            lax.psum_scatter(a, "shard", scatter_dimension=0, tiled=True), "rep"
        )
        sums = [total_of(g) for g in (*total[:8], total[8:12].reshape(-1))]
        order = [turned(p) for p in range(BLOCKS)]
        down_keep, down_send, up_keep, up_send = (
            a[:, order] for a in (down_keep, down_send, up_keep, up_send)
        )
        down = jnp.stack([down_keep, down_send]).transpose(2, 0, 1, 3, 4)
        grad_w_down = total_of(down.reshape(hidden_width, width).astype(F32))
        up = jnp.stack([up_keep, up_send]).reshape(
            2, 2, BLOCKS, quarter, groups, up_cut + out_cut
        )
        up = up.transpose(2, 1, 3, 0, 4, 5)
        grad_w_up = total_of(up[..., :up_cut].reshape(width, hidden_width).astype(F32))
        grad_w_out = total_of(up[..., up_cut:].reshape(width, width).astype(F32))
        qkv_sum = jnp.stack([qkv_keep[:, order], qkv_send[:, order]])
        qkv_sum = qkv_sum.reshape(2, 2, BLOCKS, quarter, 3, half)
        qkv_sum = qkv_sum.transpose(2, 1, 3, 4, 0, 5).reshape(width, 3 * width)
        grad_w_qkv = total_of(qkv_sum.astype(F32))
    return (
        layer_out.reshape(seqs, seq_len, width),
        input_grad.reshape(seqs, seq_len, width),
        grad_w_qkv,
        sums[0],
        sums[1],
        grad_w_out,
        sums[2],
        sums[3],
        sums[4],
        grad_w_up,
        sums[8],
        grad_w_down,
        sums[5],
        sums[6],
        sums[7],
    )


def solution(mesh):
    fast = mesh.shape["shard"] == BLOCKS and mesh.shape["rep"] == 4
    by_seq = P(("shard", "rep"), None, None)
    one, two = P("shard"), P("shard", None)
    in_specs = (by_seq, P(("shard", "rep")), two, one, one, two, one, one, one)
    in_specs = in_specs + (two, one, two, one, one, one, by_seq)
    out_specs = (by_seq, by_seq, two, one, one, two, one, one, one, two, one, two, one, one, one)
    return jax.shard_map(
        functools.partial(local, fast),
        mesh=mesh,
        in_specs=in_specs,
        out_specs=out_specs,
        check_vma=False,
    )
```
